256 devices in a mesh: layer: 4 (over x), plane: 64 (over y, z, core).
Axes of the slice: x: 4, y: 4, z: 8, core: 2. Of those that a mesh axis runs over, the one named last changes fastest.
Arguments:
- basis_init: float32 [8, 64, 512, 128], P(None, 'layer', 'plane'), may hold values from 0.05 to 1
- permeability: float32 [64, 512, 128], P('layer', 'plane'), may hold values from 0.02 to 0.2
- accumulation: float32 [64, 512, 128], P('layer', 'plane'), may hold values from 0.002 to 0.02
- pressure: float32 [64, 512, 128], P('layer', 'plane'), may hold values from -1.2 to 1.2
- source: float32 [64, 512, 128], P('layer', 'plane'), may hold values from -0.6 to 0.6
- support: int32 [8, 64, 512, 128], P(None, 'layer', 'plane'), may hold values from 0 to 1, as said below
- block_of: int32 [64, 512, 128], P('layer', 'plane'), may hold values from 0 to 9359, as said below
- curve_rank: int32 [9360], replicated, may hold values from 0 to 9359, as said below
Outputs:
- smoothed_basis: float32 [8, 64, 512, 128], P(None, 'layer', 'plane')
- coarse_matrix: float32 [27, 9472], P(None, ('layer', 'plane'))
- coarse_residual: float32 [9472], P(('layer', 'plane'))
The draws below stay inside these ranges and needn't reach their ends.
Inputs may be any that keep to these rules, and one draw needn't show every extreme that they name: `block_of`: cells with equal (z + 4) // 8, (x + 4) // 8 and y // 8 share one label, and distinct such bricks carry distinct labels. `curve_rank`: A permutation of the block labels' positions along the curve. `support`: slot 0 is 1 at every cell; a slot is 0 wherever its coarse block lies outside the 9 x 65 x 16 coarse grid.
All inputs are finite; a program needn't handle non-finite values.
Results may differ from the reference program's by a relative error of at most 0.00022.
Values sent between devices are 32-bit elements; how exact they have to be, the bound alone decides.
A program may use at most 128 MiB of HBM per device.

```python
import math
import jax
import jax.numpy as jnp

NY = 128
SLOTS = 8
ITERS = 2
NZ = 64
NX = 512
CBX = 65
CBY = 16
NBLK = 9360
ROWS = 9472


def shared_labels(key):
    return jax.random.permutation(key, NBLK).astype(jnp.int32)


def draw_block_of(key, part):
    labels = shared_labels(key)
    z_block = (jnp.arange(NZ) + 4) // 8
    x_block = (jnp.arange(NX) + 4) // 8
    y_block = jnp.arange(NY) // 8
    geometric = (z_block[:, None, None] * CBX + x_block[None, :, None]) * CBY + y_block[None, None, :]
    return labels[geometric].astype(jnp.int32)


def draw_curve_rank(key, part):
    key = jax.random.fold_in(key, 2)
    return jax.random.permutation(key, NBLK).astype(jnp.int32)


def draw_support(key, part):
    key = jax.random.fold_in(key, 3)
    coin_flip = jax.random.randint(key, (SLOTS, NZ, NX, NY), 0, 4) > 0
    y_pos = jnp.arange(NY)
    toward = jnp.where(y_pos % 8 >= 4, 1, -1)
    y_far = y_pos // 8 + toward
    inside_y = (y_far >= 0) & (y_far < CBY)
    y_bit = jnp.arange(SLOTS) % 2
    inside = jnp.where(y_bit[:, None] == 1, inside_y[None, :], True)
    support_on = coin_flip & inside[:, None, None, :]
    support_on = support_on.at[0].set(True)
    return support_on.astype(jnp.int32)


def block_scale(own_key, shape, pieces, smallest, top_value):
    level, own = 1.0, jax.random.fold_in(own_key, 6)
    for dim, parts in pieces:
        heights = jnp.exp(jax.random.uniform(jax.random.fold_in(own, dim), (parts,), jnp.float32, smallest / len(pieces), top_value / len(pieces)))
        level = level * jnp.repeat(heights, shape[dim] // parts).reshape([-1 if axis == dim else 1 for axis in range(len(shape))])
    return level


def scatter_about(key, extent, deviation, reach, shards=(), kind=jnp.bfloat16):
    array = jax.random.normal(key, extent, jnp.float32) * deviation
    if len(shards) > 0:
        array = block_scale(key, extent, shards, -0.22, 0.18) * array
    return jnp.clip(array, min=-reach, max=reach).astype(kind)


def setup_inputs(seed: int = 0) -> dict:
    key_list = jax.random.split(jax.random.key(seed), 9)
    return {
        "basis_init": jnp.clip(0.05 + 0.95 * jax.random.uniform(key_list[0], (SLOTS, NZ, NX, NY), jnp.float32) ** block_scale(key_list[0], (SLOTS, NZ, NX, NY), ((1, 4), (2, 64)), -0.2, 0.2), 0.05, 1.0),
        "permeability": jnp.clip(jnp.exp(math.log(0.2) - 2.3025851 * jax.random.uniform(key_list[1], (NZ, NX, NY), jnp.float32) ** block_scale(key_list[1], (NZ, NX, NY), ((0, 4), (1, 64)), -0.2, 0.2)), 0.02, 0.2),
        "accumulation": jnp.clip(jnp.exp(math.log(0.02) - 2.30258502 * jax.random.uniform(key_list[2], (NZ, NX, NY), jnp.float32) ** block_scale(key_list[2], (NZ, NX, NY), ((0, 4), (1, 64)), -0.2, 0.2)), 0.002, 0.02),
        "pressure": scatter_about(key_list[3], (NZ, NX, NY), 0.2, 1.2, ((0, 4), (1, 64)), jnp.float32),
        "source": scatter_about(key_list[4], (NZ, NX, NY), 0.1, 0.6, ((0, 4), (1, 64)), jnp.float32),
        "support": draw_support(jax.random.fold_in(key_list[8], 71), 0),
        "block_of": draw_block_of(jax.random.fold_in(key_list[8], 71), 0),
        "curve_rank": draw_curve_rank(jax.random.fold_in(key_list[8], 71), 0),
    }


OMEGA = 2.0 / 3.0
CELL_SHIFTS = (4, 4, 0)


def two_blocks(where_at, shift_by):
    moved_pos = where_at + shift_by
    anchor = moved_pos // 8
    toward = jnp.where(moved_pos % 8 >= 4, 1, -1)
    return jnp.stack([anchor, anchor + toward]).astype(jnp.int32)


def make_coords(positions):
    home_q, lower_q, upper_q = [], [], []
    for grid_dim in range(3):
        where_at = positions[grid_dim]
        shift_by = CELL_SHIFTS[grid_dim]
        home_q.append(two_blocks(where_at, shift_by))
        lower_q.append(two_blocks(where_at - 1, shift_by))
        upper_q.append(two_blocks(where_at + 1, shift_by))
    return tuple(home_q), tuple(lower_q), tuple(upper_q)


def near_slice(padded, grid_dim, side_sign):
    windows = [slice(1, -1)] * 3
    windows[grid_dim] = slice(0, -2) if side_sign < 0 else slice(2, None)
    leading = [slice(None)] * (padded.ndim - 3)
    return padded[tuple(leading + windows)]


def pick_same(beside_vals, home_blocks, beside_blocks, grid_dim):
    agree = (home_blocks[:, None, :] == beside_blocks[None, :, :]).astype(jnp.float32)
    shape_one = [2, 2, 1, 1, 1]
    shape_one[2 + grid_dim] = home_blocks.shape[1]
    agree = agree.reshape(shape_one)
    leading = jnp.moveaxis(beside_vals, grid_dim, 0)
    result = agree[:, 0][:, None, None] * leading[0][None] + agree[:, 1][:, None, None] * leading[1][None]
    return jnp.moveaxis(result, 0, grid_dim)


def apply_basis(basis_now, padded, rock_perm, rock_padded, accum_rate, coords):
    home_q, lower_q, upper_q = coords
    applied = accum_rate * basis_now
    diagonal = accum_rate
    for grid_dim in range(3):
        for side_sign, beside_q in ((-1, lower_q), (1, upper_q)):
            beside_vals = near_slice(padded, grid_dim, side_sign)
            beside_perm = near_slice(rock_padded, grid_dim, side_sign)
            transmit = 2.0 * rock_perm * beside_perm / (rock_perm + beside_perm)
            matched = pick_same(beside_vals, home_q[grid_dim], beside_q[grid_dim], grid_dim)
            applied = applied + transmit * (basis_now - matched)
            diagonal = diagonal + transmit
    return applied, diagonal


def apply_scalar(field, padded, rock_perm, rock_padded, accum_rate):
    applied = accum_rate * field
    for grid_dim in range(3):
        for side_sign in (-1, 1):
            beside_vals = near_slice(padded, grid_dim, side_sign)
            beside_perm = near_slice(rock_padded, grid_dim, side_sign)
            transmit = 2.0 * rock_perm * beside_perm / (rock_perm + beside_perm)
            applied = applied + transmit * (field - beside_vals)
    return applied


def fold_bits(values, lookup, bit_axis, grid_dim):
    leading = jnp.moveaxis(values, bit_axis, 0)
    rest_nd = leading.ndim - 1
    shape_one = [1] * rest_nd
    shape_one[rest_nd - 3 + grid_dim] = lookup.shape[2]
    result = lookup[:, 0].reshape([3] + shape_one) * leading[0][None] + lookup[:, 1].reshape([3] + shape_one) * leading[1][None]
    return jnp.moveaxis(result, 0, bit_axis)


def block_terms(applied, residual, home_q):
    folded = applied
    for grid_dim in range(3):
        toward = home_q[grid_dim][1] - home_q[grid_dim][0]
        offset = jnp.stack([jnp.zeros_like(toward), toward])
        lookup = (offset[None] + 1 == jnp.arange(3)[:, None, None]).astype(jnp.float32)
        folded = fold_bits(folded, lookup, grid_dim, grid_dim)
    folded = folded.reshape((27,) + applied.shape[3:])
    return jnp.concatenate([folded, residual[None]], axis=0)


def sum_blocks(terms):
    padded = jnp.pad(terms, ((0, 0), (4, 4), (4, 4), (0, 0)))
    count, z_len, x_len, y_len = padded.shape
    grouped = padded.reshape(count, z_len // 8, 8, x_len // 8, 8, y_len // 8, 8)
    return grouped.sum(axis=(2, 4, 6)).reshape(count, -1)


def block_labels(block_of):
    z_len, x_len, y_len = block_of.shape
    rep_z = jnp.clip(8 * jnp.arange(z_len // 8 + 1) - 4, 0, z_len - 1)
    rep_x = jnp.clip(8 * jnp.arange(x_len // 8 + 1) - 4, 0, x_len - 1)
    rep_y = 8 * jnp.arange(y_len // 8)
    return block_of[rep_z[:, None, None], rep_x[None, :, None], rep_y[None, None, :]].reshape(-1)


def reference(basis_init, permeability, accumulation, pressure, source, support, block_of, curve_rank):
    coords = make_coords((jnp.arange(NZ), jnp.arange(NX), jnp.arange(NY)))
    grid_shape = (2, 2, 2, NZ, NX, NY)
    in_support = support.reshape(grid_shape).astype(jnp.float32)
    initial = basis_init.reshape(grid_shape) * in_support
    basis_now = initial / jnp.sum(initial, axis=(0, 1, 2))
    rock_padded = jnp.pad(permeability, 1)
    press_padded = jnp.pad(pressure, 1)
    for sweep_idx in range(ITERS):
        padded = jnp.pad(basis_now, ((0, 0),) * 3 + ((1, 1),) * 3)
        applied, diagonal = apply_basis(basis_now, padded, permeability, rock_padded, accumulation, coords)
        basis_now = in_support * (basis_now - OMEGA * applied / diagonal)
        basis_now = basis_now / jnp.sum(basis_now, axis=(0, 1, 2))
    padded = jnp.pad(basis_now, ((0, 0),) * 3 + ((1, 1),) * 3)
    applied, diagonal = apply_basis(basis_now, padded, permeability, rock_padded, accumulation, coords)
    residual = source - apply_scalar(pressure, press_padded, permeability, rock_padded, accumulation)
    partial_rows = sum_blocks(block_terms(applied, residual, coords[0]))
    row_ranks = curve_rank[block_labels(block_of)]
    dense_rows = jnp.zeros((28, ROWS), jnp.float32).at[:, row_ranks].set(partial_rows)
    return basis_now.reshape(SLOTS, NZ, NX, NY), dense_rows[:27], dense_rows[27]
```

```python
import functools

import jax
import jax.numpy as jnp
from jax import lax
from jax.experimental import pallas as pl
from jax.experimental.pallas import tpu as pltpu
from jax.sharding import PartitionSpec as P

MESH = pl.DeviceIdType.MESH
F32, BF16, I32 = jnp.float32, jnp.bfloat16, jnp.int32

YC, CC = 4, 2
THIRD, TWO_THIRDS = 1.0 / 3.0, 2.0 / 3.0
B0 = (0, 1, 4, 5)
A0 = (0, 1, 2, 3)


def roll_x(v, shift):
    rows = v.shape[0]
    return pltpu.roll(v.reshape(rows // 8, 8, 128), shift, 1).reshape(rows, 128)


def roll_y(v, shift):
    return pltpu.roll(v, shift, 1)


def harmonic(k, n):
    return 2.0 * k * n / (k + n)


def plane_sum(v):
    return v.reshape(-1, 8, 128).sum(axis=0)


def kernel(
    dims,
    bi_hbm, k_hbm, a_hbm, p_hbm, s_hbm, sup_hbm, blk_hbm, tab_hbm,
    v_out, cm_out, cr_out,
    bi, sup, kk, aa, pp, ss, blk, tab,
    v0, v1, sf, nn, tc, hx, hxs, hxr, hzs, hzr, hxs2, hxr2, hzs2, hzr2,
    rks, rkr, oh, xs, xb, es, cs, crv, hs, hr, ft,
    in_sem, out_sem, halo_s, halo_r, rk_s, rk_r, g_s, g_r, h_s, h_r,
):
    lx, plane, zc, own, width = dims
    gn, hn = lx * YC, zc * CC
    ml, mp = lax.axis_index("layer"), lax.axis_index("plane")
    my, mz, mc = mp // (zc * CC), (mp // CC) % zc, mp % CC

    def g_peer(r):
        dx, dy = r // YC, r % YC
        return ((ml + dx) % lx, (((my + dy) % YC) * zc + mz) * CC + mc)

    def g_inv(r):
        return ((lx - r // YC) % lx) * YC + (YC - r % YC) % YC

    def h_peer(r):
        dz, dc = r // CC, r % CC
        return (ml, (my * zc + (mz + dz) % zc) * CC + (mc + dc) % CC)

    def h_inv(r):
        return ((zc - r // CC) % zc) * CC + (CC - r % CC) % CC

    up_x, down_x = (ml, (mp + 1) % plane), (ml, (mp + plane - 1) % plane)
    up_z, down_z = ((ml + 1) % lx, mp), ((ml + lx - 1) % lx, mp)

    loads = [
        pltpu.make_async_copy(k_hbm, kk, in_sem.at[0]),
        pltpu.make_async_copy(bi_hbm, bi, in_sem.at[1]),
        pltpu.make_async_copy(sup_hbm, sup, in_sem.at[2]),
        pltpu.make_async_copy(blk_hbm, blk, in_sem.at[3]),
        pltpu.make_async_copy(tab_hbm, tab, in_sem.at[4]),
        pltpu.make_async_copy(a_hbm, aa, in_sem.at[5]),
        pltpu.make_async_copy(p_hbm, pp, in_sem.at[6]),
        pltpu.make_async_copy(s_hbm, ss, in_sem.at[7]),
    ]
    for load in loads:
        load.start()

    barrier = pltpu.get_barrier_semaphore()
    partners = [up_x, down_x]
    partners += [g_peer(r) for r in range(1, gn)] + [h_peer(r) for r in range(1, hn)]
    for who in partners:
        pl.semaphore_signal(barrier, inc=1, device_id=who, device_id_type=MESH)

    hx[...] = jnp.zeros_like(hx)

    lane = lax.broadcasted_iota(I32, (32, 128), 1)
    row = lax.broadcasted_iota(I32, (32, 128), 0)
    m, x = lane % 8, row % 8
    m1, x1 = m[:8], x[:8]
    is_m = [m == i for i in range(8)]
    is_x = [x == i for i in range(8)]

    loads[0].wait()
    loads[1].wait()
    loads[2].wait()

    def first(g, carry):
        rows = pl.ds(pl.multiple_of(g * 32, 32), 32)
        vals = []
        for s in range(8):
            on = sup[s, rows, :].astype(F32)
            sf[s, rows, :] = on
            vals.append(bi[s, rows, :] * on)
        total = sum(vals[1:], vals[0])
        inv = 1.0 / total
        for s in range(8):
            v0[s, rows, :] = vals[s] * inv
        return carry

    lax.fori_loop(0, 4, first, 0)

    def pack(v, xs_buf, zs_buf, extra):
        for i, s in enumerate(B0):
            xs_buf[0, extra + i] = v[s, pl.ds(0, 16, stride=8), :]
            xs_buf[1, extra + i] = v[s, pl.ds(7, 16, stride=8), :]
        for i, s in enumerate(A0):
            zs_buf[0, extra + i] = v[s, 0:8, :]
            zs_buf[1, extra + i] = v[s, 120:128, :]

    def exchange(xs_buf, xr_buf, zs_buf, zr_buf, base):
        copies = []
        for j, (src, dst, slot, who) in enumerate((
            (xs_buf.at[1], xr_buf.at[0], 0, up_x), (xs_buf.at[0], xr_buf.at[1], 1, down_x),
            (zs_buf.at[1], zr_buf.at[0], 2, up_z), (zs_buf.at[0], zr_buf.at[1], 3, down_z),
        )):
            copies.append(pltpu.make_async_remote_copy(
                src_ref=src, dst_ref=dst, send_sem=halo_s.at[base + j], recv_sem=halo_r.at[base + slot],
                device_id=who, device_id_type=MESH))
        for copy in copies:
            copy.start()
        return copies

    pack(v0, hxs, hzs, 1)
    hxs[0, 0] = kk[pl.ds(0, 16, stride=8), :]
    hxs[1, 0] = kk[pl.ds(7, 16, stride=8), :]
    hzs[0, 0] = kk[0:8, :]
    hzs[1, 0] = kk[120:128, :]

    pl.semaphore_wait(barrier, len(partners))
    sent = exchange(hxs, hxr, hzs, hzr, 0)

    loads[3].wait()
    loads[4].wait()
    label = blk[0, 0:1, :]
    for u, (j, r) in enumerate(((0, 0), (0, 4), (1, 0), (1, 4), (2, 0), (2, 4))):
        label = jnp.where(m1[0:1] == u, blk[j, r:r + 1, :], label)
    t_rows = tab.shape[0]
    l_hi, l_lo = label >> 7, label & 127
    w_iota = lax.broadcasted_iota(I32, (128, 128), 0)
    pick = jnp.where(w_iota == l_lo, 1.0, 0.0).astype(BF16)
    ranks = tab[...]
    parts = jnp.concatenate([(ranks >> 7).astype(F32), (ranks & 127).astype(F32)], axis=0).astype(BF16)
    looked = jnp.dot(parts, pick, preferred_element_type=F32)
    t_iota = lax.broadcasted_iota(I32, (t_rows, 128), 0)
    looked = looked[:t_rows] * 128.0 + looked[t_rows:]
    rank = jnp.sum(jnp.where(t_iota == l_hi, looked, 0.0), axis=0, keepdims=True)
    rank = jnp.where(m1[0:1] < 6, rank, -1.0).astype(I32)
    rks[...] = rank
    rkr[0] = rank
    rank_copies = []
    for r in range(1, gn):
        rank_copies.append(pltpu.make_async_remote_copy(
            src_ref=rks, dst_ref=rkr.at[g_inv(r)], send_sem=rk_s.at[r], recv_sem=rk_r.at[g_inv(r)],
            device_id=g_peer(r), device_id_type=MESH))
        rank_copies[-1].start()

    TYM, TYP, TYM1, TYP1, TXM, TXP, TXB, TZM, TZP, RD = range(10)
    k3 = kk[...]
    lane3 = lax.broadcasted_iota(I32, (128, 128), 1)
    x3 = lax.broadcasted_iota(I32, (128, 128), 0) % 8
    m3 = lane3 % 8
    tym = jnp.where(lane3 == 0, 0.0, harmonic(k3, roll_y(k3, 1)))
    typ = roll_y(tym, 127)
    tc[TYM] = tym
    tc[TYP] = typ
    tc[TYM1] = jnp.where(m3 == 4, 0.0, tym)
    tc[TYP1] = jnp.where(m3 == 3, 0.0, typ)
    txm = jnp.where(x3 == 0, 0.0, harmonic(k3, roll_x(k3, 1)))
    tc[TXM] = txm
    tc[TXP] = roll_x(txm, 7)
    tz = harmonic(k3[8:], k3[:-8])
    tc[TZM, 8:128, :] = tz
    tc[TZP, 0:120, :] = tz
    tc[TXB] = jnp.zeros((128, 128), F32)

    def inner(v):
        for g in range(4):
            lo, hi = 32 * g, 32 * g + 32
            rows = slice(lo, hi)
            coef = [tc[i, rows, :] for i in range(9)]
            vals = [v[s, rows, :] for s in range(8)]
            for s in range(8):
                here = vals[s]
                tm, tp = (coef[TYM1], coef[TYP1]) if s & 1 else (coef[TYM], coef[TYP])
                acc = tm * roll_y(jnp.where(is_m[7], vals[s ^ 1], here), 1)
                acc += tp * roll_y(jnp.where(is_m[0], vals[s ^ 1], here), 127)
                acc += coef[TXM] * roll_x(jnp.where(is_x[3], vals[s ^ 2], here), 1)
                acc += coef[TXP] * roll_x(jnp.where(is_x[4], vals[s ^ 2], here), 7)
                zero = jnp.zeros((8, 128), F32)
                if g in (1, 3):
                    below = coef[TZM][0:8] * v[s ^ 4, lo - 8:lo, :]
                elif g == 2 and s < 4:
                    below = coef[TZM][0:8] * v[s, lo - 8:lo, :]
                else:
                    below = zero
                if g in (0, 2):
                    above = coef[TZP][24:32] * v[s ^ 4, hi:hi + 8, :]
                elif g == 1 and s < 4:
                    above = coef[TZP][24:32] * v[s, hi:hi + 8, :]
                else:
                    above = zero
                acc += jnp.concatenate([below, coef[TZM][8:32] * here[0:24]], axis=0)
                acc += jnp.concatenate([coef[TZP][0:24] * here[8:32], above], axis=0)
                nn[s, rows, :] = acc

    def outer(v, new, zr_buf, extra):
        for g in range(4):
            rows = slice(32 * g, 32 * g + 32)
            rd, txb = tc[RD, rows, :], tc[TXB, rows, :]
            vals = []
            for s in range(8):
                near = nn[s, rows, :]
                if s in B0:
                    near += txb * hx[B0.index(s), rows, :]
                if s in A0 and g == 0:
                    near = jnp.concatenate(
                        [near[0:8] + tc[TZM, 0:8, :] * zr_buf[0, extra + s], near[8:32]], axis=0)
                if s in A0 and g == 3:
                    near = jnp.concatenate(
                        [near[0:24], near[24:32] + tc[TZP, 120:128, :] * zr_buf[1, extra + s]], axis=0)
                vals.append((v[s, rows, :] * THIRD + rd * near) * sf[s, rows, :])
            total = sum(vals[1:], vals[0])
            inv = 1.0 / total
            for s in range(8):
                new[s, rows, :] = vals[s] * inv

    def place_x(xr_buf, extra):
        for i in range(4):
            hx[i, pl.ds(0, 16, stride=8), :] = xr_buf[0, extra + i]
            hx[i, pl.ds(7, 16, stride=8), :] = xr_buf[1, extra + i]

    inner(v0)

    for load in loads[5:]:
        load.wait()
    for copy in sent:
        copy.wait_recv()

    k_first, k_last = kk[pl.ds(0, 16, stride=8), :], kk[pl.ds(7, 16, stride=8), :]
    tc[TXB, pl.ds(0, 16, stride=8), :] = jnp.where(mp > 0, harmonic(k_first, hxr[0, 0]), 0.0)
    tc[TXB, pl.ds(7, 16, stride=8), :] = jnp.where(mp < plane - 1, harmonic(k_last, hxr[1, 0]), 0.0)
    tc[TZM, 0:8, :] = jnp.where(ml > 0, harmonic(kk[0:8, :], hzr[0, 0]), 0.0)
    tc[TZP, 120:128, :] = jnp.where(ml < lx - 1, harmonic(kk[120:128, :], hzr[1, 0]), 0.0)
    diag = aa[...] + tc[TYM] + tc[TYP] + tc[TXM] + tc[TXP] + tc[TXB] + tc[TZM] + tc[TZP]
    tc[RD] = TWO_THIRDS / diag

    place_x(hxr, 1)
    outer(v0, v1, hzr, 1)

    pack(v1, hxs2, hzs2, 0)
    sent2 = exchange(hxs2, hxr2, hzs2, hzr2, 4)
    inner(v1)

    n_idx = hn * width
    idx = lax.broadcasted_iota(I32, (n_idx, 128), 0)
    peer = jnp.zeros_like(idx)
    for t in range(1, hn):
        peer += jnp.where(idx >= t * width, 1, 0)
    col = idx - peer * width
    dz, dc = peer // CC, peer % CC
    pz, pc = mz + dz, mc + dc
    pz = jnp.where(pz >= zc, pz - zc, pz)
    pc = jnp.where(pc >= CC, pc - CC, pc)
    dev = ml * plane + (my * zc + pz) * CC + pc
    want = dev * own + col
    wants = [jnp.where(col + q * width < own, want + q * width, -7) for q in range(4)]
    for copy in rank_copies:
        copy.wait_recv()

    def build(r, carry):
        lanes = pl.ds(pl.multiple_of(r * 128, 128), 128)
        have = rkr[r]
        for q in range(4):
            oh[q * n_idx:(q + 1) * n_idx, lanes] = jnp.where(wants[q] == have, 1.0, 0.0).astype(BF16)
        return carry

    lax.fori_loop(0, gn, build, 0)

    for copy in sent2:
        copy.wait_recv()
    place_x(hxr2, 0)
    outer(v1, v0, hzr2, 0)
    store = pltpu.make_async_copy(v0, v_out, out_sem.at[0])
    store.start()

    r_sum = [[None] * 4 for _ in range(9)]
    qx = [[None] * 4 for _ in range(9)]
    qy = [[None] * 4 for _ in range(9)]
    for g in range(4):
        lo = 32 * g
        rows = slice(lo, lo + 32)
        tym, typ, txm, txp = (tc[i, rows, :] for i in (TYM, TYP, TXM, TXP))
        sx0 = jnp.where(is_x[3], txp, 0.0) + jnp.where(is_x[4], txm, 0.0)
        sx1 = sx0 + tc[TXB, rows, :]
        sy0 = jnp.where(is_m[7], typ, 0.0) + jnp.where(is_m[0], tym, 0.0)
        sy1 = sy0 + jnp.where(is_m[3], typ, 0.0) + jnp.where(is_m[4], tym, 0.0)
        zero = jnp.zeros((24, 128), F32)
        lower, upper = tc[TZM, lo:lo + 8, :], tc[TZP, lo + 24:lo + 32, :]
        acc = aa[rows, :]
        if g in (0, 2):
            swap_t, far = upper, slice(lo + 32, lo + 40)
            az0 = acc + jnp.concatenate([zero, upper], axis=0)
            az1 = az0 + jnp.concatenate([lower, zero], axis=0)
        else:
            swap_t, far = lower, slice(lo - 8, lo)
            az0 = acc + jnp.concatenate([lower, zero], axis=0)
            az1 = az0 + jnp.concatenate([zero, upper], axis=0)
        dxy = [[az + sx for sx in (sx0, sx1)] for az in (az0, az1)]
        for s in range(8):
            a, b, c = s >> 2, (s >> 1) & 1, s & 1
            here = v0[s, rows, :]
            d = dxy[a][b] + (sy1 if c else sy0)
            r_sum[s][g] = plane_sum(d * here) - swap_t * v0[s ^ 4, far, :]
            qx[s][g] = plane_sum(sx0 * here)
            qy[s][g] = plane_sum(sy0 * here)
        here = pp[rows, :]
        d = dxy[0][0] + sy0
        r_sum[8][g] = plane_sum(d * here - ss[rows, :]) - swap_t * pp[far, :]
        qx[8][g] = plane_sum(sx0 * here)
        qy[8][g] = plane_sum(sy0 * here)

    def x_swap(q):
        return jnp.where(x1 == 3, roll_x(q, 7), jnp.where(x1 == 4, roll_x(q, 1), 0.0))

    def y_swap(q):
        return jnp.where(m1 == 7, roll_y(q, 127), jnp.where(m1 == 0, roll_y(q, 1), 0.0))

    full = [[None] * 4 for _ in range(9)]
    for s in range(9):
        for g in range(4):
            sx, sy = (s ^ 2, s ^ 1) if s < 8 else (8, 8)
            full[s][g] = r_sum[s][g] - x_swap(qx[sx][g]) - y_swap(qy[sy][g])

    nil = jnp.zeros((8, 128), F32)
    for j in range(3):
        for b in (1, 0):
            for pz in range(3):
                if pz == 1:
                    groups, a = ((0,), (1, 2), (3,))[j], 0
                elif pz == 0:
                    groups, a = ((), (1,), (3,))[j], 1
                else:
                    groups, a = ((0,), (2,), ())[j], 1
                for py in range(3):
                    s = 4 * a + 2 * b + (0 if py == 1 else 1)
                    term = nil
                    for i, g in enumerate(groups):
                        term = full[s][g] if i == 0 else term + full[s][g]
                    if py == 0:
                        term = jnp.where(m1 < 4, term, 0.0)
                    elif py == 2:
                        term = jnp.where(m1 >= 4, term, 0.0)
                    at = (1 - b) * 9 + 3 * pz + py
                    es[j, 8 * at:8 * at + 8, :] = term
        groups = ((0,), (1, 2), (3,))[j]
        term = full[8][groups[0]]
        for g in groups[1:]:
            term += full[8][g]
        es[j, 144:152, :] = -term
        es[j, 152:192, :] = jnp.zeros((40, 128), F32)

    m24 = lax.broadcasted_iota(I32, (24, 128), 1) % 8
    rows_out = jnp.zeros((24, 128), F32)
    for j in range(3):
        for xi in range(2):
            t = es[j, pl.ds(4 * xi, 24, stride=8), :]
            for i in range(1, 4):
                t += es[j, pl.ds(4 * xi + i, 24, stride=8), :]
            t += roll_y(t, 127)
            t += roll_y(t, 126)
            t += roll_y(t, 124)
            u = 2 * j + xi
            rows_out = jnp.where(m24 == u, roll_y(t, u) if u else t, rows_out)
    cs[...] = rows_out[0:20]
    crv[0] = rows_out[0:20]

    g_copies = []
    for r in range(1, gn):
        g_copies.append(pltpu.make_async_remote_copy(
            src_ref=cs, dst_ref=crv.at[g_inv(r)], send_sem=g_s.at[r], recv_sem=g_r.at[g_inv(r)],
            device_id=g_peer(r), device_id_type=MESH))
        g_copies[-1].start()

    xs[...] = jnp.zeros_like(xs)
    xb[64:128, :] = jnp.zeros((64, gn * 128), BF16)
    row20 = lax.broadcasted_iota(I32, (20, 128), 0)
    odd20 = lax.broadcasted_iota(I32, (20, 128), 1) % 2 == 1
    odd9 = lax.broadcasted_iota(I32, (9, 128), 1) % 2 == 1
    drop = (row20 < 9) & odd20
    for copy in g_copies:
        copy.wait_recv()

    def spread(r, carry):
        lanes = pl.ds(pl.multiple_of(r * 128, 128), 128)
        got = crv[r]
        xs[0:20, :] = jnp.where(drop, 0.0, got)
        xs[19:28, :] = jnp.where(odd9, got[0:9], 0.0)
        vals = xs[...]
        high = vals.astype(BF16)
        xb[0:32, lanes] = high
        xb[32:64, lanes] = (vals - high.astype(F32)).astype(BF16)
        return carry

    lax.fori_loop(0, gn, spread, 0)
    routed = lax.dot_general(
        oh[...], xb[...], (((1,), (1,)), ((), ())), preferred_element_type=F32)
    lane_n = lax.broadcasted_iota(I32, (n_idx, 128), 1)
    packed = jnp.zeros((n_idx, 128), F32)
    for q in range(4):
        part = routed[q * n_idx:(q + 1) * n_idx]
        both = jnp.where(lane_n < 32, part + roll_y(part, 96), 0.0)
        packed += roll_y(both, 32 * q) if q else both
    for r in range(hn):
        hs[r] = packed[r * width:(r + 1) * width]

    h_copies = []
    for r in range(1, hn):
        h_copies.append(pltpu.make_async_remote_copy(
            src_ref=hs.at[r], dst_ref=hr.at[h_inv(r)], send_sem=h_s.at[r], recv_sem=h_r.at[h_inv(r)],
            device_id=h_peer(r), device_id_type=MESH))
        h_copies[-1].start()
    ft[...] = jnp.zeros_like(ft)
    for copy in h_copies:
        copy.wait_recv()
    final = hs[0]
    for r in range(1, hn):
        final += hr[r]
    ft[0:width, :] = final
    turned = ft[...].T
    lane_f = lax.broadcasted_iota(I32, (32, 128), 1)
    done = jnp.zeros((32, 128), F32)
    for q in range(4):
        part = turned[32 * q:32 * q + 32]
        here = (lane_f >= q * width) & (lane_f < (q + 1) * width)
        done = jnp.where(here, roll_y(part, q * width) if q else part, done)
    for pz in range(3):
        for px, base in ((0, 19), (1, 9), (2, 0)):
            k = 9 * pz + 3 * px
            cm_out[k:k + 3, :] = done[base + 3 * pz:base + 3 * pz + 3, 0:own]
    cr_out[...] = done[18:19, 0:own]

    store.wait()
    for copy in sent + sent2 + rank_copies + g_copies + h_copies:
        copy.wait_send()


def per_device(sizes, basis_init, permeability, accumulation, pressure, source, support, block_of, curve_rank):
    lx, plane = sizes
    zc = plane // (YC * CC)
    gn, hn = lx * YC, zc * CC
    devices = lx * plane
    own = (curve_rank.shape[0] + devices - 1) // devices
    width = (own + 3) // 4
    flat = lambda v: v.reshape(v.shape[:-3] + (128, 128))
    t_rows = -(-curve_rank.shape[0] // 2048) * 16
    table = jnp.pad(curve_rank, (0, t_rows * 128 - curve_rank.shape[0])).reshape(t_rows, 128)
    labels = jnp.stack([block_of[0], block_of[4], block_of[12]])
    anywhere = pl.BlockSpec(memory_space=pl.ANY)
    vmem = pl.BlockSpec(memory_space=pltpu.VMEM)
    dma = pltpu.SemaphoreType.DMA
    cells = lambda *lead: pltpu.VMEM(lead + (128, 128), F32)
    basis, matrix, residual = pl.pallas_call(
        functools.partial(kernel, (lx, plane, zc, own, width)),
        out_shape=(
            jax.ShapeDtypeStruct((8, 128, 128), F32),
            jax.ShapeDtypeStruct((27, own), F32),
            jax.ShapeDtypeStruct((1, own), F32),
        ),
        in_specs=[anywhere] * 8,
        out_specs=(anywhere, vmem, vmem),
        scratch_shapes=[
            cells(8), pltpu.VMEM((8, 128, 128), I32), cells(), cells(), cells(), cells(),
            pltpu.VMEM((3, 8, 128), I32), pltpu.VMEM((t_rows, 128), I32),
            cells(8), cells(8), cells(8), cells(8), cells(10), cells(4),
            pltpu.VMEM((2, 5, 16, 128), F32), pltpu.VMEM((2, 5, 16, 128), F32),
            pltpu.VMEM((2, 5, 8, 128), F32), pltpu.VMEM((2, 5, 8, 128), F32),
            pltpu.VMEM((2, 4, 16, 128), F32), pltpu.VMEM((2, 4, 16, 128), F32),
            pltpu.VMEM((2, 4, 8, 128), F32), pltpu.VMEM((2, 4, 8, 128), F32),
            pltpu.VMEM((1, 128), I32), pltpu.VMEM((gn, 1, 128), I32),
            pltpu.VMEM((4 * hn * width, gn * 128), BF16),
            pltpu.VMEM((32, 128), F32), pltpu.VMEM((128, gn * 128), BF16),
            pltpu.VMEM((3, 192, 128), F32),
            pltpu.VMEM((20, 128), F32), pltpu.VMEM((gn, 20, 128), F32),
            pltpu.VMEM((hn, width, 128), F32), pltpu.VMEM((hn, width, 128), F32),
            pltpu.VMEM((128, 128), F32),
            dma((8,)), dma((1,)), dma((8,)), dma((8,)),
            dma((gn,)), dma((gn,)), dma((gn,)), dma((gn,)), dma((hn,)), dma((hn,)),
        ],
        compiler_params=pltpu.CompilerParams(
            collective_id=0, has_side_effects=True, vmem_limit_bytes=40 * 1024 * 1024),
        cost_estimate=pl.CostEstimate(flops=20_000_000, bytes_accessed=2_000_000, transcendentals=0),
    )(
        flat(basis_init), flat(permeability), flat(accumulation), flat(pressure), flat(source),
        flat(support), labels, table,
    )
    return basis.reshape(basis_init.shape), matrix, residual.reshape(own)


def solution(mesh):
    return jax.shard_map(
        functools.partial(per_device, (mesh.shape["layer"], mesh.shape["plane"])),
        mesh=mesh,
        in_specs=(
            P(None, "layer", "plane", None),
            P("layer", "plane", None),
            P("layer", "plane", None),
            P("layer", "plane", None),
            P("layer", "plane", None),
            P(None, "layer", "plane", None),
            P("layer", "plane", None),
            P(),
        ),
        out_specs=(
            P(None, "layer", "plane", None),
            P(None, ("layer", "plane")),
            P(("layer", "plane")),
        ),
        check_vma=False,
    )
```

```python
import functools

import jax
import jax.numpy as jnp
from jax import lax
from jax.experimental import pallas as pl
from jax.experimental.pallas import tpu as pltpu
from jax.sharding import PartitionSpec as P

MESH = pl.DeviceIdType.MESH
F32, BF16, I32 = jnp.float32, jnp.bfloat16, jnp.int32

YC, CC = 4, 2
VMEM_GRANT = 60 * 1024 * 1024
THIRD, TWO_THIRDS = 1.0 / 3.0, 2.0 / 3.0
B0 = (0, 1, 4, 5)
A0 = (0, 1, 2, 3)


def roll_x(v, shift):
    rows = v.shape[0]
    return pltpu.roll(v.reshape(rows // 8, 8, 128), shift, 1).reshape(rows, 128)


def roll_y(v, shift):
    return pltpu.roll(v, shift, 1)


def harmonic(k, n):
    return 2.0 * k * n / (k + n)


def plane_sum(v):
    return v.reshape(-1, 8, 128).sum(axis=0)


def kernel(
    dims,
    bi_hbm, k_hbm, a_hbm, p_hbm, s_hbm, sup_hbm, blk_hbm, cr_hbm,
    v_out, f_out,
    bi, sup, kk, aa, pp, ss, blk, cr1, tab,
    v0, v1, sf, nn, tc, ec, hx, hxs, hxr, hzs, hzr, hxs2, hxr2, hzs2, hzr2,
    rks, rkr, oh, xb, es, cs, crv, hs, hr,
    in_sem, out_sem, halo_s, halo_r, rk_s, rk_r, g_s, g_r, h_s, h_r,
):
    lx, plane, zc, own, width = dims
    gn, hn = lx * YC, zc * CC
    ml, mp = lax.axis_index("layer"), lax.axis_index("plane")
    my, mz, mc = mp // (zc * CC), (mp // CC) % zc, mp % CC

    def g_peer(r):
        dx, dy = r // YC, r % YC
        return ((ml + dx) % lx, (((my + dy) % YC) * zc + mz) * CC + mc)

    def g_inv(r):
        return ((lx - r // YC) % lx) * YC + (YC - r % YC) % YC

    def h_peer(r):
        dz, dc = r // CC, r % CC
        return (ml, (my * zc + (mz + dz) % zc) * CC + (mc + dc) % CC)

    def h_inv(r):
        return ((zc - r // CC) % zc) * CC + (CC - r % CC) % CC

    up_x, down_x = (ml, (mp + 1) % plane), (ml, (mp + plane - 1) % plane)
    up_z, down_z = ((ml + 1) % lx, mp), ((ml + lx - 1) % lx, mp)

    loads = [
        pltpu.make_async_copy(k_hbm, kk, in_sem.at[0]),
        pltpu.make_async_copy(bi_hbm, bi, in_sem.at[1]),
        pltpu.make_async_copy(sup_hbm, sup, in_sem.at[2]),
        pltpu.make_async_copy(a_hbm, aa, in_sem.at[3]),
        pltpu.make_async_copy(cr_hbm, cr1, in_sem.at[4]),
        pltpu.make_async_copy(p_hbm, pp, in_sem.at[5]),
        pltpu.make_async_copy(s_hbm, ss, in_sem.at[6]),
    ]
    for j, z in enumerate((0, 4, 12)):
        loads.append(pltpu.make_async_copy(blk_hbm.at[pl.ds(8 * z, 8)], blk.at[j], in_sem.at[7 + j]))
    for load in loads:
        load.start()

    barrier = pltpu.get_barrier_semaphore()
    partners = [up_x, down_x]
    partners += [g_peer(r) for r in range(1, gn)] + [h_peer(r) for r in range(1, hn)]
    for who in partners:
        pl.semaphore_signal(barrier, inc=1, device_id=who, device_id_type=MESH)

    hx[...] = jnp.zeros_like(hx)

    lane = lax.broadcasted_iota(I32, (32, 128), 1)
    row = lax.broadcasted_iota(I32, (32, 128), 0)
    m, x = lane % 8, row % 8
    m1, x1 = m[:8], x[:8]
    is_m = [m == i for i in range(8)]
    is_x = [x == i for i in range(8)]

    loads[0].wait()

    TYM, TYP, TYM1, TYP1, TXM, TXP, TXB, TZM, TZP, RD = range(10)
    k3 = kk[...]
    lane3 = lax.broadcasted_iota(I32, (128, 128), 1)
    x3 = lax.broadcasted_iota(I32, (128, 128), 0) % 8
    m3 = lane3 % 8
    tym = jnp.where(lane3 == 0, 0.0, harmonic(k3, roll_y(k3, 1)))
    typ = roll_y(tym, 127)
    tc[TYM] = tym
    tc[TYP] = typ
    tc[TYM1] = jnp.where(m3 == 4, 0.0, tym)
    tc[TYP1] = jnp.where(m3 == 3, 0.0, typ)
    txm = jnp.where(x3 == 0, 0.0, harmonic(k3, roll_x(k3, 1)))
    tc[TXM] = txm
    tc[TXP] = roll_x(txm, 7)
    tz = harmonic(k3[8:], k3[:-8])
    tc[TZM, 8:128, :] = tz
    tc[TZP, 0:120, :] = tz
    tc[TXB] = jnp.zeros((128, 128), F32)

    loads[1].wait()
    loads[2].wait()

    for g in range(4):
        rows = slice(32 * g, 32 * g + 32)
        vals = []
        for s in range(8):
            on = sup[s, rows, :].astype(F32)
            sf[s, rows, :] = on
            vals.append(bi[s, rows, :] * on)
        total = sum(vals[1:], vals[0])
        inv = 1.0 / total
        for s in range(8):
            v0[s, rows, :] = vals[s] * inv

    def pack(v, xs_buf, zs_buf, extra):
        for i, s in enumerate(B0):
            xs_buf[0, extra + i] = v[s, pl.ds(0, 16, stride=8), :]
            xs_buf[1, extra + i] = v[s, pl.ds(7, 16, stride=8), :]
        for i, s in enumerate(A0):
            zs_buf[0, extra + i] = v[s, 0:8, :]
            zs_buf[1, extra + i] = v[s, 120:128, :]

    def exchange(xs_buf, xr_buf, zs_buf, zr_buf, base):
        copies = []
        for j, (src, dst, slot, who) in enumerate((
            (xs_buf.at[1], xr_buf.at[0], 0, up_x), (xs_buf.at[0], xr_buf.at[1], 1, down_x),
            (zs_buf.at[1], zr_buf.at[0], 2, up_z), (zs_buf.at[0], zr_buf.at[1], 3, down_z),
        )):
            copies.append(pltpu.make_async_remote_copy(
                src_ref=src, dst_ref=dst, send_sem=halo_s.at[base + j], recv_sem=halo_r.at[base + slot],
                device_id=who, device_id_type=MESH))
        for copy in copies:
            copy.start()
        return copies

    pack(v0, hxs, hzs, 1)
    hxs[0, 0] = kk[pl.ds(0, 16, stride=8), :]
    hxs[1, 0] = kk[pl.ds(7, 16, stride=8), :]
    hzs[0, 0] = kk[0:8, :]
    hzs[1, 0] = kk[120:128, :]

    pl.semaphore_wait(barrier, len(partners))
    sent = exchange(hxs, hxr, hzs, hzr, 0)

    def inner(v):
        for g in range(4):
            lo, hi = 32 * g, 32 * g + 32
            rows = slice(lo, hi)
            coef = [tc[i, rows, :] for i in range(9)]
            vals = [v[s, rows, :] for s in range(8)]
            for s in range(8):
                here = vals[s]
                tm, tp = (coef[TYM1], coef[TYP1]) if s & 1 else (coef[TYM], coef[TYP])
                acc = tm * roll_y(jnp.where(is_m[7], vals[s ^ 1], here), 1)
                acc += tp * roll_y(jnp.where(is_m[0], vals[s ^ 1], here), 127)
                acc += coef[TXM] * roll_x(jnp.where(is_x[3], vals[s ^ 2], here), 1)
                acc += coef[TXP] * roll_x(jnp.where(is_x[4], vals[s ^ 2], here), 7)
                zero = jnp.zeros((8, 128), F32)
                if g in (1, 3):
                    below = coef[TZM][0:8] * v[s ^ 4, lo - 8:lo, :]
                elif g == 2 and s < 4:
                    below = coef[TZM][0:8] * v[s, lo - 8:lo, :]
                else:
                    below = zero
                if g in (0, 2):
                    above = coef[TZP][24:32] * v[s ^ 4, hi:hi + 8, :]
                elif g == 1 and s < 4:
                    above = coef[TZP][24:32] * v[s, hi:hi + 8, :]
                else:
                    above = zero
                acc += jnp.concatenate([below, coef[TZM][8:32] * here[0:24]], axis=0)
                acc += jnp.concatenate([coef[TZP][0:24] * here[8:32], above], axis=0)
                nn[s, rows, :] = acc

    def outer(v, new, zr_buf, extra):
        for g in range(4):
            rows = slice(32 * g, 32 * g + 32)
            rd, txb = tc[RD, rows, :], tc[TXB, rows, :]
            vals = []
            for s in range(8):
                near = nn[s, rows, :]
                if s in B0:
                    near += txb * hx[B0.index(s), rows, :]
                if s in A0 and g == 0:
                    near = jnp.concatenate(
                        [near[0:8] + tc[TZM, 0:8, :] * zr_buf[0, extra + s], near[8:32]], axis=0)
                if s in A0 and g == 3:
                    near = jnp.concatenate(
                        [near[0:24], near[24:32] + tc[TZP, 120:128, :] * zr_buf[1, extra + s]], axis=0)
                vals.append((v[s, rows, :] * THIRD + rd * near) * sf[s, rows, :])
            total = sum(vals[1:], vals[0])
            inv = 1.0 / total
            for s in range(8):
                new[s, rows, :] = vals[s] * inv

    def place_x(xr_buf, extra):
        for i in range(4):
            hx[i, pl.ds(0, 16, stride=8), :] = xr_buf[0, extra + i]
            hx[i, pl.ds(7, 16, stride=8), :] = xr_buf[1, extra + i]

    inner(v0)

    for load in loads[3:]:
        load.wait()
    for copy in sent:
        copy.wait_recv()

    k_first, k_last = kk[pl.ds(0, 16, stride=8), :], kk[pl.ds(7, 16, stride=8), :]
    tc[TXB, pl.ds(0, 16, stride=8), :] = jnp.where(mp > 0, harmonic(k_first, hxr[0, 0]), 0.0)
    tc[TXB, pl.ds(7, 16, stride=8), :] = jnp.where(mp < plane - 1, harmonic(k_last, hxr[1, 0]), 0.0)
    tc[TZM, 0:8, :] = jnp.where(ml > 0, harmonic(kk[0:8, :], hzr[0, 0]), 0.0)
    tc[TZP, 120:128, :] = jnp.where(ml < lx - 1, harmonic(kk[120:128, :], hzr[1, 0]), 0.0)
    diag = aa[...] + tc[TYM] + tc[TYP] + tc[TXM] + tc[TXP] + tc[TXB] + tc[TZM] + tc[TZP]
    tc[RD] = TWO_THIRDS / diag

    place_x(hxr, 1)
    outer(v0, v1, hzr, 1)

    pack(v1, hxs2, hzs2, 0)
    sent2 = exchange(hxs2, hxr2, hzs2, hzr2, 4)
    inner(v1)

    label = blk[0, 0:1, :]
    for u, (j, r) in enumerate(((0, 0), (0, 4), (1, 0), (1, 4), (2, 0), (2, 4))):
        label = jnp.where(m1[0:1] == u, blk[j, r:r + 1, :], label)
    t_rows = tab.shape[0]
    labels = cr1.shape[0]
    tab[labels // 128:, :] = jnp.zeros((t_rows - labels // 128, 128), I32)
    for t in range(labels // 128):
        tab[t:t + 1, :] = cr1[pl.ds(t * 128, 128)].reshape(1, 128)
    if labels % 128:
        t = labels // 128
        tab[t:t + 1, 0:labels % 128] = cr1[pl.ds(t * 128, labels % 128)].reshape(1, labels % 128)
    l_hi, l_lo = label >> 7, label & 127
    w_iota = lax.broadcasted_iota(I32, (128, 128), 0)
    pick = jnp.where(w_iota == l_lo, 1.0, 0.0).astype(BF16)
    ranks = tab[...]
    parts = jnp.concatenate([(ranks >> 7).astype(F32), (ranks & 127).astype(F32)], axis=0).astype(BF16)
    looked = jnp.dot(parts, pick, preferred_element_type=F32)
    t_iota = lax.broadcasted_iota(I32, (t_rows, 128), 0)
    looked = looked[:t_rows] * 128.0 + looked[t_rows:]
    rank = jnp.sum(jnp.where(t_iota == l_hi, looked, 0.0), axis=0, keepdims=True)
    rank = jnp.where(m1[0:1] < 6, rank, -1.0).astype(I32)
    rks[...] = rank
    rkr[0] = rank
    rank_copies = []
    for r in range(1, gn):
        rank_copies.append(pltpu.make_async_remote_copy(
            src_ref=rks, dst_ref=rkr.at[g_inv(r)], send_sem=rk_s.at[r], recv_sem=rk_r.at[g_inv(r)],
            device_id=g_peer(r), device_id_type=MESH))
        rank_copies[-1].start()

    def swaps(g):
        lo = 32 * g
        if g in (0, 2):
            return tc[TZP, lo + 24:lo + 32, :], slice(lo + 32, lo + 40)
        return tc[TZM, lo:lo + 8, :], slice(lo - 8, lo)

    r_sum = [[None] * 4 for _ in range(9)]
    qx = [[None] * 4 for _ in range(9)]
    qy = [[None] * 4 for _ in range(9)]
    zero = jnp.zeros((24, 128), F32)
    for g in range(4):
        lo = 32 * g
        rows = slice(lo, lo + 32)
        tym, typ, txm, txp = (tc[i, rows, :] for i in (TYM, TYP, TXM, TXP))
        sx0 = jnp.where(is_x[3], txp, 0.0) + jnp.where(is_x[4], txm, 0.0)
        sx1 = sx0 + tc[TXB, rows, :]
        sy0 = jnp.where(is_m[7], typ, 0.0) + jnp.where(is_m[0], tym, 0.0)
        sy1 = sy0 + jnp.where(is_m[3], typ, 0.0) + jnp.where(is_m[4], tym, 0.0)
        lower, upper = tc[TZM, lo:lo + 8, :], tc[TZP, lo + 24:lo + 32, :]
        acc = aa[rows, :]
        if g in (0, 2):
            az0 = acc + jnp.concatenate([zero, upper], axis=0)
            az1 = az0 + jnp.concatenate([lower, zero], axis=0)
        else:
            az0 = acc + jnp.concatenate([lower, zero], axis=0)
            az1 = az0 + jnp.concatenate([zero, upper], axis=0)
        for s in range(8):
            ec[s, rows, :] = (az1 if s & 4 else az0) + (sx1 if s & 2 else sx0) + (sy1 if s & 1 else sy0)
        ec[8, rows, :] = sx0
        ec[9, rows, :] = sy0
        here = pp[rows, :]
        swap_t, far = swaps(g)
        r_sum[8][g] = plane_sum((az0 + sx0 + sy0) * here - ss[rows, :]) - swap_t * pp[far, :]
        qx[8][g] = plane_sum(sx0 * here)
        qy[8][g] = plane_sum(sy0 * here)

    for copy in sent2:
        copy.wait_recv()
    place_x(hxr2, 0)
    outer(v1, v0, hzr2, 0)
    store = pltpu.make_async_copy(v0, v_out, out_sem.at[0])
    store.start()

    for g in range(4):
        lo = 32 * g
        rows = slice(lo, lo + 32)
        sx0, sy0 = ec[8, rows, :], ec[9, rows, :]
        swap_t, far = swaps(g)
        for s in range(8):
            here = v0[s, rows, :]
            r_sum[s][g] = plane_sum(ec[s, rows, :] * here) - swap_t * v0[s ^ 4, far, :]
            qx[s][g] = plane_sum(sx0 * here)
            qy[s][g] = plane_sum(sy0 * here)

    def x_swap(q):
        return jnp.where(x1 == 3, roll_x(q, 7), jnp.where(x1 == 4, roll_x(q, 1), 0.0))

    def y_swap(q):
        return jnp.where(m1 == 7, roll_y(q, 127), jnp.where(m1 == 0, roll_y(q, 1), 0.0))

    full = [[None] * 4 for _ in range(9)]
    for s in range(9):
        for g in range(4):
            sx, sy = (s ^ 2, s ^ 1) if s < 8 else (8, 8)
            full[s][g] = r_sum[s][g] - x_swap(qx[sx][g]) - y_swap(qy[sy][g])

    nil = jnp.zeros((8, 128), F32)
    for j in range(3):
        for b in (1, 0):
            for pz in range(3):
                if pz == 1:
                    groups, a = ((0,), (1, 2), (3,))[j], 0
                elif pz == 0:
                    groups, a = ((), (1,), (3,))[j], 1
                else:
                    groups, a = ((0,), (2,), ())[j], 1
                for py in range(3):
                    s = 4 * a + 2 * b + (0 if py == 1 else 1)
                    term = nil
                    for i, g in enumerate(groups):
                        term = full[s][g] if i == 0 else term + full[s][g]
                    if py == 0:
                        term = jnp.where(m1 < 4, term, 0.0)
                    elif py == 2:
                        term = jnp.where(m1 >= 4, term, 0.0)
                    at = (1 - b) * 9 + 3 * pz + py
                    es[j, 8 * at:8 * at + 8, :] = term
        groups = ((0,), (1, 2), (3,))[j]
        term = full[8][groups[0]]
        for g in groups[1:]:
            term += full[8][g]
        es[j, 144:152, :] = -term
        es[j, 152:192, :] = jnp.zeros((40, 128), F32)

    m24 = lax.broadcasted_iota(I32, (24, 128), 1) % 8
    rows_out = jnp.zeros((24, 128), F32)
    for j in range(3):
        for xi in range(2):
            t = es[j, pl.ds(4 * xi, 24, stride=8), :]
            for i in range(1, 4):
                t += es[j, pl.ds(4 * xi + i, 24, stride=8), :]
            t += roll_y(t, 127)
            t += roll_y(t, 126)
            t += roll_y(t, 124)
            u = 2 * j + xi
            rows_out = jnp.where(m24 == u, roll_y(t, u) if u else t, rows_out)
    cs[...] = rows_out
    crv[0] = rows_out

    g_copies = []
    for r in range(1, gn):
        g_copies.append(pltpu.make_async_remote_copy(
            src_ref=cs, dst_ref=crv.at[g_inv(r)], send_sem=g_s.at[r], recv_sem=g_r.at[g_inv(r)],
            device_id=g_peer(r), device_id_type=MESH))
        g_copies[-1].start()

    n_idx = hn * width
    idx = lax.broadcasted_iota(I32, (n_idx, 128), 0)
    peer = jnp.zeros_like(idx)
    for t in range(1, hn):
        peer += jnp.where(idx >= t * width, 1, 0)
    col = idx - peer * width
    dz, dc = peer // CC, peer % CC
    pz, pc = mz + dz, mc + dc
    pz = jnp.where(pz >= zc, pz - zc, pz)
    pc = jnp.where(pc >= CC, pc - CC, pc)
    dev = ml * plane + (my * zc + pz) * CC + pc
    want = dev * own + col
    wants = [jnp.where(col + q * width < own, want + q * width, -7) for q in range(4)]
    for copy in rank_copies:
        copy.wait_recv()

    def build(r, carry):
        lanes = pl.ds(pl.multiple_of(r * 128, 128), 128)
        have = rkr[r]
        for q in range(4):
            oh[q * n_idx:(q + 1) * n_idx, lanes] = jnp.where(wants[q] == have, 1.0, 0.0).astype(BF16)
        return carry

    lax.fori_loop(0, gn, build, 0)

    xb[64:128, :] = jnp.zeros((64, gn * 128), BF16)
    odd = m1 % 2 == 1
    for copy in g_copies:
        copy.wait_recv()
    for r in range(gn):
        got = [crv[r, 8 * i:8 * i + 8, :] for i in range(3)]
        turn = [pltpu.roll(jnp.where(odd, got[i], 0.0), 3, 0) for i in range(2)]
        vals = jnp.concatenate([
            jnp.where(odd, 0.0, got[0]), jnp.where(odd & (x1 == 0), 0.0, got[1]),
            jnp.where(x1 < 3, got[2], turn[0]), jnp.where(x1 < 3, turn[0], turn[1])], axis=0)
        high = vals.astype(BF16)
        lanes = slice(128 * r, 128 * r + 128)
        xb[0:32, lanes] = high
        xb[32:64, lanes] = (vals - high.astype(F32)).astype(BF16)
    routed = lax.dot_general(
        oh[...], xb[...], (((1,), (1,)), ((), ())), preferred_element_type=F32)
    lane_n = lax.broadcasted_iota(I32, (n_idx, 128), 1)
    packed = jnp.zeros((n_idx, 128), F32)
    for q in range(4):
        part = routed[q * n_idx:(q + 1) * n_idx]
        both = jnp.where(lane_n < 32, part + roll_y(part, 96), 0.0)
        packed += roll_y(both, 32 * q) if q else both
    for r in range(hn):
        hs[r] = packed[r * width:(r + 1) * width]

    h_copies = []
    for r in range(1, hn):
        h_copies.append(pltpu.make_async_remote_copy(
            src_ref=hs.at[r], dst_ref=hr.at[h_inv(r)], send_sem=h_s.at[r], recv_sem=h_r.at[h_inv(r)],
            device_id=h_peer(r), device_id_type=MESH))
        h_copies[-1].start()
    for copy in h_copies:
        copy.wait_recv()
    final = hs[0]
    for r in range(1, hn):
        final += hr[r]
    f_out[0:width, :] = final

    store.wait()
    for copy in sent + sent2 + rank_copies + g_copies + h_copies:
        copy.wait_send()


def finish(own, width, v_in, f_in, v_out, cm_out, cr_out, ft, sem):
    store = pltpu.make_async_copy(v_in, v_out, sem)
    store.start()
    ft[0:16, :] = f_in[...]
    turned = ft[...].T
    lane = lax.broadcasted_iota(I32, (32, 128), 1)
    done = jnp.zeros((32, 128), F32)
    for q in range(4):
        part = turned[32 * q:32 * q + 32]
        here = (lane >= q * width) & (lane < (q + 1) * width)
        done = jnp.where(here, pltpu.roll(part, q * width, 1) if q else part, done)
    for pz in range(3):
        for px, base in ((0, 19), (1, 9), (2, 0)):
            k = 9 * pz + 3 * px
            cm_out[k:k + 3, :] = done[base + 3 * pz:base + 3 * pz + 3, 0:own]
    cr_out[...] = done[18:19, 0:own]
    store.wait()


def per_device(sizes, basis_init, permeability, accumulation, pressure, source, support, block_of, curve_rank):
    lx, plane = sizes
    zc = plane // (YC * CC)
    gn, hn = lx * YC, zc * CC
    devices = lx * plane
    own = (curve_rank.shape[0] + devices - 1) // devices
    width = (own + 3) // 4
    flat = lambda v: v.reshape(v.shape[:-3] + (128, 128))
    t_rows = -(-curve_rank.shape[0] // 2048) * 16
    anywhere = pl.BlockSpec(memory_space=pl.ANY)
    vmem = pl.BlockSpec(memory_space=pltpu.VMEM)
    dma = pltpu.SemaphoreType.DMA
    cells = lambda *lead: pltpu.VMEM(lead + (128, 128), F32)
    basis, rows = pl.pallas_call(
        functools.partial(kernel, (lx, plane, zc, own, width)),
        out_shape=(
            jax.ShapeDtypeStruct((8, 128, 128), F32),
            jax.ShapeDtypeStruct((16, 128), F32),
        ),
        in_specs=[anywhere] * 8,
        out_specs=(anywhere, vmem),
        scratch_shapes=[
            cells(8), pltpu.VMEM((8, 128, 128), I32), cells(), cells(), cells(), cells(),
            pltpu.VMEM((3, 8, 128), I32), pltpu.VMEM(curve_rank.shape, I32), pltpu.VMEM((t_rows, 128), I32),
            cells(8), cells(8), cells(8), cells(8), cells(10), cells(10), cells(4),
            pltpu.VMEM((2, 5, 16, 128), F32), pltpu.VMEM((2, 5, 16, 128), F32),
            pltpu.VMEM((2, 5, 8, 128), F32), pltpu.VMEM((2, 5, 8, 128), F32),
            pltpu.VMEM((2, 4, 16, 128), F32), pltpu.VMEM((2, 4, 16, 128), F32),
            pltpu.VMEM((2, 4, 8, 128), F32), pltpu.VMEM((2, 4, 8, 128), F32),
            pltpu.VMEM((1, 128), I32), pltpu.VMEM((gn, 1, 128), I32),
            pltpu.VMEM((4 * hn * width, gn * 128), BF16),
            pltpu.VMEM((128, gn * 128), BF16),
            pltpu.VMEM((3, 192, 128), F32),
            pltpu.VMEM((24, 128), F32), pltpu.VMEM((gn, 24, 128), F32),
            pltpu.VMEM((hn, width, 128), F32), pltpu.VMEM((hn, width, 128), F32),
            dma((10,)), dma((1,)), dma((8,)), dma((8,)),
            dma((gn,)), dma((gn,)), dma((gn,)), dma((gn,)), dma((hn,)), dma((hn,)),
        ],
        compiler_params=pltpu.CompilerParams(
            collective_id=0, has_side_effects=True, vmem_limit_bytes=VMEM_GRANT),
        cost_estimate=pl.CostEstimate(flops=20_000_000, bytes_accessed=2_000_000, transcendentals=0),
    )(
        flat(basis_init), flat(permeability), flat(accumulation), flat(pressure), flat(source),
        flat(support), flat(block_of), curve_rank,
    )
    basis, matrix, residual = pl.pallas_call(
        functools.partial(finish, own, width),
        out_shape=(
            jax.ShapeDtypeStruct((8, 128, 128), F32),
            jax.ShapeDtypeStruct((27, own), F32),
            jax.ShapeDtypeStruct((1, own), F32),
        ),
        in_specs=[anywhere, vmem],
        out_specs=(anywhere, vmem, vmem),
        scratch_shapes=[pltpu.VMEM((128, 128), F32), dma],
        compiler_params=pltpu.CompilerParams(vmem_limit_bytes=VMEM_GRANT),
    )(basis, rows)
    return basis.reshape(basis_init.shape), matrix, residual.reshape(own)


def solution(mesh):
    return jax.shard_map(
        functools.partial(per_device, (mesh.shape["layer"], mesh.shape["plane"])),
        mesh=mesh,
        in_specs=(
            P(None, "layer", "plane", None),
            P("layer", "plane", None),
            P("layer", "plane", None),
            P("layer", "plane", None),
            P("layer", "plane", None),
            P(None, "layer", "plane", None),
            P("layer", "plane", None),
            P(),
        ),
        out_specs=(
            P(None, "layer", "plane", None),
            P(None, ("layer", "plane")),
            P(("layer", "plane")),
        ),
        check_vma=False,
    )
```

```python
import functools

import jax
import jax.numpy as jnp
from jax import lax
from jax.experimental import pallas as pl
from jax.experimental.pallas import tpu as pltpu
from jax.sharding import PartitionSpec as P

MESH = pl.DeviceIdType.MESH
F32, BF16, I32 = jnp.float32, jnp.bfloat16, jnp.int32

YC, CC = 4, 2
VMEM_GRANT = 60 * 1024 * 1024
THIRD, TWO_THIRDS = 1.0 / 3.0, 2.0 / 3.0
B0 = (0, 1, 4, 5)
A0 = (0, 1, 2, 3)


def roll_x(v, shift):
    rows = v.shape[0]
    return pltpu.roll(v.reshape(rows // 8, 8, 128), shift, 1).reshape(rows, 128)


def roll_y(v, shift):
    return pltpu.roll(v, shift, 1)


def harmonic(k, n):
    return 2.0 * k * n / (k + n)


def plane_sum(v):
    return v.reshape(-1, 8, 128).sum(axis=0)


TYM, TYP, TYM1, TYP1, TXM, TXP, TZM, TZP, TZM1, TZP1, TXB, RD = range(12)


def kernel(
    dims,
    bi_hbm, k_hbm, a_hbm, p_hbm, s_hbm, sup_hbm, blk_hbm, cr_hbm,
    v_out, f_out,
    bi, sup, aa, pp, ss, blk, cr1, tab,
    va, vb, sf, nn, tc, tzb, ec, sw, fl, hx, hxs, hxr, hzr, hxs2, hxr2, hzr2,
    rks, rkr, wt, oh, xb, es, cs, crv, acc, hs, hr,
    in_sem, out_sem, halo_s, halo_r, rk_s, rk_r, g_s, g_r, h_s, h_r,
):
    lx, plane, zc, own, width = dims
    gn, hn = lx * YC, zc * CC
    n_idx = hn * width
    ml, mp = lax.axis_index("layer"), lax.axis_index("plane")
    my, mz, mc = mp // (zc * CC), (mp // CC) % zc, mp % CC

    def g_peer(r):
        dx, dy = r // YC, r % YC
        return ((ml + dx) % lx, (((my + dy) % YC) * zc + mz) * CC + mc)

    def g_inv(r):
        return ((lx - r // YC) % lx) * YC + (YC - r % YC) % YC

    def h_peer(r):
        dz, dc = r // CC, r % CC
        return (ml, (my * zc + (mz + dz) % zc) * CC + (mc + dc) % CC)

    def h_inv(r):
        return ((zc - r // CC) % zc) * CC + (CC - r % CC) % CC

    up_x, down_x = (ml, (mp + 1) % plane), (ml, (mp + plane - 1) % plane)
    up_z, down_z = ((ml + 1) % lx, mp), ((ml + lx - 1) % lx, mp)

    def loop(n, body, start=0):
        def step(i, carry):
            body(i)
            return carry

        lax.fori_loop(start, n, step, 0)

    def group(g):
        return pl.ds(pl.multiple_of(g * 32, 32), 32)

    def one_plane(z):
        return pl.ds(pl.multiple_of(z * 8, 8), 8)

    loads = [
        pltpu.make_async_copy(k_hbm, va.at[0], in_sem.at[0]),
        pltpu.make_async_copy(bi_hbm, bi, in_sem.at[1]),
        pltpu.make_async_copy(sup_hbm, sup, in_sem.at[2]),
        pltpu.make_async_copy(a_hbm, aa, in_sem.at[3]),
        pltpu.make_async_copy(cr_hbm, cr1, in_sem.at[4]),
        pltpu.make_async_copy(p_hbm, pp, in_sem.at[5]),
        pltpu.make_async_copy(s_hbm, ss, in_sem.at[6]),
    ]
    for j, z in enumerate((0, 4, 12)):
        loads.append(pltpu.make_async_copy(blk_hbm.at[pl.ds(8 * z, 8)], blk.at[j], in_sem.at[7 + j]))
    for load in loads:
        load.start()

    barrier = pltpu.get_barrier_semaphore()

    def greet(who):
        pl.semaphore_signal(barrier, inc=1, device_id=who, device_id_type=MESH)

    greet(up_x)
    greet(down_x)
    loop(gn, lambda r: greet(g_peer(r)), 1)
    loop(hn, lambda r: greet(h_peer(r)), 1)

    lane = lax.broadcasted_iota(I32, (32, 128), 1)
    m, x = lane % 8, lax.broadcasted_iota(I32, (32, 128), 0) % 8
    m1, x1 = m[:8], x[:8]
    lane1, row1 = lane[:8], x[:8]
    is_m = {i: m == i for i in (0, 3, 4, 7)}
    is_x = {i: x == i for i in (3, 4)}

    hx[...] = jnp.zeros_like(hx)
    es[...] = jnp.zeros_like(es)
    tc[TXB] = jnp.zeros((128, 128), F32)

    def blank(i):
        xb[i, 64:128, :] = jnp.zeros((64, 256), BF16)

    loop(gn // 2, blank)

    def wanted(i):
        idx = row1 + i * 8
        peer = jnp.zeros_like(idx)
        for t in range(1, hn):
            peer += jnp.where(idx >= t * width, 1, 0)
        col = idx - peer * width
        pz, pc = mz + (peer >> (CC - 1)), mc + (peer & (CC - 1))
        pz = jnp.where(pz >= zc, pz - zc, pz)
        pc = jnp.where(pc >= CC, pc - CC, pc)
        want = (ml * plane + (my * zc + pz) * CC + pc) * own + col
        for q in range(4):
            wt[one_plane(i + q * (n_idx // 8)), :] = jnp.where(col + q * width < own, want + q * width, -7)

    loop(n_idx // 8, wanted)

    loads[0].wait()

    def faces(g):
        rows, below = group(g), one_plane((4 * g + 15) % 16)
        k = va[0, rows, :]
        tym = jnp.where(lane == 0, 0.0, harmonic(k, roll_y(k, 1)))
        typ = roll_y(tym, 127)
        tc[TYM, rows, :] = tym
        tc[TYP, rows, :] = typ
        tc[TYM1, rows, :] = jnp.where(is_m[4], 0.0, tym)
        tc[TYP1, rows, :] = jnp.where(is_m[3], 0.0, typ)
        txm = jnp.where(x == 0, 0.0, harmonic(k, roll_x(k, 1)))
        tc[TXM, rows, :] = txm
        tc[TXP, rows, :] = roll_x(txm, 7)
        tz = harmonic(k, jnp.concatenate([va[0, below, :], k[0:24]], axis=0))
        tc[TZM, rows, :] = tz
        tc[TZP, below, :] = tz[0:8]
        tc[TZP, pl.ds(pl.multiple_of(g * 32, 32), 24), :] = tz[8:32]
        tc[TZM1, rows, :] = tz
        tc[TZP1, below, :] = tz[0:8]
        tc[TZP1, pl.ds(pl.multiple_of(g * 32, 32), 24), :] = tz[8:32]

    loop(4, faces)
    nil = jnp.zeros((8, 128), F32)
    tc[TZM, 0:8, :] = nil
    tc[TZP, 120:128, :] = nil
    tc[TZM1, 0:8, :] = nil
    tc[TZP1, 120:128, :] = nil
    tc[TZM1, 64:72, :] = nil
    tc[TZP1, 56:64, :] = nil
    for i, (t, z) in enumerate(((TZP, 3), (TZM, 4), (TZP, 11), (TZM, 12))):
        sw[i] = tc[t, 8 * z:8 * z + 8, :]

    loads[1].wait()
    loads[2].wait()

    def first(g):
        rows = group(g)
        vals = []
        for s in range(8):
            on = sup[s, rows, :].astype(F32)
            sf[s, rows, :] = on
            vals.append(bi[s, rows, :] * on)
        inv = 1.0 / sum(vals[1:], vals[0])
        for s in range(8):
            va[1 + s, rows, :] = vals[s] * inv

    loop(4, first)

    def exchange(v, off, xs_buf, xr_buf, zr_buf, base):
        for i, s in enumerate(B0):
            xs_buf[0, off + i] = v[off + s, pl.ds(0, 16, stride=8), :]
            xs_buf[1, off + i] = v[off + s, pl.ds(7, 16, stride=8), :]
        if off:
            xs_buf[0, 0] = v[0, pl.ds(0, 16, stride=8), :]
            xs_buf[1, 0] = v[0, pl.ds(7, 16, stride=8), :]
            pl.semaphore_wait(barrier, gn + hn)
        last, lead = v.at[pl.ds(0, off + 4), pl.ds(120, 8)], v.at[pl.ds(0, off + 4), pl.ds(0, 8)]
        copies = []
        for j, (src, dst, who) in enumerate((
            (xs_buf.at[1], xr_buf.at[0], up_x), (xs_buf.at[0], xr_buf.at[1], down_x),
            (last, zr_buf.at[0], up_z), (lead, zr_buf.at[1], down_z),
        )):
            copies.append(pltpu.make_async_remote_copy(
                src_ref=src, dst_ref=dst, send_sem=halo_s.at[base + j], recv_sem=halo_r.at[base + j],
                device_id=who, device_id_type=MESH))
        for copy in copies:
            copy.start()
        return copies

    def inner(v, off):
        def part(g):
            rows = group(g)
            odd = g % 2
            below, above = one_plane((4 * g + 15) % 16), one_plane((4 * g + 4) % 16)
            coef = [tc[i, rows, :] for i in range(10)]
            vals = [v[off + s, rows, :] for s in range(8)]
            for s in range(8):
                here, turn = vals[s], 4 - (s & 4) * 2
                tm, tp = (coef[TYM1], coef[TYP1]) if s & 1 else (coef[TYM], coef[TYP])
                zm, zp = (coef[TZM1], coef[TZP1]) if s & 4 else (coef[TZM], coef[TZP])
                near = tm * roll_y(jnp.where(is_m[7], vals[s ^ 1], here), 1)
                near += tp * roll_y(jnp.where(is_m[0], vals[s ^ 1], here), 127)
                near += coef[TXM] * roll_x(jnp.where(is_x[3], vals[s ^ 2], here), 1)
                near += coef[TXP] * roll_x(jnp.where(is_x[4], vals[s ^ 2], here), 7)
                lo, hi = v[off + s + turn * odd, below, :], v[off + s + turn * (1 - odd), above, :]
                near += zm * jnp.concatenate([lo, here[0:24]], axis=0)
                near += zp * jnp.concatenate([here[8:32], hi], axis=0)
                nn[s, rows, :] = near

        loop(4, part)

    def outer(v, off, new, off2, xr_buf, zr_buf, extra):
        for i in range(4):
            hx[i, pl.ds(0, 16, stride=8), :] = xr_buf[0, extra + i]
            hx[i, pl.ds(7, 16, stride=8), :] = xr_buf[1, extra + i]
            nn[i, 0:8, :] += tzb[0] * zr_buf[0, extra + i]
            nn[i, 120:128, :] += tzb[1] * zr_buf[1, extra + i]

        def part(g):
            rows = group(g)
            rd, txb = tc[RD, rows, :], tc[TXB, rows, :]
            vals = []
            for s in range(8):
                near = nn[s, rows, :]
                if s in B0:
                    near += txb * hx[B0.index(s), rows, :]
                vals.append((v[off + s, rows, :] * THIRD + rd * near) * sf[s, rows, :])
            inv = 1.0 / sum(vals[1:], vals[0])
            for s in range(8):
                new[off2 + s, rows, :] = vals[s] * inv

        loop(4, part)

    sent = exchange(va, 1, hxs, hxr, hzr, 0)
    inner(va, 1)
    loads[3].wait()
    for copy in sent:
        copy.wait_recv()

    tc[TXB, pl.ds(0, 16, stride=8), :] = jnp.where(mp > 0, harmonic(hxs[0, 0], hxr[0, 0]), 0.0)
    tc[TXB, pl.ds(7, 16, stride=8), :] = jnp.where(mp < plane - 1, harmonic(hxs[1, 0], hxr[1, 0]), 0.0)
    tzb[0] = jnp.where(ml > 0, harmonic(va[0, 0:8, :], hzr[0, 0]), 0.0)
    tzb[1] = jnp.where(ml < lx - 1, harmonic(va[0, 120:128, :], hzr[1, 0]), 0.0)

    def scale(g):
        rows = group(g)
        diag = aa[rows, :]
        for t in (TYM, TYP, TXM, TXP, TXB, TZM, TZP):
            diag += tc[t, rows, :]
        tc[RD, rows, :] = diag

    loop(4, scale)
    tc[RD, 0:8, :] += tzb[0]
    tc[RD, 120:128, :] += tzb[1]
    tc[RD] = TWO_THIRDS / tc[RD]

    outer(va, 1, vb, 0, hxr, hzr, 1)
    sent2 = exchange(vb, 0, hxs2, hxr2, hzr2, 4)

    for load in loads[4:]:
        load.wait()
    label = blk[0, 0:1, :]
    for u, (j, r) in enumerate(((0, 0), (0, 4), (1, 0), (1, 4), (2, 0), (2, 4))):
        label = jnp.where(m1[0:1] == u, blk[j, r:r + 1, :], label)
    t_rows, labels = tab.shape[0], cr1.shape[0]
    tab[labels // 128:, :] = jnp.zeros((t_rows - labels // 128, 128), I32)

    def table(t):
        tab[pl.ds(t, 1), :] = cr1[pl.ds(pl.multiple_of(t * 128, 128), 128)].reshape(1, 128)

    loop(labels // 128, table)
    if labels % 128:
        t = labels // 128
        tab[t:t + 1, 0:labels % 128] = cr1[pl.ds(t * 128, labels % 128)].reshape(1, labels % 128)
    l_hi, l_lo = label >> 7, label & 127
    w_iota = lax.broadcasted_iota(I32, (128, 128), 0)
    pick = jnp.where(w_iota == l_lo, 1.0, 0.0).astype(BF16)
    ranks = tab[...]
    parts = jnp.concatenate([(ranks >> 7).astype(F32), (ranks & 127).astype(F32)], axis=0).astype(BF16)
    looked = jnp.dot(parts, pick, preferred_element_type=F32)
    t_iota = lax.broadcasted_iota(I32, (t_rows, 128), 0)
    looked = looked[:t_rows] * 128.0 + looked[t_rows:]
    rank = jnp.sum(jnp.where(t_iota == l_hi, looked, 0.0), axis=0, keepdims=True)
    rank = jnp.where(m1[0:1] < 6, rank, -1.0).astype(I32)
    rks[...] = rank
    rkr[0] = rank

    def rank_copy(r):
        return pltpu.make_async_remote_copy(
            src_ref=rks, dst_ref=rkr.at[g_inv(r)], send_sem=rk_s.at[r], recv_sem=rk_r.at[g_inv(r)],
            device_id=g_peer(r), device_id_type=MESH)

    loop(gn, lambda r: rank_copy(r).start(), 1)

    inner(vb, 0)

    def weigh(g):
        rows = group(g)
        tym, typ, txm, txp = (tc[i, rows, :] for i in (TYM, TYP, TXM, TXP))
        sx0 = jnp.where(is_x[3], txp, 0.0) + jnp.where(is_x[4], txm, 0.0)
        sx1 = sx0 + tc[TXB, rows, :]
        sy0 = jnp.where(is_m[7], typ, 0.0) + jnp.where(is_m[0], tym, 0.0)
        sy1 = sy0 + jnp.where(is_m[3], typ, 0.0) + jnp.where(is_m[4], tym, 0.0)
        for s in range(4):
            d = aa[rows, :] + (sx1 if s & 2 else sx0) + (sy1 if s & 1 else sy0)
            ec[s, rows, :] = d
            ec[4 + s, rows, :] = d
        ec[8, rows, :] = sx0
        ec[9, rows, :] = sy0

    loop(4, weigh)
    for i, z in enumerate((3, 4, 11, 12)):
        for s in range(8):
            ec[s, 8 * z:8 * z + 8, :] += sw[i]
    for t, z in ((tzb[0], 0), (tc[TZP, 56:64, :], 7), (tc[TZM, 64:72, :], 8), (tzb[1], 15)):
        for s in range(4, 8):
            ec[s, 8 * z:8 * z + 8, :] += t

    def x_swap(q):
        return jnp.where(x1 == 3, roll_x(q, 7), jnp.where(x1 == 4, roll_x(q, 1), 0.0))

    def y_swap(q):
        return jnp.where(m1 == 7, roll_y(q, 127), jnp.where(m1 == 0, roll_y(q, 1), 0.0))

    def far(g):
        return one_plane(4 * g + 4 - 5 * (g % 2))

    def rest(g):
        rows = group(g)
        here = pp[rows, :]
        full = plane_sum(ec[0, rows, :] * here - ss[rows, :]) - sw[g] * pp[far(g), :]
        fl[8, one_plane(g), :] = (
            full - x_swap(plane_sum(ec[8, rows, :] * here)) - y_swap(plane_sum(ec[9, rows, :] * here)))

    loop(4, rest)

    for copy in sent2:
        copy.wait_recv()
    for copy in sent:
        copy.wait_send()
    outer(vb, 0, va, 1, hxr2, hzr2, 0)
    store = pltpu.make_async_copy(va.at[pl.ds(1, 8)], v_out, out_sem.at[0])
    store.start()

    def gather(g):
        rows = group(g)
        sx0, sy0 = ec[8, rows, :], ec[9, rows, :]
        vals = [va[1 + s, rows, :] for s in range(8)]
        qx = [x_swap(plane_sum(sx0 * v)) for v in vals]
        qy = [y_swap(plane_sum(sy0 * v)) for v in vals]
        for s in range(8):
            full = plane_sum(ec[s, rows, :] * vals[s]) - sw[g] * va[1 + (s ^ 4), far(g), :]
            fl[s, one_plane(g), :] = full - qx[s ^ 2] - qy[s ^ 1]

    loop(4, gather)

    for j in range(3):
        for pz in range(3):
            if pz == 1:
                groups, a = ((0,), (1, 2), (3,))[j], 0
            elif pz == 0:
                groups, a = ((), (1,), (3,))[j], 1
            else:
                groups, a = ((0,), (2,), ())[j], 1
            if not groups:
                continue
            for b in (1, 0):
                at = 8 * ((1 - b) * 9 + 3 * pz)
                for c in (0, 1):
                    s = 4 * a + 2 * b + c
                    term = fl[s, 8 * groups[0]:8 * groups[0] + 8, :]
                    for g in groups[1:]:
                        term += fl[s, 8 * g:8 * g + 8, :]
                    if c:
                        es[j, at:at + 8, :] = jnp.where(m1 < 4, term, 0.0)
                        es[j, at + 16:at + 24, :] = jnp.where(m1 < 4, 0.0, term)
                    else:
                        es[j, at + 8:at + 16, :] = term
        groups = ((0,), (1, 2), (3,))[j]
        term = fl[8, 8 * groups[0]:8 * groups[0] + 8, :]
        for g in groups[1:]:
            term += fl[8, 8 * g:8 * g + 8, :]
        es[j, 144:152, :] = -term

    m24 = m[:24]
    rows_out = jnp.zeros((24, 128), F32)
    for j in range(3):
        for xi in range(2):
            t = es[j, pl.ds(4 * xi, 24, stride=8), :]
            for i in range(1, 4):
                t += es[j, pl.ds(4 * xi + i, 24, stride=8), :]
            t += roll_y(t, 127)
            t += roll_y(t, 126)
            t += roll_y(t, 124)
            u = 2 * j + xi
            rows_out = jnp.where(m24 == u, roll_y(t, u) if u else t, rows_out)
    cs[...] = rows_out
    crv[0] = rows_out

    def g_copy(r):
        return pltpu.make_async_remote_copy(
            src_ref=cs, dst_ref=crv.at[g_inv(r)], send_sem=g_s.at[r], recv_sem=g_r.at[g_inv(r)],
            device_id=g_peer(r), device_id_type=MESH)

    loop(gn, lambda r: g_copy(r).start(), 1)

    loop(gn, lambda r: rank_copy(r).wait_recv(), 1)

    def build(i):
        at = pl.multiple_of(i * 16, 16)
        want = wt[pl.ds(at, 16), :]
        for r in range(gn):
            oh[r // 2, pl.ds(at, 16), 128 * (r % 2):128 * (r % 2) + 128] = (
                jnp.where(want == rkr[r], 1.0, 0.0).astype(BF16))

    loop(4 * n_idx // 16, build)

    odd = m1 % 2 == 1
    loop(gn, lambda r: g_copy(r).wait_recv(), 1)

    def spread(i):
        for h in range(2):
            got = [crv[2 * i + h, 8 * k:8 * k + 8, :] for k in range(3)]
            turn = [pltpu.roll(jnp.where(odd, got[k], 0.0), 3, 0) for k in range(2)]
            vals = jnp.concatenate([
                jnp.where(odd, 0.0, got[0]), jnp.where(odd & (x1 == 0), 0.0, got[1]),
                jnp.where(x1 < 3, got[2], turn[0]), jnp.where(x1 < 3, turn[0], turn[1])], axis=0)
            high = vals.astype(BF16)
            lanes = slice(128 * h, 128 * h + 128)
            xb[i, 0:32, lanes] = high
            xb[i, 32:64, lanes] = (vals - high.astype(F32)).astype(BF16)

    loop(gn // 2, spread)

    def product(i):
        return lax.dot_general(oh[i], xb[i], (((1,), (1,)), ((), ())), preferred_element_type=F32)

    acc[...] = product(0) + product(1)

    def add_product(i):
        acc[...] += product(2 * i) + product(2 * i + 1)

    loop(gn // 4, add_product, 1)

    low_lanes = lax.broadcasted_iota(I32, (n_idx, 128), 1) < 32
    packed = jnp.zeros((n_idx, 128), F32)
    for q in range(4):
        part = acc[q * n_idx:(q + 1) * n_idx, :]
        both = jnp.where(low_lanes, part + roll_y(part, 96), 0.0)
        packed += roll_y(both, 32 * q) if q else both
    for r in range(hn):
        hs[r] = packed[r * width:(r + 1) * width]

    def h_copy(r):
        return pltpu.make_async_remote_copy(
            src_ref=hs.at[r], dst_ref=hr.at[h_inv(r)], send_sem=h_s.at[r], recv_sem=h_r.at[h_inv(r)],
            device_id=h_peer(r), device_id_type=MESH)

    loop(hn, lambda r: h_copy(r).start(), 1)
    loop(hn, lambda r: h_copy(r).wait_recv(), 1)
    final = hs[0]
    for r in range(1, hn):
        final += hr[r]
    f_out[0:width, :] = final

    store.wait()
    for copy in sent2:
        copy.wait_send()

    def drain(r):
        rank_copy(r).wait_send()
        g_copy(r).wait_send()

    loop(gn, drain, 1)
    loop(hn, lambda r: h_copy(r).wait_send(), 1)


def finish(own, width, v_in, f_in, v_out, cm_out, cr_out, vv, ft, sem):
    fetch = [pltpu.make_async_copy(v_in.at[s], vv.at[s], sem.at[0, s]) for s in range(8)]
    store = [pltpu.make_async_copy(vv.at[s], v_out.at[s], sem.at[1, s]) for s in range(8)]
    for copy in fetch:
        copy.start()
    for s in range(8):
        fetch[s].wait()
        store[s].start()
    ft[0:16, :] = f_in[...]
    turned = ft[...].T
    lane = lax.broadcasted_iota(I32, (32, 128), 1)
    done = jnp.zeros((32, 128), F32)
    for q in range(4):
        part = turned[32 * q:32 * q + 32]
        here = (lane >= q * width) & (lane < (q + 1) * width)
        done = jnp.where(here, pltpu.roll(part, q * width, 1) if q else part, done)
    for pz in range(3):
        for px, base in ((0, 19), (1, 9), (2, 0)):
            k = 9 * pz + 3 * px
            cm_out[k:k + 3, :] = done[base + 3 * pz:base + 3 * pz + 3, 0:own]
    cr_out[...] = done[18:19, 0:own]
    for copy in store:
        copy.wait()


def per_device(sizes, basis_init, permeability, accumulation, pressure, source, support, block_of, curve_rank):
    lx, plane = sizes
    zc = plane // (YC * CC)
    gn, hn = lx * YC, zc * CC
    devices = lx * plane
    own = (curve_rank.shape[0] + devices - 1) // devices
    width = (own + 3) // 4
    flat = lambda v: v.reshape(v.shape[:-3] + (128, 128))
    t_rows = -(-curve_rank.shape[0] // 2048) * 16
    anywhere = pl.BlockSpec(memory_space=pl.ANY)
    vmem = pl.BlockSpec(memory_space=pltpu.VMEM)
    dma = pltpu.SemaphoreType.DMA
    cells = lambda *lead: pltpu.VMEM(lead + (128, 128), F32)
    basis, rows = pl.pallas_call(
        functools.partial(kernel, (lx, plane, zc, own, width)),
        out_shape=(
            jax.ShapeDtypeStruct((8, 128, 128), F32),
            jax.ShapeDtypeStruct((16, 128), F32),
        ),
        in_specs=[anywhere] * 8,
        out_specs=(anywhere, vmem),
        scratch_shapes=[
            cells(8), pltpu.VMEM((8, 128, 128), I32), cells(), cells(), cells(),
            pltpu.VMEM((3, 8, 128), I32), pltpu.VMEM(curve_rank.shape, I32), pltpu.VMEM((t_rows, 128), I32),
            cells(9), cells(8), cells(8), cells(8), cells(12),
            pltpu.VMEM((2, 8, 128), F32), cells(10), pltpu.VMEM((4, 8, 128), F32),
            pltpu.VMEM((9, 32, 128), F32), cells(4),
            pltpu.VMEM((2, 5, 16, 128), F32), pltpu.VMEM((2, 5, 16, 128), F32), pltpu.VMEM((2, 5, 8, 128), F32),
            pltpu.VMEM((2, 4, 16, 128), F32), pltpu.VMEM((2, 4, 16, 128), F32), pltpu.VMEM((2, 4, 8, 128), F32),
            pltpu.VMEM((1, 128), I32), pltpu.VMEM((gn, 1, 128), I32),
            pltpu.VMEM((4 * hn * width, 128), I32), pltpu.VMEM((gn // 2, 4 * hn * width, 256), BF16),
            pltpu.VMEM((gn // 2, 128, 256), BF16), pltpu.VMEM((3, 192, 128), F32),
            pltpu.VMEM((24, 128), F32), pltpu.VMEM((gn, 24, 128), F32),
            pltpu.VMEM((4 * hn * width, 128), F32),
            pltpu.VMEM((hn, width, 128), F32), pltpu.VMEM((hn, width, 128), F32),
            dma((10,)), dma((1,)), dma((8,)), dma((8,)),
            dma((gn,)), dma((gn,)), dma((gn,)), dma((gn,)), dma((hn,)), dma((hn,)),
        ],
        compiler_params=pltpu.CompilerParams(
            collective_id=0, has_side_effects=True, vmem_limit_bytes=VMEM_GRANT),
        cost_estimate=pl.CostEstimate(flops=20_000_000, bytes_accessed=2_000_000, transcendentals=0),
    )(
        flat(basis_init), flat(permeability), flat(accumulation), flat(pressure), flat(source),
        flat(support), flat(block_of), curve_rank,
    )
    basis, matrix, residual = pl.pallas_call(
        functools.partial(finish, own, width),
        out_shape=(
            jax.ShapeDtypeStruct((8, 128, 128), F32),
            jax.ShapeDtypeStruct((27, own), F32),
            jax.ShapeDtypeStruct((1, own), F32),
        ),
        in_specs=[anywhere, vmem],
        out_specs=(anywhere, vmem, vmem),
        scratch_shapes=[cells(8), cells(), dma((2, 8))],
        compiler_params=pltpu.CompilerParams(vmem_limit_bytes=VMEM_GRANT),
    )(basis, rows)
    return basis.reshape(basis_init.shape), matrix, residual.reshape(own)


def solution(mesh):
    return jax.shard_map(
        functools.partial(per_device, (mesh.shape["layer"], mesh.shape["plane"])),
        mesh=mesh,
        in_specs=(
            P(None, "layer", "plane", None),
            P("layer", "plane", None),
            P("layer", "plane", None),
            P("layer", "plane", None),
            P("layer", "plane", None),
            P(None, "layer", "plane", None),
            P("layer", "plane", None),
            P(),
        ),
        out_specs=(
            P(None, "layer", "plane", None),
            P(None, ("layer", "plane")),
            P(("layer", "plane")),
        ),
        check_vma=False,
    )
```

```python
import functools

import jax
import jax.numpy as jnp
from jax import lax
from jax.experimental import pallas as pl
from jax.experimental.pallas import tpu as pltpu
from jax.sharding import PartitionSpec as P

MESH = pl.DeviceIdType.MESH
F32, BF16, I32 = jnp.float32, jnp.bfloat16, jnp.int32

G_BITS = (("layer", 1), ("layer", 2), ("plane", 16), ("plane", 32))
H_BITS = (("plane", 1), ("plane", 2), ("plane", 4), ("plane", 8))
VMEM_GRANT = 32 * 1024 * 1024
THIRD, TWO_THIRDS = 1.0 / 3.0, 2.0 / 3.0
B0 = (0, 1, 4, 5)
A0 = (0, 1, 2, 3)
TYM, TYP, TYM1, TYP1, TXM, TXP, TZM, TZP, TZM1, TZP1, TXB, RD = range(12)


def roll_x(v, shift):
    rows = v.shape[0]
    return pltpu.roll(v.reshape(rows // 8, 8, 128), shift, 1).reshape(rows, 128)


def roll_y(v, shift):
    return pltpu.roll(v, shift, 1)


def harmonic(k, n):
    return 2.0 * k * n / (k + n)


def plane_sum(v):
    return v.reshape(-1, 8, 128).sum(axis=0)


def kernel(
    dims,
    bi_hbm, k_hbm, a_hbm, p_hbm, s_hbm, sup_hbm, blk_hbm, cr_hbm,
    v_out, f_out,
    bi, sup, aa, pp, ss, blk, cr1, tab,
    va, vb, sf, nn, tc, tzb, ec, sw, fl, hx, hxs, hxr, hzr, hxs2, hxr2, hzr2,
    rks, rkr, wt, oh, xb, es, cs, crv, hs, hr,
    in_sem, out_sem, halo_s, halo_r, rk_s, rk_r, g_s, g_r, h_s, h_r,
):
    lx, plane, own, width = dims
    gn, hn = 2 ** len(G_BITS), 2 ** len(H_BITS)
    n_idx = hn * width
    ml, mp = lax.axis_index("layer"), lax.axis_index("plane")

    def flips(bits):
        steps = []
        for axis, bit in bits:
            at = ml if axis == "layer" else mp
            steps.append((axis == "layer", bit * (1 - 2 * ((at // bit) % 2))))
        return steps

    g_flips, h_flips = flips(G_BITS), flips(H_BITS)

    def partner(steps, r):
        to_l, to_p = ml, mp
        for i, (on_layer, step) in enumerate(steps):
            if (r >> i) & 1:
                to_l, to_p = (to_l + step, to_p) if on_layer else (to_l, to_p + step)
        return (to_l, to_p)

    up_x, down_x = (ml, (mp + 1) % plane), (ml, (mp + plane - 1) % plane)
    up_z, down_z = ((ml + 1) % lx, mp), ((ml + lx - 1) % lx, mp)

    def loop(n, body, start=0):
        for i in range(start, n):
            body(i)

    def group(g):
        return slice(g * 32, g * 32 + 32)

    def one_plane(z):
        return slice(z * 8, z * 8 + 8)

    loads = [
        pltpu.make_async_copy(k_hbm, va.at[0], in_sem.at[0]),
        pltpu.make_async_copy(bi_hbm, bi, in_sem.at[1]),
        pltpu.make_async_copy(sup_hbm, sup, in_sem.at[2]),
        pltpu.make_async_copy(a_hbm, aa, in_sem.at[3]),
        pltpu.make_async_copy(cr_hbm, cr1, in_sem.at[4]),
        pltpu.make_async_copy(p_hbm, pp, in_sem.at[5]),
        pltpu.make_async_copy(s_hbm, ss, in_sem.at[6]),
    ]
    for j, z in enumerate((0, 4, 12)):
        loads.append(pltpu.make_async_copy(blk_hbm.at[pl.ds(8 * z, 8)], blk.at[j], in_sem.at[7 + j]))
    for load in loads:
        load.start()

    barrier = pltpu.get_barrier_semaphore()

    def greet(who):
        pl.semaphore_signal(barrier, inc=1, device_id=who, device_id_type=MESH)

    greet(up_x)
    greet(down_x)
    loop(gn, lambda r: greet(partner(g_flips, r)), 1)
    loop(hn, lambda r: greet(partner(h_flips, r)), 1)

    lane = lax.broadcasted_iota(I32, (32, 128), 1)
    m, x = lane % 8, lax.broadcasted_iota(I32, (32, 128), 0) % 8
    m1, x1 = m[:8], x[:8]
    lane1, row1 = lane[:8], x[:8]
    is_m = {i: m == i for i in (0, 3, 4, 7)}
    is_x = {i: x == i for i in (3, 4)}

    hx[...] = jnp.zeros_like(hx)
    es[...] = jnp.zeros_like(es)
    tc[TXB] = jnp.zeros((128, 128), F32)
    xb[64:128, :] = jnp.zeros((64, gn * 128), BF16)

    def wanted(i):
        idx = row1 + i * 8
        peer = jnp.zeros_like(idx)
        for t in range(1, hn):
            peer += jnp.where(idx >= t * width, 1, 0)
        col = idx - peer * width
        dev = jnp.zeros_like(idx) + (ml * plane + mp)
        for b, (on_layer, step) in enumerate(h_flips):
            dev += ((peer >> b) & 1) * (step * plane if on_layer else step)
        want = dev * own + col
        for q in range(4):
            wt[one_plane(i + q * (n_idx // 8)), :] = jnp.where(col + q * width < own, want + q * width, -7)

    loop(n_idx // 8, wanted)

    loads[0].wait()

    def faces(g):
        rows, below = group(g), one_plane((4 * g + 15) % 16)
        k = va[0, rows, :]
        tym = jnp.where(lane == 0, 0.0, harmonic(k, roll_y(k, 1)))
        typ = roll_y(tym, 127)
        tc[TYM, rows, :] = tym
        tc[TYP, rows, :] = typ
        tc[TYM1, rows, :] = jnp.where(is_m[4], 0.0, tym)
        tc[TYP1, rows, :] = jnp.where(is_m[3], 0.0, typ)
        txm = jnp.where(x == 0, 0.0, harmonic(k, roll_x(k, 1)))
        tc[TXM, rows, :] = txm
        tc[TXP, rows, :] = roll_x(txm, 7)
        tz = harmonic(k, jnp.concatenate([va[0, below, :], k[0:24]], axis=0))
        tc[TZM, rows, :] = tz
        tc[TZP, below, :] = tz[0:8]
        tc[TZP, slice(g * 32, g * 32 + 24), :] = tz[8:32]
        tc[TZM1, rows, :] = tz
        tc[TZP1, below, :] = tz[0:8]
        tc[TZP1, slice(g * 32, g * 32 + 24), :] = tz[8:32]

    loop(4, faces)
    nil = jnp.zeros((8, 128), F32)
    tc[TZM, 0:8, :] = nil
    tc[TZP, 120:128, :] = nil
    tc[TZM1, 0:8, :] = nil
    tc[TZP1, 120:128, :] = nil
    tc[TZM1, 64:72, :] = nil
    tc[TZP1, 56:64, :] = nil
    for i, (t, z) in enumerate(((TZP, 3), (TZM, 4), (TZP, 11), (TZM, 12))):
        sw[i] = tc[t, 8 * z:8 * z + 8, :]

    loads[1].wait()
    loads[2].wait()

    def first(g):
        rows = group(g)
        vals = []
        for s in range(8):
            on = sup[s, rows, :].astype(F32)
            sf[s, rows, :] = on
            vals.append(bi[s, rows, :] * on)
        inv = 1.0 / sum(vals[1:], vals[0])
        for s in range(8):
            va[1 + s, rows, :] = vals[s] * inv

    loop(4, first)

    def exchange(v, off, xs_buf, xr_buf, zr_buf, base):
        for i, s in enumerate(B0):
            xs_buf[0, off + i] = v[off + s, pl.ds(0, 16, stride=8), :]
            xs_buf[1, off + i] = v[off + s, pl.ds(7, 16, stride=8), :]
        if off:
            xs_buf[0, 0] = v[0, pl.ds(0, 16, stride=8), :]
            xs_buf[1, 0] = v[0, pl.ds(7, 16, stride=8), :]
            pl.semaphore_wait(barrier, gn + hn)
        last, lead = v.at[pl.ds(0, off + 4), pl.ds(120, 8)], v.at[pl.ds(0, off + 4), pl.ds(0, 8)]
        copies = []
        for j, (src, dst, who) in enumerate((
            (xs_buf.at[1], xr_buf.at[0], up_x), (xs_buf.at[0], xr_buf.at[1], down_x),
            (last, zr_buf.at[0], up_z), (lead, zr_buf.at[1], down_z),
        )):
            copies.append(pltpu.make_async_remote_copy(
                src_ref=src, dst_ref=dst, send_sem=halo_s.at[base + j], recv_sem=halo_r.at[base + j],
                device_id=who, device_id_type=MESH))
        for copy in copies:
            copy.start()
        return copies

    def inner(v, off):
        def part(g):
            rows = group(g)
            odd = g % 2
            below, above = one_plane((4 * g + 15) % 16), one_plane((4 * g + 4) % 16)
            for s in range(8):
                if s % 4 == 0:
                    vals = [v[off + s + i, rows, :] for i in range(4)]
                    txm, txp = tc[TXM, rows, :], tc[TXP, rows, :]
                    tym, typ = [tc[i, rows, :] for i in (TYM, TYM1)], [tc[i, rows, :] for i in (TYP, TYP1)]
                    zm, zp = tc[TZM1 if s else TZM, rows, :], tc[TZP1 if s else TZP, rows, :]
                here, by_y, by_x, turn = vals[s % 4], vals[s % 4 ^ 1], vals[s % 4 ^ 2], 4 - (s & 4) * 2
                near = tym[s & 1] * roll_y(jnp.where(is_m[7], by_y, here), 1)
                near += typ[s & 1] * roll_y(jnp.where(is_m[0], by_y, here), 127)
                near += txm * roll_x(jnp.where(is_x[3], by_x, here), 1)
                near += txp * roll_x(jnp.where(is_x[4], by_x, here), 7)
                lo, hi = v[off + s + turn * odd, below, :], v[off + s + turn * (1 - odd), above, :]
                near += zm * jnp.concatenate([lo, here[0:24]], axis=0)
                near += zp * jnp.concatenate([here[8:32], hi], axis=0)
                nn[s, rows, :] = near

        loop(4, part)

    def outer(v, off, new, off2, xr_buf, zr_buf, extra):
        for i in range(4):
            hx[i, pl.ds(0, 16, stride=8), :] = xr_buf[0, extra + i]
            hx[i, pl.ds(7, 16, stride=8), :] = xr_buf[1, extra + i]
            nn[i, 0:8, :] += tzb[0] * zr_buf[0, extra + i]
            nn[i, 120:128, :] += tzb[1] * zr_buf[1, extra + i]

        def part(g):
            rows = group(g)
            rd, txb = tc[RD, rows, :], tc[TXB, rows, :]
            vals = []
            for s in range(8):
                near = nn[s, rows, :]
                if s in B0:
                    near += txb * hx[B0.index(s), rows, :]
                vals.append((v[off + s, rows, :] * THIRD + rd * near) * sf[s, rows, :])
            inv = 1.0 / sum(vals[1:], vals[0])
            for s in range(8):
                new[off2 + s, rows, :] = vals[s] * inv

        loop(4, part)

    sent = exchange(va, 1, hxs, hxr, hzr, 0)
    inner(va, 1)
    loads[3].wait()
    for copy in sent:
        copy.wait_recv()

    tc[TXB, pl.ds(0, 16, stride=8), :] = jnp.where(mp > 0, harmonic(hxs[0, 0], hxr[0, 0]), 0.0)
    tc[TXB, pl.ds(7, 16, stride=8), :] = jnp.where(mp < plane - 1, harmonic(hxs[1, 0], hxr[1, 0]), 0.0)
    tzb[0] = jnp.where(ml > 0, harmonic(va[0, 0:8, :], hzr[0, 0]), 0.0)
    tzb[1] = jnp.where(ml < lx - 1, harmonic(va[0, 120:128, :], hzr[1, 0]), 0.0)

    def scale(g):
        rows = group(g)
        diag = aa[rows, :]
        for t in (TYM, TYP, TXM, TXP, TXB, TZM, TZP):
            diag += tc[t, rows, :]
        tc[RD, rows, :] = diag

    loop(4, scale)
    tc[RD, 0:8, :] += tzb[0]
    tc[RD, 120:128, :] += tzb[1]
    tc[RD] = TWO_THIRDS / tc[RD]

    outer(va, 1, vb, 0, hxr, hzr, 1)
    sent2 = exchange(vb, 0, hxs2, hxr2, hzr2, 4)

    for load in loads[4:]:
        load.wait()
    label = blk[0, 0:1, :]
    for u, (j, r) in enumerate(((0, 0), (0, 4), (1, 0), (1, 4), (2, 0), (2, 4), (1, 0), (1, 4))):
        label = jnp.where(m1[0:1] == u, blk[j, r:r + 1, :], label)
    t_rows, labels = tab.shape[0], cr1.shape[0]
    tab[labels // 128:, :] = jnp.zeros((t_rows - labels // 128, 128), I32)

    def table(t):
        tab[t:t + 1, :] = cr1[pl.ds(t * 128, 128)].reshape(1, 128)

    loop(labels // 128, table)
    if labels % 128:
        t = labels // 128
        tab[t:t + 1, 0:labels % 128] = cr1[pl.ds(t * 128, labels % 128)].reshape(1, labels % 128)
    l_hi, l_lo = label >> 7, label & 127
    w_iota = lax.broadcasted_iota(I32, (128, 128), 0)
    pick = jnp.where(w_iota == l_lo, 1.0, 0.0).astype(BF16)
    ranks = tab[...]
    parts = jnp.concatenate([(ranks >> 7).astype(F32), (ranks & 127).astype(F32)], axis=0).astype(BF16)
    looked = jnp.dot(parts, pick, preferred_element_type=F32)
    t_iota = lax.broadcasted_iota(I32, (t_rows, 128), 0)
    looked = looked[:t_rows] * 128.0 + looked[t_rows:]
    rank = jnp.sum(jnp.where(t_iota == l_hi, looked, 0.0), axis=0, keepdims=True)
    rank = rank.astype(I32)
    rks[...] = rank
    rkr[0] = rank

    def rank_copy(r):
        return pltpu.make_async_remote_copy(
            src_ref=rks, dst_ref=rkr.at[r], send_sem=rk_s.at[r], recv_sem=rk_r.at[r],
            device_id=partner(g_flips, r), device_id_type=MESH)

    loop(gn, lambda r: rank_copy(r).start(), 1)

    inner(vb, 0)

    def weigh(g):
        rows = group(g)
        tym, typ, txm, txp = (tc[i, rows, :] for i in (TYM, TYP, TXM, TXP))
        sx0 = jnp.where(is_x[3], txp, 0.0) + jnp.where(is_x[4], txm, 0.0)
        sx1 = sx0 + tc[TXB, rows, :]
        sy0 = jnp.where(is_m[7], typ, 0.0) + jnp.where(is_m[0], tym, 0.0)
        sy1 = sy0 + jnp.where(is_m[3], typ, 0.0) + jnp.where(is_m[4], tym, 0.0)
        for s in range(4):
            d = aa[rows, :] + (sx1 if s & 2 else sx0) + (sy1 if s & 1 else sy0)
            ec[s, rows, :] = d
            ec[4 + s, rows, :] = d
        ec[8, rows, :] = sx0
        ec[9, rows, :] = sy0

    loop(4, weigh)
    for i, z in enumerate((3, 4, 11, 12)):
        for s in range(8):
            ec[s, 8 * z:8 * z + 8, :] += sw[i]
    for t, z in ((tzb[0], 0), (tc[TZP, 56:64, :], 7), (tc[TZM, 64:72, :], 8), (tzb[1], 15)):
        for s in range(4, 8):
            ec[s, 8 * z:8 * z + 8, :] += t

    def x_swap(q):
        return jnp.where(x1 == 3, roll_x(q, 7), jnp.where(x1 == 4, roll_x(q, 1), 0.0))

    def y_swap(q):
        return jnp.where(m1 == 7, roll_y(q, 127), jnp.where(m1 == 0, roll_y(q, 1), 0.0))

    def far(g):
        return one_plane(4 * g + 4 - 5 * (g % 2))

    def rest(g):
        rows = group(g)
        here = pp[rows, :]
        full = plane_sum(ec[0, rows, :] * here - ss[rows, :]) - sw[g] * pp[far(g), :]
        fl[8, one_plane(g), :] = (
            full - x_swap(plane_sum(ec[8, rows, :] * here)) - y_swap(plane_sum(ec[9, rows, :] * here)))

    loop(4, rest)

    for copy in sent2:
        copy.wait_recv()
    for copy in sent:
        copy.wait_send()
    outer(vb, 0, va, 1, hxr2, hzr2, 0)
    store = pltpu.make_async_copy(va.at[pl.ds(1, 8)], v_out, out_sem.at[0])
    store.start()

    def gather(g):
        rows = group(g)
        sx0, sy0 = ec[8, rows, :], ec[9, rows, :]
        vals = [va[1 + s, rows, :] for s in range(8)]
        qx = [x_swap(plane_sum(sx0 * v)) for v in vals]
        qy = [y_swap(plane_sum(sy0 * v)) for v in vals]
        for s in range(8):
            full = plane_sum(ec[s, rows, :] * vals[s]) - sw[g] * va[1 + (s ^ 4), far(g), :]
            fl[s, one_plane(g), :] = full - qx[s ^ 2] - qy[s ^ 1]

    loop(4, gather)

    def z_part(j, pz, s):
        groups = ((0,), (1, 2), (3,))[j] if pz == 1 else {(1, 0): (1,), (2, 0): (3,), (0, 2): (0,), (1, 2): (2,)}[j, pz]
        term = fl[s, one_plane(groups[0]), :]
        for g in groups[1:]:
            term += fl[s, one_plane(g), :]
        return term

    for k, (j, halves) in enumerate(((0, (1, 2)), (1, (1, 2)), (2, (1, 0)), (1, (0,)))):
        for half, pz in enumerate(halves):
            for b in range(2):
                at, s = 64 * half + 24 * b, (0 if pz == 1 else 4) + 2 * b
                side = z_part(j, pz, s + 1)
                es[k, at:at + 8, :] = jnp.where(m1 < 4, side, 0.0)
                es[k, at + 8:at + 16, :] = z_part(j, pz, s)
                es[k, at + 16:at + 24, :] = jnp.where(m1 < 4, 0.0, side)
        if k < 3:
            es[k, 48:56, :] = -z_part(j, 1, 8)

    m16 = m[:16]
    sums = []
    for k in range(4):
        for xi in range(2):
            t = es[k, pl.ds(4 * xi, 16, stride=8), :]
            for i in range(1, 4):
                t += es[k, pl.ds(4 * xi + i, 16, stride=8), :]
            sums.append(t)
    for bit in (4, 2, 1):
        high = (m16 & bit) != 0
        merged = []
        for u in range(bit):
            one, two = sums[u], sums[u + bit]
            move = jnp.where(high, one, two)
            merged.append(jnp.where(high, two, one) + jnp.where(high, roll_y(move, bit), roll_y(move, 128 - bit)))
        sums = merged
    rows_out = sums[0]
    cs[...] = rows_out
    crv[0] = rows_out

    def g_copy(r):
        return pltpu.make_async_remote_copy(
            src_ref=cs, dst_ref=crv.at[r], send_sem=g_s.at[r], recv_sem=g_r.at[r],
            device_id=partner(g_flips, r), device_id_type=MESH)

    loop(gn, lambda r: g_copy(r).start(), 1)

    loop(gn, lambda r: rank_copy(r).wait_recv(), 1)

    have = [rkr[r] for r in range(gn)]

    def build(i, carry):
        at = pl.multiple_of(i * 16, 16)
        want = wt[pl.ds(at, 16), :]
        for r in range(gn):
            oh[pl.ds(at, 16), 128 * r:128 * r + 128] = jnp.where(want == have[r], 1.0, 0.0).astype(BF16)
        return carry

    lax.fori_loop(0, 4 * n_idx // 16, build, 0)

    odd = m1 % 2 == 1
    b1 = (x1 >= 3) & (x1 < 6)
    b1_odd = b1 & odd
    loop(gn, lambda r: g_copy(r).wait_recv(), 1)
    for r in range(gn):
        got1, got2 = crv[r, 0:8, :], crv[r, 8:16, :]
        pz1 = jnp.where(m1 < 6, got1, 0.0)
        pz2 = jnp.where(m1 < 4, got2, 0.0)
        pz0 = jnp.where(m1 < 4, 0.0, jnp.where(m1 < 6, got2, got1))
        low1, low2, low0 = (jnp.where(b1_odd, v, 0.0) for v in (pz1, pz2, pz0))
        last = pltpu.roll(low1, 5, 0) + low2 + jnp.where(x1 >= 6, pltpu.roll(low0, 3, 0), 0.0)
        vals = jnp.concatenate([
            pz1 - low1 + jnp.where(x1 == 7, pltpu.roll(low0, 2, 0), 0.0), pz2 - low2, pz0 - low0, last], axis=0)
        high = vals.astype(BF16)
        lanes = slice(128 * r, 128 * r + 128)
        xb[0:32, lanes] = high
        xb[32:64, lanes] = (vals - high.astype(F32)).astype(BF16)

    routed = lax.dot_general(
        oh[...], xb[...], (((1,), (1,)), ((), ())), preferred_element_type=F32)
    quarter = lax.broadcasted_iota(I32, (n_idx, 128), 1) >> 5
    packed = jnp.zeros((n_idx, 128), F32)
    for q in range(4):
        part = routed[q * n_idx:(q + 1) * n_idx]
        first_half = roll_y(part, 32 * q) if q else part
        second_half = part if q == 1 else roll_y(part, (32 * q + 96) % 128)
        packed = jnp.where(quarter == q, first_half + second_half, packed)
    for r in range(hn):
        hs[r] = packed[r * width:(r + 1) * width]

    def h_copy(r):
        return pltpu.make_async_remote_copy(
            src_ref=hs.at[r], dst_ref=hr.at[r], send_sem=h_s.at[r], recv_sem=h_r.at[r],
            device_id=partner(h_flips, r), device_id_type=MESH)

    loop(hn, lambda r: h_copy(r).start(), 1)
    loop(hn, lambda r: h_copy(r).wait_recv(), 1)
    final = hs[0]
    for r in range(1, hn):
        final += hr[r]
    f_out[0:width, :] = final

    store.wait()
    for copy in sent2:
        copy.wait_send()

    def drain(r):
        rank_copy(r).wait_send()
        g_copy(r).wait_send()

    loop(gn, drain, 1)
    loop(hn, lambda r: h_copy(r).wait_send(), 1)


def finish(own, width, v_in, f_in, v_out, cm_out, cr_out, ft, sem):
    store = pltpu.make_async_copy(v_in, v_out, sem)
    store.start()
    ft[0:16, :] = f_in[...]
    turned = ft[...].T
    lane = lax.broadcasted_iota(I32, (32, 128), 1)
    done = jnp.zeros((32, 128), F32)
    for q in range(4):
        part = turned[32 * q:32 * q + 32]
        here = (lane >= q * width) & (lane < (q + 1) * width)
        done = jnp.where(here, pltpu.roll(part, q * width, 1) if q else part, done)
    for pz, px, base in (
        (1, 1, 0), (1, 2, 3), (2, 1, 8), (2, 2, 11), (0, 1, 16), (0, 2, 19), (1, 0, 24), (2, 0, 27)):
        k = 9 * pz + 3 * px
        cm_out[k:k + 3, :] = done[base:base + 3, 0:own]
    cm_out[0:2, :] = done[30:32, 0:own]
    cm_out[2:3, :] = done[7:8, 0:own]
    cr_out[...] = done[6:7, 0:own]
    store.wait()


def per_device(sizes, basis_init, permeability, accumulation, pressure, source, support, block_of, curve_rank):
    lx, plane = sizes
    gn, hn = 2 ** len(G_BITS), 2 ** len(H_BITS)
    devices = lx * plane
    own = (curve_rank.shape[0] + devices - 1) // devices
    width = (own + 3) // 4
    flat = lambda v: v.reshape(v.shape[:-3] + (128, 128))
    t_rows = -(-curve_rank.shape[0] // 2048) * 16
    anywhere = pl.BlockSpec(memory_space=pl.ANY)
    vmem = pl.BlockSpec(memory_space=pltpu.VMEM)
    dma = pltpu.SemaphoreType.DMA
    cells = lambda *lead: pltpu.VMEM(lead + (128, 128), F32)
    basis, rows = pl.pallas_call(
        functools.partial(kernel, (lx, plane, own, width)),
        out_shape=(
            jax.ShapeDtypeStruct((8, 128, 128), F32),
            jax.ShapeDtypeStruct((16, 128), F32),
        ),
        in_specs=[anywhere] * 8,
        out_specs=(anywhere, vmem),
        scratch_shapes=[
            cells(8), pltpu.VMEM((8, 128, 128), I32), cells(), cells(), cells(),
            pltpu.VMEM((3, 8, 128), I32), pltpu.VMEM(curve_rank.shape, I32), pltpu.VMEM((t_rows, 128), I32),
            cells(9), cells(8), cells(8), cells(8), cells(12),
            pltpu.VMEM((2, 8, 128), F32), cells(10), pltpu.VMEM((4, 8, 128), F32),
            pltpu.VMEM((9, 32, 128), F32), cells(4),
            pltpu.VMEM((2, 5, 16, 128), F32), pltpu.VMEM((2, 5, 16, 128), F32), pltpu.VMEM((2, 5, 8, 128), F32),
            pltpu.VMEM((2, 4, 16, 128), F32), pltpu.VMEM((2, 4, 16, 128), F32), pltpu.VMEM((2, 4, 8, 128), F32),
            pltpu.VMEM((1, 128), I32), pltpu.VMEM((gn, 1, 128), I32),
            pltpu.VMEM((4 * hn * width, 128), I32), pltpu.VMEM((4 * hn * width, gn * 128), BF16),
            pltpu.VMEM((128, gn * 128), BF16), pltpu.VMEM((4, 128, 128), F32),
            pltpu.VMEM((16, 128), F32), pltpu.VMEM((gn, 16, 128), F32),
            pltpu.VMEM((hn, width, 128), F32), pltpu.VMEM((hn, width, 128), F32),
            dma((10,)), dma((1,)), dma((8,)), dma((8,)),
            dma((gn,)), dma((gn,)), dma((gn,)), dma((gn,)), dma((hn,)), dma((hn,)),
        ],
        compiler_params=pltpu.CompilerParams(
            collective_id=0, has_side_effects=True, vmem_limit_bytes=VMEM_GRANT),
        cost_estimate=pl.CostEstimate(flops=20_000_000, bytes_accessed=2_000_000, transcendentals=0),
    )(*(pltpu.with_memory_space_constraint(v, pltpu.HBM) for v in (
        flat(basis_init), flat(permeability), flat(accumulation), flat(pressure), flat(source),
        flat(support), flat(block_of), curve_rank,
    )))
    basis, matrix, residual = pl.pallas_call(
        functools.partial(finish, own, width),
        out_shape=(
            jax.ShapeDtypeStruct((8, 128, 128), F32),
            jax.ShapeDtypeStruct((27, own), F32),
            jax.ShapeDtypeStruct((1, own), F32),
        ),
        in_specs=[anywhere, vmem],
        out_specs=(anywhere, vmem, vmem),
        scratch_shapes=[cells(), dma],
        compiler_params=pltpu.CompilerParams(vmem_limit_bytes=VMEM_GRANT),
    )(basis, rows)
    return basis.reshape(basis_init.shape), matrix, residual.reshape(own)


def solution(mesh):
    return jax.shard_map(
        functools.partial(per_device, (mesh.shape["layer"], mesh.shape["plane"])),
        mesh=mesh,
        in_specs=(
            P(None, "layer", "plane", None),
            P("layer", "plane", None),
            P("layer", "plane", None),
            P("layer", "plane", None),
            P("layer", "plane", None),
            P(None, "layer", "plane", None),
            P("layer", "plane", None),
            P(),
        ),
        out_specs=(
            P(None, "layer", "plane", None),
            P(None, ("layer", "plane")),
            P(("layer", "plane")),
        ),
        check_vma=False,
    )
```

```python
import functools

import jax
import jax.numpy as jnp
from jax import lax
from jax.experimental import pallas as pl
from jax.experimental.pallas import tpu as pltpu
from jax.sharding import PartitionSpec as P

MESH = pl.DeviceIdType.MESH
F32, BF16, I32 = jnp.float32, jnp.bfloat16, jnp.int32

G_BITS = (("layer", 1), ("layer", 2), ("plane", 16), ("plane", 32))
H_BITS = (("plane", 1), ("plane", 2), ("plane", 4), ("plane", 8))
VMEM_GRANT = 32 * 1024 * 1024
THIRD, TWO_THIRDS = 1.0 / 3.0, 2.0 / 3.0
B0 = (0, 1, 4, 5)
A0 = (0, 1, 2, 3)
TYM, TYP, TYM1, TYP1, TXM, TXP, TZM, TZP, TZM1, TZP1, TXB, RD = range(12)


def roll_x(v, shift):
    rows = v.shape[0]
    return pltpu.roll(v.reshape(rows // 8, 8, 128), shift, 1).reshape(rows, 128)


def roll_y(v, shift):
    return pltpu.roll(v, shift, 1)


def harmonic(k, n):
    return 2.0 * k * n / (k + n)


def plane_sum(v):
    return v.reshape(-1, 8, 128).sum(axis=0)


def kernel(
    dims,
    bi_hbm, k_hbm, a_hbm, p_hbm, s_hbm, sup_hbm, blk_hbm, cr_hbm,
    v_out, f_out,
    bi, sup, aa, pp, ss, blk, cr1, tab,
    va, vb, sf, nn, tc, tzb, ec, sw, fl, hx, hxs, hxr, hzr, hxs2, hxr2, hzr2,
    rks, rkr, wt, oh, xb, es, cs, crv, hs, hr,
    in_sem, out_sem, halo_s, halo_r, rk_s, rk_r, g_s, g_r, h_s, h_r,
):
    lx, plane, own, width = dims
    gn, hn = 2 ** len(G_BITS), 2 ** len(H_BITS)
    n_idx = hn * width
    ml, mp = lax.axis_index("layer"), lax.axis_index("plane")

    def flips(bits):
        steps = []
        for axis, bit in bits:
            at = ml if axis == "layer" else mp
            steps.append((axis == "layer", bit * (1 - 2 * ((at // bit) % 2))))
        return steps

    g_flips, h_flips = flips(G_BITS), flips(H_BITS)

    def partner(steps, r):
        to_l, to_p = ml, mp
        for i, (on_layer, step) in enumerate(steps):
            if (r >> i) & 1:
                to_l, to_p = (to_l + step, to_p) if on_layer else (to_l, to_p + step)
        return (to_l, to_p)

    up_x, down_x = (ml, (mp + 1) % plane), (ml, (mp + plane - 1) % plane)
    up_z, down_z = ((ml + 1) % lx, mp), ((ml + lx - 1) % lx, mp)

    def loop(n, body, start=0):
        for i in range(start, n):
            body(i)

    def group(g):
        return slice(g * 32, g * 32 + 32)

    def one_plane(z):
        return slice(z * 8, z * 8 + 8)

    loads = [
        pltpu.make_async_copy(k_hbm, va.at[0], in_sem.at[0]),
        pltpu.make_async_copy(bi_hbm, bi, in_sem.at[1]),
        pltpu.make_async_copy(sup_hbm, sup, in_sem.at[2]),
        pltpu.make_async_copy(a_hbm, aa, in_sem.at[3]),
        pltpu.make_async_copy(cr_hbm, cr1, in_sem.at[4]),
        pltpu.make_async_copy(p_hbm, pp, in_sem.at[5]),
        pltpu.make_async_copy(s_hbm, ss, in_sem.at[6]),
    ]
    for j, z in enumerate((0, 4, 12)):
        loads.append(pltpu.make_async_copy(blk_hbm.at[pl.ds(8 * z, 8)], blk.at[j], in_sem.at[7 + j]))
    barrier = pltpu.get_barrier_semaphore()

    def greet(who):
        pl.semaphore_signal(barrier, inc=1, device_id=who, device_id_type=MESH)

    greet(up_x)
    greet(down_x)
    g_order = [1, 3, 2][:gn - 1] + list(range(4, gn))
    for r in g_order[:2]:
        greet(partner(g_flips, r))
    for load in loads[:3]:
        load.start()
    for r in g_order[2:]:
        greet(partner(g_flips, r))
    loop(hn, lambda r: greet(partner(h_flips, r)), 1)
    for load in loads[3:]:
        load.start()

    lane = lax.broadcasted_iota(I32, (32, 128), 1)
    m, x = lane % 8, lax.broadcasted_iota(I32, (32, 128), 0) % 8
    m1, x1 = m[:8], x[:8]
    lane1, row1 = lane[:8], x[:8]
    is_m = {i: m == i for i in (0, 3, 4, 7)}
    is_x = {i: x == i for i in (3, 4)}

    hx[...] = jnp.zeros_like(hx)
    tc[TXB] = jnp.zeros((128, 128), F32)

    loads[0].wait()

    def faces(g):
        rows, below = group(g), one_plane((4 * g + 15) % 16)
        k = va[0, rows, :]
        tym = jnp.where(lane == 0, 0.0, harmonic(k, roll_y(k, 1)))
        typ = roll_y(tym, 127)
        tc[TYM, rows, :] = tym
        tc[TYP, rows, :] = typ
        tc[TYM1, rows, :] = jnp.where(is_m[4], 0.0, tym)
        tc[TYP1, rows, :] = jnp.where(is_m[3], 0.0, typ)
        txm = jnp.where(x == 0, 0.0, harmonic(k, roll_x(k, 1)))
        tc[TXM, rows, :] = txm
        tc[TXP, rows, :] = roll_x(txm, 7)
        tz = harmonic(k, jnp.concatenate([va[0, below, :], k[0:24]], axis=0))
        tc[TZM, rows, :] = tz
        tc[TZP, below, :] = tz[0:8]
        tc[TZP, slice(g * 32, g * 32 + 24), :] = tz[8:32]
        tc[TZM1, rows, :] = tz
        tc[TZP1, below, :] = tz[0:8]
        tc[TZP1, slice(g * 32, g * 32 + 24), :] = tz[8:32]

    loop(4, faces)
    nil = jnp.zeros((8, 128), F32)
    tc[TZM, 0:8, :] = nil
    tc[TZP, 120:128, :] = nil
    tc[TZM1, 0:8, :] = nil
    tc[TZP1, 120:128, :] = nil
    tc[TZM1, 64:72, :] = nil
    tc[TZP1, 56:64, :] = nil
    for i, (t, z) in enumerate(((TZP, 3), (TZM, 4), (TZP, 11), (TZM, 12))):
        sw[i] = tc[t, 8 * z:8 * z + 8, :]

    loads[1].wait()
    loads[2].wait()

    def first(g):
        rows = group(g)
        vals = []
        for s in range(8):
            on = sup[s, rows, :].astype(F32)
            sf[s, rows, :] = on
            vals.append(bi[s, rows, :] * on)
        inv = 1.0 / sum(vals[1:], vals[0])
        for s in range(8):
            va[1 + s, rows, :] = vals[s] * inv

    loop(4, first)

    def exchange(v, off, xs_buf, xr_buf, zr_buf, base):
        for i, s in enumerate(B0):
            xs_buf[0, off + i] = v[off + s, pl.ds(0, 16, stride=8), :]
            xs_buf[1, off + i] = v[off + s, pl.ds(7, 16, stride=8), :]
        if off:
            xs_buf[0, 0] = v[0, pl.ds(0, 16, stride=8), :]
            xs_buf[1, 0] = v[0, pl.ds(7, 16, stride=8), :]
            pl.semaphore_wait(barrier, gn + hn)
        last, lead = v.at[pl.ds(0, off + 4), pl.ds(120, 8)], v.at[pl.ds(0, off + 4), pl.ds(0, 8)]
        copies = []
        for j, (src, dst, who) in enumerate((
            (xs_buf.at[1], xr_buf.at[0], up_x), (xs_buf.at[0], xr_buf.at[1], down_x),
            (last, zr_buf.at[0], up_z), (lead, zr_buf.at[1], down_z),
        )):
            copies.append(pltpu.make_async_remote_copy(
                src_ref=src, dst_ref=dst, send_sem=halo_s.at[base + j], recv_sem=halo_r.at[base + j],
                device_id=who, device_id_type=MESH))
        for copy in copies:
            copy.start()
        return copies

    def inner(v, off):
        def part(g):
            rows = group(g)
            odd = g % 2
            below, above = one_plane((4 * g + 15) % 16), one_plane((4 * g + 4) % 16)
            for s in range(8):
                if s % 4 == 0:
                    vals = [v[off + s + i, rows, :] for i in range(4)]
                    txm, txp = tc[TXM, rows, :], tc[TXP, rows, :]
                    tym, typ = [tc[i, rows, :] for i in (TYM, TYM1)], [tc[i, rows, :] for i in (TYP, TYP1)]
                    zm, zp = tc[TZM1 if s else TZM, rows, :], tc[TZP1 if s else TZP, rows, :]
                here, by_y, by_x, turn = vals[s % 4], vals[s % 4 ^ 1], vals[s % 4 ^ 2], 4 - (s & 4) * 2
                near = tym[s & 1] * roll_y(jnp.where(is_m[7], by_y, here), 1)
                near += typ[s & 1] * roll_y(jnp.where(is_m[0], by_y, here), 127)
                near += txm * roll_x(jnp.where(is_x[3], by_x, here), 1)
                near += txp * roll_x(jnp.where(is_x[4], by_x, here), 7)
                lo, hi = v[off + s + turn * odd, below, :], v[off + s + turn * (1 - odd), above, :]
                near += zm * jnp.concatenate([lo, here[0:24]], axis=0)
                near += zp * jnp.concatenate([here[8:32], hi], axis=0)
                nn[s, rows, :] = near

        loop(4, part)

    def outer(v, off, new, off2, xr_buf, zr_buf, extra):
        for i in range(4):
            hx[i, pl.ds(0, 16, stride=8), :] = xr_buf[0, extra + i]
            hx[i, pl.ds(7, 16, stride=8), :] = xr_buf[1, extra + i]
            nn[i, 0:8, :] += tzb[0] * zr_buf[0, extra + i]
            nn[i, 120:128, :] += tzb[1] * zr_buf[1, extra + i]

        def part(g):
            rows = group(g)
            rd, txb = tc[RD, rows, :], tc[TXB, rows, :]
            vals = []
            for s in range(8):
                near = nn[s, rows, :]
                if s in B0:
                    near += txb * hx[B0.index(s), rows, :]
                vals.append((v[off + s, rows, :] * THIRD + rd * near) * sf[s, rows, :])
            inv = 1.0 / sum(vals[1:], vals[0])
            for s in range(8):
                new[off2 + s, rows, :] = vals[s] * inv

        loop(4, part)

    sent = exchange(va, 1, hxs, hxr, hzr, 0)
    inner(va, 1)
    loads[3].wait()
    for copy in sent:
        copy.wait_recv()

    tc[TXB, pl.ds(0, 16, stride=8), :] = jnp.where(mp > 0, harmonic(hxs[0, 0], hxr[0, 0]), 0.0)
    tc[TXB, pl.ds(7, 16, stride=8), :] = jnp.where(mp < plane - 1, harmonic(hxs[1, 0], hxr[1, 0]), 0.0)
    tzb[0] = jnp.where(ml > 0, harmonic(va[0, 0:8, :], hzr[0, 0]), 0.0)
    tzb[1] = jnp.where(ml < lx - 1, harmonic(va[0, 120:128, :], hzr[1, 0]), 0.0)

    def scale(g):
        rows = group(g)
        diag = aa[rows, :]
        for t in (TYM, TYP, TXM, TXP, TXB, TZM, TZP):
            diag += tc[t, rows, :]
        tc[RD, rows, :] = diag

    loop(4, scale)
    tc[RD, 0:8, :] += tzb[0]
    tc[RD, 120:128, :] += tzb[1]
    tc[RD] = TWO_THIRDS / tc[RD]

    outer(va, 1, vb, 0, hxr, hzr, 1)
    sent2 = exchange(vb, 0, hxs2, hxr2, hzr2, 4)

    for load in loads[4:]:
        load.wait()
    label = blk[0, 0:1, :]
    for u, (j, r) in enumerate(((0, 0), (0, 4), (1, 0), (1, 4), (2, 0), (2, 4), (1, 0), (1, 4))):
        label = jnp.where(m1[0:1] == u, blk[j, r:r + 1, :], label)
    t_rows, labels = tab.shape[0], cr1.shape[0]
    tab[labels // 128:, :] = jnp.zeros((t_rows - labels // 128, 128), I32)

    def table(t):
        tab[t:t + 1, :] = cr1[pl.ds(t * 128, 128)].reshape(1, 128)

    loop(labels // 128, table)
    if labels % 128:
        t = labels // 128
        tab[t:t + 1, 0:labels % 128] = cr1[pl.ds(t * 128, labels % 128)].reshape(1, labels % 128)
    l_hi, l_lo = label >> 7, label & 127
    w_iota = lax.broadcasted_iota(I32, (128, 128), 0)
    pick = jnp.where(w_iota == l_lo, 1.0, 0.0).astype(BF16)
    ranks = tab[...]
    parts = jnp.concatenate([(ranks >> 7).astype(F32), (ranks & 127).astype(F32)], axis=0).astype(BF16)
    looked = jnp.dot(parts, pick, preferred_element_type=F32)
    t_iota = lax.broadcasted_iota(I32, (t_rows, 128), 0)
    looked = looked[:t_rows] * 128.0 + looked[t_rows:]
    rank = jnp.sum(jnp.where(t_iota == l_hi, looked, 0.0), axis=0, keepdims=True)
    rank = rank.astype(I32)
    rks[...] = rank
    rkr[0] = rank

    def rank_copy(r):
        return pltpu.make_async_remote_copy(
            src_ref=rks, dst_ref=rkr.at[r], send_sem=rk_s.at[r], recv_sem=rk_r.at[r],
            device_id=partner(g_flips, r), device_id_type=MESH)

    loop(gn, lambda r: rank_copy(r).start(), 1)
    es[...] = jnp.zeros_like(es)

    inner(vb, 0)

    def weigh(g):
        rows = group(g)
        tym, typ, txm, txp = (tc[i, rows, :] for i in (TYM, TYP, TXM, TXP))
        sx0 = jnp.where(is_x[3], txp, 0.0) + jnp.where(is_x[4], txm, 0.0)
        sx1 = sx0 + tc[TXB, rows, :]
        sy0 = jnp.where(is_m[7], typ, 0.0) + jnp.where(is_m[0], tym, 0.0)
        sy1 = sy0 + jnp.where(is_m[3], typ, 0.0) + jnp.where(is_m[4], tym, 0.0)
        for s in range(4):
            d = aa[rows, :] + (sx1 if s & 2 else sx0) + (sy1 if s & 1 else sy0)
            ec[s, rows, :] = d
            ec[4 + s, rows, :] = d
        ec[8, rows, :] = sx0
        ec[9, rows, :] = sy0

    loop(4, weigh)
    for i, z in enumerate((3, 4, 11, 12)):
        for s in range(8):
            ec[s, 8 * z:8 * z + 8, :] += sw[i]
    for t, z in ((tzb[0], 0), (tc[TZP, 56:64, :], 7), (tc[TZM, 64:72, :], 8), (tzb[1], 15)):
        for s in range(4, 8):
            ec[s, 8 * z:8 * z + 8, :] += t

    def x_swap(q):
        return jnp.where(x1 == 3, roll_x(q, 7), jnp.where(x1 == 4, roll_x(q, 1), 0.0))

    def y_swap(q):
        return jnp.where(m1 == 7, roll_y(q, 127), jnp.where(m1 == 0, roll_y(q, 1), 0.0))

    def far(g):
        return one_plane(4 * g + 4 - 5 * (g % 2))

    def rest(g):
        rows = group(g)
        here = pp[rows, :]
        full = plane_sum(ec[0, rows, :] * here - ss[rows, :]) - sw[g] * pp[far(g), :]
        fl[8, one_plane(g), :] = (
            full - x_swap(plane_sum(ec[8, rows, :] * here)) - y_swap(plane_sum(ec[9, rows, :] * here)))

    loop(4, rest)

    for copy in sent2:
        copy.wait_recv()
    for copy in sent:
        copy.wait_send()
    outer(vb, 0, va, 1, hxr2, hzr2, 0)
    store = pltpu.make_async_copy(va.at[pl.ds(1, 8)], v_out, out_sem.at[0])
    store.start()

    def gather(g):
        rows = group(g)
        sx0, sy0 = ec[8, rows, :], ec[9, rows, :]
        vals = [va[1 + s, rows, :] for s in range(8)]
        qx = [x_swap(plane_sum(sx0 * v)) for v in vals]
        qy = [y_swap(plane_sum(sy0 * v)) for v in vals]
        for s in range(8):
            full = plane_sum(ec[s, rows, :] * vals[s]) - sw[g] * va[1 + (s ^ 4), far(g), :]
            fl[s, one_plane(g), :] = full - qx[s ^ 2] - qy[s ^ 1]

    loop(4, gather)

    def z_part(j, pz, s):
        groups = ((0,), (1, 2), (3,))[j] if pz == 1 else {(1, 0): (1,), (2, 0): (3,), (0, 2): (0,), (1, 2): (2,)}[j, pz]
        term = fl[s, one_plane(groups[0]), :]
        for g in groups[1:]:
            term += fl[s, one_plane(g), :]
        return term

    for k, (j, halves) in enumerate(((0, (1, 2)), (1, (1, 2)), (2, (1, 0)), (1, (0,)))):
        for half, pz in enumerate(halves):
            for b in range(2):
                at, s = 64 * half + 24 * b, (0 if pz == 1 else 4) + 2 * b
                side = z_part(j, pz, s + 1)
                es[k, at:at + 8, :] = jnp.where(m1 < 4, side, 0.0)
                es[k, at + 8:at + 16, :] = z_part(j, pz, s)
                es[k, at + 16:at + 24, :] = jnp.where(m1 < 4, 0.0, side)
        if k < 3:
            es[k, 48:56, :] = -z_part(j, 1, 8)

    m16 = m[:16]
    sums = []
    for k in range(4):
        for xi in range(2):
            t = es[k, pl.ds(4 * xi, 16, stride=8), :]
            for i in range(1, 4):
                t += es[k, pl.ds(4 * xi + i, 16, stride=8), :]
            sums.append(t)
    for bit in (4, 2, 1):
        high = (m16 & bit) != 0
        merged = []
        for u in range(bit):
            one, two = sums[u], sums[u + bit]
            move = jnp.where(high, one, two)
            merged.append(jnp.where(high, two, one) + jnp.where(high, roll_y(move, bit), roll_y(move, 128 - bit)))
        sums = merged
    rows_out = sums[0]
    cs[...] = rows_out
    crv[0] = rows_out

    def g_copy(r):
        return pltpu.make_async_remote_copy(
            src_ref=cs, dst_ref=crv.at[r], send_sem=g_s.at[r], recv_sem=g_r.at[r],
            device_id=partner(g_flips, r), device_id_type=MESH)

    loop(gn, lambda r: g_copy(r).start(), 1)

    xb[64:128, :] = jnp.zeros((64, gn * 128), BF16)

    def wanted(i):
        idx = row1 + i * 8
        peer = jnp.zeros_like(idx)
        for t in range(1, hn):
            peer += jnp.where(idx >= t * width, 1, 0)
        col = idx - peer * width
        dev = jnp.zeros_like(idx) + (ml * plane + mp)
        for b, (on_layer, step) in enumerate(h_flips):
            dev += ((peer >> b) & 1) * (step * plane if on_layer else step)
        want = dev * own + col
        for q in range(4):
            wt[one_plane(i + q * (n_idx // 8)), :] = jnp.where(col + q * width < own, want + q * width, -7)

    loop(n_idx // 8, wanted)

    loop(gn, lambda r: rank_copy(r).wait_recv(), 1)

    have = [rkr[r] for r in range(gn)]

    def build(i, carry):
        at = pl.multiple_of(i * 16, 16)
        want = wt[pl.ds(at, 16), :]
        for r in range(gn):
            oh[pl.ds(at, 16), 128 * r:128 * r + 128] = jnp.where(want == have[r], 1.0, 0.0).astype(BF16)
        return carry

    lax.fori_loop(0, 4 * n_idx // 16, build, 0)

    odd = m1 % 2 == 1
    b1 = (x1 >= 3) & (x1 < 6)
    b1_odd = b1 & odd

    def spread(r):
        got1, got2 = crv[r, 0:8, :], crv[r, 8:16, :]
        pz1 = jnp.where(m1 < 6, got1, 0.0)
        pz2 = jnp.where(m1 < 4, got2, 0.0)
        pz0 = jnp.where(m1 < 4, 0.0, jnp.where(m1 < 6, got2, got1))
        low1, low2, low0 = (jnp.where(b1_odd, v, 0.0) for v in (pz1, pz2, pz0))
        last = pltpu.roll(low1, 5, 0) + low2 + jnp.where(x1 >= 6, pltpu.roll(low0, 3, 0), 0.0)
        vals = jnp.concatenate([
            pz1 - low1 + jnp.where(x1 == 7, pltpu.roll(low0, 2, 0), 0.0), pz2 - low2, pz0 - low0, last], axis=0)
        high = vals.astype(BF16)
        lanes = slice(128 * r, 128 * r + 128)
        xb[0:32, lanes] = high
        xb[32:64, lanes] = (vals - high.astype(F32)).astype(BF16)

    def product(part):
        return lax.dot_general(
            oh[:, part], xb[:, part], (((1,), (1,)), ((), ())), preferred_element_type=F32)

    half = gn // 2
    loop(half, lambda r: g_copy(r).wait_recv(), 1)
    loop(half, spread)
    routed = product(slice(0, half * 128))
    loop(gn, lambda r: g_copy(r).wait_recv(), half)
    loop(gn, spread, half)
    routed += product(slice(half * 128, gn * 128))
    quarter = lax.broadcasted_iota(I32, (n_idx, 128), 1) >> 5
    packed = jnp.zeros((n_idx, 128), F32)
    for q in range(4):
        part = routed[q * n_idx:(q + 1) * n_idx]
        first_half = roll_y(part, 32 * q) if q else part
        second_half = part if q == 1 else roll_y(part, (32 * q + 96) % 128)
        packed = jnp.where(quarter == q, first_half + second_half, packed)
    for r in range(hn):
        hs[r] = packed[r * width:(r + 1) * width]

    def h_copy(r):
        return pltpu.make_async_remote_copy(
            src_ref=hs.at[r], dst_ref=hr.at[r], send_sem=h_s.at[r], recv_sem=h_r.at[r],
            device_id=partner(h_flips, r), device_id_type=MESH)

    loop(hn, lambda r: h_copy(r).start(), 1)
    loop(hn, lambda r: h_copy(r).wait_recv(), 1)
    final = hs[0]
    for r in range(1, hn):
        final += hr[r]
    f_out[0:width, :] = final

    store.wait()
    for copy in sent2:
        copy.wait_send()

    def drain(r):
        rank_copy(r).wait_send()
        g_copy(r).wait_send()

    loop(gn, drain, 1)
    loop(hn, lambda r: h_copy(r).wait_send(), 1)


def finish(own, width, v_in, f_in, v_out, cm_out, cr_out, ft, sem):
    store = pltpu.make_async_copy(v_in, v_out, sem)
    store.start()
    ft[0:16, :] = f_in[...]
    turned = ft[...].T
    lane = lax.broadcasted_iota(I32, (32, 128), 1)
    done = jnp.zeros((32, 128), F32)
    for q in range(4):
        part = turned[32 * q:32 * q + 32]
        here = (lane >= q * width) & (lane < (q + 1) * width)
        done = jnp.where(here, pltpu.roll(part, q * width, 1) if q else part, done)
    for pz, px, base in (
        (1, 1, 0), (1, 2, 3), (2, 1, 8), (2, 2, 11), (0, 1, 16), (0, 2, 19), (1, 0, 24), (2, 0, 27)):
        k = 9 * pz + 3 * px
        cm_out[k:k + 3, :] = done[base:base + 3, 0:own]
    cm_out[0:2, :] = done[30:32, 0:own]
    cm_out[2:3, :] = done[7:8, 0:own]
    cr_out[...] = done[6:7, 0:own]
    store.wait()


def per_device(sizes, basis_init, permeability, accumulation, pressure, source, support, block_of, curve_rank):
    lx, plane = sizes
    gn, hn = 2 ** len(G_BITS), 2 ** len(H_BITS)
    devices = lx * plane
    own = (curve_rank.shape[0] + devices - 1) // devices
    width = (own + 3) // 4
    flat = lambda v: v.reshape(v.shape[:-3] + (128, 128))
    t_rows = -(-curve_rank.shape[0] // 2048) * 16
    anywhere = pl.BlockSpec(memory_space=pl.ANY)
    vmem = pl.BlockSpec(memory_space=pltpu.VMEM)
    dma = pltpu.SemaphoreType.DMA
    cells = lambda *lead: pltpu.VMEM(lead + (128, 128), F32)
    basis, rows = pl.pallas_call(
        functools.partial(kernel, (lx, plane, own, width)),
        out_shape=(
            jax.ShapeDtypeStruct((8, 128, 128), F32),
            jax.ShapeDtypeStruct((16, 128), F32),
        ),
        in_specs=[anywhere] * 8,
        out_specs=(anywhere, vmem),
        scratch_shapes=[
            cells(8), pltpu.VMEM((8, 128, 128), I32), cells(), cells(), cells(),
            pltpu.VMEM((3, 8, 128), I32), pltpu.VMEM(curve_rank.shape, I32), pltpu.VMEM((t_rows, 128), I32),
            cells(9), cells(8), cells(8), cells(8), cells(12),
            pltpu.VMEM((2, 8, 128), F32), cells(10), pltpu.VMEM((4, 8, 128), F32),
            pltpu.VMEM((9, 32, 128), F32), cells(4),
            pltpu.VMEM((2, 5, 16, 128), F32), pltpu.VMEM((2, 5, 16, 128), F32), pltpu.VMEM((2, 5, 8, 128), F32),
            pltpu.VMEM((2, 4, 16, 128), F32), pltpu.VMEM((2, 4, 16, 128), F32), pltpu.VMEM((2, 4, 8, 128), F32),
            pltpu.VMEM((1, 128), I32), pltpu.VMEM((gn, 1, 128), I32),
            pltpu.VMEM((4 * hn * width, 128), I32), pltpu.VMEM((4 * hn * width, gn * 128), BF16),
            pltpu.VMEM((128, gn * 128), BF16), pltpu.VMEM((4, 128, 128), F32),
            pltpu.VMEM((16, 128), F32), pltpu.VMEM((gn, 16, 128), F32),
            pltpu.VMEM((hn, width, 128), F32), pltpu.VMEM((hn, width, 128), F32),
            dma((10,)), dma((1,)), dma((8,)), dma((8,)),
            dma((gn,)), dma((gn,)), dma((gn,)), dma((gn,)), dma((hn,)), dma((hn,)),
        ],
        compiler_params=pltpu.CompilerParams(
            collective_id=0, has_side_effects=True, vmem_limit_bytes=VMEM_GRANT),
        cost_estimate=pl.CostEstimate(flops=20_000_000, bytes_accessed=2_000_000, transcendentals=0),
    )(*(pltpu.with_memory_space_constraint(v, pltpu.HBM) for v in (
        flat(basis_init), flat(permeability), flat(accumulation), flat(pressure), flat(source),
        flat(support), flat(block_of), curve_rank,
    )))
    basis, matrix, residual = pl.pallas_call(
        functools.partial(finish, own, width),
        out_shape=(
            jax.ShapeDtypeStruct((8, 128, 128), F32),
            jax.ShapeDtypeStruct((27, own), F32),
            jax.ShapeDtypeStruct((1, own), F32),
        ),
        in_specs=[anywhere, vmem],
        out_specs=(anywhere, vmem, vmem),
        scratch_shapes=[cells(), dma],
        compiler_params=pltpu.CompilerParams(vmem_limit_bytes=VMEM_GRANT),
    )(basis, rows)
    return basis.reshape(basis_init.shape), matrix, residual.reshape(own)


def solution(mesh):
    return jax.shard_map(
        functools.partial(per_device, (mesh.shape["layer"], mesh.shape["plane"])),
        mesh=mesh,
        in_specs=(
            P(None, "layer", "plane", None),
            P("layer", "plane", None),
            P("layer", "plane", None),
            P("layer", "plane", None),
            P("layer", "plane", None),
            P(None, "layer", "plane", None),
            P("layer", "plane", None),
            P(),
        ),
        out_specs=(
            P(None, "layer", "plane", None),
            P(None, ("layer", "plane")),
            P(("layer", "plane")),
        ),
        check_vma=False,
    )
```

```python
import functools

import jax
import jax.numpy as jnp
from jax import lax
from jax.experimental import pallas as pl
from jax.experimental.pallas import tpu as pltpu
from jax.sharding import PartitionSpec as P

MESH = pl.DeviceIdType.MESH
F32, BF16, I32 = jnp.float32, jnp.bfloat16, jnp.int32

G_BITS = (("layer", 1), ("plane", 1), ("plane", 2), ("plane", 16))
H_BITS = (("layer", 2), ("plane", 4), ("plane", 8), ("plane", 32))
VMEM_GRANT = 32 * 1024 * 1024
THIRD, TWO_THIRDS = 1.0 / 3.0, 2.0 / 3.0
B0 = (0, 1, 4, 5)
A0 = (0, 1, 2, 3)
TYM, TYP, TYM1, TYP1, TXM, TXP, TZM, TZP, TZM1, TZP1, TXB, RD = range(12)


def roll_x(v, shift):
    rows = v.shape[0]
    return pltpu.roll(v.reshape(rows // 8, 8, 128), shift, 1).reshape(rows, 128)


def roll_y(v, shift):
    return pltpu.roll(v, shift, 1)


def harmonic(k, n):
    return 2.0 * k * n / (k + n)


def plane_sum(v):
    return v.reshape(-1, 8, 128).sum(axis=0)


def kernel(
    dims,
    bi_hbm, k_hbm, a_hbm, p_hbm, s_hbm, sup_hbm, blk_hbm, cr_hbm,
    v_out, f_out,
    bi, sup, aa, pp, ss, blk, cr1, tab,
    va, vb, sf, nn, tc, tzb, ec, sw, fl, hx, hxs, hxr, hzr, hxs2, hxr2, hzr2,
    rks, rkr, wt, oh, xb, es, cs, crv, hs, hr,
    in_sem, out_sem, halo_s, halo_r, rk_s, rk_r, g_s, g_r, h_s, h_r,
):
    lx, plane, own, width = dims
    gn, hn = 2 ** len(G_BITS), 2 ** len(H_BITS)
    n_idx = hn * width
    ml, mp = lax.axis_index("layer"), lax.axis_index("plane")

    def flips(bits):
        steps = []
        for axis, bit in bits:
            at = ml if axis == "layer" else mp
            steps.append((axis == "layer", bit * (1 - 2 * ((at // bit) % 2))))
        return steps

    g_flips, h_flips = flips(G_BITS), flips(H_BITS)

    def partner(steps, r):
        to_l, to_p = ml, mp
        for i, (on_layer, step) in enumerate(steps):
            if (r >> i) & 1:
                to_l, to_p = (to_l + step, to_p) if on_layer else (to_l, to_p + step)
        return (to_l, to_p)

    up_x, down_x = (ml, (mp + 1) % plane), (ml, (mp + plane - 1) % plane)
    up_z, down_z = ((ml + 1) % lx, mp), ((ml + lx - 1) % lx, mp)

    def loop(n, body, start=0):
        for i in range(start, n):
            body(i)

    def group(g):
        return slice(g * 32, g * 32 + 32)

    def one_plane(z):
        return slice(z * 8, z * 8 + 8)

    loads = [
        pltpu.make_async_copy(k_hbm, va.at[0], in_sem.at[0]),
        pltpu.make_async_copy(bi_hbm, bi, in_sem.at[1]),
        pltpu.make_async_copy(sup_hbm, sup, in_sem.at[2]),
        pltpu.make_async_copy(a_hbm, aa, in_sem.at[3]),
        pltpu.make_async_copy(cr_hbm, cr1, in_sem.at[4]),
        pltpu.make_async_copy(p_hbm, pp, in_sem.at[5]),
        pltpu.make_async_copy(s_hbm, ss, in_sem.at[6]),
    ]
    for j, z in enumerate((0, 4, 12)):
        loads.append(pltpu.make_async_copy(blk_hbm.at[pl.ds(8 * z, 8)], blk.at[j], in_sem.at[7 + j]))
    barrier = pltpu.get_barrier_semaphore()

    def greet(who):
        pl.semaphore_signal(barrier, inc=1, device_id=who, device_id_type=MESH)

    greet(up_x)
    greet(down_x)
    greet(up_z)
    greet(down_z)
    for load in loads[:3]:
        load.start()
    loop(gn, lambda r: greet(partner(g_flips, r)), 1)
    loop(hn, lambda r: greet(partner(h_flips, r)), 1)
    for load in loads[3:]:
        load.start()

    lane = lax.broadcasted_iota(I32, (32, 128), 1)
    m, x = lane % 8, lax.broadcasted_iota(I32, (32, 128), 0) % 8
    m1, x1 = m[:8], x[:8]
    lane1, row1 = lane[:8], x[:8]
    is_m = {i: m == i for i in (0, 3, 4, 7)}
    is_x = {i: x == i for i in (3, 4)}

    hx[...] = jnp.zeros_like(hx)
    tc[TXB] = jnp.zeros((128, 128), F32)

    loads[0].wait()

    def faces(g):
        rows, below = group(g), one_plane((4 * g + 15) % 16)
        k = va[0, rows, :]
        tym = jnp.where(lane == 0, 0.0, harmonic(k, roll_y(k, 1)))
        typ = roll_y(tym, 127)
        tc[TYM, rows, :] = tym
        tc[TYP, rows, :] = typ
        tc[TYM1, rows, :] = jnp.where(is_m[4], 0.0, tym)
        tc[TYP1, rows, :] = jnp.where(is_m[3], 0.0, typ)
        txm = jnp.where(x == 0, 0.0, harmonic(k, roll_x(k, 1)))
        tc[TXM, rows, :] = txm
        tc[TXP, rows, :] = roll_x(txm, 7)
        tz = harmonic(k, jnp.concatenate([va[0, below, :], k[0:24]], axis=0))
        tc[TZM, rows, :] = tz
        tc[TZP, below, :] = tz[0:8]
        tc[TZP, slice(g * 32, g * 32 + 24), :] = tz[8:32]
        tc[TZM1, rows, :] = tz
        tc[TZP1, below, :] = tz[0:8]
        tc[TZP1, slice(g * 32, g * 32 + 24), :] = tz[8:32]

    loop(4, faces)
    nil = jnp.zeros((8, 128), F32)
    tc[TZM, 0:8, :] = nil
    tc[TZP, 120:128, :] = nil
    tc[TZM1, 0:8, :] = nil
    tc[TZP1, 120:128, :] = nil
    tc[TZM1, 64:72, :] = nil
    tc[TZP1, 56:64, :] = nil
    for i, (t, z) in enumerate(((TZP, 3), (TZM, 4), (TZP, 11), (TZM, 12))):
        sw[i] = tc[t, 8 * z:8 * z + 8, :]

    loads[1].wait()
    loads[2].wait()

    def first(g):
        rows = group(g)
        vals = []
        for s in range(8):
            on = sup[s, rows, :].astype(F32)
            sf[s, rows, :] = on
            vals.append(bi[s, rows, :] * on)
        inv = 1.0 / sum(vals[1:], vals[0])
        for s in range(8):
            va[1 + s, rows, :] = vals[s] * inv

    loop(4, first)

    def exchange(v, off, xs_buf, xr_buf, zr_buf, base):
        for i, s in enumerate(B0):
            xs_buf[0, off + i] = v[off + s, pl.ds(0, 16, stride=8), :]
            xs_buf[1, off + i] = v[off + s, pl.ds(7, 16, stride=8), :]
        if off:
            xs_buf[0, 0] = v[0, pl.ds(0, 16, stride=8), :]
            xs_buf[1, 0] = v[0, pl.ds(7, 16, stride=8), :]
            pl.semaphore_wait(barrier, 2 + gn + hn)
        last, lead = v.at[pl.ds(0, off + 4), pl.ds(120, 8)], v.at[pl.ds(0, off + 4), pl.ds(0, 8)]
        copies = []
        for j, (src, dst, who) in enumerate((
            (xs_buf.at[1], xr_buf.at[0], up_x), (xs_buf.at[0], xr_buf.at[1], down_x),
            (last, zr_buf.at[0], up_z), (lead, zr_buf.at[1], down_z),
        )):
            copies.append(pltpu.make_async_remote_copy(
                src_ref=src, dst_ref=dst, send_sem=halo_s.at[base + j], recv_sem=halo_r.at[base + j],
                device_id=who, device_id_type=MESH))
        for copy in copies:
            copy.start()
        return copies

    def inner(v, off):
        def part(g):
            rows = group(g)
            odd = g % 2
            below, above = one_plane((4 * g + 15) % 16), one_plane((4 * g + 4) % 16)
            for s in range(8):
                if s % 4 == 0:
                    vals = [v[off + s + i, rows, :] for i in range(4)]
                    txm, txp = tc[TXM, rows, :], tc[TXP, rows, :]
                    tym, typ = [tc[i, rows, :] for i in (TYM, TYM1)], [tc[i, rows, :] for i in (TYP, TYP1)]
                    zm, zp = tc[TZM1 if s else TZM, rows, :], tc[TZP1 if s else TZP, rows, :]
                here, by_y, by_x, turn = vals[s % 4], vals[s % 4 ^ 1], vals[s % 4 ^ 2], 4 - (s & 4) * 2
                near = tym[s & 1] * roll_y(jnp.where(is_m[7], by_y, here), 1)
                near += typ[s & 1] * roll_y(jnp.where(is_m[0], by_y, here), 127)
                near += txm * roll_x(jnp.where(is_x[3], by_x, here), 1)
                near += txp * roll_x(jnp.where(is_x[4], by_x, here), 7)
                lo, hi = v[off + s + turn * odd, below, :], v[off + s + turn * (1 - odd), above, :]
                near += zm * jnp.concatenate([lo, here[0:24]], axis=0)
                near += zp * jnp.concatenate([here[8:32], hi], axis=0)
                nn[s, rows, :] = near

        loop(4, part)

    def outer(v, off, new, off2, xr_buf, zr_buf, extra):
        for i in range(4):
            hx[i, pl.ds(0, 16, stride=8), :] = xr_buf[0, extra + i]
            hx[i, pl.ds(7, 16, stride=8), :] = xr_buf[1, extra + i]
            nn[i, 0:8, :] += tzb[0] * zr_buf[0, extra + i]
            nn[i, 120:128, :] += tzb[1] * zr_buf[1, extra + i]

        def part(g):
            rows = group(g)
            rd, txb = tc[RD, rows, :], tc[TXB, rows, :]
            vals = []
            for s in range(8):
                near = nn[s, rows, :]
                if s in B0:
                    near += txb * hx[B0.index(s), rows, :]
                vals.append((v[off + s, rows, :] * THIRD + rd * near) * sf[s, rows, :])
            inv = 1.0 / sum(vals[1:], vals[0])
            for s in range(8):
                new[off2 + s, rows, :] = vals[s] * inv

        loop(4, part)

    sent = exchange(va, 1, hxs, hxr, hzr, 0)
    inner(va, 1)
    loads[3].wait()
    for copy in sent:
        copy.wait_recv()

    tc[TXB, pl.ds(0, 16, stride=8), :] = jnp.where(mp > 0, harmonic(hxs[0, 0], hxr[0, 0]), 0.0)
    tc[TXB, pl.ds(7, 16, stride=8), :] = jnp.where(mp < plane - 1, harmonic(hxs[1, 0], hxr[1, 0]), 0.0)
    tzb[0] = jnp.where(ml > 0, harmonic(va[0, 0:8, :], hzr[0, 0]), 0.0)
    tzb[1] = jnp.where(ml < lx - 1, harmonic(va[0, 120:128, :], hzr[1, 0]), 0.0)

    def scale(g):
        rows = group(g)
        diag = aa[rows, :]
        for t in (TYM, TYP, TXM, TXP, TXB, TZM, TZP):
            diag += tc[t, rows, :]
        tc[RD, rows, :] = diag

    loop(4, scale)
    tc[RD, 0:8, :] += tzb[0]
    tc[RD, 120:128, :] += tzb[1]
    tc[RD] = TWO_THIRDS / tc[RD]

    outer(va, 1, vb, 0, hxr, hzr, 1)
    sent2 = exchange(vb, 0, hxs2, hxr2, hzr2, 4)

    for load in loads[4:]:
        load.wait()
    label = blk[0, 0:1, :]
    for u, (j, r) in enumerate(((0, 0), (0, 4), (1, 0), (1, 4), (2, 0), (2, 4), (1, 0), (1, 4))):
        label = jnp.where(m1[0:1] == u, blk[j, r:r + 1, :], label)
    t_rows, labels = tab.shape[0], cr1.shape[0]
    tab[labels // 128:, :] = jnp.zeros((t_rows - labels // 128, 128), I32)

    def table(t):
        tab[t:t + 1, :] = cr1[pl.ds(t * 128, 128)].reshape(1, 128)

    loop(labels // 128, table)
    if labels % 128:
        t = labels // 128
        tab[t:t + 1, 0:labels % 128] = cr1[pl.ds(t * 128, labels % 128)].reshape(1, labels % 128)
    l_hi, l_lo = label >> 7, label & 127
    w_iota = lax.broadcasted_iota(I32, (128, 128), 0)
    pick = jnp.where(w_iota == l_lo, 1.0, 0.0).astype(BF16)
    ranks = tab[...]
    parts = jnp.concatenate([(ranks >> 7).astype(F32), (ranks & 127).astype(F32)], axis=0).astype(BF16)
    looked = jnp.dot(parts, pick, preferred_element_type=F32)
    t_iota = lax.broadcasted_iota(I32, (t_rows, 128), 0)
    looked = looked[:t_rows] * 128.0 + looked[t_rows:]
    rank = jnp.sum(jnp.where(t_iota == l_hi, looked, 0.0), axis=0, keepdims=True)
    rank = rank.astype(I32)
    rks[...] = rank
    rkr[0] = rank

    def rank_copy(r):
        return pltpu.make_async_remote_copy(
            src_ref=rks, dst_ref=rkr.at[r], send_sem=rk_s.at[r], recv_sem=rk_r.at[r],
            device_id=partner(g_flips, r), device_id_type=MESH)

    loop(gn, lambda r: rank_copy(r).start(), 1)
    es[...] = jnp.zeros_like(es)

    inner(vb, 0)

    def weigh(g):
        rows = group(g)
        tym, typ, txm, txp = (tc[i, rows, :] for i in (TYM, TYP, TXM, TXP))
        sx0 = jnp.where(is_x[3], txp, 0.0) + jnp.where(is_x[4], txm, 0.0)
        sx1 = sx0 + tc[TXB, rows, :]
        sy0 = jnp.where(is_m[7], typ, 0.0) + jnp.where(is_m[0], tym, 0.0)
        sy1 = sy0 + jnp.where(is_m[3], typ, 0.0) + jnp.where(is_m[4], tym, 0.0)
        for s in range(4):
            d = aa[rows, :] + (sx1 if s & 2 else sx0) + (sy1 if s & 1 else sy0)
            ec[s, rows, :] = d
            ec[4 + s, rows, :] = d
        ec[8, rows, :] = sx0
        ec[9, rows, :] = sy0

    loop(4, weigh)
    for i, z in enumerate((3, 4, 11, 12)):
        for s in range(8):
            ec[s, 8 * z:8 * z + 8, :] += sw[i]
    for t, z in ((tzb[0], 0), (tc[TZP, 56:64, :], 7), (tc[TZM, 64:72, :], 8), (tzb[1], 15)):
        for s in range(4, 8):
            ec[s, 8 * z:8 * z + 8, :] += t

    def x_swap(q):
        return jnp.where(x1 == 3, roll_x(q, 7), jnp.where(x1 == 4, roll_x(q, 1), 0.0))

    def y_swap(q):
        return jnp.where(m1 == 7, roll_y(q, 127), jnp.where(m1 == 0, roll_y(q, 1), 0.0))

    def far(g):
        return one_plane(4 * g + 4 - 5 * (g % 2))

    def rest(g):
        rows = group(g)
        here = pp[rows, :]
        full = plane_sum(ec[0, rows, :] * here - ss[rows, :]) - sw[g] * pp[far(g), :]
        fl[8, one_plane(g), :] = (
            full - x_swap(plane_sum(ec[8, rows, :] * here)) - y_swap(plane_sum(ec[9, rows, :] * here)))

    loop(4, rest)

    for copy in sent2:
        copy.wait_recv()
    for copy in sent:
        copy.wait_send()
    outer(vb, 0, va, 1, hxr2, hzr2, 0)
    store = pltpu.make_async_copy(va.at[pl.ds(1, 8)], v_out, out_sem.at[0])
    store.start()

    def gather(g):
        rows = group(g)
        sx0, sy0 = ec[8, rows, :], ec[9, rows, :]
        vals = [va[1 + s, rows, :] for s in range(8)]
        qx = [x_swap(plane_sum(sx0 * v)) for v in vals]
        qy = [y_swap(plane_sum(sy0 * v)) for v in vals]
        for s in range(8):
            full = plane_sum(ec[s, rows, :] * vals[s]) - sw[g] * va[1 + (s ^ 4), far(g), :]
            fl[s, one_plane(g), :] = full - qx[s ^ 2] - qy[s ^ 1]

    loop(4, gather)

    def z_part(j, pz, s):
        groups = ((0,), (1, 2), (3,))[j] if pz == 1 else {(1, 0): (1,), (2, 0): (3,), (0, 2): (0,), (1, 2): (2,)}[j, pz]
        term = fl[s, one_plane(groups[0]), :]
        for g in groups[1:]:
            term += fl[s, one_plane(g), :]
        return term

    for k, (j, halves) in enumerate(((0, (1, 2)), (1, (1, 2)), (2, (1, 0)), (1, (0,)))):
        for half, pz in enumerate(halves):
            for b in range(2):
                at, s = 64 * half + 24 * b, (0 if pz == 1 else 4) + 2 * b
                side = z_part(j, pz, s + 1)
                es[k, at:at + 8, :] = jnp.where(m1 < 4, side, 0.0)
                es[k, at + 8:at + 16, :] = z_part(j, pz, s)
                es[k, at + 16:at + 24, :] = jnp.where(m1 < 4, 0.0, side)
        if k < 3:
            es[k, 48:56, :] = -z_part(j, 1, 8)

    m16 = m[:16]
    sums = []
    for k in range(4):
        for xi in range(2):
            t = es[k, pl.ds(4 * xi, 16, stride=8), :]
            for i in range(1, 4):
                t += es[k, pl.ds(4 * xi + i, 16, stride=8), :]
            sums.append(t)
    for bit in (4, 2, 1):
        high = (m16 & bit) != 0
        merged = []
        for u in range(bit):
            one, two = sums[u], sums[u + bit]
            move = jnp.where(high, one, two)
            merged.append(jnp.where(high, two, one) + jnp.where(high, roll_y(move, bit), roll_y(move, 128 - bit)))
        sums = merged
    rows_out = sums[0]
    cs[...] = rows_out
    crv[0] = rows_out

    def g_copy(r):
        return pltpu.make_async_remote_copy(
            src_ref=cs, dst_ref=crv.at[r], send_sem=g_s.at[r], recv_sem=g_r.at[r],
            device_id=partner(g_flips, r), device_id_type=MESH)

    loop(gn, lambda r: g_copy(r).start(), 1)

    xb[64:128, :] = jnp.zeros((64, gn * 128), BF16)

    def wanted(i):
        idx = row1 + i * 8
        peer = jnp.zeros_like(idx)
        for t in range(1, hn):
            peer += jnp.where(idx >= t * width, 1, 0)
        col = idx - peer * width
        dev = jnp.zeros_like(idx) + (ml * plane + mp)
        for b, (on_layer, step) in enumerate(h_flips):
            dev += ((peer >> b) & 1) * (step * plane if on_layer else step)
        want = dev * own + col
        for q in range(4):
            wt[one_plane(i + q * (n_idx // 8)), :] = jnp.where(col + q * width < own, want + q * width, -7)

    loop(n_idx // 8, wanted)

    loop(gn, lambda r: rank_copy(r).wait_recv(), 1)

    have = [rkr[r] for r in range(gn)]

    def build(i, carry):
        at = pl.multiple_of(i * 16, 16)
        want = wt[pl.ds(at, 16), :]
        for r in range(gn):
            oh[pl.ds(at, 16), 128 * r:128 * r + 128] = jnp.where(want == have[r], 1.0, 0.0).astype(BF16)
        return carry

    lax.fori_loop(0, 4 * n_idx // 16, build, 0)

    odd = m1 % 2 == 1
    b1 = (x1 >= 3) & (x1 < 6)
    b1_odd = b1 & odd

    def spread(r):
        got1, got2 = crv[r, 0:8, :], crv[r, 8:16, :]
        pz1 = jnp.where(m1 < 6, got1, 0.0)
        pz2 = jnp.where(m1 < 4, got2, 0.0)
        pz0 = jnp.where(m1 < 4, 0.0, jnp.where(m1 < 6, got2, got1))
        low1, low2, low0 = (jnp.where(b1_odd, v, 0.0) for v in (pz1, pz2, pz0))
        last = pltpu.roll(low1, 5, 0) + low2 + jnp.where(x1 >= 6, pltpu.roll(low0, 3, 0), 0.0)
        vals = jnp.concatenate([
            pz1 - low1 + jnp.where(x1 == 7, pltpu.roll(low0, 2, 0), 0.0), pz2 - low2, pz0 - low0, last], axis=0)
        high = vals.astype(BF16)
        lanes = slice(128 * r, 128 * r + 128)
        xb[0:32, lanes] = high
        xb[32:64, lanes] = (vals - high.astype(F32)).astype(BF16)

    def product(part):
        return lax.dot_general(
            oh[:, part], xb[:, part], (((1,), (1,)), ((), ())), preferred_element_type=F32)

    half = gn // 2
    loop(half, lambda r: g_copy(r).wait_recv(), 1)
    loop(half, spread)
    routed = product(slice(0, half * 128))
    loop(gn, lambda r: g_copy(r).wait_recv(), half)
    loop(gn, spread, half)
    routed += product(slice(half * 128, gn * 128))
    quarter = lax.broadcasted_iota(I32, (n_idx, 128), 1) >> 5
    packed = jnp.zeros((n_idx, 128), F32)
    for q in range(4):
        part = routed[q * n_idx:(q + 1) * n_idx]
        first_half = roll_y(part, 32 * q) if q else part
        second_half = part if q == 1 else roll_y(part, (32 * q + 96) % 128)
        packed = jnp.where(quarter == q, first_half + second_half, packed)
    for r in range(hn):
        hs[r] = packed[r * width:(r + 1) * width]

    def h_copy(r):
        return pltpu.make_async_remote_copy(
            src_ref=hs.at[r], dst_ref=hr.at[r], send_sem=h_s.at[r], recv_sem=h_r.at[r],
            device_id=partner(h_flips, r), device_id_type=MESH)

    loop(hn, lambda r: h_copy(r).start(), 1)
    loop(hn, lambda r: h_copy(r).wait_recv(), 1)
    final = hs[0]
    for r in range(1, hn):
        final += hr[r]
    f_out[0:width, :] = final

    store.wait()
    for copy in sent2:
        copy.wait_send()

    def drain(r):
        rank_copy(r).wait_send()
        g_copy(r).wait_send()

    loop(gn, drain, 1)
    loop(hn, lambda r: h_copy(r).wait_send(), 1)


def finish(own, width, v_in, f_in, v_out, cm_out, cr_out, ft, sem):
    store = pltpu.make_async_copy(v_in, v_out, sem)
    store.start()
    ft[0:16, :] = f_in[...]
    turned = ft[...].T
    lane = lax.broadcasted_iota(I32, (32, 128), 1)
    done = jnp.zeros((32, 128), F32)
    for q in range(4):
        part = turned[32 * q:32 * q + 32]
        here = (lane >= q * width) & (lane < (q + 1) * width)
        done = jnp.where(here, pltpu.roll(part, q * width, 1) if q else part, done)
    for pz, px, base in (
        (1, 1, 0), (1, 2, 3), (2, 1, 8), (2, 2, 11), (0, 1, 16), (0, 2, 19), (1, 0, 24), (2, 0, 27)):
        k = 9 * pz + 3 * px
        cm_out[k:k + 3, :] = done[base:base + 3, 0:own]
    cm_out[0:2, :] = done[30:32, 0:own]
    cm_out[2:3, :] = done[7:8, 0:own]
    cr_out[...] = done[6:7, 0:own]
    store.wait()


def per_device(sizes, basis_init, permeability, accumulation, pressure, source, support, block_of, curve_rank):
    lx, plane = sizes
    gn, hn = 2 ** len(G_BITS), 2 ** len(H_BITS)
    devices = lx * plane
    own = (curve_rank.shape[0] + devices - 1) // devices
    width = (own + 3) // 4
    flat = lambda v: v.reshape(v.shape[:-3] + (128, 128))
    t_rows = -(-curve_rank.shape[0] // 2048) * 16
    anywhere = pl.BlockSpec(memory_space=pl.ANY)
    vmem = pl.BlockSpec(memory_space=pltpu.VMEM)
    dma = pltpu.SemaphoreType.DMA
    cells = lambda *lead: pltpu.VMEM(lead + (128, 128), F32)
    basis, rows = pl.pallas_call(
        functools.partial(kernel, (lx, plane, own, width)),
        out_shape=(
            jax.ShapeDtypeStruct((8, 128, 128), F32),
            jax.ShapeDtypeStruct((16, 128), F32),
        ),
        in_specs=[anywhere] * 8,
        out_specs=(anywhere, vmem),
        scratch_shapes=[
            cells(8), pltpu.VMEM((8, 128, 128), I32), cells(), cells(), cells(),
            pltpu.VMEM((3, 8, 128), I32), pltpu.VMEM(curve_rank.shape, I32), pltpu.VMEM((t_rows, 128), I32),
            cells(9), cells(8), cells(8), cells(8), cells(12),
            pltpu.VMEM((2, 8, 128), F32), cells(10), pltpu.VMEM((4, 8, 128), F32),
            pltpu.VMEM((9, 32, 128), F32), cells(4),
            pltpu.VMEM((2, 5, 16, 128), F32), pltpu.VMEM((2, 5, 16, 128), F32), pltpu.VMEM((2, 5, 8, 128), F32),
            pltpu.VMEM((2, 4, 16, 128), F32), pltpu.VMEM((2, 4, 16, 128), F32), pltpu.VMEM((2, 4, 8, 128), F32),
            pltpu.VMEM((1, 128), I32), pltpu.VMEM((gn, 1, 128), I32),
            pltpu.VMEM((4 * hn * width, 128), I32), pltpu.VMEM((4 * hn * width, gn * 128), BF16),
            pltpu.VMEM((128, gn * 128), BF16), pltpu.VMEM((4, 128, 128), F32),
            pltpu.VMEM((16, 128), F32), pltpu.VMEM((gn, 16, 128), F32),
            pltpu.VMEM((hn, width, 128), F32), pltpu.VMEM((hn, width, 128), F32),
            dma((10,)), dma((1,)), dma((8,)), dma((8,)),
            dma((gn,)), dma((gn,)), dma((gn,)), dma((gn,)), dma((hn,)), dma((hn,)),
        ],
        compiler_params=pltpu.CompilerParams(
            collective_id=0, has_side_effects=True, vmem_limit_bytes=VMEM_GRANT),
        cost_estimate=pl.CostEstimate(flops=20_000_000, bytes_accessed=2_000_000, transcendentals=0),
    )(*(pltpu.with_memory_space_constraint(v, pltpu.HBM) for v in (
        flat(basis_init), flat(permeability), flat(accumulation), flat(pressure), flat(source),
        flat(support), flat(block_of), curve_rank,
    )))
    basis, matrix, residual = pl.pallas_call(
        functools.partial(finish, own, width),
        out_shape=(
            jax.ShapeDtypeStruct((8, 128, 128), F32),
            jax.ShapeDtypeStruct((27, own), F32),
            jax.ShapeDtypeStruct((1, own), F32),
        ),
        in_specs=[anywhere, vmem],
        out_specs=(anywhere, vmem, vmem),
        scratch_shapes=[cells(), dma],
        compiler_params=pltpu.CompilerParams(vmem_limit_bytes=VMEM_GRANT),
    )(basis, rows)
    return basis.reshape(basis_init.shape), matrix, residual.reshape(own)


def solution(mesh):
    return jax.shard_map(
        functools.partial(per_device, (mesh.shape["layer"], mesh.shape["plane"])),
        mesh=mesh,
        in_specs=(
            P(None, "layer", "plane", None),
            P("layer", "plane", None),
            P("layer", "plane", None),
            P("layer", "plane", None),
            P("layer", "plane", None),
            P(None, "layer", "plane", None),
            P("layer", "plane", None),
            P(),
        ),
        out_specs=(
            P(None, "layer", "plane", None),
            P(None, ("layer", "plane")),
            P(("layer", "plane")),
        ),
        check_vma=False,
    )
```

```python
import functools

import jax
import jax.numpy as jnp
from jax import lax
from jax.experimental import pallas as pl
from jax.experimental.pallas import tpu as pltpu
from jax.sharding import PartitionSpec as P

MESH = pl.DeviceIdType.MESH
F32, BF16, I32 = jnp.float32, jnp.bfloat16, jnp.int32

G_BITS = (("layer", 1), ("layer", 2), ("plane", 16), ("plane", 32))
H_BITS = (("plane", 1), ("plane", 2), ("plane", 4), ("plane", 8))
VMEM_GRANT = 32 * 1024 * 1024
THIRD, TWO_THIRDS = 1.0 / 3.0, 2.0 / 3.0
B0 = (0, 1, 4, 5)
A0 = (0, 1, 2, 3)
TYM, TYP, TYM1, TYP1, TXM, TXP, TZM, TZP, TZM1, TZP1, TXB, RD = range(12)


def roll_x(v, shift):
    rows = v.shape[0]
    return pltpu.roll(v.reshape(rows // 8, 8, 128), shift, 1).reshape(rows, 128)


def roll_y(v, shift):
    return pltpu.roll(v, shift, 1)


def harmonic(k, n):
    return 2.0 * k * n / (k + n)


def plane_sum(v):
    return v.reshape(-1, 8, 128).sum(axis=0)


def kernel(
    dims,
    bi_hbm, k_hbm, a_hbm, p_hbm, s_hbm, sup_hbm, blk_hbm, cr_hbm,
    v_out, f_out,
    bi, sup, aa, pp, ss, blk, cr1, tab,
    va, vb, sf, nn, tc, tzb, ec, sw, fl, hx, hxs, hxr, hzr, hxs2, hxr2, hzr2,
    rks, rkr, wt, oh, xb, es, cs, crv, hs, hr,
    round_y, round_z, in_sem, out_sem, halo_s, halo_r, rk_s, rk_r, g_s, g_r, h_s, h_r,
):
    lx, plane, own, width = dims
    gn, hn = 2 ** len(G_BITS), 2 ** len(H_BITS)
    zc = hn // 2
    n_idx = hn * width
    ml, mp = lax.axis_index("layer"), lax.axis_index("plane")

    def flips(bits):
        steps = []
        for axis, bit in bits:
            at = ml if axis == "layer" else mp
            steps.append((axis == "layer", bit * (1 - 2 * ((at // bit) % 2))))
        return steps

    g_flips, h_flips = flips(G_BITS), flips(H_BITS)

    def partner(steps, r):
        to_l, to_p = ml, mp
        for i, (on_layer, step) in enumerate(steps):
            if (r >> i) & 1:
                to_l, to_p = (to_l + step, to_p) if on_layer else (to_l, to_p + step)
        return (to_l, to_p)

    up_x, down_x = (ml, (mp + 1) % plane), (ml, (mp + plane - 1) % plane)
    up_z, down_z = ((ml + 1) % lx, mp), ((ml + lx - 1) % lx, mp)

    def loop(n, body, start=0):
        for i in range(start, n):
            body(i)

    def group(g):
        return slice(g * 32, g * 32 + 32)

    def one_plane(z):
        return slice(z * 8, z * 8 + 8)

    loads = [
        pltpu.make_async_copy(k_hbm, va.at[0], in_sem.at[0]),
        pltpu.make_async_copy(bi_hbm, bi, in_sem.at[1]),
        pltpu.make_async_copy(sup_hbm, sup, in_sem.at[2]),
        pltpu.make_async_copy(a_hbm, aa, in_sem.at[3]),
        pltpu.make_async_copy(cr_hbm, cr1, in_sem.at[4]),
        pltpu.make_async_copy(p_hbm, pp, in_sem.at[5]),
        pltpu.make_async_copy(s_hbm, ss, in_sem.at[6]),
    ]
    for j, z in enumerate((0, 4, 12)):
        loads.append(pltpu.make_async_copy(blk_hbm.at[pl.ds(8 * z, 8)], blk.at[j], in_sem.at[7 + j]))
    barrier = pltpu.get_barrier_semaphore()

    def greet(who):
        pl.semaphore_signal(barrier, inc=1, device_id=who, device_id_type=MESH)

    def along_z(dz, dc):
        return (ml, mp + dc * (1 - 2 * (mp % 2)) + 2 * ((mp // 2 + dz) % zc - (mp // 2) % zc))

    x_mask = sum(1 << i for i, (axis, _) in enumerate(G_BITS) if axis == "layer")
    x_peers = [r for r in range(1, gn) if r & x_mask == r]
    y_peers = [r for r in range(1, gn) if r & x_mask == 0]
    z_peers = [(dz, dc) for dz in (1, zc - 1, 2, zc - 2) for dc in (0, 1)] + [(0, 1)]
    greet(up_x)
    greet(down_x)
    for r in x_peers:
        greet(partner(g_flips, r))
    for load in loads[:3]:
        load.start()
    for r in y_peers:
        greet(partner(g_flips, r))
    for dz, dc in z_peers:
        greet(along_z(dz, dc))
    for load in loads[3:]:
        load.start()
    greeted = 2 + len(x_peers) + len(y_peers) + len(z_peers)

    def second_round():
        for r in y_peers:
            pl.semaphore_signal(round_y, inc=1, device_id=partner(g_flips, r), device_id_type=MESH)
        for dz in (2, zc - 2):
            pl.semaphore_signal(round_z, inc=1, device_id=along_z(dz, 0), device_id_type=MESH)

    lane = lax.broadcasted_iota(I32, (32, 128), 1)
    m, x = lane % 8, lax.broadcasted_iota(I32, (32, 128), 0) % 8
    m1, x1 = m[:8], x[:8]
    lane1, row1 = lane[:8], x[:8]
    is_m = {i: m == i for i in (0, 3, 4, 7)}
    is_x = {i: x == i for i in (3, 4)}

    hx[...] = jnp.zeros_like(hx)
    tc[TXB] = jnp.zeros((128, 128), F32)

    loads[0].wait()

    def faces(g):
        rows, below = group(g), one_plane((4 * g + 15) % 16)
        k = va[0, rows, :]
        tym = jnp.where(lane == 0, 0.0, harmonic(k, roll_y(k, 1)))
        typ = roll_y(tym, 127)
        tc[TYM, rows, :] = tym
        tc[TYP, rows, :] = typ
        tc[TYM1, rows, :] = jnp.where(is_m[4], 0.0, tym)
        tc[TYP1, rows, :] = jnp.where(is_m[3], 0.0, typ)
        txm = jnp.where(x == 0, 0.0, harmonic(k, roll_x(k, 1)))
        tc[TXM, rows, :] = txm
        tc[TXP, rows, :] = roll_x(txm, 7)
        tz = harmonic(k, jnp.concatenate([va[0, below, :], k[0:24]], axis=0))
        tc[TZM, rows, :] = tz
        tc[TZP, below, :] = tz[0:8]
        tc[TZP, slice(g * 32, g * 32 + 24), :] = tz[8:32]
        tc[TZM1, rows, :] = tz
        tc[TZP1, below, :] = tz[0:8]
        tc[TZP1, slice(g * 32, g * 32 + 24), :] = tz[8:32]

    loop(4, faces)
    nil = jnp.zeros((8, 128), F32)
    tc[TZM, 0:8, :] = nil
    tc[TZP, 120:128, :] = nil
    tc[TZM1, 0:8, :] = nil
    tc[TZP1, 120:128, :] = nil
    tc[TZM1, 64:72, :] = nil
    tc[TZP1, 56:64, :] = nil
    for i, (t, z) in enumerate(((TZP, 3), (TZM, 4), (TZP, 11), (TZM, 12))):
        sw[i] = tc[t, 8 * z:8 * z + 8, :]

    loads[1].wait()
    loads[2].wait()

    def first(g):
        rows = group(g)
        vals = []
        for s in range(8):
            on = sup[s, rows, :].astype(F32)
            sf[s, rows, :] = on
            vals.append(bi[s, rows, :] * on)
        inv = 1.0 / sum(vals[1:], vals[0])
        for s in range(8):
            va[1 + s, rows, :] = vals[s] * inv

    loop(4, first)

    def exchange(v, off, xs_buf, xr_buf, zr_buf, base):
        for i, s in enumerate(B0):
            xs_buf[0, off + i] = v[off + s, pl.ds(0, 16, stride=8), :]
            xs_buf[1, off + i] = v[off + s, pl.ds(7, 16, stride=8), :]
        if off:
            xs_buf[0, 0] = v[0, pl.ds(0, 16, stride=8), :]
            xs_buf[1, 0] = v[0, pl.ds(7, 16, stride=8), :]
            pl.semaphore_wait(barrier, greeted)
        last, lead = v.at[pl.ds(0, off + 4), pl.ds(120, 8)], v.at[pl.ds(0, off + 4), pl.ds(0, 8)]
        copies = []
        for j, (src, dst, who) in enumerate((
            (xs_buf.at[1], xr_buf.at[0], up_x), (xs_buf.at[0], xr_buf.at[1], down_x),
            (last, zr_buf.at[0], up_z), (lead, zr_buf.at[1], down_z),
        )):
            copies.append(pltpu.make_async_remote_copy(
                src_ref=src, dst_ref=dst, send_sem=halo_s.at[base + j], recv_sem=halo_r.at[base + j],
                device_id=who, device_id_type=MESH))
        for copy in copies:
            copy.start()
        if off:
            second_round()
        return copies

    def inner(v, off):
        def part(g):
            rows = group(g)
            odd = g % 2
            below, above = one_plane((4 * g + 15) % 16), one_plane((4 * g + 4) % 16)
            for s in range(8):
                if s % 4 == 0:
                    vals = [v[off + s + i, rows, :] for i in range(4)]
                    txm, txp = tc[TXM, rows, :], tc[TXP, rows, :]
                    tym, typ = [tc[i, rows, :] for i in (TYM, TYM1)], [tc[i, rows, :] for i in (TYP, TYP1)]
                    zm, zp = tc[TZM1 if s else TZM, rows, :], tc[TZP1 if s else TZP, rows, :]
                here, by_y, by_x, turn = vals[s % 4], vals[s % 4 ^ 1], vals[s % 4 ^ 2], 4 - (s & 4) * 2
                near = tym[s & 1] * roll_y(jnp.where(is_m[7], by_y, here), 1)
                near += typ[s & 1] * roll_y(jnp.where(is_m[0], by_y, here), 127)
                near += txm * roll_x(jnp.where(is_x[3], by_x, here), 1)
                near += txp * roll_x(jnp.where(is_x[4], by_x, here), 7)
                lo, hi = v[off + s + turn * odd, below, :], v[off + s + turn * (1 - odd), above, :]
                near += zm * jnp.concatenate([lo, here[0:24]], axis=0)
                near += zp * jnp.concatenate([here[8:32], hi], axis=0)
                nn[s, rows, :] = near

        loop(4, part)

    def outer(v, off, new, off2, xr_buf, zr_buf, extra):
        for i in range(4):
            hx[i, pl.ds(0, 16, stride=8), :] = xr_buf[0, extra + i]
            hx[i, pl.ds(7, 16, stride=8), :] = xr_buf[1, extra + i]
            nn[i, 0:8, :] += tzb[0] * zr_buf[0, extra + i]
            nn[i, 120:128, :] += tzb[1] * zr_buf[1, extra + i]

        def part(g):
            rows = group(g)
            rd, txb = tc[RD, rows, :], tc[TXB, rows, :]
            vals = []
            for s in range(8):
                near = nn[s, rows, :]
                if s in B0:
                    near += txb * hx[B0.index(s), rows, :]
                vals.append((v[off + s, rows, :] * THIRD + rd * near) * sf[s, rows, :])
            inv = 1.0 / sum(vals[1:], vals[0])
            for s in range(8):
                new[off2 + s, rows, :] = vals[s] * inv

        loop(4, part)

    sent = exchange(va, 1, hxs, hxr, hzr, 0)
    inner(va, 1)
    loads[3].wait()
    for copy in sent:
        copy.wait_recv()

    tc[TXB, pl.ds(0, 16, stride=8), :] = jnp.where(mp > 0, harmonic(hxs[0, 0], hxr[0, 0]), 0.0)
    tc[TXB, pl.ds(7, 16, stride=8), :] = jnp.where(mp < plane - 1, harmonic(hxs[1, 0], hxr[1, 0]), 0.0)
    tzb[0] = jnp.where(ml > 0, harmonic(va[0, 0:8, :], hzr[0, 0]), 0.0)
    tzb[1] = jnp.where(ml < lx - 1, harmonic(va[0, 120:128, :], hzr[1, 0]), 0.0)

    def scale(g):
        rows = group(g)
        diag = aa[rows, :]
        for t in (TYM, TYP, TXM, TXP, TXB, TZM, TZP):
            diag += tc[t, rows, :]
        tc[RD, rows, :] = diag

    loop(4, scale)
    tc[RD, 0:8, :] += tzb[0]
    tc[RD, 120:128, :] += tzb[1]
    tc[RD] = TWO_THIRDS / tc[RD]

    outer(va, 1, vb, 0, hxr, hzr, 1)
    sent2 = exchange(vb, 0, hxs2, hxr2, hzr2, 4)

    for load in loads[4:]:
        load.wait()
    label = blk[0, 0:1, :]
    for u, (j, r) in enumerate(((0, 0), (0, 4), (1, 0), (1, 4), (2, 0), (2, 4), (1, 0), (1, 4))):
        label = jnp.where(m1[0:1] == u, blk[j, r:r + 1, :], label)
    t_rows, labels = tab.shape[0], cr1.shape[0]
    tab[labels // 128:, :] = jnp.zeros((t_rows - labels // 128, 128), I32)

    def table(t):
        tab[t:t + 1, :] = cr1[pl.ds(t * 128, 128)].reshape(1, 128)

    loop(labels // 128, table)
    if labels % 128:
        t = labels // 128
        tab[t:t + 1, 0:labels % 128] = cr1[pl.ds(t * 128, labels % 128)].reshape(1, labels % 128)
    l_hi, l_lo = label >> 7, label & 127
    w_iota = lax.broadcasted_iota(I32, (128, 128), 0)
    pick = jnp.where(w_iota == l_lo, 1.0, 0.0).astype(BF16)
    ranks = tab[...]
    parts = jnp.concatenate([(ranks >> 7).astype(F32), (ranks & 127).astype(F32)], axis=0).astype(BF16)
    looked = jnp.dot(parts, pick, preferred_element_type=F32)
    t_iota = lax.broadcasted_iota(I32, (t_rows, 128), 0)
    looked = looked[:t_rows] * 128.0 + looked[t_rows:]
    rank = jnp.sum(jnp.where(t_iota == l_hi, looked, 0.0), axis=0, keepdims=True)
    rank = rank.astype(I32)
    rks[...] = rank
    rkr[0] = rank

    def rank_copy(r):
        return pltpu.make_async_remote_copy(
            src_ref=rks, dst_ref=rkr.at[r], send_sem=rk_s.at[r], recv_sem=rk_r.at[r],
            device_id=partner(g_flips, r), device_id_type=MESH)

    pl.semaphore_wait(round_y, len(y_peers))
    loop(gn, lambda r: rank_copy(r).start(), 1)
    es[...] = jnp.zeros_like(es)

    inner(vb, 0)

    def weigh(g):
        rows = group(g)
        tym, typ, txm, txp = (tc[i, rows, :] for i in (TYM, TYP, TXM, TXP))
        sx0 = jnp.where(is_x[3], txp, 0.0) + jnp.where(is_x[4], txm, 0.0)
        sx1 = sx0 + tc[TXB, rows, :]
        sy0 = jnp.where(is_m[7], typ, 0.0) + jnp.where(is_m[0], tym, 0.0)
        sy1 = sy0 + jnp.where(is_m[3], typ, 0.0) + jnp.where(is_m[4], tym, 0.0)
        for s in range(4):
            d = aa[rows, :] + (sx1 if s & 2 else sx0) + (sy1 if s & 1 else sy0)
            ec[s, rows, :] = d
            ec[4 + s, rows, :] = d
        ec[8, rows, :] = sx0
        ec[9, rows, :] = sy0

    loop(4, weigh)
    for i, z in enumerate((3, 4, 11, 12)):
        for s in range(8):
            ec[s, 8 * z:8 * z + 8, :] += sw[i]
    for t, z in ((tzb[0], 0), (tc[TZP, 56:64, :], 7), (tc[TZM, 64:72, :], 8), (tzb[1], 15)):
        for s in range(4, 8):
            ec[s, 8 * z:8 * z + 8, :] += t

    def x_swap(q):
        return jnp.where(x1 == 3, roll_x(q, 7), jnp.where(x1 == 4, roll_x(q, 1), 0.0))

    def y_swap(q):
        return jnp.where(m1 == 7, roll_y(q, 127), jnp.where(m1 == 0, roll_y(q, 1), 0.0))

    def far(g):
        return one_plane(4 * g + 4 - 5 * (g % 2))

    def rest(g):
        rows = group(g)
        here = pp[rows, :]
        full = plane_sum(ec[0, rows, :] * here - ss[rows, :]) - sw[g] * pp[far(g), :]
        fl[8, one_plane(g), :] = (
            full - x_swap(plane_sum(ec[8, rows, :] * here)) - y_swap(plane_sum(ec[9, rows, :] * here)))

    loop(4, rest)

    for copy in sent2:
        copy.wait_recv()
    for copy in sent:
        copy.wait_send()
    outer(vb, 0, va, 1, hxr2, hzr2, 0)
    store = pltpu.make_async_copy(va.at[pl.ds(1, 8)], v_out, out_sem.at[0])
    store.start()

    def gather(g):
        rows = group(g)
        sx0, sy0 = ec[8, rows, :], ec[9, rows, :]
        vals = [va[1 + s, rows, :] for s in range(8)]
        qx = [x_swap(plane_sum(sx0 * v)) for v in vals]
        qy = [y_swap(plane_sum(sy0 * v)) for v in vals]
        for s in range(8):
            full = plane_sum(ec[s, rows, :] * vals[s]) - sw[g] * va[1 + (s ^ 4), far(g), :]
            fl[s, one_plane(g), :] = full - qx[s ^ 2] - qy[s ^ 1]

    loop(4, gather)

    def z_part(j, pz, s):
        groups = ((0,), (1, 2), (3,))[j] if pz == 1 else {(1, 0): (1,), (2, 0): (3,), (0, 2): (0,), (1, 2): (2,)}[j, pz]
        term = fl[s, one_plane(groups[0]), :]
        for g in groups[1:]:
            term += fl[s, one_plane(g), :]
        return term

    for k, (j, halves) in enumerate(((0, (1, 2)), (1, (1, 2)), (2, (1, 0)), (1, (0,)))):
        for half, pz in enumerate(halves):
            for b in range(2):
                at, s = 64 * half + 24 * b, (0 if pz == 1 else 4) + 2 * b
                side = z_part(j, pz, s + 1)
                es[k, at:at + 8, :] = jnp.where(m1 < 4, side, 0.0)
                es[k, at + 8:at + 16, :] = z_part(j, pz, s)
                es[k, at + 16:at + 24, :] = jnp.where(m1 < 4, 0.0, side)
        if k < 3:
            es[k, 48:56, :] = -z_part(j, 1, 8)

    m16 = m[:16]
    sums = []
    for k in range(4):
        for xi in range(2):
            t = es[k, pl.ds(4 * xi, 16, stride=8), :]
            for i in range(1, 4):
                t += es[k, pl.ds(4 * xi + i, 16, stride=8), :]
            sums.append(t)
    for bit in (4, 2, 1):
        high = (m16 & bit) != 0
        merged = []
        for u in range(bit):
            one, two = sums[u], sums[u + bit]
            move = jnp.where(high, one, two)
            merged.append(jnp.where(high, two, one) + jnp.where(high, roll_y(move, bit), roll_y(move, 128 - bit)))
        sums = merged
    rows_out = sums[0]
    cs[...] = rows_out
    crv[0] = rows_out

    def g_copy(r):
        return pltpu.make_async_remote_copy(
            src_ref=cs, dst_ref=crv.at[r], send_sem=g_s.at[r], recv_sem=g_r.at[r],
            device_id=partner(g_flips, r), device_id_type=MESH)

    loop(gn, lambda r: g_copy(r).start(), 1)

    xb[64:128, :] = jnp.zeros((64, gn * 128), BF16)

    def wanted(i):
        idx = row1 + i * 8
        peer = jnp.zeros_like(idx)
        for t in range(1, hn):
            peer += jnp.where(idx >= t * width, 1, 0)
        col = idx - peer * width
        dev = jnp.zeros_like(idx) + (ml * plane + mp)
        for b, (on_layer, step) in enumerate(h_flips):
            dev += ((peer >> b) & 1) * (step * plane if on_layer else step)
        want = dev * own + col
        for q in range(4):
            wt[one_plane(i + q * (n_idx // 8)), :] = jnp.where(col + q * width < own, want + q * width, -7)

    loop(n_idx // 8, wanted)

    loop(gn, lambda r: rank_copy(r).wait_recv(), 1)

    have = [rkr[r] for r in range(gn)]

    def build(i, carry):
        at = pl.multiple_of(i * 16, 16)
        want = wt[pl.ds(at, 16), :]
        for r in range(gn):
            oh[pl.ds(at, 16), 128 * r:128 * r + 128] = jnp.where(want == have[r], 1.0, 0.0).astype(BF16)
        return carry

    lax.fori_loop(0, 4 * n_idx // 16, build, 0)

    odd = m1 % 2 == 1
    b1 = (x1 >= 3) & (x1 < 6)
    b1_odd = b1 & odd

    def spread(r):
        got1, got2 = crv[r, 0:8, :], crv[r, 8:16, :]
        pz1 = jnp.where(m1 < 6, got1, 0.0)
        pz2 = jnp.where(m1 < 4, got2, 0.0)
        pz0 = jnp.where(m1 < 4, 0.0, jnp.where(m1 < 6, got2, got1))
        low1, low2, low0 = (jnp.where(b1_odd, v, 0.0) for v in (pz1, pz2, pz0))
        last = pltpu.roll(low1, 5, 0) + low2 + jnp.where(x1 >= 6, pltpu.roll(low0, 3, 0), 0.0)
        vals = jnp.concatenate([
            pz1 - low1 + jnp.where(x1 == 7, pltpu.roll(low0, 2, 0), 0.0), pz2 - low2, pz0 - low0, last], axis=0)
        high = vals.astype(BF16)
        lanes = slice(128 * r, 128 * r + 128)
        xb[0:32, lanes] = high
        xb[32:64, lanes] = (vals - high.astype(F32)).astype(BF16)

    def product(part):
        return lax.dot_general(
            oh[:, part], xb[:, part], (((1,), (1,)), ((), ())), preferred_element_type=F32)

    half = gn // 2
    loop(half, lambda r: g_copy(r).wait_recv(), 1)
    loop(half, spread)
    routed = product(slice(0, half * 128))
    loop(gn, lambda r: g_copy(r).wait_recv(), half)
    loop(gn, spread, half)
    routed += product(slice(half * 128, gn * 128))
    quarter = lax.broadcasted_iota(I32, (n_idx, 128), 1) >> 5
    packed = jnp.zeros((n_idx, 128), F32)
    for q in range(4):
        part = routed[q * n_idx:(q + 1) * n_idx]
        first_half = roll_y(part, 32 * q) if q else part
        second_half = part if q == 1 else roll_y(part, (32 * q + 96) % 128)
        packed = jnp.where(quarter == q, first_half + second_half, packed)
    for r in range(hn):
        hs[r] = packed[r * width:(r + 1) * width]

    def h_copy(r):
        return pltpu.make_async_remote_copy(
            src_ref=hs.at[r], dst_ref=hr.at[r], send_sem=h_s.at[r], recv_sem=h_r.at[r],
            device_id=partner(h_flips, r), device_id_type=MESH)

    pl.semaphore_wait(round_z, 2)
    loop(hn, lambda r: h_copy(r).start(), 1)
    loop(hn, lambda r: h_copy(r).wait_recv(), 1)
    final = hs[0]
    for r in range(1, hn):
        final += hr[r]
    f_out[0:width, :] = final

    store.wait()
    for copy in sent2:
        copy.wait_send()

    def drain(r):
        rank_copy(r).wait_send()
        g_copy(r).wait_send()

    loop(gn, drain, 1)
    loop(hn, lambda r: h_copy(r).wait_send(), 1)


def finish(own, width, v_in, f_in, v_out, cm_out, cr_out, ft, sem):
    store = pltpu.make_async_copy(v_in, v_out, sem)
    store.start()
    ft[0:16, :] = f_in[...]
    turned = ft[...].T
    lane = lax.broadcasted_iota(I32, (32, 128), 1)
    done = jnp.zeros((32, 128), F32)
    for q in range(4):
        part = turned[32 * q:32 * q + 32]
        here = (lane >= q * width) & (lane < (q + 1) * width)
        done = jnp.where(here, pltpu.roll(part, q * width, 1) if q else part, done)
    for pz, px, base in (
        (1, 1, 0), (1, 2, 3), (2, 1, 8), (2, 2, 11), (0, 1, 16), (0, 2, 19), (1, 0, 24), (2, 0, 27)):
        k = 9 * pz + 3 * px
        cm_out[k:k + 3, :] = done[base:base + 3, 0:own]
    cm_out[0:2, :] = done[30:32, 0:own]
    cm_out[2:3, :] = done[7:8, 0:own]
    cr_out[...] = done[6:7, 0:own]
    store.wait()


def per_device(sizes, basis_init, permeability, accumulation, pressure, source, support, block_of, curve_rank):
    lx, plane = sizes
    gn, hn = 2 ** len(G_BITS), 2 ** len(H_BITS)
    devices = lx * plane
    own = (curve_rank.shape[0] + devices - 1) // devices
    width = (own + 3) // 4
    flat = lambda v: v.reshape(v.shape[:-3] + (128, 128))
    t_rows = -(-curve_rank.shape[0] // 2048) * 16
    anywhere = pl.BlockSpec(memory_space=pl.ANY)
    vmem = pl.BlockSpec(memory_space=pltpu.VMEM)
    dma = pltpu.SemaphoreType.DMA
    cells = lambda *lead: pltpu.VMEM(lead + (128, 128), F32)
    basis, rows = pl.pallas_call(
        functools.partial(kernel, (lx, plane, own, width)),
        out_shape=(
            jax.ShapeDtypeStruct((8, 128, 128), F32),
            jax.ShapeDtypeStruct((16, 128), F32),
        ),
        in_specs=[anywhere] * 8,
        out_specs=(anywhere, vmem),
        scratch_shapes=[
            cells(8), pltpu.VMEM((8, 128, 128), I32), cells(), cells(), cells(),
            pltpu.VMEM((3, 8, 128), I32), pltpu.VMEM(curve_rank.shape, I32), pltpu.VMEM((t_rows, 128), I32),
            cells(9), cells(8), cells(8), cells(8), cells(12),
            pltpu.VMEM((2, 8, 128), F32), cells(10), pltpu.VMEM((4, 8, 128), F32),
            pltpu.VMEM((9, 32, 128), F32), cells(4),
            pltpu.VMEM((2, 5, 16, 128), F32), pltpu.VMEM((2, 5, 16, 128), F32), pltpu.VMEM((2, 5, 8, 128), F32),
            pltpu.VMEM((2, 4, 16, 128), F32), pltpu.VMEM((2, 4, 16, 128), F32), pltpu.VMEM((2, 4, 8, 128), F32),
            pltpu.VMEM((1, 128), I32), pltpu.VMEM((gn, 1, 128), I32),
            pltpu.VMEM((4 * hn * width, 128), I32), pltpu.VMEM((4 * hn * width, gn * 128), BF16),
            pltpu.VMEM((128, gn * 128), BF16), pltpu.VMEM((4, 128, 128), F32),
            pltpu.VMEM((16, 128), F32), pltpu.VMEM((gn, 16, 128), F32),
            pltpu.VMEM((hn, width, 128), F32), pltpu.VMEM((hn, width, 128), F32),
            pltpu.SemaphoreType.REGULAR, pltpu.SemaphoreType.REGULAR, dma((10,)), dma((1,)), dma((8,)), dma((8,)),
            dma((gn,)), dma((gn,)), dma((gn,)), dma((gn,)), dma((hn,)), dma((hn,)),
        ],
        compiler_params=pltpu.CompilerParams(
            collective_id=0, has_side_effects=True, vmem_limit_bytes=VMEM_GRANT),
        cost_estimate=pl.CostEstimate(flops=20_000_000, bytes_accessed=2_000_000, transcendentals=0),
    )(*(pltpu.with_memory_space_constraint(v, pltpu.HBM) for v in (
        flat(basis_init), flat(permeability), flat(accumulation), flat(pressure), flat(source),
        flat(support), flat(block_of), curve_rank,
    )))
    basis, matrix, residual = pl.pallas_call(
        functools.partial(finish, own, width),
        out_shape=(
            jax.ShapeDtypeStruct((8, 128, 128), F32),
            jax.ShapeDtypeStruct((27, own), F32),
            jax.ShapeDtypeStruct((1, own), F32),
        ),
        in_specs=[anywhere, vmem],
        out_specs=(anywhere, vmem, vmem),
        scratch_shapes=[cells(), dma],
        compiler_params=pltpu.CompilerParams(vmem_limit_bytes=VMEM_GRANT),
    )(basis, rows)
    return basis.reshape(basis_init.shape), matrix, residual.reshape(own)


def solution(mesh):
    return jax.shard_map(
        functools.partial(per_device, (mesh.shape["layer"], mesh.shape["plane"])),
        mesh=mesh,
        in_specs=(
            P(None, "layer", "plane", None),
            P("layer", "plane", None),
            P("layer", "plane", None),
            P("layer", "plane", None),
            P("layer", "plane", None),
            P(None, "layer", "plane", None),
            P("layer", "plane", None),
            P(),
        ),
        out_specs=(
            P(None, "layer", "plane", None),
            P(None, ("layer", "plane")),
            P(("layer", "plane")),
        ),
        check_vma=False,
    )
```

```python
import functools

import jax
import jax.numpy as jnp
from jax import lax
from jax.experimental import pallas as pl
from jax.experimental.pallas import tpu as pltpu
from jax.sharding import PartitionSpec as P

MESH = pl.DeviceIdType.MESH
F32, BF16, I32 = jnp.float32, jnp.bfloat16, jnp.int32

G_BITS = (("layer", 1), ("layer", 2), ("plane", 16), ("plane", 32))
H_BITS = (("plane", 1), ("plane", 2), ("plane", 4), ("plane", 8))
VMEM_GRANT = 32 * 1024 * 1024
THIRD, TWO_THIRDS = 1.0 / 3.0, 2.0 / 3.0
B0 = (0, 1, 4, 5)
A0 = (0, 1, 2, 3)
TYM, TYP, TYM1, TYP1, TXM, TXP, TZM, TZP, TZM1, TZP1, TXB, RD = range(12)


def roll_x(v, shift):
    rows = v.shape[0]
    return pltpu.roll(v.reshape(rows // 8, 8, 128), shift, 1).reshape(rows, 128)


def roll_y(v, shift):
    return pltpu.roll(v, shift, 1)


def harmonic(k, n):
    return 2.0 * k * n / (k + n)


def plane_sum(v):
    return v.reshape(-1, 8, 128).sum(axis=0)


def far_first(bits):
    def hops(r):
        reach = {"layer": 0, "y": 0, "z": 0}
        for i, (axis, bit) in enumerate(bits):
            if (r >> i) & 1:
                kind, step = (axis, bit) if axis == "layer" else ("y", bit // 16) if bit >= 16 else ("z", bit // 2)
                reach[kind] += step
        return sum(min(n, size - n) for n, size in ((reach["layer"], 4), (reach["y"], 4), (reach["z"], 8)))

    return sorted(range(1, 2 ** len(bits)), key=lambda r: -hops(r))


def kernel(
    dims,
    bi_hbm, k_hbm, a_hbm, p_hbm, s_hbm, sup_hbm, blk_hbm, cr_hbm,
    v_out, f_out,
    bi, sup, aa, pp, ss, blk, cr1, tab,
    va, vb, sf, nn, tc, tzb, ec, sw, fl, hx, hxs, hxr, hzr, hxs2, hxr2, hzr2,
    rks, rkr, wt, oh, xb, es, cs, crv, hs, hr,
    round_y, round_z, in_sem, out_sem, halo_s, halo_r, rk_s, rk_r, g_s, g_r, h_s, h_r,
):
    lx, plane, own, width = dims
    gn, hn = 2 ** len(G_BITS), 2 ** len(H_BITS)
    zc = hn // 2
    n_idx = hn * width
    ml, mp = lax.axis_index("layer"), lax.axis_index("plane")

    def flips(bits):
        steps = []
        for axis, bit in bits:
            at = ml if axis == "layer" else mp
            steps.append((axis == "layer", bit * (1 - 2 * ((at // bit) % 2))))
        return steps

    g_flips, h_flips = flips(G_BITS), flips(H_BITS)

    def partner(steps, r):
        to_l, to_p = ml, mp
        for i, (on_layer, step) in enumerate(steps):
            if (r >> i) & 1:
                to_l, to_p = (to_l + step, to_p) if on_layer else (to_l, to_p + step)
        return (to_l, to_p)

    up_x, down_x = (ml, (mp + 1) % plane), (ml, (mp + plane - 1) % plane)
    up_z, down_z = ((ml + 1) % lx, mp), ((ml + lx - 1) % lx, mp)

    def loop(n, body, start=0):
        for i in range(start, n):
            body(i)

    def group(g):
        return slice(g * 32, g * 32 + 32)

    def one_plane(z):
        return slice(z * 8, z * 8 + 8)

    loads = [
        pltpu.make_async_copy(k_hbm, va.at[0], in_sem.at[0]),
        pltpu.make_async_copy(bi_hbm, bi, in_sem.at[1]),
        pltpu.make_async_copy(sup_hbm, sup, in_sem.at[2]),
        pltpu.make_async_copy(a_hbm, aa, in_sem.at[3]),
        pltpu.make_async_copy(cr_hbm, cr1, in_sem.at[4]),
        pltpu.make_async_copy(p_hbm, pp, in_sem.at[5]),
        pltpu.make_async_copy(s_hbm, ss, in_sem.at[6]),
    ]
    for j, z in enumerate((0, 4, 12)):
        loads.append(pltpu.make_async_copy(blk_hbm.at[pl.ds(8 * z, 8)], blk.at[j], in_sem.at[7 + j]))
    barrier = pltpu.get_barrier_semaphore()

    def greet(who):
        pl.semaphore_signal(barrier, inc=1, device_id=who, device_id_type=MESH)

    def along_z(dz, dc):
        return (ml, mp + dc * (1 - 2 * (mp % 2)) + 2 * ((mp // 2 + dz) % zc - (mp // 2) % zc))

    x_mask = sum(1 << i for i, (axis, _) in enumerate(G_BITS) if axis == "layer")
    x_peers = [r for r in range(1, gn) if r & x_mask == r]
    y_peers = [r for r in range(1, gn) if r & x_mask == 0]
    z_peers = [(dz, dc) for dz in (1, zc - 1, 2, zc - 2) for dc in (0, 1)] + [(0, 1)]
    greet(up_x)
    greet(down_x)
    for r in x_peers:
        greet(partner(g_flips, r))
    for load in loads[:3]:
        load.start()
    for r in y_peers:
        greet(partner(g_flips, r))
    for dz, dc in z_peers:
        greet(along_z(dz, dc))
    for load in loads[3:]:
        load.start()
    greeted = 2 + len(x_peers) + len(y_peers) + len(z_peers)

    def second_round():
        for r in y_peers:
            pl.semaphore_signal(round_y, inc=1, device_id=partner(g_flips, r), device_id_type=MESH)
        for dz in (2, zc - 2):
            pl.semaphore_signal(round_z, inc=1, device_id=along_z(dz, 0), device_id_type=MESH)

    lane = lax.broadcasted_iota(I32, (32, 128), 1)
    m, x = lane % 8, lax.broadcasted_iota(I32, (32, 128), 0) % 8
    m1, x1 = m[:8], x[:8]
    lane1, row1 = lane[:8], x[:8]
    is_m = {i: m == i for i in (0, 3, 4, 7)}
    is_x = {i: x == i for i in (3, 4)}

    hx[...] = jnp.zeros_like(hx)
    tc[TXB] = jnp.zeros((128, 128), F32)

    loads[0].wait()

    def faces(g):
        rows, below = group(g), one_plane((4 * g + 15) % 16)
        k = va[0, rows, :]
        tym = jnp.where(lane == 0, 0.0, harmonic(k, roll_y(k, 1)))
        typ = roll_y(tym, 127)
        tc[TYM, rows, :] = tym
        tc[TYP, rows, :] = typ
        tc[TYM1, rows, :] = jnp.where(is_m[4], 0.0, tym)
        tc[TYP1, rows, :] = jnp.where(is_m[3], 0.0, typ)
        txm = jnp.where(x == 0, 0.0, harmonic(k, roll_x(k, 1)))
        tc[TXM, rows, :] = txm
        tc[TXP, rows, :] = roll_x(txm, 7)
        tz = harmonic(k, jnp.concatenate([va[0, below, :], k[0:24]], axis=0))
        tc[TZM, rows, :] = tz
        tc[TZP, below, :] = tz[0:8]
        tc[TZP, slice(g * 32, g * 32 + 24), :] = tz[8:32]
        tc[TZM1, rows, :] = tz
        tc[TZP1, below, :] = tz[0:8]
        tc[TZP1, slice(g * 32, g * 32 + 24), :] = tz[8:32]

    loop(4, faces)
    nil = jnp.zeros((8, 128), F32)
    tc[TZM, 0:8, :] = nil
    tc[TZP, 120:128, :] = nil
    tc[TZM1, 0:8, :] = nil
    tc[TZP1, 120:128, :] = nil
    tc[TZM1, 64:72, :] = nil
    tc[TZP1, 56:64, :] = nil
    for i, (t, z) in enumerate(((TZP, 3), (TZM, 4), (TZP, 11), (TZM, 12))):
        sw[i] = tc[t, 8 * z:8 * z + 8, :]

    loads[1].wait()
    loads[2].wait()

    def first(g):
        rows = group(g)
        vals = []
        for s in range(8):
            on = sup[s, rows, :].astype(F32)
            sf[s, rows, :] = on
            vals.append(bi[s, rows, :] * on)
        inv = 1.0 / sum(vals[1:], vals[0])
        for s in range(8):
            va[1 + s, rows, :] = vals[s] * inv

    loop(4, first)

    def exchange(v, off, xs_buf, xr_buf, zr_buf, base):
        for i, s in enumerate(B0):
            xs_buf[0, off + i] = v[off + s, pl.ds(0, 16, stride=8), :]
            xs_buf[1, off + i] = v[off + s, pl.ds(7, 16, stride=8), :]
        if off:
            xs_buf[0, 0] = v[0, pl.ds(0, 16, stride=8), :]
            xs_buf[1, 0] = v[0, pl.ds(7, 16, stride=8), :]
            pl.semaphore_wait(barrier, greeted)
        last, lead = v.at[pl.ds(0, off + 4), pl.ds(120, 8)], v.at[pl.ds(0, off + 4), pl.ds(0, 8)]
        copies = []
        for j, (src, dst, who) in enumerate((
            (xs_buf.at[1], xr_buf.at[0], up_x), (xs_buf.at[0], xr_buf.at[1], down_x),
            (last, zr_buf.at[0], up_z), (lead, zr_buf.at[1], down_z),
        )):
            copies.append(pltpu.make_async_remote_copy(
                src_ref=src, dst_ref=dst, send_sem=halo_s.at[base + j], recv_sem=halo_r.at[base + j],
                device_id=who, device_id_type=MESH))
        for copy in copies:
            copy.start()
        if off:
            second_round()
        return copies

    def inner(v, off):
        def part(g):
            rows = group(g)
            odd = g % 2
            below, above = one_plane((4 * g + 15) % 16), one_plane((4 * g + 4) % 16)
            for s in range(8):
                if s % 4 == 0:
                    vals = [v[off + s + i, rows, :] for i in range(4)]
                    txm, txp = tc[TXM, rows, :], tc[TXP, rows, :]
                    tym, typ = [tc[i, rows, :] for i in (TYM, TYM1)], [tc[i, rows, :] for i in (TYP, TYP1)]
                    zm, zp = tc[TZM1 if s else TZM, rows, :], tc[TZP1 if s else TZP, rows, :]
                here, by_y, by_x, turn = vals[s % 4], vals[s % 4 ^ 1], vals[s % 4 ^ 2], 4 - (s & 4) * 2
                near = tym[s & 1] * roll_y(jnp.where(is_m[7], by_y, here), 1)
                near += typ[s & 1] * roll_y(jnp.where(is_m[0], by_y, here), 127)
                near += txm * roll_x(jnp.where(is_x[3], by_x, here), 1)
                near += txp * roll_x(jnp.where(is_x[4], by_x, here), 7)
                lo, hi = v[off + s + turn * odd, below, :], v[off + s + turn * (1 - odd), above, :]
                near += zm * jnp.concatenate([lo, here[0:24]], axis=0)
                near += zp * jnp.concatenate([here[8:32], hi], axis=0)
                nn[s, rows, :] = near

        loop(4, part)

    def outer(v, off, new, off2, xr_buf, zr_buf, extra):
        for i in range(4):
            hx[i, pl.ds(0, 16, stride=8), :] = xr_buf[0, extra + i]
            hx[i, pl.ds(7, 16, stride=8), :] = xr_buf[1, extra + i]
            nn[i, 0:8, :] += tzb[0] * zr_buf[0, extra + i]
            nn[i, 120:128, :] += tzb[1] * zr_buf[1, extra + i]

        def part(g):
            rows = group(g)
            rd, txb = tc[RD, rows, :], tc[TXB, rows, :]
            vals = []
            for s in range(8):
                near = nn[s, rows, :]
                if s in B0:
                    near += txb * hx[B0.index(s), rows, :]
                vals.append((v[off + s, rows, :] * THIRD + rd * near) * sf[s, rows, :])
            inv = 1.0 / sum(vals[1:], vals[0])
            for s in range(8):
                new[off2 + s, rows, :] = vals[s] * inv

        loop(4, part)

    sent = exchange(va, 1, hxs, hxr, hzr, 0)
    inner(va, 1)

    for load in loads[3:]:
        load.wait()
    label = blk[0, 0:1, :]
    for u, (j, r) in enumerate(((0, 0), (0, 4), (1, 0), (1, 4), (2, 0), (2, 4), (1, 0), (1, 4))):
        label = jnp.where(m1[0:1] == u, blk[j, r:r + 1, :], label)
    t_rows, labels = tab.shape[0], cr1.shape[0]
    tab[labels // 128:, :] = jnp.zeros((t_rows - labels // 128, 128), I32)

    def table(t):
        tab[t:t + 1, :] = cr1[pl.ds(t * 128, 128)].reshape(1, 128)

    loop(labels // 128, table)
    if labels % 128:
        t = labels // 128
        tab[t:t + 1, 0:labels % 128] = cr1[pl.ds(t * 128, labels % 128)].reshape(1, labels % 128)
    l_hi, l_lo = label >> 7, label & 127
    w_iota = lax.broadcasted_iota(I32, (128, 128), 0)
    pick = jnp.where(w_iota == l_lo, 1.0, 0.0).astype(BF16)
    ranks = tab[...]
    parts = jnp.concatenate([(ranks >> 7).astype(F32), (ranks & 127).astype(F32)], axis=0).astype(BF16)
    looked = jnp.dot(parts, pick, preferred_element_type=F32)
    t_iota = lax.broadcasted_iota(I32, (t_rows, 128), 0)
    looked = looked[:t_rows] * 128.0 + looked[t_rows:]
    rank = jnp.sum(jnp.where(t_iota == l_hi, looked, 0.0), axis=0, keepdims=True)
    rank = rank.astype(I32)
    rks[...] = rank
    rkr[0] = rank

    def diagonal(g):
        rows = group(g)
        diag = aa[rows, :]
        for t in (TYM, TYP, TXM, TXP, TZM, TZP):
            diag += tc[t, rows, :]
        tc[RD, rows, :] = diag

    loop(4, diagonal)
    for copy in sent:
        copy.wait_recv()

    tc[TXB, pl.ds(0, 16, stride=8), :] = jnp.where(mp > 0, harmonic(hxs[0, 0], hxr[0, 0]), 0.0)
    tc[TXB, pl.ds(7, 16, stride=8), :] = jnp.where(mp < plane - 1, harmonic(hxs[1, 0], hxr[1, 0]), 0.0)
    tzb[0] = jnp.where(ml > 0, harmonic(va[0, 0:8, :], hzr[0, 0]), 0.0)
    tzb[1] = jnp.where(ml < lx - 1, harmonic(va[0, 120:128, :], hzr[1, 0]), 0.0)

    tc[RD, 0:8, :] += tzb[0]
    tc[RD, 120:128, :] += tzb[1]
    tc[RD] = TWO_THIRDS / (tc[RD] + tc[TXB])

    outer(va, 1, vb, 0, hxr, hzr, 1)
    sent2 = exchange(vb, 0, hxs2, hxr2, hzr2, 4)

    def rank_copy(r):
        return pltpu.make_async_remote_copy(
            src_ref=rks, dst_ref=rkr.at[r], send_sem=rk_s.at[r], recv_sem=rk_r.at[r],
            device_id=partner(g_flips, r), device_id_type=MESH)

    pl.semaphore_wait(round_y, len(y_peers))
    loop(gn, lambda r: rank_copy(r).start(), 1)
    es[...] = jnp.zeros_like(es)

    inner(vb, 0)

    def weigh(g):
        rows = group(g)
        tym, typ, txm, txp = (tc[i, rows, :] for i in (TYM, TYP, TXM, TXP))
        sx0 = jnp.where(is_x[3], txp, 0.0) + jnp.where(is_x[4], txm, 0.0)
        sx1 = sx0 + tc[TXB, rows, :]
        sy0 = jnp.where(is_m[7], typ, 0.0) + jnp.where(is_m[0], tym, 0.0)
        sy1 = sy0 + jnp.where(is_m[3], typ, 0.0) + jnp.where(is_m[4], tym, 0.0)
        for s in range(4):
            d = aa[rows, :] + (sx1 if s & 2 else sx0) + (sy1 if s & 1 else sy0)
            ec[s, rows, :] = d
            ec[4 + s, rows, :] = d
        ec[8, rows, :] = sx0
        ec[9, rows, :] = sy0

    loop(4, weigh)
    for i, z in enumerate((3, 4, 11, 12)):
        for s in range(8):
            ec[s, 8 * z:8 * z + 8, :] += sw[i]
    for t, z in ((tzb[0], 0), (tc[TZP, 56:64, :], 7), (tc[TZM, 64:72, :], 8), (tzb[1], 15)):
        for s in range(4, 8):
            ec[s, 8 * z:8 * z + 8, :] += t

    def x_swap(q):
        return roll_x(q, 4)

    def y_swap(q):
        return jnp.where(m1 == 7, roll_y(q, 127), jnp.where(m1 == 0, roll_y(q, 1), 0.0))

    def far(g):
        return one_plane(4 * g + 4 - 5 * (g % 2))

    def rest(g):
        rows = group(g)
        here = pp[rows, :]
        full = plane_sum(ec[0, rows, :] * here - ss[rows, :]) - sw[g] * pp[far(g), :]
        fl[8, one_plane(g), :] = (
            full - x_swap(plane_sum(ec[8, rows, :] * here)) - y_swap(plane_sum(ec[9, rows, :] * here)))

    loop(4, rest)

    for copy in sent2:
        copy.wait_recv()
    for copy in sent:
        copy.wait_send()
    outer(vb, 0, va, 1, hxr2, hzr2, 0)
    store = pltpu.make_async_copy(va.at[pl.ds(1, 8)], v_out, out_sem.at[0])
    store.start()

    def gather(g):
        rows = group(g)
        sx0, sy0 = ec[8, rows, :], ec[9, rows, :]
        vals = [va[1 + s, rows, :] for s in range(8)]
        qx = [x_swap(plane_sum(sx0 * v)) for v in vals]
        qy = [y_swap(plane_sum(sy0 * v)) for v in vals]
        for s in range(8):
            full = plane_sum(ec[s, rows, :] * vals[s]) - sw[g] * va[1 + (s ^ 4), far(g), :]
            fl[s, one_plane(g), :] = full - qx[s ^ 2] - qy[s ^ 1]

    loop(4, gather)

    def z_part(j, pz, s):
        groups = ((0,), (1, 2), (3,))[j] if pz == 1 else {(1, 0): (1,), (2, 0): (3,), (0, 2): (0,), (1, 2): (2,)}[j, pz]
        term = fl[s, one_plane(groups[0]), :]
        for g in groups[1:]:
            term += fl[s, one_plane(g), :]
        return term

    for k, (j, halves) in enumerate(((0, (1, 2)), (1, (1, 2)), (2, (1, 0)), (1, (0,)))):
        for half, pz in enumerate(halves):
            for b in range(2):
                at, s = 64 * half + 24 * b, (0 if pz == 1 else 4) + 2 * b
                side = z_part(j, pz, s + 1)
                es[k, at:at + 8, :] = jnp.where(m1 < 4, side, 0.0)
                es[k, at + 8:at + 16, :] = z_part(j, pz, s)
                es[k, at + 16:at + 24, :] = jnp.where(m1 < 4, 0.0, side)
        if k < 3:
            es[k, 48:56, :] = -z_part(j, 1, 8)

    m16 = m[:16]
    sums = []
    for k in range(4):
        for xi in range(2):
            t = es[k, pl.ds(4 * xi, 16, stride=8), :]
            for i in range(1, 4):
                t += es[k, pl.ds(4 * xi + i, 16, stride=8), :]
            sums.append(t)
    for bit in (4, 2, 1):
        high = (m16 & bit) != 0
        merged = []
        for u in range(bit):
            one, two = sums[u], sums[u + bit]
            move = jnp.where(high, one, two)
            merged.append(jnp.where(high, two, one) + jnp.where(high, roll_y(move, bit), roll_y(move, 128 - bit)))
        sums = merged
    rows_out = sums[0]
    cs[...] = rows_out
    crv[0] = rows_out

    def g_copy(r):
        return pltpu.make_async_remote_copy(
            src_ref=cs, dst_ref=crv.at[r], send_sem=g_s.at[r], recv_sem=g_r.at[r],
            device_id=partner(g_flips, r), device_id_type=MESH)

    for r in far_first(G_BITS):
        g_copy(r).start()

    xb[64:128, :] = jnp.zeros((64, gn * 128), BF16)

    def wanted(i):
        idx = row1 + i * 8
        peer = jnp.zeros_like(idx)
        for t in range(1, hn):
            peer += jnp.where(idx >= t * width, 1, 0)
        col = idx - peer * width
        dev = jnp.zeros_like(idx) + (ml * plane + mp)
        for b, (on_layer, step) in enumerate(h_flips):
            dev += ((peer >> b) & 1) * (step * plane if on_layer else step)
        want = dev * own + col
        for q in range(4):
            wt[one_plane(i + q * (n_idx // 8)), :] = jnp.where(col + q * width < own, want + q * width, -7)

    loop(n_idx // 8, wanted)

    loop(gn, lambda r: rank_copy(r).wait_recv(), 1)

    have = [rkr[r] for r in range(gn)]

    def build(i, carry):
        at = pl.multiple_of(i * 16, 16)
        want = wt[pl.ds(at, 16), :]
        for r in range(gn):
            oh[pl.ds(at, 16), 128 * r:128 * r + 128] = jnp.where(want == have[r], 1.0, 0.0).astype(BF16)
        return carry

    lax.fori_loop(0, 4 * n_idx // 16, build, 0)

    odd = m1 % 2 == 1
    b1 = (x1 >= 3) & (x1 < 6)
    b1_odd = b1 & odd

    def spread(r):
        got1, got2 = crv[r, 0:8, :], crv[r, 8:16, :]
        pz1 = jnp.where(m1 < 6, got1, 0.0)
        pz2 = jnp.where(m1 < 4, got2, 0.0)
        pz0 = jnp.where(m1 < 4, 0.0, jnp.where(m1 < 6, got2, got1))
        low1, low2, low0 = (jnp.where(b1_odd, v, 0.0) for v in (pz1, pz2, pz0))
        last = pltpu.roll(low1, 5, 0) + low2 + jnp.where(x1 >= 6, pltpu.roll(low0, 3, 0), 0.0)
        vals = jnp.concatenate([
            pz1 - low1 + jnp.where(x1 == 7, pltpu.roll(low0, 2, 0), 0.0), pz2 - low2, pz0 - low0, last], axis=0)
        high = vals.astype(BF16)
        lanes = slice(128 * r, 128 * r + 128)
        xb[0:32, lanes] = high
        xb[32:64, lanes] = (vals - high.astype(F32)).astype(BF16)

    def product(part):
        return lax.dot_general(
            oh[:, part], xb[:, part], (((1,), (1,)), ((), ())), preferred_element_type=F32)

    half = gn // 2
    loop(half, lambda r: g_copy(r).wait_recv(), 1)
    loop(half, spread)
    routed = product(slice(0, half * 128))
    loop(gn, lambda r: g_copy(r).wait_recv(), half)
    loop(gn, spread, half)
    routed += product(slice(half * 128, gn * 128))
    quarter = lax.broadcasted_iota(I32, (n_idx, 128), 1) >> 5
    packed = jnp.zeros((n_idx, 128), F32)
    for q in range(4):
        part = routed[q * n_idx:(q + 1) * n_idx]
        first_half = roll_y(part, 32 * q) if q else part
        second_half = part if q == 1 else roll_y(part, (32 * q + 96) % 128)
        packed = jnp.where(quarter == q, first_half + second_half, packed)
    def h_copy(r):
        return pltpu.make_async_remote_copy(
            src_ref=hs.at[r], dst_ref=hr.at[r], send_sem=h_s.at[r], recv_sem=h_r.at[r],
            device_id=partner(h_flips, r), device_id_type=MESH)

    pl.semaphore_wait(round_z, 2)
    for r in far_first(H_BITS):
        hs[r] = packed[r * width:(r + 1) * width]
        h_copy(r).start()
    hs[0] = packed[0:width]
    loop(hn, lambda r: h_copy(r).wait_recv(), 1)
    final = hs[0]
    for r in range(1, hn):
        final += hr[r]
    f_out[0:width, :] = final

    store.wait()
    for copy in sent2:
        copy.wait_send()

    def drain(r):
        rank_copy(r).wait_send()
        g_copy(r).wait_send()

    loop(gn, drain, 1)
    loop(hn, lambda r: h_copy(r).wait_send(), 1)


def finish(own, width, v_in, f_in, v_out, cm_hbm, cr_hbm, ft, cm_out, cr_out, sem):
    stores = [pltpu.make_async_copy(src, dst, sem.at[i]) for i, (src, dst) in enumerate((
        (v_in, v_out), (cm_out, cm_hbm), (cr_out, cr_hbm)))]
    stores[0].start()
    ft[0:16, :] = f_in[...]
    turned = ft[...].T
    lane = lax.broadcasted_iota(I32, (32, 128), 1)
    done = jnp.zeros((32, 128), F32)
    for q in range(4):
        part = turned[32 * q:32 * q + 32]
        here = (lane >= q * width) & (lane < (q + 1) * width)
        done = jnp.where(here, pltpu.roll(part, q * width, 1) if q else part, done)
    for pz, px, base in (
        (1, 1, 0), (1, 2, 3), (2, 1, 8), (2, 2, 11), (0, 1, 16), (0, 2, 19), (1, 0, 24), (2, 0, 27)):
        k = 9 * pz + 3 * px
        cm_out[k:k + 3, :] = done[base:base + 3, 0:own]
    cm_out[0:2, :] = done[30:32, 0:own]
    cm_out[2:3, :] = done[7:8, 0:own]
    cr_out[...] = done[6:7, 0:own]
    stores[1].start()
    stores[2].start()
    for store in stores:
        store.wait()


def per_device(sizes, basis_init, permeability, accumulation, pressure, source, support, block_of, curve_rank):
    lx, plane = sizes
    gn, hn = 2 ** len(G_BITS), 2 ** len(H_BITS)
    devices = lx * plane
    own = (curve_rank.shape[0] + devices - 1) // devices
    width = (own + 3) // 4
    flat = lambda v: v.reshape(v.shape[:-3] + (128, 128))
    t_rows = -(-curve_rank.shape[0] // 2048) * 16
    anywhere = pl.BlockSpec(memory_space=pl.ANY)
    vmem = pl.BlockSpec(memory_space=pltpu.VMEM)
    dma = pltpu.SemaphoreType.DMA
    cells = lambda *lead: pltpu.VMEM(lead + (128, 128), F32)
    basis, rows = pl.pallas_call(
        functools.partial(kernel, (lx, plane, own, width)),
        out_shape=(
            jax.ShapeDtypeStruct((8, 128, 128), F32),
            jax.ShapeDtypeStruct((16, 128), F32),
        ),
        in_specs=[anywhere] * 8,
        out_specs=(anywhere, vmem),
        scratch_shapes=[
            cells(8), pltpu.VMEM((8, 128, 128), I32), cells(), cells(), cells(),
            pltpu.VMEM((3, 8, 128), I32), pltpu.VMEM(curve_rank.shape, I32), pltpu.VMEM((t_rows, 128), I32),
            cells(9), cells(8), cells(8), cells(8), cells(12),
            pltpu.VMEM((2, 8, 128), F32), cells(10), pltpu.VMEM((4, 8, 128), F32),
            pltpu.VMEM((9, 32, 128), F32), cells(4),
            pltpu.VMEM((2, 5, 16, 128), F32), pltpu.VMEM((2, 5, 16, 128), F32), pltpu.VMEM((2, 5, 8, 128), F32),
            pltpu.VMEM((2, 4, 16, 128), F32), pltpu.VMEM((2, 4, 16, 128), F32), pltpu.VMEM((2, 4, 8, 128), F32),
            pltpu.VMEM((1, 128), I32), pltpu.VMEM((gn, 1, 128), I32),
            pltpu.VMEM((4 * hn * width, 128), I32), pltpu.VMEM((4 * hn * width, gn * 128), BF16),
            pltpu.VMEM((128, gn * 128), BF16), pltpu.VMEM((4, 128, 128), F32),
            pltpu.VMEM((16, 128), F32), pltpu.VMEM((gn, 16, 128), F32),
            pltpu.VMEM((hn, width, 128), F32), pltpu.VMEM((hn, width, 128), F32),
            pltpu.SemaphoreType.REGULAR, pltpu.SemaphoreType.REGULAR, dma((10,)), dma((1,)), dma((8,)), dma((8,)),
            dma((gn,)), dma((gn,)), dma((gn,)), dma((gn,)), dma((hn,)), dma((hn,)),
        ],
        compiler_params=pltpu.CompilerParams(
            collective_id=0, has_side_effects=True, vmem_limit_bytes=VMEM_GRANT),
        cost_estimate=pl.CostEstimate(flops=20_000_000, bytes_accessed=2_000_000, transcendentals=0),
    )(*(pltpu.with_memory_space_constraint(v, pltpu.HBM) for v in (
        flat(basis_init), flat(permeability), flat(accumulation), flat(pressure), flat(source),
        flat(support), flat(block_of), curve_rank,
    )))
    basis, matrix, residual = pl.pallas_call(
        functools.partial(finish, own, width),
        out_shape=(
            jax.ShapeDtypeStruct((8, 128, 128), F32),
            jax.ShapeDtypeStruct((27, own), F32),
            jax.ShapeDtypeStruct((1, own), F32),
        ),
        in_specs=[anywhere, vmem],
        out_specs=(anywhere, anywhere, anywhere),
        scratch_shapes=[cells(), pltpu.VMEM((27, own), F32), pltpu.VMEM((1, own), F32), dma((3,))],
        compiler_params=pltpu.CompilerParams(vmem_limit_bytes=VMEM_GRANT),
    )(basis, rows)
    return basis.reshape(basis_init.shape), matrix, residual.reshape(own)


def solution(mesh):
    return jax.shard_map(
        functools.partial(per_device, (mesh.shape["layer"], mesh.shape["plane"])),
        mesh=mesh,
        in_specs=(
            P(None, "layer", "plane", None),
            P("layer", "plane", None),
            P("layer", "plane", None),
            P("layer", "plane", None),
            P("layer", "plane", None),
            P(None, "layer", "plane", None),
            P("layer", "plane", None),
            P(),
        ),
        out_specs=(
            P(None, "layer", "plane", None),
            P(None, ("layer", "plane")),
            P(("layer", "plane")),
        ),
        check_vma=False,
    )
```

```python
import functools

import jax
import jax.numpy as jnp
from jax import lax
from jax.experimental import pallas as pl
from jax.experimental.pallas import tpu as pltpu
from jax.sharding import PartitionSpec as P

MESH = pl.DeviceIdType.MESH
F32, BF16, I32 = jnp.float32, jnp.bfloat16, jnp.int32

G_BITS = (("layer", 1), ("layer", 2), ("plane", 16), ("plane", 32))
H_BITS = (("plane", 1), ("plane", 2), ("plane", 4), ("plane", 8))
VMEM_GRANT = 32 * 1024 * 1024
THIRD, TWO_THIRDS = 1.0 / 3.0, 2.0 / 3.0
B0 = (0, 1, 4, 5)
A0 = (0, 1, 2, 3)
TYM, TYP, TYM1, TYP1, TXM, TXP, TZM, TZP, TZM1, TZP1, TXB, RD = range(12)


def roll_x(v, shift):
    rows = v.shape[0]
    return pltpu.roll(v.reshape(rows // 8, 8, 128), shift, 1).reshape(rows, 128)


def roll_y(v, shift):
    return pltpu.roll(v, shift, 1)


def harmonic(k, n):
    return 2.0 * k * n / (k + n)


def plane_sum(v):
    return v.reshape(-1, 8, 128).sum(axis=0)


def far_first(bits):
    def hops(r):
        reach = {"layer": 0, "y": 0, "z": 0}
        for i, (axis, bit) in enumerate(bits):
            if (r >> i) & 1:
                kind, step = (axis, bit) if axis == "layer" else ("y", bit // 16) if bit >= 16 else ("z", bit // 2)
                reach[kind] += step
        return sum(min(n, size - n) for n, size in ((reach["layer"], 4), (reach["y"], 4), (reach["z"], 8)))

    return sorted(range(1, 2 ** len(bits)), key=lambda r: -hops(r))


def kernel(
    dims,
    bi_hbm, k_hbm, a_hbm, p_hbm, s_hbm, sup_hbm, blk_hbm, cr_hbm,
    v_out, f_out,
    bi, sup, aa, pp, ss, blk, cr1, tab,
    va, vb, sf, nn, tc, tzb, ec, sw, fl, hx, hxs, hxr, hzr, hxs2, hxr2, hzr2,
    rks, rkr, wt, oh, xb, es, cs, crv, hs, hr,
    round_y, round_z, in_sem, out_sem, halo_s, halo_r, rk_s, rk_r, g_s, g_r, h_s, h_r,
):
    lx, plane, own, width = dims
    gn, hn = 2 ** len(G_BITS), 2 ** len(H_BITS)
    zc = hn // 2
    n_idx = hn * width
    ml, mp = lax.axis_index("layer"), lax.axis_index("plane")

    def flips(bits):
        steps = []
        for axis, bit in bits:
            at = ml if axis == "layer" else mp
            steps.append((axis == "layer", bit * (1 - 2 * ((at // bit) % 2))))
        return steps

    g_flips, h_flips = flips(G_BITS), flips(H_BITS)

    def partner(steps, r):
        to_l, to_p = ml, mp
        for i, (on_layer, step) in enumerate(steps):
            if (r >> i) & 1:
                to_l, to_p = (to_l + step, to_p) if on_layer else (to_l, to_p + step)
        return (to_l, to_p)

    up_x, down_x = (ml, (mp + 1) % plane), (ml, (mp + plane - 1) % plane)
    up_z, down_z = ((ml + 1) % lx, mp), ((ml + lx - 1) % lx, mp)

    def loop(n, body, start=0):
        for i in range(start, n):
            body(i)

    def group(g):
        return slice(g * 32, g * 32 + 32)

    def one_plane(z):
        return slice(z * 8, z * 8 + 8)

    loads = [
        pltpu.make_async_copy(k_hbm, va.at[0], in_sem.at[0]),
        pltpu.make_async_copy(bi_hbm, bi, in_sem.at[1]),
        pltpu.make_async_copy(sup_hbm, sup, in_sem.at[2]),
        pltpu.make_async_copy(a_hbm, aa, in_sem.at[3]),
        pltpu.make_async_copy(cr_hbm, cr1, in_sem.at[4]),
        pltpu.make_async_copy(p_hbm, pp, in_sem.at[5]),
        pltpu.make_async_copy(s_hbm, ss, in_sem.at[6]),
    ]
    for j, z in enumerate((0, 4, 12)):
        loads.append(pltpu.make_async_copy(blk_hbm.at[pl.ds(8 * z, 8)], blk.at[j], in_sem.at[7 + j]))
    barrier = pltpu.get_barrier_semaphore()

    def greet(who):
        pl.semaphore_signal(barrier, inc=1, device_id=who, device_id_type=MESH)

    def along_z(dz, dc):
        return (ml, mp + dc * (1 - 2 * (mp % 2)) + 2 * ((mp // 2 + dz) % zc - (mp // 2) % zc))

    x_mask = sum(1 << i for i, (axis, _) in enumerate(G_BITS) if axis == "layer")
    x_peers = [r for r in range(1, gn) if r & x_mask == r]
    y_peers = [r for r in range(1, gn) if r & x_mask == 0]
    z_peers = [(dz, dc) for dz in (1, zc - 1, 2, zc - 2) for dc in (0, 1)] + [(0, 1)]
    greet(up_x)
    greet(down_x)
    for r in x_peers:
        greet(partner(g_flips, r))
    for load in loads[:3]:
        load.start()
    for r in y_peers:
        greet(partner(g_flips, r))
    for dz, dc in z_peers:
        greet(along_z(dz, dc))
    for load in loads[3:]:
        load.start()
    greeted = 2 + len(x_peers) + len(y_peers) + len(z_peers)

    def second_round():
        for r in y_peers:
            pl.semaphore_signal(round_y, inc=1, device_id=partner(g_flips, r), device_id_type=MESH)
        for dz in (2, zc - 2):
            pl.semaphore_signal(round_z, inc=1, device_id=along_z(dz, 0), device_id_type=MESH)

    lane = lax.broadcasted_iota(I32, (32, 128), 1)
    m, x = lane % 8, lax.broadcasted_iota(I32, (32, 128), 0) % 8
    m1, x1 = m[:8], x[:8]
    lane1, row1 = lane[:8], x[:8]
    is_m = {i: m == i for i in (0, 3, 4, 7)}
    is_x = {i: x == i for i in (3, 4)}

    hx[...] = jnp.zeros_like(hx)
    tc[TXB] = jnp.zeros((128, 128), F32)

    loads[0].wait()

    def faces(g):
        rows, below = group(g), one_plane((4 * g + 15) % 16)
        k = va[0, rows, :]
        tym = jnp.where(lane == 0, 0.0, harmonic(k, roll_y(k, 1)))
        typ = roll_y(tym, 127)
        tc[TYM, rows, :] = tym
        tc[TYP, rows, :] = typ
        tc[TYM1, rows, :] = jnp.where(is_m[4], 0.0, tym)
        tc[TYP1, rows, :] = jnp.where(is_m[3], 0.0, typ)
        txm = jnp.where(x == 0, 0.0, harmonic(k, roll_x(k, 1)))
        tc[TXM, rows, :] = txm
        tc[TXP, rows, :] = roll_x(txm, 7)
        tz = harmonic(k, jnp.concatenate([va[0, below, :], k[0:24]], axis=0))
        tc[TZM, rows, :] = tz
        tc[TZP, below, :] = tz[0:8]
        tc[TZP, slice(g * 32, g * 32 + 24), :] = tz[8:32]
        tc[TZM1, rows, :] = tz
        tc[TZP1, below, :] = tz[0:8]
        tc[TZP1, slice(g * 32, g * 32 + 24), :] = tz[8:32]

    loop(4, faces)
    nil = jnp.zeros((8, 128), F32)
    tc[TZM, 0:8, :] = nil
    tc[TZP, 120:128, :] = nil
    tc[TZM1, 0:8, :] = nil
    tc[TZP1, 120:128, :] = nil
    tc[TZM1, 64:72, :] = nil
    tc[TZP1, 56:64, :] = nil
    for i, (t, z) in enumerate(((TZP, 3), (TZM, 4), (TZP, 11), (TZM, 12))):
        sw[i] = tc[t, 8 * z:8 * z + 8, :]

    loads[1].wait()
    loads[2].wait()

    def first(g):
        rows = group(g)
        vals = []
        for s in range(8):
            on = sup[s, rows, :].astype(F32)
            sf[s, rows, :] = on
            vals.append(bi[s, rows, :] * on)
        inv = 1.0 / sum(vals[1:], vals[0])
        for s in range(8):
            va[1 + s, rows, :] = vals[s] * inv

    loop(4, first)

    def exchange(v, off, xs_buf, xr_buf, zr_buf, base):
        for i, s in enumerate(B0):
            xs_buf[0, off + i] = v[off + s, pl.ds(0, 16, stride=8), :]
            xs_buf[1, off + i] = v[off + s, pl.ds(7, 16, stride=8), :]
        if off:
            xs_buf[0, 0] = v[0, pl.ds(0, 16, stride=8), :]
            xs_buf[1, 0] = v[0, pl.ds(7, 16, stride=8), :]
            pl.semaphore_wait(barrier, greeted)
        last, lead = v.at[pl.ds(0, off + 4), pl.ds(120, 8)], v.at[pl.ds(0, off + 4), pl.ds(0, 8)]
        copies = []
        for j, (src, dst, who) in enumerate((
            (xs_buf.at[1], xr_buf.at[0], up_x), (xs_buf.at[0], xr_buf.at[1], down_x),
            (last, zr_buf.at[0], up_z), (lead, zr_buf.at[1], down_z),
        )):
            copies.append(pltpu.make_async_remote_copy(
                src_ref=src, dst_ref=dst, send_sem=halo_s.at[base + j // 2], recv_sem=halo_r.at[base + j // 2],
                device_id=who, device_id_type=MESH))
        for copy in copies:
            copy.start()
        if off:
            second_round()
        return [pltpu.make_async_remote_copy(
            src_ref=buf, dst_ref=buf, send_sem=halo_s.at[base + j], recv_sem=halo_r.at[base + j],
            device_id=up_x, device_id_type=MESH) for j, buf in enumerate((xr_buf, zr_buf))]

    def inner(v, off):
        def part(g):
            rows = group(g)
            odd = g % 2
            below, above = one_plane((4 * g + 15) % 16), one_plane((4 * g + 4) % 16)
            for s in range(8):
                if s % 4 == 0:
                    vals = [v[off + s + i, rows, :] for i in range(4)]
                    txm, txp = tc[TXM, rows, :], tc[TXP, rows, :]
                    tym, typ = [tc[i, rows, :] for i in (TYM, TYM1)], [tc[i, rows, :] for i in (TYP, TYP1)]
                    zm, zp = tc[TZM1 if s else TZM, rows, :], tc[TZP1 if s else TZP, rows, :]
                here, by_y, by_x, turn = vals[s % 4], vals[s % 4 ^ 1], vals[s % 4 ^ 2], 4 - (s & 4) * 2
                near = tym[s & 1] * roll_y(jnp.where(is_m[7], by_y, here), 1)
                near += typ[s & 1] * roll_y(jnp.where(is_m[0], by_y, here), 127)
                near += txm * roll_x(jnp.where(is_x[3], by_x, here), 1)
                near += txp * roll_x(jnp.where(is_x[4], by_x, here), 7)
                lo, hi = v[off + s + turn * odd, below, :], v[off + s + turn * (1 - odd), above, :]
                near += zm * jnp.concatenate([lo, here[0:24]], axis=0)
                near += zp * jnp.concatenate([here[8:32], hi], axis=0)
                nn[s, rows, :] = near

        loop(4, part)

    def outer(v, off, new, off2, xr_buf, zr_buf, extra):
        for i in range(4):
            hx[i, pl.ds(0, 16, stride=8), :] = xr_buf[0, extra + i]
            hx[i, pl.ds(7, 16, stride=8), :] = xr_buf[1, extra + i]
            nn[i, 0:8, :] += tzb[0] * zr_buf[0, extra + i]
            nn[i, 120:128, :] += tzb[1] * zr_buf[1, extra + i]

        def part(g):
            rows = group(g)
            rd, txb = tc[RD, rows, :], tc[TXB, rows, :]
            vals = []
            for s in range(8):
                near = nn[s, rows, :]
                if s in B0:
                    near += txb * hx[B0.index(s), rows, :]
                vals.append((v[off + s, rows, :] * THIRD + rd * near) * sf[s, rows, :])
            inv = 1.0 / sum(vals[1:], vals[0])
            for s in range(8):
                new[off2 + s, rows, :] = vals[s] * inv

        loop(4, part)

    sent = exchange(va, 1, hxs, hxr, hzr, 0)
    inner(va, 1)

    for load in loads[3:]:
        load.wait()
    label = blk[0, 0:1, :]
    for u, (j, r) in enumerate(((0, 0), (0, 4), (1, 0), (1, 4), (2, 0), (2, 4), (1, 0), (1, 4))):
        label = jnp.where(m1[0:1] == u, blk[j, r:r + 1, :], label)
    t_rows, labels = tab.shape[0], cr1.shape[0]
    tab[labels // 128:, :] = jnp.zeros((t_rows - labels // 128, 128), I32)

    def table(t):
        tab[t:t + 1, :] = cr1[pl.ds(t * 128, 128)].reshape(1, 128)

    loop(labels // 128, table)
    if labels % 128:
        t = labels // 128
        tab[t:t + 1, 0:labels % 128] = cr1[pl.ds(t * 128, labels % 128)].reshape(1, labels % 128)
    l_hi, l_lo = label >> 7, label & 127
    w_iota = lax.broadcasted_iota(I32, (128, 128), 0)
    pick = jnp.where(w_iota == l_lo, 1.0, 0.0).astype(BF16)
    ranks = tab[...]
    parts = jnp.concatenate([(ranks >> 7).astype(F32), (ranks & 127).astype(F32)], axis=0).astype(BF16)
    looked = jnp.dot(parts, pick, preferred_element_type=F32)
    t_iota = lax.broadcasted_iota(I32, (t_rows, 128), 0)
    looked = looked[:t_rows] * 128.0 + looked[t_rows:]
    rank = jnp.sum(jnp.where(t_iota == l_hi, looked, 0.0), axis=0, keepdims=True)
    rank = rank.astype(I32)
    rks[...] = rank
    rkr[0] = rank

    def diagonal(g):
        rows = group(g)
        diag = aa[rows, :]
        for t in (TYM, TYP, TXM, TXP, TZM, TZP):
            diag += tc[t, rows, :]
        tc[RD, rows, :] = diag

    loop(4, diagonal)
    for copy in sent:
        copy.wait_recv()

    tc[TXB, pl.ds(0, 16, stride=8), :] = jnp.where(mp > 0, harmonic(hxs[0, 0], hxr[0, 0]), 0.0)
    tc[TXB, pl.ds(7, 16, stride=8), :] = jnp.where(mp < plane - 1, harmonic(hxs[1, 0], hxr[1, 0]), 0.0)
    tzb[0] = jnp.where(ml > 0, harmonic(va[0, 0:8, :], hzr[0, 0]), 0.0)
    tzb[1] = jnp.where(ml < lx - 1, harmonic(va[0, 120:128, :], hzr[1, 0]), 0.0)

    tc[RD, 0:8, :] += tzb[0]
    tc[RD, 120:128, :] += tzb[1]
    tc[RD] = TWO_THIRDS / (tc[RD] + tc[TXB])

    outer(va, 1, vb, 0, hxr, hzr, 1)
    sent2 = exchange(vb, 0, hxs2, hxr2, hzr2, 2)

    def every(buf, sems):
        return pltpu.make_async_remote_copy(
            src_ref=buf.at[pl.ds(1, gn - 1)], dst_ref=buf.at[pl.ds(1, gn - 1)], send_sem=sems[0], recv_sem=sems[1],
            device_id=partner(g_flips, 1), device_id_type=MESH)

    def rank_copy(r):
        return pltpu.make_async_remote_copy(
            src_ref=rks, dst_ref=rkr.at[r], send_sem=rk_s, recv_sem=rk_r,
            device_id=partner(g_flips, r), device_id_type=MESH)

    pl.semaphore_wait(round_y, len(y_peers))
    loop(gn, lambda r: rank_copy(r).start(), 1)
    es[...] = jnp.zeros_like(es)

    inner(vb, 0)

    def weigh(g):
        rows = group(g)
        tym, typ, txm, txp = (tc[i, rows, :] for i in (TYM, TYP, TXM, TXP))
        sx0 = jnp.where(is_x[3], txp, 0.0) + jnp.where(is_x[4], txm, 0.0)
        sx1 = sx0 + tc[TXB, rows, :]
        sy0 = jnp.where(is_m[7], typ, 0.0) + jnp.where(is_m[0], tym, 0.0)
        sy1 = sy0 + jnp.where(is_m[3], typ, 0.0) + jnp.where(is_m[4], tym, 0.0)
        for s in range(4):
            d = aa[rows, :] + (sx1 if s & 2 else sx0) + (sy1 if s & 1 else sy0)
            ec[s, rows, :] = d
            ec[4 + s, rows, :] = d
        ec[8, rows, :] = sx0
        ec[9, rows, :] = sy0

    loop(4, weigh)
    for i, z in enumerate((3, 4, 11, 12)):
        for s in range(8):
            ec[s, 8 * z:8 * z + 8, :] += sw[i]
    for t, z in ((tzb[0], 0), (tc[TZP, 56:64, :], 7), (tc[TZM, 64:72, :], 8), (tzb[1], 15)):
        for s in range(4, 8):
            ec[s, 8 * z:8 * z + 8, :] += t

    def x_swap(q):
        return roll_x(q, 4)

    def y_swap(q):
        return jnp.where(m1 == 7, roll_y(q, 127), jnp.where(m1 == 0, roll_y(q, 1), 0.0))

    def far(g):
        return one_plane(4 * g + 4 - 5 * (g % 2))

    def rest(g):
        rows = group(g)
        here = pp[rows, :]
        full = plane_sum(ec[0, rows, :] * here - ss[rows, :]) - sw[g] * pp[far(g), :]
        fl[8, one_plane(g), :] = (
            full - x_swap(plane_sum(ec[8, rows, :] * here)) - y_swap(plane_sum(ec[9, rows, :] * here)))

    loop(4, rest)

    for copy in sent2:
        copy.wait_recv()
    for copy in sent:
        copy.wait_send()
    outer(vb, 0, va, 1, hxr2, hzr2, 0)
    store = pltpu.make_async_copy(va.at[pl.ds(1, 8)], v_out, out_sem.at[0])
    store.start()

    def gather(g):
        rows = group(g)
        sx0, sy0 = ec[8, rows, :], ec[9, rows, :]
        vals = [va[1 + s, rows, :] for s in range(8)]
        qx = [x_swap(plane_sum(sx0 * v)) for v in vals]
        qy = [y_swap(plane_sum(sy0 * v)) for v in vals]
        for s in range(8):
            full = plane_sum(ec[s, rows, :] * vals[s]) - sw[g] * va[1 + (s ^ 4), far(g), :]
            fl[s, one_plane(g), :] = full - qx[s ^ 2] - qy[s ^ 1]

    loop(4, gather)

    def z_part(j, pz, s):
        groups = ((0,), (1, 2), (3,))[j] if pz == 1 else {(1, 0): (1,), (2, 0): (3,), (0, 2): (0,), (1, 2): (2,)}[j, pz]
        term = fl[s, one_plane(groups[0]), :]
        for g in groups[1:]:
            term += fl[s, one_plane(g), :]
        return term

    for k, (j, halves) in enumerate(((0, (1, 2)), (1, (1, 2)), (2, (1, 0)), (1, (0,)))):
        for half, pz in enumerate(halves):
            for b in range(2):
                at, s = 64 * half + 24 * b, (0 if pz == 1 else 4) + 2 * b
                side = z_part(j, pz, s + 1)
                es[k, at:at + 8, :] = jnp.where(m1 < 4, side, 0.0)
                es[k, at + 8:at + 16, :] = z_part(j, pz, s)
                es[k, at + 16:at + 24, :] = jnp.where(m1 < 4, 0.0, side)
        if k < 3:
            es[k, 48:56, :] = -z_part(j, 1, 8)

    m16 = m[:16]
    sums = []
    for k in range(4):
        for xi in range(2):
            t = es[k, pl.ds(4 * xi, 16, stride=8), :]
            for i in range(1, 4):
                t += es[k, pl.ds(4 * xi + i, 16, stride=8), :]
            sums.append(t)
    for bit in (4, 2, 1):
        high = (m16 & bit) != 0
        merged = []
        for u in range(bit):
            one, two = sums[u], sums[u + bit]
            move = jnp.where(high, one, two)
            merged.append(jnp.where(high, two, one) + jnp.where(high, roll_y(move, bit), roll_y(move, 128 - bit)))
        sums = merged
    rows_out = sums[0]
    cs[...] = rows_out
    crv[0] = rows_out

    def g_copy(r):
        return pltpu.make_async_remote_copy(
            src_ref=cs, dst_ref=crv.at[r], send_sem=g_s, recv_sem=g_r,
            device_id=partner(g_flips, r), device_id_type=MESH)

    for r in far_first(G_BITS):
        g_copy(r).start()

    xb[64:128, :] = jnp.zeros((64, gn * 128), BF16)

    def wanted(i):
        idx = row1 + i * 8
        peer = jnp.zeros_like(idx)
        for t in range(1, hn):
            peer += jnp.where(idx >= t * width, 1, 0)
        col = idx - peer * width
        dev = jnp.zeros_like(idx) + (ml * plane + mp)
        for b, (on_layer, step) in enumerate(h_flips):
            dev += ((peer >> b) & 1) * (step * plane if on_layer else step)
        want = dev * own + col
        for q in range(4):
            wt[one_plane(i + q * (n_idx // 8)), :] = jnp.where(col + q * width < own, want + q * width, -7)

    loop(n_idx // 8, wanted)

    every(rkr, (rk_s, rk_r)).wait_recv()

    have = [rkr[r] for r in range(gn)]

    def build(i, carry):
        at = pl.multiple_of(i * 16, 16)
        want = wt[pl.ds(at, 16), :]
        for r in range(gn):
            oh[pl.ds(at, 16), 128 * r:128 * r + 128] = jnp.where(want == have[r], 1.0, 0.0).astype(BF16)
        return carry

    lax.fori_loop(0, 4 * n_idx // 16, build, 0)

    odd = m1 % 2 == 1
    b1 = (x1 >= 3) & (x1 < 6)
    b1_odd = b1 & odd

    def spread(r):
        got1, got2 = crv[r, 0:8, :], crv[r, 8:16, :]
        pz1 = jnp.where(m1 < 6, got1, 0.0)
        pz2 = jnp.where(m1 < 4, got2, 0.0)
        pz0 = jnp.where(m1 < 4, 0.0, jnp.where(m1 < 6, got2, got1))
        low1, low2, low0 = (jnp.where(b1_odd, v, 0.0) for v in (pz1, pz2, pz0))
        last = pltpu.roll(low1, 5, 0) + low2 + jnp.where(x1 >= 6, pltpu.roll(low0, 3, 0), 0.0)
        vals = jnp.concatenate([
            pz1 - low1 + jnp.where(x1 == 7, pltpu.roll(low0, 2, 0), 0.0), pz2 - low2, pz0 - low0, last], axis=0)
        high = vals.astype(BF16)
        lanes = slice(128 * r, 128 * r + 128)
        xb[0:32, lanes] = high
        xb[32:64, lanes] = (vals - high.astype(F32)).astype(BF16)

    every(crv, (g_s, g_r)).wait_recv()
    loop(gn, spread)
    routed = lax.dot_general(
        oh[...], xb[...], (((1,), (1,)), ((), ())), preferred_element_type=F32)
    quarter = lax.broadcasted_iota(I32, (n_idx, 128), 1) >> 5
    packed = jnp.zeros((n_idx, 128), F32)
    for q in range(4):
        part = routed[q * n_idx:(q + 1) * n_idx]
        first_half = roll_y(part, 32 * q) if q else part
        second_half = part if q == 1 else roll_y(part, (32 * q + 96) % 128)
        packed = jnp.where(quarter == q, first_half + second_half, packed)
    def h_copy(r):
        return pltpu.make_async_remote_copy(
            src_ref=hs.at[r], dst_ref=hr.at[r], send_sem=h_s.at[r], recv_sem=h_r.at[r],
            device_id=partner(h_flips, r), device_id_type=MESH)

    pl.semaphore_wait(round_z, 2)
    for r in far_first(H_BITS):
        hs[r] = packed[r * width:(r + 1) * width]
        h_copy(r).start()
    hs[0] = packed[0:width]
    store.wait()
    for copy in sent2:
        copy.wait_send()
    every(rkr, (rk_s, rk_r)).wait_send()
    every(crv, (g_s, g_r)).wait_send()
    loop(hn, lambda r: h_copy(r).wait_send(), 1)
    loop(hn, lambda r: h_copy(r).wait_recv(), 1)
    final = hs[0]
    for r in range(1, hn):
        final += hr[r]
    f_out[0:width, :] = final


def finish(own, width, v_in, f_in, v_out, cm_hbm, cr_hbm, ft, cm_out, cr_out, sem):
    stores = [pltpu.make_async_copy(src, dst, sem.at[i]) for i, (src, dst) in enumerate((
        (v_in, v_out), (cm_out, cm_hbm), (cr_out, cr_hbm)))]
    stores[0].start()
    ft[0:16, :] = f_in[...]
    turned = ft[...].T
    lane = lax.broadcasted_iota(I32, (32, 128), 1)
    done = jnp.zeros((32, 128), F32)
    for q in range(4):
        part = turned[32 * q:32 * q + 32]
        here = (lane >= q * width) & (lane < (q + 1) * width)
        done = jnp.where(here, pltpu.roll(part, q * width, 1) if q else part, done)
    for pz, px, base in (
        (1, 1, 0), (1, 2, 3), (2, 1, 8), (2, 2, 11), (0, 1, 16), (0, 2, 19), (1, 0, 24), (2, 0, 27)):
        k = 9 * pz + 3 * px
        cm_out[k:k + 3, :] = done[base:base + 3, 0:own]
    cm_out[0:2, :] = done[30:32, 0:own]
    cm_out[2:3, :] = done[7:8, 0:own]
    cr_out[...] = done[6:7, 0:own]
    stores[1].start()
    stores[2].start()
    for store in stores:
        store.wait()


def per_device(sizes, basis_init, permeability, accumulation, pressure, source, support, block_of, curve_rank):
    lx, plane = sizes
    gn, hn = 2 ** len(G_BITS), 2 ** len(H_BITS)
    devices = lx * plane
    own = (curve_rank.shape[0] + devices - 1) // devices
    width = (own + 3) // 4
    flat = lambda v: v.reshape(v.shape[:-3] + (128, 128))
    t_rows = -(-curve_rank.shape[0] // 2048) * 16
    anywhere = pl.BlockSpec(memory_space=pl.ANY)
    vmem = pl.BlockSpec(memory_space=pltpu.VMEM)
    dma = pltpu.SemaphoreType.DMA
    cells = lambda *lead: pltpu.VMEM(lead + (128, 128), F32)
    basis, rows = pl.pallas_call(
        functools.partial(kernel, (lx, plane, own, width)),
        out_shape=(
            jax.ShapeDtypeStruct((8, 128, 128), F32),
            jax.ShapeDtypeStruct((16, 128), F32),
        ),
        in_specs=[anywhere] * 8,
        out_specs=(anywhere, vmem),
        scratch_shapes=[
            cells(8), pltpu.VMEM((8, 128, 128), I32), cells(), cells(), cells(),
            pltpu.VMEM((3, 8, 128), I32), pltpu.VMEM(curve_rank.shape, I32), pltpu.VMEM((t_rows, 128), I32),
            cells(9), cells(8), cells(8), cells(8), cells(12),
            pltpu.VMEM((2, 8, 128), F32), cells(10), pltpu.VMEM((4, 8, 128), F32),
            pltpu.VMEM((9, 32, 128), F32), cells(4),
            pltpu.VMEM((2, 5, 16, 128), F32), pltpu.VMEM((2, 5, 16, 128), F32), pltpu.VMEM((2, 5, 8, 128), F32),
            pltpu.VMEM((2, 4, 16, 128), F32), pltpu.VMEM((2, 4, 16, 128), F32), pltpu.VMEM((2, 4, 8, 128), F32),
            pltpu.VMEM((1, 128), I32), pltpu.VMEM((gn, 1, 128), I32),
            pltpu.VMEM((4 * hn * width, 128), I32), pltpu.VMEM((4 * hn * width, gn * 128), BF16),
            pltpu.VMEM((128, gn * 128), BF16), pltpu.VMEM((4, 128, 128), F32),
            pltpu.VMEM((16, 128), F32), pltpu.VMEM((gn, 16, 128), F32),
            pltpu.VMEM((hn, width, 128), F32), pltpu.VMEM((hn, width, 128), F32),
            pltpu.SemaphoreType.REGULAR, pltpu.SemaphoreType.REGULAR, dma((10,)), dma((1,)), dma((4,)), dma((4,)),
            dma, dma, dma, dma, dma((hn,)), dma((hn,)),
        ],
        compiler_params=pltpu.CompilerParams(
            collective_id=0, has_side_effects=True, vmem_limit_bytes=VMEM_GRANT),
        cost_estimate=pl.CostEstimate(flops=20_000_000, bytes_accessed=2_000_000, transcendentals=0),
    )(*(pltpu.with_memory_space_constraint(v, pltpu.HBM) for v in (
        flat(basis_init), flat(permeability), flat(accumulation), flat(pressure), flat(source),
        flat(support), flat(block_of), curve_rank,
    )))
    basis, matrix, residual = pl.pallas_call(
        functools.partial(finish, own, width),
        out_shape=(
            jax.ShapeDtypeStruct((8, 128, 128), F32),
            jax.ShapeDtypeStruct((27, own), F32),
            jax.ShapeDtypeStruct((1, own), F32),
        ),
        in_specs=[anywhere, vmem],
        out_specs=(anywhere, anywhere, anywhere),
        scratch_shapes=[cells(), pltpu.VMEM((27, own), F32), pltpu.VMEM((1, own), F32), dma((3,))],
        compiler_params=pltpu.CompilerParams(vmem_limit_bytes=VMEM_GRANT),
    )(basis, rows)
    return basis.reshape(basis_init.shape), matrix, residual.reshape(own)


def solution(mesh):
    return jax.shard_map(
        functools.partial(per_device, (mesh.shape["layer"], mesh.shape["plane"])),
        mesh=mesh,
        in_specs=(
            P(None, "layer", "plane", None),
            P("layer", "plane", None),
            P("layer", "plane", None),
            P("layer", "plane", None),
            P("layer", "plane", None),
            P(None, "layer", "plane", None),
            P("layer", "plane", None),
            P(),
        ),
        out_specs=(
            P(None, "layer", "plane", None),
            P(None, ("layer", "plane")),
            P(("layer", "plane")),
        ),
        check_vma=False,
    )
```

```python
import functools

import jax
import jax.numpy as jnp
from jax import lax
from jax.experimental import pallas as pl
from jax.experimental.pallas import tpu as pltpu
from jax.sharding import PartitionSpec as P

MESH = pl.DeviceIdType.MESH
F32, BF16, I32 = jnp.float32, jnp.bfloat16, jnp.int32

G_BITS = (("layer", 1), ("layer", 2), ("plane", 16), ("plane", 32))
H_BITS = (("plane", 1), ("plane", 2), ("plane", 4), ("plane", 8))
VMEM_GRANT = 32 * 1024 * 1024
THIRD, TWO_THIRDS = 1.0 / 3.0, 2.0 / 3.0
B0 = (0, 1, 4, 5)
A0 = (0, 1, 2, 3)
TYM, TYP, TYM1, TYP1, TXM, TXP, TZM, TZP, TZM1, TZP1, TXB, RD = range(12)


def roll_x(v, shift):
    rows = v.shape[0]
    return pltpu.roll(v.reshape(rows // 8, 8, 128), shift, 1).reshape(rows, 128)


def roll_y(v, shift):
    return pltpu.roll(v, shift, 1)


def harmonic(k, n):
    return 2.0 * k * n / (k + n)


def plane_sum(v):
    return v.reshape(-1, 8, 128).sum(axis=0)


def far_first(bits):
    def hops(r):
        reach = {"layer": 0, "y": 0, "z": 0}
        for i, (axis, bit) in enumerate(bits):
            if (r >> i) & 1:
                kind, step = (axis, bit) if axis == "layer" else ("y", bit // 16) if bit >= 16 else ("z", bit // 2)
                reach[kind] += step
        return sum(min(n, size - n) for n, size in ((reach["layer"], 4), (reach["y"], 4), (reach["z"], 8)))

    return sorted(range(1, 2 ** len(bits)), key=lambda r: -hops(r))


def kernel(
    dims,
    bi_hbm, k_hbm, a_hbm, p_hbm, s_hbm, sup_hbm, blk_hbm, cr_hbm,
    v_out, f_out,
    bi, sup, aa, pp, ss, blk, cr1, tab,
    va, vb, sf, nn, tc, tzb, ec, sw, fl, hx, hxs, hxr, hzr, hxs2, hxr2, hzr2,
    rks, rkr, rkt, oh, xb, es, cs, crv, hs, hr,
    round_y, round_z, in_sem, out_sem, halo_s, halo_r, rk_s, rk_r, g_s, g_r, h_s, h_r,
):
    lx, plane, own, width = dims
    gn, hn = 2 ** len(G_BITS), 2 ** len(H_BITS)
    zc = hn // 2
    n_idx = hn * width
    ml, mp = lax.axis_index("layer"), lax.axis_index("plane")

    def flips(bits):
        steps = []
        for axis, bit in bits:
            at = ml if axis == "layer" else mp
            steps.append((axis == "layer", bit * (1 - 2 * ((at // bit) % 2))))
        return steps

    g_flips, h_flips = flips(G_BITS), flips(H_BITS)

    def partner(steps, r):
        to_l, to_p = ml, mp
        for i, (on_layer, step) in enumerate(steps):
            if (r >> i) & 1:
                to_l, to_p = (to_l + step, to_p) if on_layer else (to_l, to_p + step)
        return (to_l, to_p)

    up_x, down_x = (ml, (mp + 1) % plane), (ml, (mp + plane - 1) % plane)
    up_z, down_z = ((ml + 1) % lx, mp), ((ml + lx - 1) % lx, mp)

    def loop(n, body, start=0):
        for i in range(start, n):
            body(i)

    def group(g):
        return slice(g * 32, g * 32 + 32)

    def one_plane(z):
        return slice(z * 8, z * 8 + 8)

    loads = [
        pltpu.make_async_copy(k_hbm, va.at[0], in_sem.at[0]),
        pltpu.make_async_copy(bi_hbm, bi, in_sem.at[1]),
        pltpu.make_async_copy(sup_hbm, sup, in_sem.at[2]),
        pltpu.make_async_copy(a_hbm, aa, in_sem.at[3]),
        pltpu.make_async_copy(cr_hbm, cr1, in_sem.at[4]),
        pltpu.make_async_copy(p_hbm, pp, in_sem.at[5]),
        pltpu.make_async_copy(s_hbm, ss, in_sem.at[6]),
    ]
    for j, z in enumerate((0, 4, 12)):
        loads.append(pltpu.make_async_copy(blk_hbm.at[pl.ds(8 * z, 8)], blk.at[j], in_sem.at[7 + j]))
    barrier = pltpu.get_barrier_semaphore()

    def greet(who):
        pl.semaphore_signal(barrier, inc=1, device_id=who, device_id_type=MESH)

    def along_z(dz, dc):
        return (ml, mp + dc * (1 - 2 * (mp % 2)) + 2 * ((mp // 2 + dz) % zc - (mp // 2) % zc))

    x_mask = sum(1 << i for i, (axis, _) in enumerate(G_BITS) if axis == "layer")
    x_peers = [r for r in range(1, gn) if r & x_mask == r]
    y_peers = [r for r in range(1, gn) if r & x_mask == 0]
    z_peers = [(dz, dc) for dz in (1, zc - 1, 2, zc - 2) for dc in (0, 1)] + [(0, 1)]
    greet(up_x)
    greet(down_x)
    for r in x_peers:
        greet(partner(g_flips, r))
    for load in loads[:3]:
        load.start()
    for r in y_peers:
        greet(partner(g_flips, r))
    for dz, dc in z_peers:
        greet(along_z(dz, dc))
    for load in loads[3:]:
        load.start()
    greeted = 2 + len(x_peers) + len(y_peers) + len(z_peers)

    def second_round():
        for r in y_peers:
            pl.semaphore_signal(round_y, inc=1, device_id=partner(g_flips, r), device_id_type=MESH)
        for dz in (2, zc - 2):
            pl.semaphore_signal(round_z, inc=1, device_id=along_z(dz, 0), device_id_type=MESH)

    lane = lax.broadcasted_iota(I32, (32, 128), 1)
    m, x = lane % 8, lax.broadcasted_iota(I32, (32, 128), 0) % 8
    m1, x1 = m[:8], x[:8]
    lane1, row1 = lane[:8], x[:8]
    is_m = {i: m == i for i in (0, 3, 4, 7)}
    is_x = {i: x == i for i in (3, 4)}

    hx[...] = jnp.zeros_like(hx)
    tc[TXB] = jnp.zeros((128, 128), F32)

    loads[0].wait()

    def faces(g):
        rows, below = group(g), one_plane((4 * g + 15) % 16)
        k = va[0, rows, :]
        tym = jnp.where(lane == 0, 0.0, harmonic(k, roll_y(k, 1)))
        typ = roll_y(tym, 127)
        tc[TYM, rows, :] = tym
        tc[TYP, rows, :] = typ
        tc[TYM1, rows, :] = jnp.where(is_m[4], 0.0, tym)
        tc[TYP1, rows, :] = jnp.where(is_m[3], 0.0, typ)
        txm = jnp.where(x == 0, 0.0, harmonic(k, roll_x(k, 1)))
        tc[TXM, rows, :] = txm
        tc[TXP, rows, :] = roll_x(txm, 7)
        tz = harmonic(k, jnp.concatenate([va[0, below, :], k[0:24]], axis=0))
        tc[TZM, rows, :] = tz
        tc[TZP, below, :] = tz[0:8]
        tc[TZP, slice(g * 32, g * 32 + 24), :] = tz[8:32]
        tc[TZM1, rows, :] = tz
        tc[TZP1, below, :] = tz[0:8]
        tc[TZP1, slice(g * 32, g * 32 + 24), :] = tz[8:32]

    loop(4, faces)
    nil = jnp.zeros((8, 128), F32)
    tc[TZM, 0:8, :] = nil
    tc[TZP, 120:128, :] = nil
    tc[TZM1, 0:8, :] = nil
    tc[TZP1, 120:128, :] = nil
    tc[TZM1, 64:72, :] = nil
    tc[TZP1, 56:64, :] = nil
    for i, (t, z) in enumerate(((TZP, 3), (TZM, 4), (TZP, 11), (TZM, 12))):
        sw[i] = tc[t, 8 * z:8 * z + 8, :]

    loads[1].wait()
    loads[2].wait()

    def first(g):
        rows = group(g)
        vals = []
        for s in range(8):
            on = sup[s, rows, :].astype(F32)
            sf[s, rows, :] = on
            vals.append(bi[s, rows, :] * on)
        inv = 1.0 / sum(vals[1:], vals[0])
        for s in range(8):
            va[1 + s, rows, :] = vals[s] * inv

    loop(4, first)

    def exchange(v, off, xs_buf, xr_buf, zr_buf, base):
        for i, s in enumerate(B0):
            xs_buf[0, off + i] = v[off + s, pl.ds(0, 16, stride=8), :]
            xs_buf[1, off + i] = v[off + s, pl.ds(7, 16, stride=8), :]
        if off:
            xs_buf[0, 0] = v[0, pl.ds(0, 16, stride=8), :]
            xs_buf[1, 0] = v[0, pl.ds(7, 16, stride=8), :]
            pl.semaphore_wait(barrier, greeted)
        last, lead = v.at[pl.ds(0, off + 4), pl.ds(120, 8)], v.at[pl.ds(0, off + 4), pl.ds(0, 8)]
        copies = []
        for j, (src, dst, who) in enumerate((
            (xs_buf.at[1], xr_buf.at[0], up_x), (xs_buf.at[0], xr_buf.at[1], down_x),
            (last, zr_buf.at[0], up_z), (lead, zr_buf.at[1], down_z),
        )):
            copies.append(pltpu.make_async_remote_copy(
                src_ref=src, dst_ref=dst, send_sem=halo_s.at[base + j // 2], recv_sem=halo_r.at[base + j // 2],
                device_id=who, device_id_type=MESH))
        for copy in copies:
            copy.start()
        if off:
            second_round()
        return [pltpu.make_async_remote_copy(
            src_ref=buf, dst_ref=buf, send_sem=halo_s.at[base + j], recv_sem=halo_r.at[base + j],
            device_id=up_x, device_id_type=MESH) for j, buf in enumerate((xr_buf, zr_buf))]

    def inner(v, off):
        def part(g):
            rows = group(g)
            odd = g % 2
            below, above = one_plane((4 * g + 15) % 16), one_plane((4 * g + 4) % 16)
            for s in range(8):
                if s % 4 == 0:
                    vals = [v[off + s + i, rows, :] for i in range(4)]
                    txm, txp = tc[TXM, rows, :], tc[TXP, rows, :]
                    tym, typ = [tc[i, rows, :] for i in (TYM, TYM1)], [tc[i, rows, :] for i in (TYP, TYP1)]
                    zm, zp = tc[TZM1 if s else TZM, rows, :], tc[TZP1 if s else TZP, rows, :]
                here, by_y, by_x, turn = vals[s % 4], vals[s % 4 ^ 1], vals[s % 4 ^ 2], 4 - (s & 4) * 2
                near = tym[s & 1] * roll_y(jnp.where(is_m[7], by_y, here), 1)
                near += typ[s & 1] * roll_y(jnp.where(is_m[0], by_y, here), 127)
                near += txm * roll_x(jnp.where(is_x[3], by_x, here), 1)
                near += txp * roll_x(jnp.where(is_x[4], by_x, here), 7)
                lo, hi = v[off + s + turn * odd, below, :], v[off + s + turn * (1 - odd), above, :]
                near += zm * jnp.concatenate([lo, here[0:24]], axis=0)
                near += zp * jnp.concatenate([here[8:32], hi], axis=0)
                nn[s, rows, :] = near

        loop(4, part)

    def outer(v, off, new, off2, xr_buf, zr_buf, extra):
        for i in range(4):
            hx[i, pl.ds(0, 16, stride=8), :] = xr_buf[0, extra + i]
            hx[i, pl.ds(7, 16, stride=8), :] = xr_buf[1, extra + i]
            nn[i, 0:8, :] += tzb[0] * zr_buf[0, extra + i]
            nn[i, 120:128, :] += tzb[1] * zr_buf[1, extra + i]

        def part(g):
            rows = group(g)
            rd, txb = tc[RD, rows, :], tc[TXB, rows, :]
            vals = []
            for s in range(8):
                near = nn[s, rows, :]
                if s in B0:
                    near += txb * hx[B0.index(s), rows, :]
                vals.append((v[off + s, rows, :] * THIRD + rd * near) * sf[s, rows, :])
            inv = 1.0 / sum(vals[1:], vals[0])
            for s in range(8):
                new[off2 + s, rows, :] = vals[s] * inv

        loop(4, part)

    sent = exchange(va, 1, hxs, hxr, hzr, 0)
    inner(va, 1)

    for load in loads[3:]:
        load.wait()
    label = blk[0, 0:1, :]
    for u, (j, r) in enumerate(((0, 0), (0, 4), (1, 0), (1, 4), (2, 0), (2, 4), (1, 0), (1, 4))):
        label = jnp.where(m1[0:1] == u, blk[j, r:r + 1, :], label)
    t_rows, labels = tab.shape[0], cr1.shape[0]
    tab[labels // 128:, :] = jnp.zeros((t_rows - labels // 128, 128), I32)

    def table(t):
        tab[t:t + 1, :] = cr1[pl.ds(t * 128, 128)].reshape(1, 128)

    loop(labels // 128, table)
    if labels % 128:
        t = labels // 128
        tab[t:t + 1, 0:labels % 128] = cr1[pl.ds(t * 128, labels % 128)].reshape(1, labels % 128)
    l_hi, l_lo = label >> 7, label & 127
    w_iota = lax.broadcasted_iota(I32, (128, 128), 0)
    pick = jnp.where(w_iota == l_lo, 1.0, 0.0).astype(BF16)
    ranks = tab[...]
    parts = jnp.concatenate([(ranks >> 7).astype(F32), (ranks & 127).astype(F32)], axis=0).astype(BF16)
    looked = jnp.dot(parts, pick, preferred_element_type=F32)
    t_iota = lax.broadcasted_iota(I32, (t_rows, 128), 0)
    looked = looked[:t_rows] * 128.0 + looked[t_rows:]
    rank = jnp.sum(jnp.where(t_iota == l_hi, looked, 0.0), axis=0, keepdims=True)
    rank = rank.astype(I32)
    rks[...] = rank
    rkr[0] = rank

    def diagonal(g):
        rows = group(g)
        diag = aa[rows, :]
        for t in (TYM, TYP, TXM, TXP, TZM, TZP):
            diag += tc[t, rows, :]
        tc[RD, rows, :] = diag

    loop(4, diagonal)
    for copy in sent:
        copy.wait_recv()

    tc[TXB, pl.ds(0, 16, stride=8), :] = jnp.where(mp > 0, harmonic(hxs[0, 0], hxr[0, 0]), 0.0)
    tc[TXB, pl.ds(7, 16, stride=8), :] = jnp.where(mp < plane - 1, harmonic(hxs[1, 0], hxr[1, 0]), 0.0)
    tzb[0] = jnp.where(ml > 0, harmonic(va[0, 0:8, :], hzr[0, 0]), 0.0)
    tzb[1] = jnp.where(ml < lx - 1, harmonic(va[0, 120:128, :], hzr[1, 0]), 0.0)

    tc[RD, 0:8, :] += tzb[0]
    tc[RD, 120:128, :] += tzb[1]
    tc[RD] = TWO_THIRDS / (tc[RD] + tc[TXB])

    outer(va, 1, vb, 0, hxr, hzr, 1)
    sent2 = exchange(vb, 0, hxs2, hxr2, hzr2, 2)

    def every(buf, sems):
        return pltpu.make_async_remote_copy(
            src_ref=buf.at[pl.ds(1, gn - 1)], dst_ref=buf.at[pl.ds(1, gn - 1)], send_sem=sems[0], recv_sem=sems[1],
            device_id=partner(g_flips, 1), device_id_type=MESH)

    def rank_copy(r):
        return pltpu.make_async_remote_copy(
            src_ref=rks, dst_ref=rkr.at[r], send_sem=rk_s, recv_sem=rk_r,
            device_id=partner(g_flips, r), device_id_type=MESH)

    pl.semaphore_wait(round_y, len(y_peers))
    loop(gn, lambda r: rank_copy(r).start(), 1)
    es[...] = jnp.zeros_like(es)

    inner(vb, 0)

    def weigh(g):
        rows = group(g)
        tym, typ, txm, txp = (tc[i, rows, :] for i in (TYM, TYP, TXM, TXP))
        sx0 = jnp.where(is_x[3], txp, 0.0) + jnp.where(is_x[4], txm, 0.0)
        sx1 = sx0 + tc[TXB, rows, :]
        sy0 = jnp.where(is_m[7], typ, 0.0) + jnp.where(is_m[0], tym, 0.0)
        sy1 = sy0 + jnp.where(is_m[3], typ, 0.0) + jnp.where(is_m[4], tym, 0.0)
        for s in range(4):
            d = aa[rows, :] + (sx1 if s & 2 else sx0) + (sy1 if s & 1 else sy0)
            ec[s, rows, :] = d
            ec[4 + s, rows, :] = d
        ec[8, rows, :] = sx0
        ec[9, rows, :] = sy0

    loop(4, weigh)
    for i, z in enumerate((3, 4, 11, 12)):
        for s in range(8):
            ec[s, 8 * z:8 * z + 8, :] += sw[i]
    for t, z in ((tzb[0], 0), (tc[TZP, 56:64, :], 7), (tc[TZM, 64:72, :], 8), (tzb[1], 15)):
        for s in range(4, 8):
            ec[s, 8 * z:8 * z + 8, :] += t

    def x_swap(q):
        return roll_x(q, 4)

    def y_swap(q):
        return jnp.where(m1 == 7, roll_y(q, 127), jnp.where(m1 == 0, roll_y(q, 1), 0.0))

    def far(g):
        return one_plane(4 * g + 4 - 5 * (g % 2))

    def rest(g):
        rows = group(g)
        here = pp[rows, :]
        full = plane_sum(ec[0, rows, :] * here - ss[rows, :]) - sw[g] * pp[far(g), :]
        fl[8, one_plane(g), :] = (
            full - x_swap(plane_sum(ec[8, rows, :] * here)) - y_swap(plane_sum(ec[9, rows, :] * here)))

    loop(4, rest)

    for copy in sent2:
        copy.wait_recv()
    for copy in sent:
        copy.wait_send()
    outer(vb, 0, va, 1, hxr2, hzr2, 0)
    store = pltpu.make_async_copy(va.at[pl.ds(1, 8)], v_out, out_sem.at[0])
    store.start()

    def gather(g):
        rows = group(g)
        sx0, sy0 = ec[8, rows, :], ec[9, rows, :]
        vals = [va[1 + s, rows, :] for s in range(8)]
        qx = [x_swap(plane_sum(sx0 * v)) for v in vals]
        qy = [y_swap(plane_sum(sy0 * v)) for v in vals]
        for s in range(8):
            full = plane_sum(ec[s, rows, :] * vals[s]) - sw[g] * va[1 + (s ^ 4), far(g), :]
            fl[s, one_plane(g), :] = full - qx[s ^ 2] - qy[s ^ 1]

    loop(4, gather)

    def z_part(j, pz, s):
        groups = ((0,), (1, 2), (3,))[j] if pz == 1 else {(1, 0): (1,), (2, 0): (3,), (0, 2): (0,), (1, 2): (2,)}[j, pz]
        term = fl[s, one_plane(groups[0]), :]
        for g in groups[1:]:
            term += fl[s, one_plane(g), :]
        return term

    for k, (j, halves) in enumerate(((0, (1, 2)), (1, (1, 2)), (2, (1, 0)), (1, (0,)))):
        for half, pz in enumerate(halves):
            for b in range(2):
                at, s = 64 * half + 24 * b, (0 if pz == 1 else 4) + 2 * b
                side = z_part(j, pz, s + 1)
                es[k, at:at + 8, :] = jnp.where(m1 < 4, side, 0.0)
                es[k, at + 8:at + 16, :] = z_part(j, pz, s)
                es[k, at + 16:at + 24, :] = jnp.where(m1 < 4, 0.0, side)
        if k < 3:
            es[k, 48:56, :] = -z_part(j, 1, 8)

    m16 = m[:16]
    sums = []
    for k in range(4):
        for xi in range(2):
            t = es[k, pl.ds(4 * xi, 16, stride=8), :]
            for i in range(1, 4):
                t += es[k, pl.ds(4 * xi + i, 16, stride=8), :]
            sums.append(t)
    for bit in (4, 2, 1):
        high = (m16 & bit) != 0
        merged = []
        for u in range(bit):
            one, two = sums[u], sums[u + bit]
            move = jnp.where(high, one, two)
            merged.append(jnp.where(high, two, one) + jnp.where(high, roll_y(move, bit), roll_y(move, 128 - bit)))
        sums = merged
    rows_out = sums[0]
    cs[...] = rows_out
    crv[0] = rows_out

    def g_copy(r):
        return pltpu.make_async_remote_copy(
            src_ref=cs, dst_ref=crv.at[r], send_sem=g_s, recv_sem=g_r,
            device_id=partner(g_flips, r), device_id_type=MESH)

    for r in far_first(G_BITS):
        g_copy(r).start()

    def wanted(t):
        q, idx = (t, lane1) if t < 4 else (lane1 >> 5, 128 + (lane1 & 31))
        peer = jnp.zeros_like(idx)
        for p in range(1, hn):
            peer += jnp.where(idx >= p * width, 1, 0)
        col = idx - peer * width + q * width
        dev = jnp.zeros_like(idx) + (ml * plane + mp)
        for b, (on_layer, step) in enumerate(h_flips):
            dev += ((peer >> b) & 1) * (step * plane if on_layer else step)
        return jnp.where((col < own) & (idx < n_idx), dev * own + col, -7)

    wants = [wanted(t) for t in range(5)]
    every(rkr, (rk_s, rk_r)).wait_recv()
    turned = jnp.concatenate([rkr[r] for r in range(gn)] + [jnp.zeros((128 - gn, 128), I32)], axis=0).astype(F32).T
    rkt[...] = turned.astype(I32)
    for r in range(gn):
        have = jnp.broadcast_to(rkt[:, r:r + 1], (128, 128))
        for t in range(5):
            want = jnp.concatenate([wants[t]] * 16, axis=0)
            oh[128 * r:128 * r + 128, 128 * t:128 * t + 128] = jnp.where(have == want, 1.0, 0.0).astype(BF16)

    odd = m1 % 2 == 1
    b1 = (x1 >= 3) & (x1 < 6)
    b1_odd = b1 & odd

    def spread(r):
        got1, got2 = crv[r, 0:8, :], crv[r, 8:16, :]
        pz1 = jnp.where(m1 < 6, got1, 0.0)
        pz2 = jnp.where(m1 < 4, got2, 0.0)
        pz0 = jnp.where(m1 < 4, 0.0, jnp.where(m1 < 6, got2, got1))
        low1, low2, low0 = (jnp.where(b1_odd, v, 0.0) for v in (pz1, pz2, pz0))
        last = pltpu.roll(low1, 5, 0) + low2 + jnp.where(x1 >= 6, pltpu.roll(low0, 3, 0), 0.0)
        vals = jnp.concatenate([
            pz1 - low1 + jnp.where(x1 == 7, pltpu.roll(low0, 2, 0), 0.0), pz2 - low2, pz0 - low0, last], axis=0)
        high = vals.astype(BF16)
        lanes = slice(128 * r, 128 * r + 128)
        xb[0:32, lanes] = high
        xb[32:64, lanes] = (vals - high.astype(F32)).astype(BF16)

    every(crv, (g_s, g_r)).wait_recv()
    loop(gn, spread)
    routed = jnp.dot(xb[...], oh[...], preferred_element_type=F32)
    both = routed[0:32] + routed[32:64]
    parts = [both[:, 128 * q:128 * q + 128] for q in range(4)]
    over = both[:, 512:640]
    packed = jnp.concatenate([
        jnp.concatenate(parts, axis=0).T,
        jnp.concatenate([roll_y(over, (128 - 32 * q) % 128) if q else over for q in range(4)], axis=0).T], axis=0)

    def h_copy(r):
        return pltpu.make_async_remote_copy(
            src_ref=hs.at[r], dst_ref=hr.at[r], send_sem=h_s.at[r], recv_sem=h_r.at[r],
            device_id=partner(h_flips, r), device_id_type=MESH)

    pl.semaphore_wait(round_z, 2)
    for r in far_first(H_BITS):
        hs[r] = packed[r * width:(r + 1) * width]
        h_copy(r).start()
    hs[0] = packed[0:width]
    store.wait()
    for copy in sent2:
        copy.wait_send()
    every(rkr, (rk_s, rk_r)).wait_send()
    every(crv, (g_s, g_r)).wait_send()
    loop(hn, lambda r: h_copy(r).wait_send(), 1)
    loop(hn, lambda r: h_copy(r).wait_recv(), 1)
    final = hs[0]
    for r in range(1, hn):
        final += hr[r]
    f_out[0:width, :] = final


def finish(own, width, v_in, f_in, v_out, cm_hbm, cr_hbm, ft, cm_out, cr_out, sem):
    pairs = [(v_in.at[pl.ds(2 * i, 2)], v_out.at[pl.ds(2 * i, 2)]) for i in range(4)]
    pairs += [(cm_out, cm_hbm), (cr_out, cr_hbm)]
    stores = [pltpu.make_async_copy(src, dst, sem.at[i]) for i, (src, dst) in enumerate(pairs)]
    for store in stores[:4]:
        store.start()
    ft[0:16, :] = f_in[...]
    turned = ft[...].T
    lane = lax.broadcasted_iota(I32, (32, 128), 1)
    done = jnp.zeros((32, 128), F32)
    for q in range(4):
        part = turned[32 * q:32 * q + 32]
        here = (lane >= q * width) & (lane < (q + 1) * width)
        done = jnp.where(here, pltpu.roll(part, q * width, 1) if q else part, done)
    for pz, px, base in (
        (1, 1, 0), (1, 2, 3), (2, 1, 8), (2, 2, 11), (0, 1, 16), (0, 2, 19), (1, 0, 24), (2, 0, 27)):
        k = 9 * pz + 3 * px
        cm_out[k:k + 3, :] = done[base:base + 3, 0:own]
    cm_out[0:2, :] = done[30:32, 0:own]
    cm_out[2:3, :] = done[7:8, 0:own]
    cr_out[...] = done[6:7, 0:own]
    stores[4].start()
    stores[5].start()
    for store in stores:
        store.wait()


def per_device(sizes, basis_init, permeability, accumulation, pressure, source, support, block_of, curve_rank):
    lx, plane = sizes
    gn, hn = 2 ** len(G_BITS), 2 ** len(H_BITS)
    devices = lx * plane
    own = (curve_rank.shape[0] + devices - 1) // devices
    width = (own + 3) // 4
    flat = lambda v: v.reshape(v.shape[:-3] + (128, 128))
    t_rows = -(-curve_rank.shape[0] // 2048) * 16
    anywhere = pl.BlockSpec(memory_space=pl.ANY)
    vmem = pl.BlockSpec(memory_space=pltpu.VMEM)
    dma = pltpu.SemaphoreType.DMA
    cells = lambda *lead: pltpu.VMEM(lead + (128, 128), F32)
    basis, rows = pl.pallas_call(
        functools.partial(kernel, (lx, plane, own, width)),
        out_shape=(
            jax.ShapeDtypeStruct((8, 128, 128), F32),
            jax.ShapeDtypeStruct((16, 128), F32),
        ),
        in_specs=[anywhere] * 8,
        out_specs=(anywhere, vmem),
        scratch_shapes=[
            cells(8), pltpu.VMEM((8, 128, 128), I32), cells(), cells(), cells(),
            pltpu.VMEM((3, 8, 128), I32), pltpu.VMEM(curve_rank.shape, I32), pltpu.VMEM((t_rows, 128), I32),
            cells(9), cells(8), cells(8), cells(8), cells(12),
            pltpu.VMEM((2, 8, 128), F32), cells(10), pltpu.VMEM((4, 8, 128), F32),
            pltpu.VMEM((9, 32, 128), F32), cells(4),
            pltpu.VMEM((2, 5, 16, 128), F32), pltpu.VMEM((2, 5, 16, 128), F32), pltpu.VMEM((2, 5, 8, 128), F32),
            pltpu.VMEM((2, 4, 16, 128), F32), pltpu.VMEM((2, 4, 16, 128), F32), pltpu.VMEM((2, 4, 8, 128), F32),
            pltpu.VMEM((1, 128), I32), pltpu.VMEM((gn, 1, 128), I32),
            pltpu.VMEM((128, 128), I32), pltpu.VMEM((gn * 128, 640), BF16),
            pltpu.VMEM((64, gn * 128), BF16), pltpu.VMEM((4, 128, 128), F32),
            pltpu.VMEM((16, 128), F32), pltpu.VMEM((gn, 16, 128), F32),
            pltpu.VMEM((hn, width, 128), F32), pltpu.VMEM((hn, width, 128), F32),
            pltpu.SemaphoreType.REGULAR, pltpu.SemaphoreType.REGULAR, dma((10,)), dma((1,)), dma((4,)), dma((4,)),
            dma, dma, dma, dma, dma((hn,)), dma((hn,)),
        ],
        compiler_params=pltpu.CompilerParams(
            collective_id=0, has_side_effects=True, vmem_limit_bytes=VMEM_GRANT),
        cost_estimate=pl.CostEstimate(flops=20_000_000, bytes_accessed=2_000_000, transcendentals=0),
    )(*(pltpu.with_memory_space_constraint(v, pltpu.HBM) for v in (
        flat(basis_init), flat(permeability), flat(accumulation), flat(pressure), flat(source),
        flat(support), flat(block_of), curve_rank,
    )))
    basis, matrix, residual = pl.pallas_call(
        functools.partial(finish, own, width),
        out_shape=(
            jax.ShapeDtypeStruct((8, 128, 128), F32),
            jax.ShapeDtypeStruct((27, own), F32),
            jax.ShapeDtypeStruct((1, own), F32),
        ),
        in_specs=[anywhere, vmem],
        out_specs=(anywhere, anywhere, anywhere),
        scratch_shapes=[cells(), pltpu.VMEM((27, own), F32), pltpu.VMEM((1, own), F32), dma((6,))],
        compiler_params=pltpu.CompilerParams(vmem_limit_bytes=VMEM_GRANT),
    )(basis, rows)
    return basis.reshape(basis_init.shape), matrix, residual.reshape(own)


def solution(mesh):
    return jax.shard_map(
        functools.partial(per_device, (mesh.shape["layer"], mesh.shape["plane"])),
        mesh=mesh,
        in_specs=(
            P(None, "layer", "plane", None),
            P("layer", "plane", None),
            P("layer", "plane", None),
            P("layer", "plane", None),
            P("layer", "plane", None),
            P(None, "layer", "plane", None),
            P("layer", "plane", None),
            P(),
        ),
        out_specs=(
            P(None, "layer", "plane", None),
            P(None, ("layer", "plane")),
            P(("layer", "plane")),
        ),
        check_vma=False,
    )
```

```python
import functools

import jax
import jax.numpy as jnp
from jax import lax
from jax.experimental import pallas as pl
from jax.experimental.pallas import tpu as pltpu
from jax.sharding import PartitionSpec as P

MESH = pl.DeviceIdType.MESH
F32, BF16, I32 = jnp.float32, jnp.bfloat16, jnp.int32

G_BITS = (("layer", 1), ("layer", 2), ("plane", 16), ("plane", 32))
H_BITS = (("plane", 1), ("plane", 2), ("plane", 4), ("plane", 8))
VMEM_GRANT = 32 * 1024 * 1024
THIRD, TWO_THIRDS = 1.0 / 3.0, 2.0 / 3.0
B0 = (0, 1, 4, 5)
A0 = (0, 1, 2, 3)
TYM, TYP, TYM1, TYP1, TXM, TXP, TZM, TZP, TZM1, TZP1, TXB, RD = range(12)


def roll_x(v, shift):
    rows = v.shape[0]
    return pltpu.roll(v.reshape(rows // 8, 8, 128), shift, 1).reshape(rows, 128)


def roll_y(v, shift):
    return pltpu.roll(v, shift, 1)


def harmonic(k, n):
    return 2.0 * k * n / (k + n)


def plane_sum(v):
    return v.reshape(-1, 8, 128).sum(axis=0)


def far_first(bits):
    def hops(r):
        reach = {"layer": 0, "y": 0, "z": 0}
        for i, (axis, bit) in enumerate(bits):
            if (r >> i) & 1:
                kind, step = (axis, bit) if axis == "layer" else ("y", bit // 16) if bit >= 16 else ("z", bit // 2)
                reach[kind] += step
        return sum(min(n, size - n) for n, size in ((reach["layer"], 4), (reach["y"], 4), (reach["z"], 8)))

    return sorted(range(1, 2 ** len(bits)), key=lambda r: -hops(r))


def kernel(
    dims,
    bi_hbm, k_hbm, a_hbm, p_hbm, s_hbm, sup_hbm, blk_hbm, cr_hbm,
    v_out, f_out,
    bi, sup, aa, pp, ss, blk, cr1, tab,
    va, vb, sf, nn, tc, tzb, ec, sw, fl, hx, hxs, hxr, hzr, hxs2, hxr2, hzr2,
    rks, rkr, rkt, oh, xb, es, cs, crv, hs, hr,
    round_y, round_z, in_sem, out_sem, halo_s, halo_r, rk_s, rk_r, g_s, g_r, h_s, h_r,
):
    lx, plane, own, width = dims
    gn, hn = 2 ** len(G_BITS), 2 ** len(H_BITS)
    zc = hn // 2
    n_idx = hn * width
    ml, mp = lax.axis_index("layer"), lax.axis_index("plane")

    def flips(bits):
        steps = []
        for axis, bit in bits:
            at = ml if axis == "layer" else mp
            steps.append((axis == "layer", bit * (1 - 2 * ((at // bit) % 2))))
        return steps

    g_flips, h_flips = flips(G_BITS), flips(H_BITS)

    def partner(steps, r):
        to_l, to_p = ml, mp
        for i, (on_layer, step) in enumerate(steps):
            if (r >> i) & 1:
                to_l, to_p = (to_l + step, to_p) if on_layer else (to_l, to_p + step)
        return (to_l, to_p)

    up_x, down_x = (ml, (mp + 1) % plane), (ml, (mp + plane - 1) % plane)
    up_z, down_z = ((ml + 1) % lx, mp), ((ml + lx - 1) % lx, mp)

    def loop(n, body, start=0):
        for i in range(start, n):
            body(i)

    def group(g):
        return slice(g * 32, g * 32 + 32)

    def one_plane(z):
        return slice(z * 8, z * 8 + 8)

    loads = [
        pltpu.make_async_copy(k_hbm, va.at[0], in_sem.at[0]),
        pltpu.make_async_copy(bi_hbm.at[:, pl.ds(0, 64)], bi.at[:, pl.ds(0, 64)], in_sem.at[1]),
        pltpu.make_async_copy(sup_hbm.at[:, pl.ds(0, 64)], sup.at[:, pl.ds(0, 64)], in_sem.at[2]),
        pltpu.make_async_copy(bi_hbm.at[:, pl.ds(64, 64)], bi.at[:, pl.ds(64, 64)], in_sem.at[10]),
        pltpu.make_async_copy(sup_hbm.at[:, pl.ds(64, 64)], sup.at[:, pl.ds(64, 64)], in_sem.at[11]),
        pltpu.make_async_copy(a_hbm, aa, in_sem.at[3]),
        pltpu.make_async_copy(cr_hbm, cr1, in_sem.at[4]),
        pltpu.make_async_copy(p_hbm, pp, in_sem.at[5]),
        pltpu.make_async_copy(s_hbm, ss, in_sem.at[6]),
    ]
    for j, z in enumerate((0, 4, 12)):
        loads.append(pltpu.make_async_copy(blk_hbm.at[pl.ds(8 * z, 8)], blk.at[j], in_sem.at[7 + j]))
    barrier = pltpu.get_barrier_semaphore()

    def greet(who):
        pl.semaphore_signal(barrier, inc=1, device_id=who, device_id_type=MESH)

    def along_z(dz, dc):
        return (ml, mp + dc * (1 - 2 * (mp % 2)) + 2 * ((mp // 2 + dz) % zc - (mp // 2) % zc))

    x_mask = sum(1 << i for i, (axis, _) in enumerate(G_BITS) if axis == "layer")
    x_peers = [r for r in range(1, gn) if r & x_mask == r]
    y_peers = [r for r in range(1, gn) if r & x_mask == 0]
    z_peers = [(dz, dc) for dz in (1, zc - 1, 2, zc - 2) for dc in (0, 1)] + [(0, 1)]
    greet(up_x)
    greet(down_x)
    for r in x_peers:
        greet(partner(g_flips, r))
    for load in loads[:5]:
        load.start()
    for r in y_peers:
        greet(partner(g_flips, r))
    for dz, dc in z_peers:
        greet(along_z(dz, dc))
    for load in loads[5:]:
        load.start()
    greeted = 2 + len(x_peers) + len(y_peers) + len(z_peers)

    def second_round():
        for r in y_peers:
            pl.semaphore_signal(round_y, inc=1, device_id=partner(g_flips, r), device_id_type=MESH)
        for dz in (2, zc - 2):
            pl.semaphore_signal(round_z, inc=1, device_id=along_z(dz, 0), device_id_type=MESH)

    lane = lax.broadcasted_iota(I32, (32, 128), 1)
    m, x = lane % 8, lax.broadcasted_iota(I32, (32, 128), 0) % 8
    m1, x1 = m[:8], x[:8]
    lane1, row1 = lane[:8], x[:8]
    is_m = {i: m == i for i in (0, 3, 4, 7)}
    is_x = {i: x == i for i in (3, 4)}

    hx[...] = jnp.zeros_like(hx)
    tc[TXB] = jnp.zeros((128, 128), F32)

    loads[0].wait()

    def faces(g):
        rows, below = group(g), one_plane((4 * g + 15) % 16)
        k = va[0, rows, :]
        tym = jnp.where(lane == 0, 0.0, harmonic(k, roll_y(k, 1)))
        typ = roll_y(tym, 127)
        tc[TYM, rows, :] = tym
        tc[TYP, rows, :] = typ
        tc[TYM1, rows, :] = jnp.where(is_m[4], 0.0, tym)
        tc[TYP1, rows, :] = jnp.where(is_m[3], 0.0, typ)
        txm = jnp.where(x == 0, 0.0, harmonic(k, roll_x(k, 1)))
        tc[TXM, rows, :] = txm
        tc[TXP, rows, :] = roll_x(txm, 7)
        tz = harmonic(k, jnp.concatenate([va[0, below, :], k[0:24]], axis=0))
        tc[TZM, rows, :] = tz
        tc[TZP, below, :] = tz[0:8]
        tc[TZP, slice(g * 32, g * 32 + 24), :] = tz[8:32]
        tc[TZM1, rows, :] = tz
        tc[TZP1, below, :] = tz[0:8]
        tc[TZP1, slice(g * 32, g * 32 + 24), :] = tz[8:32]

    loop(4, faces)
    nil = jnp.zeros((8, 128), F32)
    tc[TZM, 0:8, :] = nil
    tc[TZP, 120:128, :] = nil
    tc[TZM1, 0:8, :] = nil
    tc[TZP1, 120:128, :] = nil
    tc[TZM1, 64:72, :] = nil
    tc[TZP1, 56:64, :] = nil
    for i, (t, z) in enumerate(((TZP, 3), (TZM, 4), (TZP, 11), (TZM, 12))):
        sw[i] = tc[t, 8 * z:8 * z + 8, :]

    loads[1].wait()
    loads[2].wait()

    def first(g):
        rows = group(g)
        vals = []
        for s in range(8):
            on = sup[s, rows, :].astype(F32)
            sf[s, rows, :] = on
            vals.append(bi[s, rows, :] * on)
        inv = 1.0 / sum(vals[1:], vals[0])
        for s in range(8):
            va[1 + s, rows, :] = vals[s] * inv

    loop(2, first)
    loads[3].wait()
    loads[4].wait()
    loop(4, first, 2)

    def exchange(v, off, xs_buf, xr_buf, zr_buf, base):
        for i, s in enumerate(B0):
            xs_buf[0, off + i] = v[off + s, pl.ds(0, 16, stride=8), :]
            xs_buf[1, off + i] = v[off + s, pl.ds(7, 16, stride=8), :]
        if off:
            xs_buf[0, 0] = v[0, pl.ds(0, 16, stride=8), :]
            xs_buf[1, 0] = v[0, pl.ds(7, 16, stride=8), :]
            pl.semaphore_wait(barrier, greeted)
        last, lead = v.at[pl.ds(0, off + 4), pl.ds(120, 8)], v.at[pl.ds(0, off + 4), pl.ds(0, 8)]
        copies = []
        for j, (src, dst, who) in enumerate((
            (xs_buf.at[1], xr_buf.at[0], up_x), (xs_buf.at[0], xr_buf.at[1], down_x),
            (last, zr_buf.at[0], up_z), (lead, zr_buf.at[1], down_z),
        )):
            copies.append(pltpu.make_async_remote_copy(
                src_ref=src, dst_ref=dst, send_sem=halo_s.at[base + j // 2], recv_sem=halo_r.at[base + j // 2],
                device_id=who, device_id_type=MESH))
        for copy in copies:
            copy.start()
        if off:
            second_round()
        return [pltpu.make_async_remote_copy(
            src_ref=buf, dst_ref=buf, send_sem=halo_s.at[base + j], recv_sem=halo_r.at[base + j],
            device_id=up_x, device_id_type=MESH) for j, buf in enumerate((xr_buf, zr_buf))]

    def inner(v, off):
        def part(g):
            rows = group(g)
            odd = g % 2
            below, above = one_plane((4 * g + 15) % 16), one_plane((4 * g + 4) % 16)
            for s in range(8):
                if s % 4 == 0:
                    vals = [v[off + s + i, rows, :] for i in range(4)]
                    txm, txp = tc[TXM, rows, :], tc[TXP, rows, :]
                    tym, typ = [tc[i, rows, :] for i in (TYM, TYM1)], [tc[i, rows, :] for i in (TYP, TYP1)]
                    zm, zp = tc[TZM1 if s else TZM, rows, :], tc[TZP1 if s else TZP, rows, :]
                here, by_y, by_x, turn = vals[s % 4], vals[s % 4 ^ 1], vals[s % 4 ^ 2], 4 - (s & 4) * 2
                near = tym[s & 1] * roll_y(jnp.where(is_m[7], by_y, here), 1)
                near += typ[s & 1] * roll_y(jnp.where(is_m[0], by_y, here), 127)
                near += txm * roll_x(jnp.where(is_x[3], by_x, here), 1)
                near += txp * roll_x(jnp.where(is_x[4], by_x, here), 7)
                lo, hi = v[off + s + turn * odd, below, :], v[off + s + turn * (1 - odd), above, :]
                near += zm * jnp.concatenate([lo, here[0:24]], axis=0)
                near += zp * jnp.concatenate([here[8:32], hi], axis=0)
                nn[s, rows, :] = near

        loop(4, part)

    def outer(v, off, new, off2, xr_buf, zr_buf, extra):
        for i in range(4):
            hx[i, pl.ds(0, 16, stride=8), :] = xr_buf[0, extra + i]
            hx[i, pl.ds(7, 16, stride=8), :] = xr_buf[1, extra + i]
            nn[i, 0:8, :] += tzb[0] * zr_buf[0, extra + i]
            nn[i, 120:128, :] += tzb[1] * zr_buf[1, extra + i]

        def part(g):
            rows = group(g)
            rd, txb = tc[RD, rows, :], tc[TXB, rows, :]
            vals = []
            for s in range(8):
                near = nn[s, rows, :]
                if s in B0:
                    near += txb * hx[B0.index(s), rows, :]
                vals.append((v[off + s, rows, :] * THIRD + rd * near) * sf[s, rows, :])
            inv = 1.0 / sum(vals[1:], vals[0])
            for s in range(8):
                new[off2 + s, rows, :] = vals[s] * inv

        loop(4, part)

    sent = exchange(va, 1, hxs, hxr, hzr, 0)
    inner(va, 1)

    for load in loads[5:]:
        load.wait()
    label = blk[0, 0:1, :]
    for u, (j, r) in enumerate(((0, 0), (0, 4), (1, 0), (1, 4), (2, 0), (2, 4), (1, 0), (1, 4))):
        label = jnp.where(m1[0:1] == u, blk[j, r:r + 1, :], label)
    t_rows, labels = tab.shape[0], cr1.shape[0]
    tab[labels // 128:, :] = jnp.zeros((t_rows - labels // 128, 128), I32)

    def table(t):
        tab[t:t + 1, :] = cr1[pl.ds(t * 128, 128)].reshape(1, 128)

    loop(labels // 128, table)
    if labels % 128:
        t = labels // 128
        tab[t:t + 1, 0:labels % 128] = cr1[pl.ds(t * 128, labels % 128)].reshape(1, labels % 128)
    l_hi, l_lo = label >> 7, label & 127
    w_iota = lax.broadcasted_iota(I32, (128, 128), 0)
    pick = jnp.where(w_iota == l_lo, 1.0, 0.0).astype(BF16)
    ranks = tab[...]
    parts = jnp.concatenate([(ranks >> 7).astype(F32), (ranks & 127).astype(F32)], axis=0).astype(BF16)
    looked = jnp.dot(parts, pick, preferred_element_type=F32)
    t_iota = lax.broadcasted_iota(I32, (t_rows, 128), 0)
    looked = looked[:t_rows] * 128.0 + looked[t_rows:]
    rank = jnp.sum(jnp.where(t_iota == l_hi, looked, 0.0), axis=0, keepdims=True)
    rank = rank.astype(I32)
    rks[...] = rank
    rkr[0] = rank

    def diagonal(g):
        rows = group(g)
        diag = aa[rows, :]
        for t in (TYM, TYP, TXM, TXP, TZM, TZP):
            diag += tc[t, rows, :]
        tc[RD, rows, :] = diag

    loop(4, diagonal)

    def every(buf, sems):
        return pltpu.make_async_remote_copy(
            src_ref=buf.at[pl.ds(1, gn - 1)], dst_ref=buf.at[pl.ds(1, gn - 1)], send_sem=sems[0], recv_sem=sems[1],
            device_id=partner(g_flips, 1), device_id_type=MESH)

    def rank_copy(r):
        return pltpu.make_async_remote_copy(
            src_ref=rks, dst_ref=rkr.at[r], send_sem=rk_s, recv_sem=rk_r,
            device_id=partner(g_flips, r), device_id_type=MESH)

    pl.semaphore_wait(round_y, len(y_peers))
    loop(gn, lambda r: rank_copy(r).start(), 1)
    for copy in sent:
        copy.wait_recv()

    tc[TXB, pl.ds(0, 16, stride=8), :] = jnp.where(mp > 0, harmonic(hxs[0, 0], hxr[0, 0]), 0.0)
    tc[TXB, pl.ds(7, 16, stride=8), :] = jnp.where(mp < plane - 1, harmonic(hxs[1, 0], hxr[1, 0]), 0.0)
    tzb[0] = jnp.where(ml > 0, harmonic(va[0, 0:8, :], hzr[0, 0]), 0.0)
    tzb[1] = jnp.where(ml < lx - 1, harmonic(va[0, 120:128, :], hzr[1, 0]), 0.0)

    tc[RD, 0:8, :] += tzb[0]
    tc[RD, 120:128, :] += tzb[1]
    tc[RD] = TWO_THIRDS / (tc[RD] + tc[TXB])

    outer(va, 1, vb, 0, hxr, hzr, 1)
    sent2 = exchange(vb, 0, hxs2, hxr2, hzr2, 2)

    es[...] = jnp.zeros_like(es)

    inner(vb, 0)

    def weigh(g):
        rows = group(g)
        tym, typ, txm, txp = (tc[i, rows, :] for i in (TYM, TYP, TXM, TXP))
        sx0 = jnp.where(is_x[3], txp, 0.0) + jnp.where(is_x[4], txm, 0.0)
        sx1 = sx0 + tc[TXB, rows, :]
        sy0 = jnp.where(is_m[7], typ, 0.0) + jnp.where(is_m[0], tym, 0.0)
        sy1 = sy0 + jnp.where(is_m[3], typ, 0.0) + jnp.where(is_m[4], tym, 0.0)
        for s in range(4):
            d = aa[rows, :] + (sx1 if s & 2 else sx0) + (sy1 if s & 1 else sy0)
            ec[s, rows, :] = d
            ec[4 + s, rows, :] = d
        ec[8, rows, :] = sx0
        ec[9, rows, :] = sy0

    loop(4, weigh)
    for i, z in enumerate((3, 4, 11, 12)):
        for s in range(8):
            ec[s, 8 * z:8 * z + 8, :] += sw[i]
    for t, z in ((tzb[0], 0), (tc[TZP, 56:64, :], 7), (tc[TZM, 64:72, :], 8), (tzb[1], 15)):
        for s in range(4, 8):
            ec[s, 8 * z:8 * z + 8, :] += t

    def x_swap(q):
        return roll_x(q, 4)

    def y_swap(q):
        return jnp.where(m1 == 7, roll_y(q, 127), jnp.where(m1 == 0, roll_y(q, 1), 0.0))

    def far(g):
        return one_plane(4 * g + 4 - 5 * (g % 2))

    def rest(g):
        rows = group(g)
        here = pp[rows, :]
        full = plane_sum(ec[0, rows, :] * here - ss[rows, :]) - sw[g] * pp[far(g), :]
        fl[8, one_plane(g), :] = (
            full - x_swap(plane_sum(ec[8, rows, :] * here)) - y_swap(plane_sum(ec[9, rows, :] * here)))

    loop(4, rest)

    for copy in sent2:
        copy.wait_recv()
    for copy in sent:
        copy.wait_send()
    outer(vb, 0, va, 1, hxr2, hzr2, 0)
    store = pltpu.make_async_copy(va.at[pl.ds(1, 8)], v_out, out_sem.at[0])
    store.start()

    def gather(g):
        rows = group(g)
        sx0, sy0 = ec[8, rows, :], ec[9, rows, :]
        vals = [va[1 + s, rows, :] for s in range(8)]
        qx = [x_swap(plane_sum(sx0 * v)) for v in vals]
        qy = [y_swap(plane_sum(sy0 * v)) for v in vals]
        for s in range(8):
            full = plane_sum(ec[s, rows, :] * vals[s]) - sw[g] * va[1 + (s ^ 4), far(g), :]
            fl[s, one_plane(g), :] = full - qx[s ^ 2] - qy[s ^ 1]

    loop(4, gather)

    def z_part(j, pz, s):
        groups = ((0,), (1, 2), (3,))[j] if pz == 1 else {(1, 0): (1,), (2, 0): (3,), (0, 2): (0,), (1, 2): (2,)}[j, pz]
        term = fl[s, one_plane(groups[0]), :]
        for g in groups[1:]:
            term += fl[s, one_plane(g), :]
        return term

    for k, (j, halves) in enumerate(((0, (1, 2)), (1, (1, 2)), (2, (1, 0)), (1, (0,)))):
        for half, pz in enumerate(halves):
            for b in range(2):
                at, s = 64 * half + 24 * b, (0 if pz == 1 else 4) + 2 * b
                side = z_part(j, pz, s + 1)
                es[k, at:at + 8, :] = jnp.where(m1 < 4, side, 0.0)
                es[k, at + 8:at + 16, :] = z_part(j, pz, s)
                es[k, at + 16:at + 24, :] = jnp.where(m1 < 4, 0.0, side)
        if k < 3:
            es[k, 48:56, :] = -z_part(j, 1, 8)

    m16 = m[:16]
    sums = []
    for k in range(4):
        for xi in range(2):
            t = es[k, pl.ds(4 * xi, 16, stride=8), :]
            for i in range(1, 4):
                t += es[k, pl.ds(4 * xi + i, 16, stride=8), :]
            sums.append(t)
    for bit in (4, 2, 1):
        high = (m16 & bit) != 0
        merged = []
        for u in range(bit):
            one, two = sums[u], sums[u + bit]
            move = jnp.where(high, one, two)
            merged.append(jnp.where(high, two, one) + jnp.where(high, roll_y(move, bit), roll_y(move, 128 - bit)))
        sums = merged
    rows_out = sums[0]
    cs[...] = rows_out
    crv[0] = rows_out

    def g_copy(r):
        return pltpu.make_async_remote_copy(
            src_ref=cs, dst_ref=crv.at[r], send_sem=g_s, recv_sem=g_r,
            device_id=partner(g_flips, r), device_id_type=MESH)

    for r in far_first(G_BITS):
        g_copy(r).start()

    def wanted(t):
        q, idx = (t, lane1) if t < 4 else (lane1 >> 5, 128 + (lane1 & 31))
        peer = jnp.zeros_like(idx)
        for p in range(1, hn):
            peer += jnp.where(idx >= p * width, 1, 0)
        col = idx - peer * width + q * width
        dev = jnp.zeros_like(idx) + (ml * plane + mp)
        for b, (on_layer, step) in enumerate(h_flips):
            dev += ((peer >> b) & 1) * (step * plane if on_layer else step)
        return jnp.where((col < own) & (idx < n_idx), dev * own + col, -7)

    wants = [wanted(t) for t in range(5)]
    every(rkr, (rk_s, rk_r)).wait_recv()
    turned = jnp.concatenate([rkr[r] for r in range(gn)] + [jnp.zeros((128 - gn, 128), I32)], axis=0).astype(F32).T
    rkt[...] = turned.astype(I32)
    for r in range(gn):
        have = jnp.broadcast_to(rkt[:, r:r + 1], (128, 128))
        for t in range(5):
            want = jnp.concatenate([wants[t]] * 16, axis=0)
            oh[128 * r:128 * r + 128, 128 * t:128 * t + 128] = jnp.where(have == want, 1.0, 0.0).astype(BF16)

    odd = m1 % 2 == 1
    b1 = (x1 >= 3) & (x1 < 6)
    b1_odd = b1 & odd

    def spread(r):
        got1, got2 = crv[r, 0:8, :], crv[r, 8:16, :]
        pz1 = jnp.where(m1 < 6, got1, 0.0)
        pz2 = jnp.where(m1 < 4, got2, 0.0)
        pz0 = jnp.where(m1 < 4, 0.0, jnp.where(m1 < 6, got2, got1))
        low1, low2, low0 = (jnp.where(b1_odd, v, 0.0) for v in (pz1, pz2, pz0))
        last = pltpu.roll(low1, 5, 0) + low2 + jnp.where(x1 >= 6, pltpu.roll(low0, 3, 0), 0.0)
        vals = jnp.concatenate([
            pz1 - low1 + jnp.where(x1 == 7, pltpu.roll(low0, 2, 0), 0.0), pz2 - low2, pz0 - low0, last], axis=0)
        high = vals.astype(BF16)
        lanes = slice(128 * r, 128 * r + 128)
        xb[0:32, lanes] = high
        xb[32:64, lanes] = (vals - high.astype(F32)).astype(BF16)

    every(crv, (g_s, g_r)).wait_recv()
    loop(gn, spread)
    routed = jnp.dot(xb[...], oh[...], preferred_element_type=F32)
    both = routed[0:32] + routed[32:64]
    parts = [both[:, 128 * q:128 * q + 128] for q in range(4)]
    over = both[:, 512:640]
    packed = jnp.concatenate([
        jnp.concatenate(parts, axis=0).T,
        jnp.concatenate([roll_y(over, (128 - 32 * q) % 128) if q else over for q in range(4)], axis=0).T], axis=0)

    def h_copy(r):
        return pltpu.make_async_remote_copy(
            src_ref=hs.at[r], dst_ref=hr.at[r], send_sem=h_s.at[r], recv_sem=h_r.at[r],
            device_id=partner(h_flips, r), device_id_type=MESH)

    pl.semaphore_wait(round_z, 2)
    for r in far_first(H_BITS):
        hs[r] = packed[r * width:(r + 1) * width]
        h_copy(r).start()
    hs[0] = packed[0:width]
    store.wait()
    for copy in sent2:
        copy.wait_send()
    every(rkr, (rk_s, rk_r)).wait_send()
    every(crv, (g_s, g_r)).wait_send()
    loop(hn, lambda r: h_copy(r).wait_send(), 1)
    loop(hn, lambda r: h_copy(r).wait_recv(), 1)
    final = hs[0]
    for r in range(1, hn):
        final += hr[r]
    f_out[0:width, :] = final


def finish(own, width, v_in, f_in, v_out, cm_hbm, cr_hbm, ft, cm_out, cr_out, sem):
    stores = [pltpu.make_async_copy(src, dst, sem.at[i]) for i, (src, dst) in enumerate((
        (v_in, v_out), (cm_out, cm_hbm), (cr_out, cr_hbm)))]
    stores[0].start()
    ft[0:16, :] = f_in[...]
    turned = ft[...].T
    lane = lax.broadcasted_iota(I32, (32, 128), 1)
    done = jnp.zeros((32, 128), F32)
    for q in range(4):
        part = turned[32 * q:32 * q + 32]
        here = (lane >= q * width) & (lane < (q + 1) * width)
        done = jnp.where(here, pltpu.roll(part, q * width, 1) if q else part, done)
    for pz, px, base in (
        (1, 1, 0), (1, 2, 3), (2, 1, 8), (2, 2, 11), (0, 1, 16), (0, 2, 19), (1, 0, 24), (2, 0, 27)):
        k = 9 * pz + 3 * px
        cm_out[k:k + 3, :] = done[base:base + 3, 0:own]
    cm_out[0:2, :] = done[30:32, 0:own]
    cm_out[2:3, :] = done[7:8, 0:own]
    cr_out[...] = done[6:7, 0:own]
    stores[1].start()
    stores[2].start()
    for store in stores:
        store.wait()


def per_device(sizes, basis_init, permeability, accumulation, pressure, source, support, block_of, curve_rank):
    lx, plane = sizes
    gn, hn = 2 ** len(G_BITS), 2 ** len(H_BITS)
    devices = lx * plane
    own = (curve_rank.shape[0] + devices - 1) // devices
    width = (own + 3) // 4
    flat = lambda v: v.reshape(v.shape[:-3] + (128, 128))
    t_rows = -(-curve_rank.shape[0] // 2048) * 16
    anywhere = pl.BlockSpec(memory_space=pl.ANY)
    vmem = pl.BlockSpec(memory_space=pltpu.VMEM)
    dma = pltpu.SemaphoreType.DMA
    cells = lambda *lead: pltpu.VMEM(lead + (128, 128), F32)
    basis, rows = pl.pallas_call(
        functools.partial(kernel, (lx, plane, own, width)),
        out_shape=(
            jax.ShapeDtypeStruct((8, 128, 128), F32),
            jax.ShapeDtypeStruct((16, 128), F32),
        ),
        in_specs=[anywhere] * 8,
        out_specs=(anywhere, vmem),
        scratch_shapes=[
            cells(8), pltpu.VMEM((8, 128, 128), I32), cells(), cells(), cells(),
            pltpu.VMEM((3, 8, 128), I32), pltpu.VMEM(curve_rank.shape, I32), pltpu.VMEM((t_rows, 128), I32),
            cells(9), cells(8), cells(8), cells(8), cells(12),
            pltpu.VMEM((2, 8, 128), F32), cells(10), pltpu.VMEM((4, 8, 128), F32),
            pltpu.VMEM((9, 32, 128), F32), cells(4),
            pltpu.VMEM((2, 5, 16, 128), F32), pltpu.VMEM((2, 5, 16, 128), F32), pltpu.VMEM((2, 5, 8, 128), F32),
            pltpu.VMEM((2, 4, 16, 128), F32), pltpu.VMEM((2, 4, 16, 128), F32), pltpu.VMEM((2, 4, 8, 128), F32),
            pltpu.VMEM((1, 128), I32), pltpu.VMEM((gn, 1, 128), I32),
            pltpu.VMEM((128, 128), I32), pltpu.VMEM((gn * 128, 640), BF16),
            pltpu.VMEM((64, gn * 128), BF16), pltpu.VMEM((4, 128, 128), F32),
            pltpu.VMEM((16, 128), F32), pltpu.VMEM((gn, 16, 128), F32),
            pltpu.VMEM((hn, width, 128), F32), pltpu.VMEM((hn, width, 128), F32),
            pltpu.SemaphoreType.REGULAR, pltpu.SemaphoreType.REGULAR, dma((12,)), dma((1,)), dma((4,)), dma((4,)),
            dma, dma, dma, dma, dma((hn,)), dma((hn,)),
        ],
        compiler_params=pltpu.CompilerParams(
            collective_id=0, has_side_effects=True, vmem_limit_bytes=VMEM_GRANT),
        cost_estimate=pl.CostEstimate(flops=20_000_000, bytes_accessed=2_000_000, transcendentals=0),
    )(*(pltpu.with_memory_space_constraint(v, pltpu.HBM) for v in (
        flat(basis_init), flat(permeability), flat(accumulation), flat(pressure), flat(source),
        flat(support), flat(block_of), curve_rank,
    )))
    basis, matrix, residual = pl.pallas_call(
        functools.partial(finish, own, width),
        out_shape=(
            jax.ShapeDtypeStruct((8, 128, 128), F32),
            jax.ShapeDtypeStruct((27, own), F32),
            jax.ShapeDtypeStruct((1, own), F32),
        ),
        in_specs=[anywhere, vmem],
        out_specs=(anywhere, anywhere, anywhere),
        scratch_shapes=[cells(), pltpu.VMEM((27, own), F32), pltpu.VMEM((1, own), F32), dma((3,))],
        compiler_params=pltpu.CompilerParams(vmem_limit_bytes=VMEM_GRANT),
    )(basis, rows)
    return basis.reshape(basis_init.shape), matrix, residual.reshape(own)


def solution(mesh):
    return jax.shard_map(
        functools.partial(per_device, (mesh.shape["layer"], mesh.shape["plane"])),
        mesh=mesh,
        in_specs=(
            P(None, "layer", "plane", None),
            P("layer", "plane", None),
            P("layer", "plane", None),
            P("layer", "plane", None),
            P("layer", "plane", None),
            P(None, "layer", "plane", None),
            P("layer", "plane", None),
            P(),
        ),
        out_specs=(
            P(None, "layer", "plane", None),
            P(None, ("layer", "plane")),
            P(("layer", "plane")),
        ),
        check_vma=False,
    )
```

```python
import functools

import jax
import jax.numpy as jnp
from jax import lax
from jax.experimental import pallas as pl
from jax.experimental.pallas import tpu as pltpu
from jax.sharding import PartitionSpec as P

MESH = pl.DeviceIdType.MESH
F32, BF16, I32 = jnp.float32, jnp.bfloat16, jnp.int32

G_BITS = (("layer", 1), ("layer", 2), ("plane", 16), ("plane", 32))
H_BITS = (("plane", 1), ("plane", 2), ("plane", 4), ("plane", 8))
VMEM_GRANT = 32 * 1024 * 1024
THIRD, TWO_THIRDS = 1.0 / 3.0, 2.0 / 3.0
B0 = (0, 1, 4, 5)
A0 = (0, 1, 2, 3)
TYM, TYP, TYM1, TYP1, TXM, TXP, TZM, TZP, TZM1, TZP1, TXB, RD = range(12)


def roll_x(v, shift):
    rows = v.shape[0]
    return pltpu.roll(v.reshape(rows // 8, 8, 128), shift, 1).reshape(rows, 128)


def roll_y(v, shift):
    return pltpu.roll(v, shift, 1)


def harmonic(k, n):
    return 2.0 * k * n / (k + n)


def plane_sum(v):
    return v.reshape(-1, 8, 128).sum(axis=0)


def far_first(bits):
    def hops(r):
        reach = {"layer": 0, "y": 0, "z": 0}
        for i, (axis, bit) in enumerate(bits):
            if (r >> i) & 1:
                kind, step = (axis, bit) if axis == "layer" else ("y", bit // 16) if bit >= 16 else ("z", bit // 2)
                reach[kind] += step
        return sum(min(n, size - n) for n, size in ((reach["layer"], 4), (reach["y"], 4), (reach["z"], 8)))

    return sorted(range(1, 2 ** len(bits)), key=lambda r: -hops(r))


def kernel(
    dims,
    bi_hbm, k_hbm, a_hbm, p_hbm, s_hbm, sup_hbm, blk_hbm, cr_hbm,
    v_out, f_out,
    bi, sup, aa, pp, ss, blk, cr1, tab,
    va, vb, sf, nn, tc, tzb, ec, sw, fl, hx, hxs, hxr, hzr, hxs2, hxr2, hzr2,
    rks, rkr, rkt, oh, xb, es, cs, crv, hs, hr,
    round_y, round_z, in_sem, out_sem, halo_s, halo_r, rk_s, rk_r, g_s, g_r, h_s, h_r,
):
    lx, plane, own, width = dims
    gn, hn = 2 ** len(G_BITS), 2 ** len(H_BITS)
    zc = hn // 2
    n_idx = hn * width
    ml, mp = lax.axis_index("layer"), lax.axis_index("plane")

    def flips(bits):
        steps = []
        for axis, bit in bits:
            at = ml if axis == "layer" else mp
            steps.append((axis == "layer", bit * (1 - 2 * ((at // bit) % 2))))
        return steps

    g_flips, h_flips = flips(G_BITS), flips(H_BITS)

    def partner(steps, r):
        to_l, to_p = ml, mp
        for i, (on_layer, step) in enumerate(steps):
            if (r >> i) & 1:
                to_l, to_p = (to_l + step, to_p) if on_layer else (to_l, to_p + step)
        return (to_l, to_p)

    up_x, down_x = (ml, (mp + 1) % plane), (ml, (mp + plane - 1) % plane)
    up_z, down_z = ((ml + 1) % lx, mp), ((ml + lx - 1) % lx, mp)

    def loop(n, body, start=0):
        for i in range(start, n):
            body(i)

    def group(g):
        return slice(g * 32, g * 32 + 32)

    def one_plane(z):
        return slice(z * 8, z * 8 + 8)

    loads = [
        pltpu.make_async_copy(k_hbm, va.at[0], in_sem.at[0]),
        pltpu.make_async_copy(bi_hbm.at[:, pl.ds(0, 64)], bi.at[:, pl.ds(0, 64)], in_sem.at[1]),
        pltpu.make_async_copy(sup_hbm.at[:, pl.ds(0, 64)], sup.at[:, pl.ds(0, 64)], in_sem.at[2]),
        pltpu.make_async_copy(bi_hbm.at[:, pl.ds(64, 64)], bi.at[:, pl.ds(64, 64)], in_sem.at[10]),
        pltpu.make_async_copy(sup_hbm.at[:, pl.ds(64, 64)], sup.at[:, pl.ds(64, 64)], in_sem.at[11]),
        pltpu.make_async_copy(a_hbm, aa, in_sem.at[3]),
        pltpu.make_async_copy(cr_hbm, cr1, in_sem.at[4]),
        pltpu.make_async_copy(p_hbm, pp, in_sem.at[5]),
        pltpu.make_async_copy(s_hbm, ss, in_sem.at[6]),
    ]
    for j, z in enumerate((0, 4, 12)):
        loads.append(pltpu.make_async_copy(blk_hbm.at[pl.ds(8 * z, 8)], blk.at[j], in_sem.at[7 + j]))
    barrier = pltpu.get_barrier_semaphore()

    def greet(who):
        pl.semaphore_signal(barrier, inc=1, device_id=who, device_id_type=MESH)

    def along_z(dz, dc):
        return (ml, mp + dc * (1 - 2 * (mp % 2)) + 2 * ((mp // 2 + dz) % zc - (mp // 2) % zc))

    x_mask = sum(1 << i for i, (axis, _) in enumerate(G_BITS) if axis == "layer")
    x_peers = [r for r in range(1, gn) if r & x_mask == r]
    y_peers = [r for r in range(1, gn) if r & x_mask == 0]
    z_peers = [(dz, dc) for dz in (1, zc - 1, 2, zc - 2) for dc in (0, 1)] + [(0, 1)]
    greet(up_x)
    greet(down_x)
    for r in x_peers:
        greet(partner(g_flips, r))
    for load in loads[:5]:
        load.start()
    for r in y_peers:
        greet(partner(g_flips, r))
    for dz, dc in z_peers:
        greet(along_z(dz, dc))
    for load in loads[5:]:
        load.start()
    greeted = 2 + len(x_peers) + len(y_peers) + len(z_peers)

    def second_round():
        for r in y_peers:
            pl.semaphore_signal(round_y, inc=1, device_id=partner(g_flips, r), device_id_type=MESH)
        for dz in (2, zc - 2):
            pl.semaphore_signal(round_z, inc=1, device_id=along_z(dz, 0), device_id_type=MESH)

    lane = lax.broadcasted_iota(I32, (32, 128), 1)
    m, x = lane % 8, lax.broadcasted_iota(I32, (32, 128), 0) % 8
    m1, x1 = m[:8], x[:8]
    lane1, row1 = lane[:8], x[:8]
    is_m = {i: m == i for i in (0, 3, 4, 7)}
    is_x = {i: x == i for i in (3, 4)}

    hx[...] = jnp.zeros_like(hx)
    tc[TXB] = jnp.zeros((128, 128), F32)

    loads[0].wait()

    def faces(g):
        rows, below = group(g), one_plane((4 * g + 15) % 16)
        k = va[0, rows, :]
        tym = jnp.where(lane == 0, 0.0, harmonic(k, roll_y(k, 1)))
        typ = roll_y(tym, 127)
        tc[TYM, rows, :] = tym
        tc[TYP, rows, :] = typ
        tc[TYM1, rows, :] = jnp.where(is_m[4], 0.0, tym)
        tc[TYP1, rows, :] = jnp.where(is_m[3], 0.0, typ)
        txm = jnp.where(x == 0, 0.0, harmonic(k, roll_x(k, 1)))
        tc[TXM, rows, :] = txm
        tc[TXP, rows, :] = roll_x(txm, 7)
        tz = harmonic(k, jnp.concatenate([va[0, below, :], k[0:24]], axis=0))
        tc[TZM, rows, :] = tz
        tc[TZP, below, :] = tz[0:8]
        tc[TZP, slice(g * 32, g * 32 + 24), :] = tz[8:32]
        tc[TZM1, rows, :] = tz
        tc[TZP1, below, :] = tz[0:8]
        tc[TZP1, slice(g * 32, g * 32 + 24), :] = tz[8:32]

    loop(4, faces)
    nil = jnp.zeros((8, 128), F32)
    tc[TZM, 0:8, :] = nil
    tc[TZP, 120:128, :] = nil
    tc[TZM1, 0:8, :] = nil
    tc[TZP1, 120:128, :] = nil
    tc[TZM1, 64:72, :] = nil
    tc[TZP1, 56:64, :] = nil
    for i, (t, z) in enumerate(((TZP, 3), (TZM, 4), (TZP, 11), (TZM, 12))):
        sw[i] = tc[t, 8 * z:8 * z + 8, :]

    loads[1].wait()
    loads[2].wait()

    def first(g):
        rows = group(g)
        vals = []
        for s in range(8):
            on = sup[s, rows, :].astype(F32)
            sf[s, rows, :] = on
            vals.append(bi[s, rows, :] * on)
        inv = 1.0 / sum(vals[1:], vals[0])
        for s in range(8):
            va[1 + s, rows, :] = vals[s] * inv

    loop(2, first)
    loads[3].wait()
    loads[4].wait()
    loop(4, first, 2)

    def exchange(v, off, xs_buf, xr_buf, zr_buf, base):
        for i, s in enumerate(B0):
            xs_buf[0, off + i] = v[off + s, pl.ds(0, 16, stride=8), :]
            xs_buf[1, off + i] = v[off + s, pl.ds(7, 16, stride=8), :]
        if off:
            xs_buf[0, 0] = v[0, pl.ds(0, 16, stride=8), :]
            xs_buf[1, 0] = v[0, pl.ds(7, 16, stride=8), :]
            pl.semaphore_wait(barrier, greeted)
        last, lead = v.at[pl.ds(0, off + 4), pl.ds(120, 8)], v.at[pl.ds(0, off + 4), pl.ds(0, 8)]
        copies = []
        for j, (src, dst, who) in enumerate((
            (xs_buf.at[1], xr_buf.at[0], up_x), (xs_buf.at[0], xr_buf.at[1], down_x),
            (last, zr_buf.at[0], up_z), (lead, zr_buf.at[1], down_z),
        )):
            copies.append(pltpu.make_async_remote_copy(
                src_ref=src, dst_ref=dst, send_sem=halo_s.at[base + j // 2], recv_sem=halo_r.at[base + j // 2],
                device_id=who, device_id_type=MESH))
        for copy in copies:
            copy.start()
        if off:
            second_round()
        return [pltpu.make_async_remote_copy(
            src_ref=buf, dst_ref=buf, send_sem=halo_s.at[base + j], recv_sem=halo_r.at[base + j],
            device_id=up_x, device_id_type=MESH) for j, buf in enumerate((xr_buf, zr_buf))]

    def inner(v, off):
        def part(g):
            rows = group(g)
            odd = g % 2
            below, above = one_plane((4 * g + 15) % 16), one_plane((4 * g + 4) % 16)
            for s in range(8):
                if s % 4 == 0:
                    vals = [v[off + s + i, rows, :] for i in range(4)]
                    txm, txp = tc[TXM, rows, :], tc[TXP, rows, :]
                    tym, typ = [tc[i, rows, :] for i in (TYM, TYM1)], [tc[i, rows, :] for i in (TYP, TYP1)]
                    zm, zp = tc[TZM1 if s else TZM, rows, :], tc[TZP1 if s else TZP, rows, :]
                here, by_y, by_x, turn = vals[s % 4], vals[s % 4 ^ 1], vals[s % 4 ^ 2], 4 - (s & 4) * 2
                near = tym[s & 1] * roll_y(jnp.where(is_m[7], by_y, here), 1)
                near += typ[s & 1] * roll_y(jnp.where(is_m[0], by_y, here), 127)
                near += txm * roll_x(jnp.where(is_x[3], by_x, here), 1)
                near += txp * roll_x(jnp.where(is_x[4], by_x, here), 7)
                lo, hi = v[off + s + turn * odd, below, :], v[off + s + turn * (1 - odd), above, :]
                near += zm * jnp.concatenate([lo, here[0:24]], axis=0)
                near += zp * jnp.concatenate([here[8:32], hi], axis=0)
                nn[s, rows, :] = near

        loop(4, part)

    def outer(v, off, new, off2, xr_buf, zr_buf, extra):
        for i in range(4):
            hx[i, pl.ds(0, 16, stride=8), :] = xr_buf[0, extra + i]
            hx[i, pl.ds(7, 16, stride=8), :] = xr_buf[1, extra + i]
            nn[i, 0:8, :] += tzb[0] * zr_buf[0, extra + i]
            nn[i, 120:128, :] += tzb[1] * zr_buf[1, extra + i]

        def part(g):
            rows = group(g)
            rd, txb = tc[RD, rows, :], tc[TXB, rows, :]
            vals = []
            for s in range(8):
                near = nn[s, rows, :]
                if s in B0:
                    near += txb * hx[B0.index(s), rows, :]
                vals.append((v[off + s, rows, :] * THIRD + rd * near) * sf[s, rows, :])
            inv = 1.0 / sum(vals[1:], vals[0])
            for s in range(8):
                new[off2 + s, rows, :] = vals[s] * inv

        loop(4, part)

    sent = exchange(va, 1, hxs, hxr, hzr, 0)
    inner(va, 1)

    for load in loads[5:]:
        load.wait()
    label = blk[0, 0:1, :]
    for u, (j, r) in enumerate(((0, 0), (0, 4), (1, 0), (1, 4), (2, 0), (2, 4), (1, 0), (1, 4))):
        label = jnp.where(m1[0:1] == u, blk[j, r:r + 1, :], label)
    t_rows, labels = tab.shape[0], cr1.shape[0]
    tab[labels // 128:, :] = jnp.zeros((t_rows - labels // 128, 128), I32)

    def table(t):
        tab[t:t + 1, :] = cr1[pl.ds(t * 128, 128)].reshape(1, 128)

    loop(labels // 128, table)
    if labels % 128:
        t = labels // 128
        tab[t:t + 1, 0:labels % 128] = cr1[pl.ds(t * 128, labels % 128)].reshape(1, labels % 128)
    l_hi, l_lo = label >> 7, label & 127
    w_iota = lax.broadcasted_iota(I32, (128, 128), 0)
    pick = jnp.where(w_iota == l_lo, 1.0, 0.0).astype(BF16)
    ranks = tab[...]
    parts = jnp.concatenate([(ranks >> 7).astype(F32), (ranks & 127).astype(F32)], axis=0).astype(BF16)
    looked = jnp.dot(parts, pick, preferred_element_type=F32)
    t_iota = lax.broadcasted_iota(I32, (t_rows, 128), 0)
    looked = looked[:t_rows] * 128.0 + looked[t_rows:]
    rank = jnp.sum(jnp.where(t_iota == l_hi, looked, 0.0), axis=0, keepdims=True)
    rank = rank.astype(I32)
    rks[...] = rank
    rkr[0] = rank

    def diagonal(g):
        rows = group(g)
        diag = aa[rows, :]
        for t in (TYM, TYP, TXM, TXP, TZM, TZP):
            diag += tc[t, rows, :]
        tc[RD, rows, :] = diag

    loop(4, diagonal)

    def every(buf, sems):
        return pltpu.make_async_remote_copy(
            src_ref=buf.at[pl.ds(1, gn - 1)], dst_ref=buf.at[pl.ds(1, gn - 1)], send_sem=sems[0], recv_sem=sems[1],
            device_id=partner(g_flips, 1), device_id_type=MESH)

    def rank_copy(r):
        return pltpu.make_async_remote_copy(
            src_ref=rks, dst_ref=rkr.at[r], send_sem=rk_s, recv_sem=rk_r,
            device_id=partner(g_flips, r), device_id_type=MESH)

    pl.semaphore_wait(round_y, len(y_peers))
    loop(gn, lambda r: rank_copy(r).start(), 1)
    for copy in sent:
        copy.wait_recv()

    tc[TXB, pl.ds(0, 16, stride=8), :] = jnp.where(mp > 0, harmonic(hxs[0, 0], hxr[0, 0]), 0.0)
    tc[TXB, pl.ds(7, 16, stride=8), :] = jnp.where(mp < plane - 1, harmonic(hxs[1, 0], hxr[1, 0]), 0.0)
    tzb[0] = jnp.where(ml > 0, harmonic(va[0, 0:8, :], hzr[0, 0]), 0.0)
    tzb[1] = jnp.where(ml < lx - 1, harmonic(va[0, 120:128, :], hzr[1, 0]), 0.0)

    tc[RD, 0:8, :] += tzb[0]
    tc[RD, 120:128, :] += tzb[1]
    tc[RD] = TWO_THIRDS / (tc[RD] + tc[TXB])

    outer(va, 1, vb, 0, hxr, hzr, 1)
    sent2 = exchange(vb, 0, hxs2, hxr2, hzr2, 2)

    es[...] = jnp.zeros_like(es)

    inner(vb, 0)

    def weigh(g):
        rows = group(g)
        tym, typ, txm, txp = (tc[i, rows, :] for i in (TYM, TYP, TXM, TXP))
        sx0 = jnp.where(is_x[3], txp, 0.0) + jnp.where(is_x[4], txm, 0.0)
        sx1 = sx0 + tc[TXB, rows, :]
        sy0 = jnp.where(is_m[7], typ, 0.0) + jnp.where(is_m[0], tym, 0.0)
        sy1 = sy0 + jnp.where(is_m[3], typ, 0.0) + jnp.where(is_m[4], tym, 0.0)
        for s in range(4):
            d = aa[rows, :] + (sx1 if s & 2 else sx0) + (sy1 if s & 1 else sy0)
            ec[s, rows, :] = d
            ec[4 + s, rows, :] = d
        ec[8, rows, :] = sx0
        ec[9, rows, :] = sy0

    loop(4, weigh)
    for i, z in enumerate((3, 4, 11, 12)):
        for s in range(8):
            ec[s, 8 * z:8 * z + 8, :] += sw[i]
    for t, z in ((tzb[0], 0), (tc[TZP, 56:64, :], 7), (tc[TZM, 64:72, :], 8), (tzb[1], 15)):
        for s in range(4, 8):
            ec[s, 8 * z:8 * z + 8, :] += t

    def x_swap(q):
        return roll_x(q, 4)

    def y_swap(q):
        return jnp.where(m1 == 7, roll_y(q, 127), jnp.where(m1 == 0, roll_y(q, 1), 0.0))

    def far(g):
        return one_plane(4 * g + 4 - 5 * (g % 2))

    def rest(g):
        rows = group(g)
        here = pp[rows, :]
        full = plane_sum(ec[0, rows, :] * here - ss[rows, :]) - sw[g] * pp[far(g), :]
        fl[8, one_plane(g), :] = (
            full - x_swap(plane_sum(ec[8, rows, :] * here)) - y_swap(plane_sum(ec[9, rows, :] * here)))

    loop(4, rest)

    for copy in sent2:
        copy.wait_recv()
    for copy in sent:
        copy.wait_send()
    outer(vb, 0, va, 1, hxr2, hzr2, 0)
    store = pltpu.make_async_copy(va.at[pl.ds(1, 8)], v_out, out_sem.at[0])
    store.start()

    def gather(g):
        rows = group(g)
        sx0, sy0 = ec[8, rows, :], ec[9, rows, :]
        vals = [va[1 + s, rows, :] for s in range(8)]
        qx = [x_swap(plane_sum(sx0 * v)) for v in vals]
        qy = [y_swap(plane_sum(sy0 * v)) for v in vals]
        for s in range(8):
            full = plane_sum(ec[s, rows, :] * vals[s]) - sw[g] * va[1 + (s ^ 4), far(g), :]
            fl[s, one_plane(g), :] = full - qx[s ^ 2] - qy[s ^ 1]

    loop(4, gather)

    def z_part(j, pz, s):
        groups = ((0,), (1, 2), (3,))[j] if pz == 1 else {(1, 0): (1,), (2, 0): (3,), (0, 2): (0,), (1, 2): (2,)}[j, pz]
        term = fl[s, one_plane(groups[0]), :]
        for g in groups[1:]:
            term += fl[s, one_plane(g), :]
        return term

    for k, (j, halves) in enumerate(((0, (1, 2)), (1, (1, 2)), (2, (1, 0)), (1, (0,)))):
        for half, pz in enumerate(halves):
            for b in range(2):
                at, s = 64 * half + 24 * b, (0 if pz == 1 else 4) + 2 * b
                side = z_part(j, pz, s + 1)
                es[k, at:at + 8, :] = jnp.where(m1 < 4, side, 0.0)
                es[k, at + 8:at + 16, :] = z_part(j, pz, s)
                es[k, at + 16:at + 24, :] = jnp.where(m1 < 4, 0.0, side)
        if k < 3:
            es[k, 48:56, :] = -z_part(j, 1, 8)

    m16 = m[:16]
    sums = []
    for k in range(4):
        for xi in range(2):
            t = es[k, pl.ds(4 * xi, 16, stride=8), :]
            for i in range(1, 4):
                t += es[k, pl.ds(4 * xi + i, 16, stride=8), :]
            sums.append(t)
    for bit in (4, 2, 1):
        high = (m16 & bit) != 0
        merged = []
        for u in range(bit):
            one, two = sums[u], sums[u + bit]
            move = jnp.where(high, one, two)
            merged.append(jnp.where(high, two, one) + jnp.where(high, roll_y(move, bit), roll_y(move, 128 - bit)))
        sums = merged
    rows_out = sums[0]
    second = pltpu.roll(rows_out[8:16], 7, 0)
    for buf in (cs, crv.at[0]):
        buf[0:8, :] = jnp.where(x1 == 7, second, rows_out[0:8])
        buf[8:13, :] = second[0:5]

    def g_copy(r):
        return pltpu.make_async_remote_copy(
            src_ref=cs, dst_ref=crv.at[r], send_sem=g_s, recv_sem=g_r,
            device_id=partner(g_flips, r), device_id_type=MESH)

    for r in far_first(G_BITS):
        g_copy(r).start()

    def wanted(t):
        q, idx = (t, lane1) if t < 4 else (lane1 >> 5, 128 + (lane1 & 31))
        peer = jnp.zeros_like(idx)
        for p in range(1, hn):
            peer += jnp.where(idx >= p * width, 1, 0)
        col = idx - peer * width + q * width
        dev = jnp.zeros_like(idx) + (ml * plane + mp)
        for b, (on_layer, step) in enumerate(h_flips):
            dev += ((peer >> b) & 1) * (step * plane if on_layer else step)
        return jnp.where((col < own) & (idx < n_idx), dev * own + col, -7)

    wants = [wanted(t) for t in range(5)]
    every(rkr, (rk_s, rk_r)).wait_recv()
    turned = jnp.concatenate([rkr[r] for r in range(gn)] + [jnp.zeros((128 - gn, 128), I32)], axis=0).astype(F32).T
    rkt[...] = turned.astype(I32)
    for r in range(gn):
        have = jnp.broadcast_to(rkt[:, r:r + 1], (128, 128))
        for t in range(5):
            want = jnp.concatenate([wants[t]] * 16, axis=0)
            oh[128 * r:128 * r + 128, 128 * t:128 * t + 128] = jnp.where(have == want, 1.0, 0.0).astype(BF16)

    odd = m1 % 2 == 1
    b1 = (x1 >= 3) & (x1 < 6)
    b1_odd = b1 & odd

    def spread(r):
        got1, got2 = crv[r, 0:8, :], pltpu.roll(crv[r, 5:13, :], 6, 0)
        pz1 = jnp.where((m1 < 6) & (x1 < 7), got1, 0.0)
        pz2 = jnp.where(m1 < 4, got2, 0.0)
        pz0 = jnp.where(m1 < 4, 0.0, jnp.where(m1 < 6, got2, got1))
        low1, low2, low0 = (jnp.where(b1_odd, v, 0.0) for v in (pz1, pz2, pz0))
        last = pltpu.roll(low1, 5, 0) + low2 + jnp.where(x1 >= 6, pltpu.roll(low0, 3, 0), 0.0)
        vals = jnp.concatenate([
            pz1 - low1 + jnp.where(x1 == 7, pltpu.roll(low0, 2, 0), 0.0), pz2 - low2, pz0 - low0, last], axis=0)
        high = vals.astype(BF16)
        lanes = slice(128 * r, 128 * r + 128)
        xb[0:32, lanes] = high
        xb[32:64, lanes] = (vals - high.astype(F32)).astype(BF16)

    every(crv, (g_s, g_r)).wait_recv()
    loop(gn, spread)
    routed = jnp.dot(xb[...], oh[...], preferred_element_type=F32)
    both = routed[0:32] + routed[32:64]
    parts = [both[:, 128 * q:128 * q + 128] for q in range(4)]
    over = both[:, 512:640]
    packed = jnp.concatenate([
        jnp.concatenate(parts, axis=0).T,
        jnp.concatenate([roll_y(over, (128 - 32 * q) % 128) if q else over for q in range(4)], axis=0).T], axis=0)

    def h_copy(r):
        return pltpu.make_async_remote_copy(
            src_ref=hs.at[r], dst_ref=hr.at[r], send_sem=h_s.at[r], recv_sem=h_r.at[r],
            device_id=partner(h_flips, r), device_id_type=MESH)

    pl.semaphore_wait(round_z, 2)
    for r in far_first(H_BITS):
        hs[r] = packed[r * width:(r + 1) * width]
        h_copy(r).start()
    hs[0] = packed[0:width]
    store.wait()
    for copy in sent2:
        copy.wait_send()
    every(rkr, (rk_s, rk_r)).wait_send()
    every(crv, (g_s, g_r)).wait_send()
    loop(hn, lambda r: h_copy(r).wait_send(), 1)
    loop(hn, lambda r: h_copy(r).wait_recv(), 1)
    final = hs[0]
    for r in range(1, hn):
        final += hr[r]
    f_out[0:width, :] = final


def finish(own, width, v_in, f_in, v_out, cm_hbm, cr_hbm, ft, cm_out, cr_out, sem):
    stores = [pltpu.make_async_copy(src, dst, sem.at[i]) for i, (src, dst) in enumerate((
        (v_in, v_out), (cm_out, cm_hbm), (cr_out, cr_hbm)))]
    stores[0].start()
    ft[0:16, :] = f_in[...]
    turned = ft[...].T
    lane = lax.broadcasted_iota(I32, (32, 128), 1)
    done = jnp.zeros((32, 128), F32)
    for q in range(4):
        part = turned[32 * q:32 * q + 32]
        here = (lane >= q * width) & (lane < (q + 1) * width)
        done = jnp.where(here, pltpu.roll(part, q * width, 1) if q else part, done)
    for pz, px, base in (
        (1, 1, 0), (1, 2, 3), (2, 1, 8), (2, 2, 11), (0, 1, 16), (0, 2, 19), (1, 0, 24), (2, 0, 27)):
        k = 9 * pz + 3 * px
        cm_out[k:k + 3, :] = done[base:base + 3, 0:own]
    cm_out[0:2, :] = done[30:32, 0:own]
    cm_out[2:3, :] = done[7:8, 0:own]
    cr_out[...] = done[6:7, 0:own]
    stores[1].start()
    stores[2].start()
    for store in stores:
        store.wait()


def per_device(sizes, basis_init, permeability, accumulation, pressure, source, support, block_of, curve_rank):
    lx, plane = sizes
    gn, hn = 2 ** len(G_BITS), 2 ** len(H_BITS)
    devices = lx * plane
    own = (curve_rank.shape[0] + devices - 1) // devices
    width = (own + 3) // 4
    flat = lambda v: v.reshape(v.shape[:-3] + (128, 128))
    t_rows = -(-curve_rank.shape[0] // 2048) * 16
    anywhere = pl.BlockSpec(memory_space=pl.ANY)
    vmem = pl.BlockSpec(memory_space=pltpu.VMEM)
    dma = pltpu.SemaphoreType.DMA
    cells = lambda *lead: pltpu.VMEM(lead + (128, 128), F32)
    basis, rows = pl.pallas_call(
        functools.partial(kernel, (lx, plane, own, width)),
        out_shape=(
            jax.ShapeDtypeStruct((8, 128, 128), F32),
            jax.ShapeDtypeStruct((16, 128), F32),
        ),
        in_specs=[anywhere] * 8,
        out_specs=(anywhere, vmem),
        scratch_shapes=[
            cells(8), pltpu.VMEM((8, 128, 128), I32), cells(), cells(), cells(),
            pltpu.VMEM((3, 8, 128), I32), pltpu.VMEM(curve_rank.shape, I32), pltpu.VMEM((t_rows, 128), I32),
            cells(9), cells(8), cells(8), cells(8), cells(12),
            pltpu.VMEM((2, 8, 128), F32), cells(10), pltpu.VMEM((4, 8, 128), F32),
            pltpu.VMEM((9, 32, 128), F32), cells(4),
            pltpu.VMEM((2, 5, 16, 128), F32), pltpu.VMEM((2, 5, 16, 128), F32), pltpu.VMEM((2, 5, 8, 128), F32),
            pltpu.VMEM((2, 4, 16, 128), F32), pltpu.VMEM((2, 4, 16, 128), F32), pltpu.VMEM((2, 4, 8, 128), F32),
            pltpu.VMEM((1, 128), I32), pltpu.VMEM((gn, 1, 128), I32),
            pltpu.VMEM((128, 128), I32), pltpu.VMEM((gn * 128, 640), BF16),
            pltpu.VMEM((64, gn * 128), BF16), pltpu.VMEM((4, 128, 128), F32),
            pltpu.VMEM((13, 128), F32), pltpu.VMEM((gn, 13, 128), F32),
            pltpu.VMEM((hn, width, 128), F32), pltpu.VMEM((hn, width, 128), F32),
            pltpu.SemaphoreType.REGULAR, pltpu.SemaphoreType.REGULAR, dma((12,)), dma((1,)), dma((4,)), dma((4,)),
            dma, dma, dma, dma, dma((hn,)), dma((hn,)),
        ],
        compiler_params=pltpu.CompilerParams(
            collective_id=0, has_side_effects=True, vmem_limit_bytes=VMEM_GRANT),
        cost_estimate=pl.CostEstimate(flops=20_000_000, bytes_accessed=2_000_000, transcendentals=0),
    )(*(pltpu.with_memory_space_constraint(v, pltpu.HBM) for v in (
        flat(basis_init), flat(permeability), flat(accumulation), flat(pressure), flat(source),
        flat(support), flat(block_of), curve_rank,
    )))
    basis, matrix, residual = pl.pallas_call(
        functools.partial(finish, own, width),
        out_shape=(
            jax.ShapeDtypeStruct((8, 128, 128), F32),
            jax.ShapeDtypeStruct((27, own), F32),
            jax.ShapeDtypeStruct((1, own), F32),
        ),
        in_specs=[anywhere, vmem],
        out_specs=(anywhere, anywhere, anywhere),
        scratch_shapes=[cells(), pltpu.VMEM((27, own), F32), pltpu.VMEM((1, own), F32), dma((3,))],
        compiler_params=pltpu.CompilerParams(vmem_limit_bytes=VMEM_GRANT),
    )(basis, rows)
    return basis.reshape(basis_init.shape), matrix, residual.reshape(own)


def solution(mesh):
    return jax.shard_map(
        functools.partial(per_device, (mesh.shape["layer"], mesh.shape["plane"])),
        mesh=mesh,
        in_specs=(
            P(None, "layer", "plane", None),
            P("layer", "plane", None),
            P("layer", "plane", None),
            P("layer", "plane", None),
            P("layer", "plane", None),
            P(None, "layer", "plane", None),
            P("layer", "plane", None),
            P(),
        ),
        out_specs=(
            P(None, "layer", "plane", None),
            P(None, ("layer", "plane")),
            P(("layer", "plane")),
        ),
        check_vma=False,
    )
```

```python
import functools

import jax
import jax.numpy as jnp
from jax import lax
from jax.experimental import pallas as pl
from jax.experimental.pallas import tpu as pltpu
from jax.sharding import PartitionSpec as P

MESH = pl.DeviceIdType.MESH
F32, BF16, I32 = jnp.float32, jnp.bfloat16, jnp.int32

G_BITS = (("layer", 1), ("layer", 2), ("plane", 16), ("plane", 32))
H_BITS = (("plane", 1), ("plane", 2), ("plane", 4), ("plane", 8))
VMEM_GRANT = 32 * 1024 * 1024
THIRD, TWO_THIRDS = 1.0 / 3.0, 2.0 / 3.0
B0 = (0, 1, 4, 5)
A0 = (0, 1, 2, 3)
TYM, TYP, TYM1, TYP1, TXM, TXP, TZM, TZP, TZM1, TZP1, TXB, RD = range(12)


def roll_x(v, shift):
    rows = v.shape[0]
    return pltpu.roll(v.reshape(rows // 8, 8, 128), shift, 1).reshape(rows, 128)


def roll_y(v, shift):
    return pltpu.roll(v, shift, 1)


def harmonic(k, n):
    return 2.0 * k * n / (k + n)


def plane_sum(v):
    return v.reshape(-1, 8, 128).sum(axis=0)


def far_first(bits):
    def hops(r):
        reach = {"layer": 0, "y": 0, "z": 0}
        for i, (axis, bit) in enumerate(bits):
            if (r >> i) & 1:
                kind, step = (axis, bit) if axis == "layer" else ("y", bit // 16) if bit >= 16 else ("z", bit // 2)
                reach[kind] += step
        return sum(min(n, size - n) for n, size in ((reach["layer"], 4), (reach["y"], 4), (reach["z"], 8)))

    return sorted(range(1, 2 ** len(bits)), key=lambda r: -hops(r))


def kernel(
    dims,
    bi_hbm, k_hbm, a_hbm, p_hbm, s_hbm, sup_hbm, blk_hbm, cr_hbm,
    v_out, f_out,
    bi, sup, aa, pp, ss, blk, cr1, tab,
    va, vb, sf, nn, tc, tzb, ec, sw, fl, hx, hxs, hxr, hzr, hxs2, hxr2, hzr2,
    rks, rkr, oh, xb, es, cs, crv, hs, hr,
    round_y, round_z, in_sem, out_sem, halo_s, halo_r, rk_s, rk_r, g_s, g_r, h_s, h_r,
):
    lx, plane, own, width = dims
    gn, hn = 2 ** len(G_BITS), 2 ** len(H_BITS)
    zc = hn // 2
    n_idx = hn * width
    ml, mp = lax.axis_index("layer"), lax.axis_index("plane")

    def flips(bits):
        steps = []
        for axis, bit in bits:
            at = ml if axis == "layer" else mp
            steps.append((axis == "layer", bit * (1 - 2 * ((at // bit) % 2))))
        return steps

    g_flips, h_flips = flips(G_BITS), flips(H_BITS)

    def partner(steps, r):
        to_l, to_p = ml, mp
        for i, (on_layer, step) in enumerate(steps):
            if (r >> i) & 1:
                to_l, to_p = (to_l + step, to_p) if on_layer else (to_l, to_p + step)
        return (to_l, to_p)

    up_x, down_x = (ml, (mp + 1) % plane), (ml, (mp + plane - 1) % plane)
    up_z, down_z = ((ml + 1) % lx, mp), ((ml + lx - 1) % lx, mp)

    def loop(n, body, start=0):
        for i in range(start, n):
            body(i)

    def steps(n, body, start=0):
        def step(i, carry):
            body(i)
            return carry

        lax.fori_loop(start, n, step, 0)

    def group(g, size=32):
        return pl.ds(pl.multiple_of(g * 32, 32), size)

    def one_plane(z):
        return pl.ds(z * 8 if isinstance(z, int) else pl.multiple_of(z * 8, 8), 8)

    loads = [
        pltpu.make_async_copy(k_hbm, va.at[0], in_sem.at[0]),
        pltpu.make_async_copy(bi_hbm.at[:, pl.ds(0, 64)], bi.at[:, pl.ds(0, 64)], in_sem.at[1]),
        pltpu.make_async_copy(sup_hbm.at[:, pl.ds(0, 64)], sup.at[:, pl.ds(0, 64)], in_sem.at[2]),
        pltpu.make_async_copy(bi_hbm.at[:, pl.ds(64, 64)], bi.at[:, pl.ds(64, 64)], in_sem.at[10]),
        pltpu.make_async_copy(sup_hbm.at[:, pl.ds(64, 64)], sup.at[:, pl.ds(64, 64)], in_sem.at[11]),
        pltpu.make_async_copy(a_hbm, aa, in_sem.at[3]),
        pltpu.make_async_copy(cr_hbm, cr1, in_sem.at[4]),
        pltpu.make_async_copy(p_hbm, pp, in_sem.at[5]),
        pltpu.make_async_copy(s_hbm, ss, in_sem.at[6]),
    ]
    for j, z in enumerate((0, 4, 12)):
        loads.append(pltpu.make_async_copy(blk_hbm.at[pl.ds(8 * z, 8)], blk.at[j], in_sem.at[7 + j]))
    barrier = pltpu.get_barrier_semaphore()

    def greet(who):
        pl.semaphore_signal(barrier, inc=1, device_id=who, device_id_type=MESH)

    def along_z(dz, dc):
        return (ml, mp + dc * (1 - 2 * (mp % 2)) + 2 * ((mp // 2 + dz) % zc - (mp // 2) % zc))

    x_mask = sum(1 << i for i, (axis, _) in enumerate(G_BITS) if axis == "layer")
    x_peers = [r for r in range(1, gn) if r & x_mask == r]
    y_peers = [r for r in range(1, gn) if r & x_mask == 0]
    z_peers = [(dz, dc) for dz in (1, zc - 1, 2, zc - 2) for dc in (0, 1)] + [(0, 1)]
    greet(up_x)
    greet(down_x)
    for r in x_peers:
        greet(partner(g_flips, r))
    for load in loads[:5]:
        load.start()
    for r in y_peers:
        greet(partner(g_flips, r))
    for dz, dc in z_peers:
        greet(along_z(dz, dc))
    for load in loads[5:]:
        load.start()
    greeted = 2 + len(x_peers) + len(y_peers) + len(z_peers)

    def second_round():
        for r in y_peers:
            pl.semaphore_signal(round_y, inc=1, device_id=partner(g_flips, r), device_id_type=MESH)
        for dz in (2, zc - 2):
            pl.semaphore_signal(round_z, inc=1, device_id=along_z(dz, 0), device_id_type=MESH)

    lane = lax.broadcasted_iota(I32, (32, 128), 1)
    m, x = lane % 8, lax.broadcasted_iota(I32, (32, 128), 0) % 8
    m1, x1 = m[:8], x[:8]
    lane1, row1 = lane[:8], x[:8]
    is_m = {i: m == i for i in (0, 3, 4, 7)}
    is_x = {i: x == i for i in (3, 4)}

    hx[...] = jnp.zeros_like(hx)
    tc[TXB] = jnp.zeros((128, 128), F32)

    loads[0].wait()

    def faces(g):
        rows, below = group(g), one_plane((4 * g + 15) % 16)
        k = va[0, rows, :]
        tym = jnp.where(lane == 0, 0.0, harmonic(k, roll_y(k, 1)))
        typ = roll_y(tym, 127)
        tc[TYM, rows, :] = tym
        tc[TYP, rows, :] = typ
        tc[TYM1, rows, :] = jnp.where(is_m[4], 0.0, tym)
        tc[TYP1, rows, :] = jnp.where(is_m[3], 0.0, typ)
        txm = jnp.where(x == 0, 0.0, harmonic(k, roll_x(k, 1)))
        tc[TXM, rows, :] = txm
        tc[TXP, rows, :] = roll_x(txm, 7)
        tz = harmonic(k, jnp.concatenate([va[0, below, :], k[0:24]], axis=0))
        tc[TZM, rows, :] = tz
        tc[TZP, below, :] = tz[0:8]
        tc[TZP, group(g, 24), :] = tz[8:32]
        tc[TZM1, rows, :] = tz
        tc[TZP1, below, :] = tz[0:8]
        tc[TZP1, group(g, 24), :] = tz[8:32]

    steps(4, faces)
    nil = jnp.zeros((8, 128), F32)
    tc[TZM, 0:8, :] = nil
    tc[TZP, 120:128, :] = nil
    tc[TZM1, 0:8, :] = nil
    tc[TZP1, 120:128, :] = nil
    tc[TZM1, 64:72, :] = nil
    tc[TZP1, 56:64, :] = nil
    for i, (t, z) in enumerate(((TZP, 3), (TZM, 4), (TZP, 11), (TZM, 12))):
        sw[i] = tc[t, 8 * z:8 * z + 8, :]

    loads[1].wait()
    loads[2].wait()

    def first(g):
        rows = group(g)
        vals = []
        for s in range(8):
            on = sup[s, rows, :].astype(F32)
            sf[s, rows, :] = on
            vals.append(bi[s, rows, :] * on)
        inv = 1.0 / sum(vals[1:], vals[0])
        for s in range(8):
            va[1 + s, rows, :] = vals[s] * inv

    steps(2, first)
    loads[3].wait()
    loads[4].wait()
    steps(4, first, 2)

    def exchange(v, off, xs_buf, xr_buf, zr_buf, base):
        for i, s in enumerate(B0):
            xs_buf[0, off + i] = v[off + s, pl.ds(0, 16, stride=8), :]
            xs_buf[1, off + i] = v[off + s, pl.ds(7, 16, stride=8), :]
        if off:
            xs_buf[0, 0] = v[0, pl.ds(0, 16, stride=8), :]
            xs_buf[1, 0] = v[0, pl.ds(7, 16, stride=8), :]
            pl.semaphore_wait(barrier, greeted)
        last, lead = v.at[pl.ds(0, off + 4), pl.ds(120, 8)], v.at[pl.ds(0, off + 4), pl.ds(0, 8)]
        copies = []
        for j, (src, dst, who) in enumerate((
            (xs_buf.at[1], xr_buf.at[0], up_x), (xs_buf.at[0], xr_buf.at[1], down_x),
            (last, zr_buf.at[0], up_z), (lead, zr_buf.at[1], down_z),
        )):
            copies.append(pltpu.make_async_remote_copy(
                src_ref=src, dst_ref=dst, send_sem=halo_s.at[base + j // 2], recv_sem=halo_r.at[base + j // 2],
                device_id=who, device_id_type=MESH))
        for copy in copies:
            copy.start()
        if off:
            second_round()
        return [pltpu.make_async_remote_copy(
            src_ref=buf, dst_ref=buf, send_sem=halo_s.at[base + j], recv_sem=halo_r.at[base + j],
            device_id=up_x, device_id_type=MESH) for j, buf in enumerate((xr_buf, zr_buf))]

    def inner(v, off):
        def part(g):
            rows = group(g)
            odd = g % 2
            below, above = one_plane((4 * g + 15) % 16), one_plane((4 * g + 4) % 16)
            for s in range(8):
                if s % 4 == 0:
                    vals = [v[off + s + i, rows, :] for i in range(4)]
                    txm, txp = tc[TXM, rows, :], tc[TXP, rows, :]
                    tym, typ = [tc[i, rows, :] for i in (TYM, TYM1)], [tc[i, rows, :] for i in (TYP, TYP1)]
                    zm, zp = tc[TZM1 if s else TZM, rows, :], tc[TZP1 if s else TZP, rows, :]
                here, by_y, by_x, turn = vals[s % 4], vals[s % 4 ^ 1], vals[s % 4 ^ 2], 4 - (s & 4) * 2
                near = tym[s & 1] * roll_y(jnp.where(is_m[7], by_y, here), 1)
                near += typ[s & 1] * roll_y(jnp.where(is_m[0], by_y, here), 127)
                near += txm * roll_x(jnp.where(is_x[3], by_x, here), 1)
                near += txp * roll_x(jnp.where(is_x[4], by_x, here), 7)
                lo, hi = v[off + s + turn * odd, below, :], v[off + s + turn * (1 - odd), above, :]
                near += zm * jnp.concatenate([lo, here[0:24]], axis=0)
                near += zp * jnp.concatenate([here[8:32], hi], axis=0)
                nn[s, rows, :] = near

        steps(4, part)

    def outer(v, off, new, off2, xr_buf, zr_buf, extra):
        for i in range(4):
            hx[i, pl.ds(0, 16, stride=8), :] = xr_buf[0, extra + i]
            hx[i, pl.ds(7, 16, stride=8), :] = xr_buf[1, extra + i]
            nn[i, 0:8, :] += tzb[0] * zr_buf[0, extra + i]
            nn[i, 120:128, :] += tzb[1] * zr_buf[1, extra + i]

        def part(g):
            rows = group(g)
            rd, txb = tc[RD, rows, :], tc[TXB, rows, :]
            vals = []
            for s in range(8):
                near = nn[s, rows, :]
                if s in B0:
                    near += txb * hx[B0.index(s), rows, :]
                vals.append((v[off + s, rows, :] * THIRD + rd * near) * sf[s, rows, :])
            inv = 1.0 / sum(vals[1:], vals[0])
            for s in range(8):
                new[off2 + s, rows, :] = vals[s] * inv

        steps(4, part)

    sent = exchange(va, 1, hxs, hxr, hzr, 0)
    inner(va, 1)

    for load in loads[5:]:
        load.wait()
    label = blk[0, 0:1, :]
    for u, (j, r) in enumerate(((0, 0), (0, 4), (1, 0), (1, 4), (2, 0), (2, 4), (1, 0), (1, 4))):
        label = jnp.where(m1[0:1] == u, blk[j, r:r + 1, :], label)
    t_rows, labels = tab.shape[0], cr1.shape[0]
    tab[labels // 128:, :] = jnp.zeros((t_rows - labels // 128, 128), I32)

    def table(t):
        tab[pl.ds(t, 1), :] = cr1[pl.ds(pl.multiple_of(t * 128, 128), 128)].reshape(1, 128)

    steps(labels // 128, table)
    if labels % 128:
        t = labels // 128
        tab[t:t + 1, 0:labels % 128] = cr1[pl.ds(t * 128, labels % 128)].reshape(1, labels % 128)
    l_hi, l_lo = label >> 7, label & 127
    w_iota = lax.broadcasted_iota(I32, (128, 128), 0)
    pick = jnp.where(w_iota == l_lo, 1.0, 0.0).astype(BF16)
    ranks = tab[...]
    parts = jnp.concatenate([(ranks >> 7).astype(F32), (ranks & 127).astype(F32)], axis=0).astype(BF16)
    looked = jnp.dot(parts, pick, preferred_element_type=F32)
    t_iota = lax.broadcasted_iota(I32, (t_rows, 128), 0)
    looked = looked[:t_rows] * 128.0 + looked[t_rows:]
    rank = jnp.sum(jnp.where(t_iota == l_hi, looked, 0.0), axis=0, keepdims=True)
    rank = rank.astype(I32)
    rks[...] = rank
    rkr[0] = rank

    def diagonal(g):
        rows = group(g)
        diag = aa[rows, :]
        for t in (TYM, TYP, TXM, TXP, TZM, TZP):
            diag += tc[t, rows, :]
        tc[RD, rows, :] = diag

    steps(4, diagonal)

    def every(buf, sems):
        return pltpu.make_async_remote_copy(
            src_ref=buf.at[pl.ds(1, gn - 1)], dst_ref=buf.at[pl.ds(1, gn - 1)], send_sem=sems[0], recv_sem=sems[1],
            device_id=partner(g_flips, 1), device_id_type=MESH)

    def rank_copy(r):
        return pltpu.make_async_remote_copy(
            src_ref=rks, dst_ref=rkr.at[r], send_sem=rk_s, recv_sem=rk_r,
            device_id=partner(g_flips, r), device_id_type=MESH)

    pl.semaphore_wait(round_y, len(y_peers))
    loop(gn, lambda r: rank_copy(r).start(), 1)
    for copy in sent:
        copy.wait_recv()

    tc[TXB, pl.ds(0, 16, stride=8), :] = jnp.where(mp > 0, harmonic(hxs[0, 0], hxr[0, 0]), 0.0)
    tc[TXB, pl.ds(7, 16, stride=8), :] = jnp.where(mp < plane - 1, harmonic(hxs[1, 0], hxr[1, 0]), 0.0)
    tzb[0] = jnp.where(ml > 0, harmonic(va[0, 0:8, :], hzr[0, 0]), 0.0)
    tzb[1] = jnp.where(ml < lx - 1, harmonic(va[0, 120:128, :], hzr[1, 0]), 0.0)

    tc[RD, 0:8, :] += tzb[0]
    tc[RD, 120:128, :] += tzb[1]
    tc[RD] = TWO_THIRDS / (tc[RD] + tc[TXB])

    outer(va, 1, vb, 0, hxr, hzr, 1)
    sent2 = exchange(vb, 0, hxs2, hxr2, hzr2, 2)

    es[...] = jnp.zeros_like(es)

    inner(vb, 0)

    def weigh(g):
        rows = group(g)
        tym, typ, txm, txp = (tc[i, rows, :] for i in (TYM, TYP, TXM, TXP))
        sx0 = jnp.where(is_x[3], txp, 0.0) + jnp.where(is_x[4], txm, 0.0)
        sx1 = sx0 + tc[TXB, rows, :]
        sy0 = jnp.where(is_m[7], typ, 0.0) + jnp.where(is_m[0], tym, 0.0)
        sy1 = sy0 + jnp.where(is_m[3], typ, 0.0) + jnp.where(is_m[4], tym, 0.0)
        for s in range(4):
            d = aa[rows, :] + (sx1 if s & 2 else sx0) + (sy1 if s & 1 else sy0)
            ec[s, rows, :] = d
            ec[4 + s, rows, :] = d
        ec[8, rows, :] = sx0
        ec[9, rows, :] = sy0

    steps(4, weigh)
    for i, z in enumerate((3, 4, 11, 12)):
        for s in range(8):
            ec[s, 8 * z:8 * z + 8, :] += sw[i]
    for t, z in ((tzb[0], 0), (tc[TZP, 56:64, :], 7), (tc[TZM, 64:72, :], 8), (tzb[1], 15)):
        for s in range(4, 8):
            ec[s, 8 * z:8 * z + 8, :] += t

    def x_swap(q):
        return roll_x(q, 4)

    def y_swap(q):
        return jnp.where(m1 == 7, roll_y(q, 127), jnp.where(m1 == 0, roll_y(q, 1), 0.0))

    def far(g):
        return one_plane(4 * g + 4 - 5 * (g % 2))

    def rest(g):
        rows = group(g)
        here = pp[rows, :]
        full = plane_sum(ec[0, rows, :] * here - ss[rows, :]) - sw[g] * pp[far(g), :]
        fl[8, one_plane(g), :] = (
            full - x_swap(plane_sum(ec[8, rows, :] * here)) - y_swap(plane_sum(ec[9, rows, :] * here)))

    steps(4, rest)

    for copy in sent2:
        copy.wait_recv()
    for copy in sent:
        copy.wait_send()
    outer(vb, 0, va, 1, hxr2, hzr2, 0)
    store = pltpu.make_async_copy(va.at[pl.ds(1, 8)], v_out, out_sem.at[0])
    store.start()

    def gather(g):
        rows = group(g)
        sx0, sy0 = ec[8, rows, :], ec[9, rows, :]
        vals = [va[1 + s, rows, :] for s in range(8)]
        qx = [x_swap(plane_sum(sx0 * v)) for v in vals]
        qy = [y_swap(plane_sum(sy0 * v)) for v in vals]
        for s in range(8):
            full = plane_sum(ec[s, rows, :] * vals[s]) - sw[g] * va[1 + (s ^ 4), far(g), :]
            fl[s, one_plane(g), :] = full - qx[s ^ 2] - qy[s ^ 1]

    steps(4, gather)

    def z_part(j, pz, s):
        groups = ((0,), (1, 2), (3,))[j] if pz == 1 else {(1, 0): (1,), (2, 0): (3,), (0, 2): (0,), (1, 2): (2,)}[j, pz]
        term = fl[s, one_plane(groups[0]), :]
        for g in groups[1:]:
            term += fl[s, one_plane(g), :]
        return term

    for k, (j, halves) in enumerate(((0, (1, 2)), (1, (1, 2)), (2, (1, 0)), (1, (0,)))):
        for half, pz in enumerate(halves):
            for b in range(2):
                at, s = 64 * half + 24 * b, (0 if pz == 1 else 4) + 2 * b
                side = z_part(j, pz, s + 1)
                es[k, at:at + 8, :] = jnp.where(m1 < 4, side, 0.0)
                es[k, at + 8:at + 16, :] = z_part(j, pz, s)
                es[k, at + 16:at + 24, :] = jnp.where(m1 < 4, 0.0, side)
        if k < 3:
            es[k, 48:56, :] = -z_part(j, 1, 8)

    m16 = m[:16]
    sums = []
    for k in range(4):
        for xi in range(2):
            t = es[k, pl.ds(4 * xi, 16, stride=8), :]
            for i in range(1, 4):
                t += es[k, pl.ds(4 * xi + i, 16, stride=8), :]
            sums.append(t)
    for bit in (4, 2, 1):
        high = (m16 & bit) != 0
        merged = []
        for u in range(bit):
            one, two = sums[u], sums[u + bit]
            move = jnp.where(high, one, two)
            merged.append(jnp.where(high, two, one) + jnp.where(high, roll_y(move, bit), roll_y(move, 128 - bit)))
        sums = merged
    rows_out = sums[0]
    second = pltpu.roll(rows_out[8:16], 7, 0)
    for buf in (cs, crv.at[0]):
        buf[0:8, :] = jnp.where(x1 == 7, second, rows_out[0:8])
        buf[8:13, :] = second[0:5]

    def g_copy(r):
        return pltpu.make_async_remote_copy(
            src_ref=cs, dst_ref=crv.at[r], send_sem=g_s, recv_sem=g_r,
            device_id=partner(g_flips, r), device_id_type=MESH)

    for r in far_first(G_BITS):
        g_copy(r).start()

    def wanted(t):
        q, idx = (t, lane1) if t < 4 else (lane1 >> 5, 128 + (lane1 & 31))
        peer = jnp.zeros_like(idx)
        for p in range(1, hn):
            peer += jnp.where(idx >= p * width, 1, 0)
        col = idx - peer * width + q * width
        dev = jnp.zeros_like(idx) + (ml * plane + mp)
        for b, (on_layer, step) in enumerate(h_flips):
            dev += ((peer >> b) & 1) * (step * plane if on_layer else step)
        return jnp.where((col < own) & (idx < n_idx), dev * own + col, -7)

    wants = [wanted(t) for t in range(5)]
    every(rkr, (rk_s, rk_r)).wait_recv()
    turned = jnp.concatenate([rkr[r] for r in range(gn)] + [jnp.zeros((128 - gn, 128), I32)], axis=0).astype(F32).T

    def build(r, ranks):
        have = jnp.broadcast_to(ranks[:, 0:1], (128, 128))
        for t in range(5):
            want = jnp.concatenate([wants[t]] * 16, axis=0)
            oh[pl.ds(pl.multiple_of(128 * r, 128), 128), 128 * t:128 * t + 128] = (
                jnp.where(have == want, 1.0, 0.0).astype(BF16))
        return roll_y(ranks, 127)

    lax.fori_loop(0, gn, build, turned.astype(I32))

    odd = m1 % 2 == 1
    b1 = (x1 >= 3) & (x1 < 6)
    b1_odd = b1 & odd

    def spread(r):
        got1, got2 = crv[r, 0:8, :], pltpu.roll(crv[r, 5:13, :], 6, 0)
        pz1 = jnp.where((m1 < 6) & (x1 < 7), got1, 0.0)
        pz2 = jnp.where(m1 < 4, got2, 0.0)
        pz0 = jnp.where(m1 < 4, 0.0, jnp.where(m1 < 6, got2, got1))
        low1, low2, low0 = (jnp.where(b1_odd, v, 0.0) for v in (pz1, pz2, pz0))
        last = pltpu.roll(low1, 5, 0) + low2 + jnp.where(x1 >= 6, pltpu.roll(low0, 3, 0), 0.0)
        vals = jnp.concatenate([
            pz1 - low1 + jnp.where(x1 == 7, pltpu.roll(low0, 2, 0), 0.0), pz2 - low2, pz0 - low0, last], axis=0)
        high = vals.astype(BF16)
        lanes = pl.ds(pl.multiple_of(128 * r, 128), 128)
        xb[0:32, lanes] = high
        xb[32:64, lanes] = (vals - high.astype(F32)).astype(BF16)

    every(crv, (g_s, g_r)).wait_recv()

    def spread_four(i):
        for j in range(4):
            spread(4 * i + j)

    steps(gn // 4, spread_four)
    routed = jnp.dot(xb[...], oh[...], preferred_element_type=F32)
    both = routed[0:32] + routed[32:64]
    parts = [both[:, 128 * q:128 * q + 128] for q in range(4)]
    over = both[:, 512:640]
    packed = jnp.concatenate([
        jnp.concatenate(parts, axis=0).T,
        jnp.concatenate([roll_y(over, (128 - 32 * q) % 128) if q else over for q in range(4)], axis=0).T], axis=0)

    def h_copy(r):
        return pltpu.make_async_remote_copy(
            src_ref=hs.at[r], dst_ref=hr.at[r], send_sem=h_s.at[r], recv_sem=h_r.at[r],
            device_id=partner(h_flips, r), device_id_type=MESH)

    pl.semaphore_wait(round_z, 2)
    for r in far_first(H_BITS):
        hs[r] = packed[r * width:(r + 1) * width]
        h_copy(r).start()
    hs[0] = packed[0:width]
    store.wait()
    for copy in sent2:
        copy.wait_send()
    every(rkr, (rk_s, rk_r)).wait_send()
    every(crv, (g_s, g_r)).wait_send()
    loop(hn, lambda r: h_copy(r).wait_send(), 1)
    loop(hn, lambda r: h_copy(r).wait_recv(), 1)
    final = hs[0]
    for r in range(1, hn):
        final += hr[r]
    f_out[0:width, :] = final


def finish(own, width, v_in, f_in, v_out, cm_hbm, cr_hbm, ft, cm_out, cr_out, sem):
    stores = [pltpu.make_async_copy(src, dst, sem.at[i]) for i, (src, dst) in enumerate((
        (v_in, v_out), (cm_out, cm_hbm), (cr_out, cr_hbm)))]
    stores[0].start()
    ft[0:16, :] = f_in[...]
    turned = ft[...].T
    lane = lax.broadcasted_iota(I32, (32, 128), 1)
    done = jnp.zeros((32, 128), F32)
    for q in range(4):
        part = turned[32 * q:32 * q + 32]
        here = (lane >= q * width) & (lane < (q + 1) * width)
        done = jnp.where(here, pltpu.roll(part, q * width, 1) if q else part, done)
    for pz, px, base in (
        (1, 1, 0), (1, 2, 3), (2, 1, 8), (2, 2, 11), (0, 1, 16), (0, 2, 19), (1, 0, 24), (2, 0, 27)):
        k = 9 * pz + 3 * px
        cm_out[k:k + 3, :] = done[base:base + 3, 0:own]
    cm_out[0:2, :] = done[30:32, 0:own]
    cm_out[2:3, :] = done[7:8, 0:own]
    cr_out[...] = done[6:7, 0:own]
    stores[1].start()
    stores[2].start()
    for store in stores:
        store.wait()


def per_device(sizes, basis_init, permeability, accumulation, pressure, source, support, block_of, curve_rank):
    lx, plane = sizes
    gn, hn = 2 ** len(G_BITS), 2 ** len(H_BITS)
    devices = lx * plane
    own = (curve_rank.shape[0] + devices - 1) // devices
    width = (own + 3) // 4
    flat = lambda v: v.reshape(v.shape[:-3] + (128, 128))
    t_rows = -(-curve_rank.shape[0] // 2048) * 16
    anywhere = pl.BlockSpec(memory_space=pl.ANY)
    vmem = pl.BlockSpec(memory_space=pltpu.VMEM)
    dma = pltpu.SemaphoreType.DMA
    cells = lambda *lead: pltpu.VMEM(lead + (128, 128), F32)
    basis, rows = pl.pallas_call(
        functools.partial(kernel, (lx, plane, own, width)),
        out_shape=(
            jax.ShapeDtypeStruct((8, 128, 128), F32),
            jax.ShapeDtypeStruct((16, 128), F32),
        ),
        in_specs=[anywhere] * 8,
        out_specs=(anywhere, vmem),
        scratch_shapes=[
            cells(8), pltpu.VMEM((8, 128, 128), I32), cells(), cells(), cells(),
            pltpu.VMEM((3, 8, 128), I32), pltpu.VMEM(curve_rank.shape, I32), pltpu.VMEM((t_rows, 128), I32),
            cells(9), cells(8), cells(8), cells(8), cells(12),
            pltpu.VMEM((2, 8, 128), F32), cells(10), pltpu.VMEM((4, 8, 128), F32),
            pltpu.VMEM((9, 32, 128), F32), cells(4),
            pltpu.VMEM((2, 5, 16, 128), F32), pltpu.VMEM((2, 5, 16, 128), F32), pltpu.VMEM((2, 5, 8, 128), F32),
            pltpu.VMEM((2, 4, 16, 128), F32), pltpu.VMEM((2, 4, 16, 128), F32), pltpu.VMEM((2, 4, 8, 128), F32),
            pltpu.VMEM((1, 128), I32), pltpu.VMEM((gn, 1, 128), I32),
            pltpu.VMEM((gn * 128, 640), BF16),
            pltpu.VMEM((64, gn * 128), BF16), pltpu.VMEM((4, 128, 128), F32),
            pltpu.VMEM((13, 128), F32), pltpu.VMEM((gn, 13, 128), F32),
            pltpu.VMEM((hn, width, 128), F32), pltpu.VMEM((hn, width, 128), F32),
            pltpu.SemaphoreType.REGULAR, pltpu.SemaphoreType.REGULAR, dma((12,)), dma((1,)), dma((4,)), dma((4,)),
            dma, dma, dma, dma, dma((hn,)), dma((hn,)),
        ],
        compiler_params=pltpu.CompilerParams(
            collective_id=0, has_side_effects=True, vmem_limit_bytes=VMEM_GRANT),
        cost_estimate=pl.CostEstimate(flops=20_000_000, bytes_accessed=2_000_000, transcendentals=0),
    )(*(pltpu.with_memory_space_constraint(v, pltpu.HBM) for v in (
        flat(basis_init), flat(permeability), flat(accumulation), flat(pressure), flat(source),
        flat(support), flat(block_of), curve_rank,
    )))
    basis, matrix, residual = pl.pallas_call(
        functools.partial(finish, own, width),
        out_shape=(
            jax.ShapeDtypeStruct((8, 128, 128), F32),
            jax.ShapeDtypeStruct((27, own), F32),
            jax.ShapeDtypeStruct((1, own), F32),
        ),
        in_specs=[anywhere, vmem],
        out_specs=(anywhere, anywhere, anywhere),
        scratch_shapes=[cells(), pltpu.VMEM((27, own), F32), pltpu.VMEM((1, own), F32), dma((3,))],
        compiler_params=pltpu.CompilerParams(vmem_limit_bytes=VMEM_GRANT),
    )(basis, rows)
    return basis.reshape(basis_init.shape), matrix, residual.reshape(own)


def solution(mesh):
    return jax.shard_map(
        functools.partial(per_device, (mesh.shape["layer"], mesh.shape["plane"])),
        mesh=mesh,
        in_specs=(
            P(None, "layer", "plane", None),
            P("layer", "plane", None),
            P("layer", "plane", None),
            P("layer", "plane", None),
            P("layer", "plane", None),
            P(None, "layer", "plane", None),
            P("layer", "plane", None),
            P(),
        ),
        out_specs=(
            P(None, "layer", "plane", None),
            P(None, ("layer", "plane")),
            P(("layer", "plane")),
        ),
        check_vma=False,
    )
```

```python
import functools

import jax
import jax.numpy as jnp
from jax import lax
from jax.experimental import pallas as pl
from jax.experimental.pallas import tpu as pltpu
from jax.sharding import PartitionSpec as P

MESH = pl.DeviceIdType.MESH
F32, BF16, I32 = jnp.float32, jnp.bfloat16, jnp.int32

G_BITS = (("layer", 1), ("layer", 2), ("plane", 16), ("plane", 32))
H_BITS = (("plane", 1), ("plane", 2), ("plane", 4), ("plane", 8))
VMEM_GRANT = 32 * 1024 * 1024
THIRD, TWO_THIRDS = 1.0 / 3.0, 2.0 / 3.0
B0 = (0, 1, 4, 5)
A0 = (0, 1, 2, 3)
TYM, TYP, TYM1, TYP1, TXM, TXP, TZM, TZP, TZM1, TZP1, TXB, RD = range(12)


def roll_x(v, shift):
    rows = v.shape[0]
    return pltpu.roll(v.reshape(rows // 8, 8, 128), shift, 1).reshape(rows, 128)


def roll_y(v, shift):
    return pltpu.roll(v, shift, 1)


def harmonic(k, n):
    return 2.0 * k * n / (k + n)


def plane_sum(v):
    return v.reshape(-1, 8, 128).sum(axis=0)


def far_first(bits):
    def hops(r):
        reach = {"layer": 0, "y": 0, "z": 0}
        for i, (axis, bit) in enumerate(bits):
            if (r >> i) & 1:
                kind, step = (axis, bit) if axis == "layer" else ("y", bit // 16) if bit >= 16 else ("z", bit // 2)
                reach[kind] += step
        return sum(min(n, size - n) for n, size in ((reach["layer"], 4), (reach["y"], 4), (reach["z"], 8)))

    return sorted(range(1, 2 ** len(bits)), key=lambda r: -hops(r))


def kernel(
    dims,
    bi_hbm, k_hbm, a_hbm, p_hbm, s_hbm, sup_hbm, blk_hbm, cr_hbm,
    v_out, f_out,
    bi, sup, aa, pp, ss, blk, cr1, tab,
    va, vb, sf, nn, tc, tzb, ec, sw, fl, hx, hxs, hxr, hzr, hxs2, hxr2, hzr2,
    rks, rkr, rkt, oh, xb, es, cs, crv, hs, hr,
    round_y, round_z, in_sem, out_sem, halo_s, halo_r, rk_s, rk_r, g_s, g_r, h_s, h_r,
):
    lx, plane, own, width = dims
    gn, hn = 2 ** len(G_BITS), 2 ** len(H_BITS)
    zc = hn // 2
    n_idx = hn * width
    ml, mp = lax.axis_index("layer"), lax.axis_index("plane")

    def flips(bits):
        steps = []
        for axis, bit in bits:
            at = ml if axis == "layer" else mp
            steps.append((axis == "layer", bit * (1 - 2 * ((at // bit) % 2))))
        return steps

    g_flips, h_flips = flips(G_BITS), flips(H_BITS)

    def partner(steps, r):
        to_l, to_p = ml, mp
        for i, (on_layer, step) in enumerate(steps):
            if (r >> i) & 1:
                to_l, to_p = (to_l + step, to_p) if on_layer else (to_l, to_p + step)
        return (to_l, to_p)

    up_x, down_x = (ml, (mp + 1) % plane), (ml, (mp + plane - 1) % plane)
    up_z, down_z = ((ml + 1) % lx, mp), ((ml + lx - 1) % lx, mp)

    def loop(n, body, start=0):
        for i in range(start, n):
            body(i)

    def group(g):
        return slice(g * 32, g * 32 + 32)

    def one_plane(z):
        return slice(z * 8, z * 8 + 8)

    loads = [
        pltpu.make_async_copy(k_hbm, va.at[0], in_sem.at[0]),
        pltpu.make_async_copy(bi_hbm.at[:, pl.ds(0, 64)], bi.at[:, pl.ds(0, 64)], in_sem.at[1]),
        pltpu.make_async_copy(sup_hbm.at[:, pl.ds(0, 64)], sup.at[:, pl.ds(0, 64)], in_sem.at[2]),
        pltpu.make_async_copy(bi_hbm.at[:, pl.ds(64, 64)], bi.at[:, pl.ds(64, 64)], in_sem.at[10]),
        pltpu.make_async_copy(sup_hbm.at[:, pl.ds(64, 64)], sup.at[:, pl.ds(64, 64)], in_sem.at[11]),
        pltpu.make_async_copy(a_hbm, aa, in_sem.at[3]),
        pltpu.make_async_copy(cr_hbm, cr1, in_sem.at[4]),
        pltpu.make_async_copy(p_hbm, pp, in_sem.at[5]),
        pltpu.make_async_copy(s_hbm, ss, in_sem.at[6]),
    ]
    for j, z in enumerate((0, 4, 12)):
        loads.append(pltpu.make_async_copy(blk_hbm.at[pl.ds(8 * z, 8)], blk.at[j], in_sem.at[7 + j]))
    barrier = pltpu.get_barrier_semaphore()

    def greet(who):
        pl.semaphore_signal(barrier, inc=1, device_id=who, device_id_type=MESH)

    def along_z(dz, dc):
        return (ml, mp + dc * (1 - 2 * (mp % 2)) + 2 * ((mp // 2 + dz) % zc - (mp // 2) % zc))

    x_mask = sum(1 << i for i, (axis, _) in enumerate(G_BITS) if axis == "layer")
    x_peers = [r for r in range(1, gn) if r & x_mask == r]
    y_peers = [r for r in range(1, gn) if r & x_mask == 0]
    z_peers = [(dz, dc) for dz in (1, zc - 1, 2, zc - 2) for dc in (0, 1)] + [(0, 1)]
    greet(up_x)
    greet(down_x)
    for r in x_peers:
        greet(partner(g_flips, r))
    for load in loads[:5]:
        load.start()
    for r in y_peers:
        greet(partner(g_flips, r))
    for dz, dc in z_peers:
        greet(along_z(dz, dc))
    for load in loads[5:]:
        load.start()
    greeted = 2 + len(x_peers) + len(y_peers) + len(z_peers)

    def second_round():
        for r in y_peers:
            pl.semaphore_signal(round_y, inc=1, device_id=partner(g_flips, r), device_id_type=MESH)
        for dz in (2, zc - 2):
            pl.semaphore_signal(round_z, inc=1, device_id=along_z(dz, 0), device_id_type=MESH)

    lane = lax.broadcasted_iota(I32, (32, 128), 1)
    m, x = lane % 8, lax.broadcasted_iota(I32, (32, 128), 0) % 8
    m1, x1 = m[:8], x[:8]
    lane1, row1 = lane[:8], x[:8]
    is_m = {i: m == i for i in (0, 3, 4, 7)}
    is_x = {i: x == i for i in (3, 4)}

    hx[...] = jnp.zeros_like(hx)
    tc[TXB] = jnp.zeros((128, 128), F32)

    loads[0].wait()

    def faces(g):
        rows, below = group(g), one_plane((4 * g + 15) % 16)
        k = va[0, rows, :]
        tym = jnp.where(lane == 0, 0.0, harmonic(k, roll_y(k, 1)))
        typ = roll_y(tym, 127)
        tc[TYM, rows, :] = tym
        tc[TYP, rows, :] = typ
        tc[TYM1, rows, :] = jnp.where(is_m[4], 0.0, tym)
        tc[TYP1, rows, :] = jnp.where(is_m[3], 0.0, typ)
        txm = jnp.where(x == 0, 0.0, harmonic(k, roll_x(k, 1)))
        tc[TXM, rows, :] = txm
        tc[TXP, rows, :] = roll_x(txm, 7)
        tz = harmonic(k, jnp.concatenate([va[0, below, :], k[0:24]], axis=0))
        tc[TZM, rows, :] = tz
        tc[TZP, below, :] = tz[0:8]
        tc[TZP, slice(g * 32, g * 32 + 24), :] = tz[8:32]
        tc[TZM1, rows, :] = tz
        tc[TZP1, below, :] = tz[0:8]
        tc[TZP1, slice(g * 32, g * 32 + 24), :] = tz[8:32]

    loop(4, faces)
    nil = jnp.zeros((8, 128), F32)
    tc[TZM, 0:8, :] = nil
    tc[TZP, 120:128, :] = nil
    tc[TZM1, 0:8, :] = nil
    tc[TZP1, 120:128, :] = nil
    tc[TZM1, 64:72, :] = nil
    tc[TZP1, 56:64, :] = nil
    for i, (t, z) in enumerate(((TZP, 3), (TZM, 4), (TZP, 11), (TZM, 12))):
        sw[i] = tc[t, 8 * z:8 * z + 8, :]

    loads[1].wait()
    loads[2].wait()

    def first(g):
        rows = group(g)
        vals = []
        for s in range(8):
            on = sup[s, rows, :].astype(F32)
            sf[s, rows, :] = on
            vals.append(bi[s, rows, :] * on)
        inv = 1.0 / sum(vals[1:], vals[0])
        for s in range(8):
            va[1 + s, rows, :] = vals[s] * inv

    loop(2, first)
    loads[3].wait()
    loads[4].wait()
    loop(4, first, 2)

    def exchange(v, off, xs_buf, xr_buf, zr_buf, base):
        for i, s in enumerate(B0):
            xs_buf[0, off + i] = v[off + s, pl.ds(0, 16, stride=8), :]
            xs_buf[1, off + i] = v[off + s, pl.ds(7, 16, stride=8), :]
        if off:
            xs_buf[0, 0] = v[0, pl.ds(0, 16, stride=8), :]
            xs_buf[1, 0] = v[0, pl.ds(7, 16, stride=8), :]
            pl.semaphore_wait(barrier, greeted)
        last, lead = v.at[pl.ds(0, off + 4), pl.ds(120, 8)], v.at[pl.ds(0, off + 4), pl.ds(0, 8)]
        copies = []
        for j, (src, dst, who) in enumerate((
            (xs_buf.at[1], xr_buf.at[0], up_x), (xs_buf.at[0], xr_buf.at[1], down_x),
            (last, zr_buf.at[0], up_z), (lead, zr_buf.at[1], down_z),
        )):
            copies.append(pltpu.make_async_remote_copy(
                src_ref=src, dst_ref=dst, send_sem=halo_s.at[base + j // 2], recv_sem=halo_r.at[base + j // 2],
                device_id=who, device_id_type=MESH))
        for copy in copies:
            copy.start()
        if off:
            second_round()
        return [pltpu.make_async_remote_copy(
            src_ref=buf, dst_ref=buf, send_sem=halo_s.at[base + j], recv_sem=halo_r.at[base + j],
            device_id=up_x, device_id_type=MESH) for j, buf in enumerate((xr_buf, zr_buf))]

    def inner(v, off):
        def part(g):
            rows = group(g)
            odd = g % 2
            below, above = one_plane((4 * g + 15) % 16), one_plane((4 * g + 4) % 16)
            for s in range(8):
                if s % 4 == 0:
                    vals = [v[off + s + i, rows, :] for i in range(4)]
                    txm, txp = tc[TXM, rows, :], tc[TXP, rows, :]
                    tym, typ = [tc[i, rows, :] for i in (TYM, TYM1)], [tc[i, rows, :] for i in (TYP, TYP1)]
                    zm, zp = tc[TZM1 if s else TZM, rows, :], tc[TZP1 if s else TZP, rows, :]
                here, by_y, by_x, turn = vals[s % 4], vals[s % 4 ^ 1], vals[s % 4 ^ 2], 4 - (s & 4) * 2
                near = tym[s & 1] * roll_y(jnp.where(is_m[7], by_y, here), 1)
                near += typ[s & 1] * roll_y(jnp.where(is_m[0], by_y, here), 127)
                near += txm * roll_x(jnp.where(is_x[3], by_x, here), 1)
                near += txp * roll_x(jnp.where(is_x[4], by_x, here), 7)
                lo, hi = v[off + s + turn * odd, below, :], v[off + s + turn * (1 - odd), above, :]
                near += zm * jnp.concatenate([lo, here[0:24]], axis=0)
                near += zp * jnp.concatenate([here[8:32], hi], axis=0)
                nn[s, rows, :] = near

        loop(4, part)

    def outer(v, off, new, off2, xr_buf, zr_buf, extra):
        for i in range(4):
            hx[i, pl.ds(0, 16, stride=8), :] = xr_buf[0, extra + i]
            hx[i, pl.ds(7, 16, stride=8), :] = xr_buf[1, extra + i]
            nn[i, 0:8, :] += tzb[0] * zr_buf[0, extra + i]
            nn[i, 120:128, :] += tzb[1] * zr_buf[1, extra + i]

        def part(g):
            rows = group(g)
            rd, txb = tc[RD, rows, :], tc[TXB, rows, :]
            vals = []
            for s in range(8):
                near = nn[s, rows, :]
                if s in B0:
                    near += txb * hx[B0.index(s), rows, :]
                vals.append((v[off + s, rows, :] * THIRD + rd * near) * sf[s, rows, :])
            inv = 1.0 / sum(vals[1:], vals[0])
            for s in range(8):
                new[off2 + s, rows, :] = vals[s] * inv

        loop(4, part)

    sent = exchange(va, 1, hxs, hxr, hzr, 0)
    inner(va, 1)

    for load in loads[5:]:
        load.wait()
    label = blk[0, 0:1, :]
    for u, (j, r) in enumerate(((0, 0), (0, 4), (1, 0), (1, 4), (2, 0), (2, 4), (1, 0), (1, 4))):
        label = jnp.where(m1[0:1] == u, blk[j, r:r + 1, :], label)
    t_rows, labels = tab.shape[0], cr1.shape[0]
    tab[labels // 128:, :] = jnp.zeros((t_rows - labels // 128, 128), I32)

    def table(t):
        tab[t:t + 1, :] = cr1[pl.ds(t * 128, 128)].reshape(1, 128)

    loop(labels // 128, table)
    if labels % 128:
        t = labels // 128
        tab[t:t + 1, 0:labels % 128] = cr1[pl.ds(t * 128, labels % 128)].reshape(1, labels % 128)
    l_hi, l_lo = label >> 7, label & 127
    w_iota = lax.broadcasted_iota(I32, (128, 128), 0)
    pick = jnp.where(w_iota == l_lo, 1.0, 0.0).astype(BF16)
    ranks = tab[...]
    parts = jnp.concatenate([(ranks >> 7).astype(F32), (ranks & 127).astype(F32)], axis=0).astype(BF16)
    looked = jnp.dot(parts, pick, preferred_element_type=F32)
    t_iota = lax.broadcasted_iota(I32, (t_rows, 128), 0)
    looked = looked[:t_rows] * 128.0 + looked[t_rows:]
    rank = jnp.sum(jnp.where(t_iota == l_hi, looked, 0.0), axis=0, keepdims=True)
    rank = rank.astype(I32)
    rks[...] = rank
    rkr[0] = rank

    def diagonal(g):
        rows = group(g)
        diag = aa[rows, :]
        for t in (TYM, TYP, TXM, TXP, TZM, TZP):
            diag += tc[t, rows, :]
        tc[RD, rows, :] = diag

    loop(4, diagonal)

    def every(buf, sems):
        return pltpu.make_async_remote_copy(
            src_ref=buf.at[pl.ds(1, buf.shape[0] - 1)], dst_ref=buf.at[pl.ds(1, buf.shape[0] - 1)],
            send_sem=sems[0], recv_sem=sems[1], device_id=partner(g_flips, 1), device_id_type=MESH)

    def rank_copy(r):
        return pltpu.make_async_remote_copy(
            src_ref=rks, dst_ref=rkr.at[r], send_sem=rk_s, recv_sem=rk_r,
            device_id=partner(g_flips, r), device_id_type=MESH)

    pl.semaphore_wait(round_y, len(y_peers))
    loop(gn, lambda r: rank_copy(r).start(), 1)
    for copy in sent:
        copy.wait_recv()

    tc[TXB, pl.ds(0, 16, stride=8), :] = jnp.where(mp > 0, harmonic(hxs[0, 0], hxr[0, 0]), 0.0)
    tc[TXB, pl.ds(7, 16, stride=8), :] = jnp.where(mp < plane - 1, harmonic(hxs[1, 0], hxr[1, 0]), 0.0)
    tzb[0] = jnp.where(ml > 0, harmonic(va[0, 0:8, :], hzr[0, 0]), 0.0)
    tzb[1] = jnp.where(ml < lx - 1, harmonic(va[0, 120:128, :], hzr[1, 0]), 0.0)

    tc[RD, 0:8, :] += tzb[0]
    tc[RD, 120:128, :] += tzb[1]
    tc[RD] = TWO_THIRDS / (tc[RD] + tc[TXB])

    outer(va, 1, vb, 0, hxr, hzr, 1)
    sent2 = exchange(vb, 0, hxs2, hxr2, hzr2, 2)

    es[...] = jnp.zeros_like(es)

    inner(vb, 0)

    def weigh(g):
        rows = group(g)
        tym, typ, txm, txp = (tc[i, rows, :] for i in (TYM, TYP, TXM, TXP))
        sx0 = jnp.where(is_x[3], txp, 0.0) + jnp.where(is_x[4], txm, 0.0)
        sx1 = sx0 + tc[TXB, rows, :]
        sy0 = jnp.where(is_m[7], typ, 0.0) + jnp.where(is_m[0], tym, 0.0)
        sy1 = sy0 + jnp.where(is_m[3], typ, 0.0) + jnp.where(is_m[4], tym, 0.0)
        for s in range(4):
            d = aa[rows, :] + (sx1 if s & 2 else sx0) + (sy1 if s & 1 else sy0)
            ec[s, rows, :] = d
            ec[4 + s, rows, :] = d
        ec[8, rows, :] = sx0
        ec[9, rows, :] = sy0

    loop(4, weigh)
    for i, z in enumerate((3, 4, 11, 12)):
        for s in range(8):
            ec[s, 8 * z:8 * z + 8, :] += sw[i]
    for t, z in ((tzb[0], 0), (tc[TZP, 56:64, :], 7), (tc[TZM, 64:72, :], 8), (tzb[1], 15)):
        for s in range(4, 8):
            ec[s, 8 * z:8 * z + 8, :] += t

    def x_swap(q):
        return roll_x(q, 4)

    def y_swap(q):
        return jnp.where(m1 == 7, roll_y(q, 127), jnp.where(m1 == 0, roll_y(q, 1), 0.0))

    def far(g):
        return one_plane(4 * g + 4 - 5 * (g % 2))

    def rest(g):
        rows = group(g)
        here = pp[rows, :]
        full = plane_sum(ec[0, rows, :] * here - ss[rows, :]) - sw[g] * pp[far(g), :]
        fl[8, one_plane(g), :] = (
            full - x_swap(plane_sum(ec[8, rows, :] * here)) - y_swap(plane_sum(ec[9, rows, :] * here)))

    loop(4, rest)

    for copy in sent2:
        copy.wait_recv()
    for copy in sent:
        copy.wait_send()
    outer(vb, 0, va, 1, hxr2, hzr2, 0)
    store = pltpu.make_async_copy(va.at[pl.ds(1, 8)], v_out, out_sem.at[0])

    def gather(g):
        rows = group(g)
        sx0, sy0 = ec[8, rows, :], ec[9, rows, :]
        vals = [va[1 + s, rows, :] for s in range(8)]
        qx = [x_swap(plane_sum(sx0 * v)) for v in vals]
        qy = [y_swap(plane_sum(sy0 * v)) for v in vals]
        for s in range(8):
            full = plane_sum(ec[s, rows, :] * vals[s]) - sw[g] * va[1 + (s ^ 4), far(g), :]
            fl[s, one_plane(g), :] = full - qx[s ^ 2] - qy[s ^ 1]

    loop(4, gather)

    def z_part(j, pz, s):
        groups = ((0,), (1, 2), (3,))[j] if pz == 1 else {(1, 0): (1,), (2, 0): (3,), (0, 2): (0,), (1, 2): (2,)}[j, pz]
        term = fl[s, one_plane(groups[0]), :]
        for g in groups[1:]:
            term += fl[s, one_plane(g), :]
        return term

    for k, (j, halves) in enumerate(((0, (1, 2)), (1, (1, 2)), (2, (1, 0)), (1, (0,)))):
        for half, pz in enumerate(halves):
            for b in range(2):
                at, s = 64 * half + 24 * b, (0 if pz == 1 else 4) + 2 * b
                side = z_part(j, pz, s + 1)
                es[k, at:at + 8, :] = jnp.where(m1 < 4, side, 0.0)
                es[k, at + 8:at + 16, :] = z_part(j, pz, s)
                es[k, at + 16:at + 24, :] = jnp.where(m1 < 4, 0.0, side)
        if k < 3:
            es[k, 48:56, :] = -z_part(j, 1, 8)

    m16 = m[:16]
    sums = []
    for k in range(4):
        for xi in range(2):
            t = es[k, pl.ds(4 * xi, 16, stride=8), :]
            for i in range(1, 4):
                t += es[k, pl.ds(4 * xi + i, 16, stride=8), :]
            sums.append(t)
    for bit in (4, 2, 1):
        high = (m16 & bit) != 0
        merged = []
        for u in range(bit):
            one, two = sums[u], sums[u + bit]
            move = jnp.where(high, one, two)
            merged.append(jnp.where(high, two, one) + jnp.where(high, roll_y(move, bit), roll_y(move, 128 - bit)))
        sums = merged
    rows_out = sums[0]
    second = pltpu.roll(rows_out[8:16], 7, 0)
    for buf in (cs, crv.at[0]):
        buf[0:8, :] = jnp.where(x1 == 7, second, rows_out[0:8])
        buf[8:13, :] = second[0:5]

    def g_copy(r):
        return pltpu.make_async_remote_copy(
            src_ref=cs, dst_ref=crv.at[r], send_sem=g_s, recv_sem=g_r,
            device_id=partner(g_flips, r), device_id_type=MESH)

    for r in far_first(G_BITS):
        g_copy(r).start()
    store.start()

    def wanted(t):
        q, idx = (t, lane1) if t < 4 else (lane1 >> 5, 128 + (lane1 & 31))
        peer = jnp.zeros_like(idx)
        for p in range(1, hn):
            peer += jnp.where(idx >= p * width, 1, 0)
        col = idx - peer * width + q * width
        dev = jnp.zeros_like(idx) + (ml * plane + mp)
        for b, (on_layer, step) in enumerate(h_flips):
            dev += ((peer >> b) & 1) * (step * plane if on_layer else step)
        return jnp.where((col < own) & (idx < n_idx), dev * own + col, -7)

    wants = [wanted(t) for t in range(5)]
    every(rkr, (rk_s, rk_r)).wait_recv()
    turned = jnp.concatenate([rkr[r] for r in range(gn)] + [jnp.zeros((128 - gn, 128), I32)], axis=0).astype(F32).T
    rkt[...] = turned.astype(I32)
    for r in range(gn):
        have = jnp.broadcast_to(rkt[:, r:r + 1], (128, 128))
        for t in range(5):
            want = jnp.concatenate([wants[t]] * 16, axis=0)
            oh[128 * r:128 * r + 128, 128 * t:128 * t + 128] = jnp.where(have == want, 1.0, 0.0).astype(BF16)

    odd = m1 % 2 == 1
    b1 = (x1 >= 3) & (x1 < 6)
    b1_odd = b1 & odd

    def spread(r):
        got1, got2 = crv[r, 0:8, :], pltpu.roll(crv[r, 5:13, :], 6, 0)
        pz1 = jnp.where((m1 < 6) & (x1 < 7), got1, 0.0)
        pz2 = jnp.where(m1 < 4, got2, 0.0)
        pz0 = jnp.where(m1 < 4, 0.0, jnp.where(m1 < 6, got2, got1))
        low1, low2, low0 = (jnp.where(b1_odd, v, 0.0) for v in (pz1, pz2, pz0))
        last = pltpu.roll(low1, 5, 0) + low2 + jnp.where(x1 >= 6, pltpu.roll(low0, 3, 0), 0.0)
        vals = jnp.concatenate([
            pz1 - low1 + jnp.where(x1 == 7, pltpu.roll(low0, 2, 0), 0.0), pz2 - low2, pz0 - low0, last], axis=0)
        high = vals.astype(BF16)
        lanes = slice(128 * r, 128 * r + 128)
        xb[0:32, lanes] = high
        xb[32:64, lanes] = (vals - high.astype(F32)).astype(BF16)

    every(crv, (g_s, g_r)).wait_recv()
    loop(gn, spread)
    routed = jnp.dot(xb[...], oh[...], preferred_element_type=F32)
    both = routed[0:32] + routed[32:64]
    parts = [both[:, 128 * q:128 * q + 128] for q in range(4)]
    over = both[:, 512:640]
    packed = jnp.concatenate([
        jnp.concatenate(parts, axis=0).T,
        jnp.concatenate([roll_y(over, (128 - 32 * q) % 128) if q else over for q in range(4)], axis=0).T], axis=0)

    def h_copy(r):
        return pltpu.make_async_remote_copy(
            src_ref=hs.at[r], dst_ref=hr.at[r], send_sem=h_s, recv_sem=h_r,
            device_id=partner(h_flips, r), device_id_type=MESH)

    pl.semaphore_wait(round_z, 2)
    for r in sorted(far_first(H_BITS), key=lambda r: r < hn // 2):
        hs[r] = packed[r * width:(r + 1) * width]
        h_copy(r).start()
    hs[0] = packed[0:width]
    store.wait()
    for copy in sent2:
        copy.wait_send()
    every(rkr, (rk_s, rk_r)).wait_send()
    every(crv, (g_s, g_r)).wait_send()
    every(hr, (h_s, h_r)).wait_send()
    every(hr, (h_s, h_r)).wait_recv()
    final = hs[0]
    for r in range(1, hn):
        final += hr[r]
    f_out[0:width, :] = final


def finish(own, width, v_in, f_in, v_out, cm_hbm, cr_hbm, ft, cm_out, cr_out, sem):
    stores = [pltpu.make_async_copy(src, dst, sem.at[i]) for i, (src, dst) in enumerate((
        (v_in, v_out), (cm_out, cm_hbm), (cr_out, cr_hbm)))]
    stores[0].start()
    ft[0:16, :] = f_in[...]
    turned = ft[...].T
    lane = lax.broadcasted_iota(I32, (32, 128), 1)
    done = jnp.zeros((32, 128), F32)
    for q in range(4):
        part = turned[32 * q:32 * q + 32]
        here = (lane >= q * width) & (lane < (q + 1) * width)
        done = jnp.where(here, pltpu.roll(part, q * width, 1) if q else part, done)
    for pz, px, base in (
        (1, 1, 0), (1, 2, 3), (2, 1, 8), (2, 2, 11), (0, 1, 16), (0, 2, 19), (1, 0, 24), (2, 0, 27)):
        k = 9 * pz + 3 * px
        cm_out[k:k + 3, :] = done[base:base + 3, 0:own]
    cm_out[0:2, :] = done[30:32, 0:own]
    cm_out[2:3, :] = done[7:8, 0:own]
    cr_out[...] = done[6:7, 0:own]
    stores[1].start()
    stores[2].start()
    for store in stores:
        store.wait()


def per_device(sizes, basis_init, permeability, accumulation, pressure, source, support, block_of, curve_rank):
    lx, plane = sizes
    gn, hn = 2 ** len(G_BITS), 2 ** len(H_BITS)
    devices = lx * plane
    own = (curve_rank.shape[0] + devices - 1) // devices
    width = (own + 3) // 4
    flat = lambda v: v.reshape(v.shape[:-3] + (128, 128))
    t_rows = -(-curve_rank.shape[0] // 2048) * 16
    anywhere = pl.BlockSpec(memory_space=pl.ANY)
    vmem = pl.BlockSpec(memory_space=pltpu.VMEM)
    dma = pltpu.SemaphoreType.DMA
    cells = lambda *lead: pltpu.VMEM(lead + (128, 128), F32)
    basis, rows = pl.pallas_call(
        functools.partial(kernel, (lx, plane, own, width)),
        out_shape=(
            jax.ShapeDtypeStruct((8, 128, 128), F32),
            jax.ShapeDtypeStruct((16, 128), F32),
        ),
        in_specs=[anywhere] * 8,
        out_specs=(anywhere, vmem),
        scratch_shapes=[
            cells(8), pltpu.VMEM((8, 128, 128), I32), cells(), cells(), cells(),
            pltpu.VMEM((3, 8, 128), I32), pltpu.VMEM(curve_rank.shape, I32), pltpu.VMEM((t_rows, 128), I32),
            cells(9), cells(8), cells(8), cells(8), cells(12),
            pltpu.VMEM((2, 8, 128), F32), cells(10), pltpu.VMEM((4, 8, 128), F32),
            pltpu.VMEM((9, 32, 128), F32), cells(4),
            pltpu.VMEM((2, 5, 16, 128), F32), pltpu.VMEM((2, 5, 16, 128), F32), pltpu.VMEM((2, 5, 8, 128), F32),
            pltpu.VMEM((2, 4, 16, 128), F32), pltpu.VMEM((2, 4, 16, 128), F32), pltpu.VMEM((2, 4, 8, 128), F32),
            pltpu.VMEM((1, 128), I32), pltpu.VMEM((gn, 1, 128), I32),
            pltpu.VMEM((128, 128), I32), pltpu.VMEM((gn * 128, 640), BF16),
            pltpu.VMEM((64, gn * 128), BF16), pltpu.VMEM((4, 128, 128), F32),
            pltpu.VMEM((13, 128), F32), pltpu.VMEM((gn, 13, 128), F32),
            pltpu.VMEM((hn, width, 128), F32), pltpu.VMEM((hn, width, 128), F32),
            pltpu.SemaphoreType.REGULAR, pltpu.SemaphoreType.REGULAR, dma((12,)), dma((1,)), dma((4,)), dma((4,)),
            dma, dma, dma, dma, dma, dma,
        ],
        compiler_params=pltpu.CompilerParams(
            collective_id=0, has_side_effects=True, vmem_limit_bytes=VMEM_GRANT),
        cost_estimate=pl.CostEstimate(flops=20_000_000, bytes_accessed=2_000_000, transcendentals=0),
    )(*(pltpu.with_memory_space_constraint(v, pltpu.HBM) for v in (
        flat(basis_init), flat(permeability), flat(accumulation), flat(pressure), flat(source),
        flat(support), flat(block_of), curve_rank,
    )))
    basis, matrix, residual = pl.pallas_call(
        functools.partial(finish, own, width),
        out_shape=(
            jax.ShapeDtypeStruct((8, 128, 128), F32),
            jax.ShapeDtypeStruct((27, own), F32),
            jax.ShapeDtypeStruct((1, own), F32),
        ),
        in_specs=[anywhere, vmem],
        out_specs=(anywhere, anywhere, anywhere),
        scratch_shapes=[cells(), pltpu.VMEM((27, own), F32), pltpu.VMEM((1, own), F32), dma((3,))],
        compiler_params=pltpu.CompilerParams(vmem_limit_bytes=VMEM_GRANT),
    )(basis, rows)
    return basis.reshape(basis_init.shape), matrix, residual.reshape(own)


def solution(mesh):
    return jax.shard_map(
        functools.partial(per_device, (mesh.shape["layer"], mesh.shape["plane"])),
        mesh=mesh,
        in_specs=(
            P(None, "layer", "plane", None),
            P("layer", "plane", None),
            P("layer", "plane", None),
            P("layer", "plane", None),
            P("layer", "plane", None),
            P(None, "layer", "plane", None),
            P("layer", "plane", None),
            P(),
        ),
        out_specs=(
            P(None, "layer", "plane", None),
            P(None, ("layer", "plane")),
            P(("layer", "plane")),
        ),
        check_vma=False,
    )
```

```python
import functools

import jax
import jax.numpy as jnp
from jax import lax
from jax.experimental import pallas as pl
from jax.experimental.pallas import tpu as pltpu
from jax.sharding import PartitionSpec as P

MESH = pl.DeviceIdType.MESH
F32, BF16, I32 = jnp.float32, jnp.bfloat16, jnp.int32

G_BITS = (("layer", 1), ("layer", 2), ("plane", 16), ("plane", 32))
H_BITS = (("plane", 1), ("plane", 2), ("plane", 4), ("plane", 8))
VMEM_GRANT = 32 * 1024 * 1024
THIRD, TWO_THIRDS = 1.0 / 3.0, 2.0 / 3.0
B0 = (0, 1, 4, 5)
A0 = (0, 1, 2, 3)
TYM, TYP, TYM1, TYP1, TXM, TXP, TZM, TZP, TZM1, TZP1, TXB, RD = range(12)


def roll_x(v, shift):
    rows = v.shape[0]
    return pltpu.roll(v.reshape(rows // 8, 8, 128), shift, 1).reshape(rows, 128)


def roll_y(v, shift):
    return pltpu.roll(v, shift, 1)


def harmonic(k, n):
    return 2.0 * k * n / (k + n)


def plane_sum(v):
    return v.reshape(-1, 8, 128).sum(axis=0)


def far_first(bits):
    def hops(r):
        reach = {"layer": 0, "y": 0, "z": 0}
        for i, (axis, bit) in enumerate(bits):
            if (r >> i) & 1:
                kind, step = (axis, bit) if axis == "layer" else ("y", bit // 16) if bit >= 16 else ("z", bit // 2)
                reach[kind] += step
        return sum(min(n, size - n) for n, size in ((reach["layer"], 4), (reach["y"], 4), (reach["z"], 8)))

    return sorted(range(1, 2 ** len(bits)), key=lambda r: -hops(r))


def kernel(
    dims,
    bi_hbm, k_hbm, a_hbm, p_hbm, s_hbm, sup_hbm, blk_hbm, cr_hbm,
    v_out, f_out,
    bi, sup, aa, pp, ss, blk, cr1, tab,
    va, vb, sf, nn, tc, tzb, ec, sw, fl, hx, hxs, hxr, hzr, hxs2, hxr2, hzr2,
    rks, rkr, rkt, oh, xb, es, cs, crv, hs, hr,
    round_y, round_z, in_sem, out_sem, halo_s, halo_r, rk_s, rk_r, g_s, g_r, h_s, h_r,
):
    lx, plane, own, width = dims
    gn, hn = 2 ** len(G_BITS), 2 ** len(H_BITS)
    zc = hn // 2
    n_idx = hn * width
    ml, mp = lax.axis_index("layer"), lax.axis_index("plane")

    def flips(bits):
        steps = []
        for axis, bit in bits:
            at = ml if axis == "layer" else mp
            steps.append((axis == "layer", bit * (1 - 2 * ((at // bit) % 2))))
        return steps

    g_flips, h_flips = flips(G_BITS), flips(H_BITS)

    def partner(steps, r):
        to_l, to_p = ml, mp
        for i, (on_layer, step) in enumerate(steps):
            if (r >> i) & 1:
                to_l, to_p = (to_l + step, to_p) if on_layer else (to_l, to_p + step)
        return (to_l, to_p)

    up_x, down_x = (ml, (mp + 1) % plane), (ml, (mp + plane - 1) % plane)
    up_z, down_z = ((ml + 1) % lx, mp), ((ml + lx - 1) % lx, mp)

    def loop(n, body, start=0):
        for i in range(start, n):
            body(i)

    def group(g):
        return slice(g * 32, g * 32 + 32)

    def one_plane(z):
        return slice(z * 8, z * 8 + 8)

    loads = [
        pltpu.make_async_copy(k_hbm, va.at[0], in_sem.at[0]),
        pltpu.make_async_copy(bi_hbm.at[:, pl.ds(0, 64)], bi.at[:, pl.ds(0, 64)], in_sem.at[1]),
        pltpu.make_async_copy(sup_hbm.at[:, pl.ds(0, 64)], sup.at[:, pl.ds(0, 64)], in_sem.at[2]),
        pltpu.make_async_copy(bi_hbm.at[:, pl.ds(64, 64)], bi.at[:, pl.ds(64, 64)], in_sem.at[10]),
        pltpu.make_async_copy(sup_hbm.at[:, pl.ds(64, 64)], sup.at[:, pl.ds(64, 64)], in_sem.at[11]),
        pltpu.make_async_copy(a_hbm, aa, in_sem.at[3]),
        pltpu.make_async_copy(cr_hbm, cr1, in_sem.at[4]),
        pltpu.make_async_copy(p_hbm, pp, in_sem.at[5]),
        pltpu.make_async_copy(s_hbm, ss, in_sem.at[6]),
    ]
    for j, z in enumerate((0, 4, 12)):
        loads.append(pltpu.make_async_copy(blk_hbm.at[pl.ds(8 * z, 8)], blk.at[j], in_sem.at[7 + j]))
    barrier = pltpu.get_barrier_semaphore()

    def greet(who):
        pl.semaphore_signal(barrier, inc=1, device_id=who, device_id_type=MESH)

    def along_z(dz, dc):
        return (ml, mp + dc * (1 - 2 * (mp % 2)) + 2 * ((mp // 2 + dz) % zc - (mp // 2) % zc))

    x_mask = sum(1 << i for i, (axis, _) in enumerate(G_BITS) if axis == "layer")
    x_peers = [r for r in range(1, gn) if r & x_mask == r]
    y_peers = [r for r in range(1, gn) if r & x_mask == 0]
    z_peers = [(dz, dc) for dz in (1, zc - 1, 2, zc - 2) for dc in (0, 1)] + [(0, 1)]
    greet(up_x)
    greet(down_x)
    for r in x_peers:
        greet(partner(g_flips, r))
    for load in loads[:5]:
        load.start()
    for r in y_peers:
        greet(partner(g_flips, r))
    for dz, dc in z_peers:
        greet(along_z(dz, dc))
    for load in loads[5:]:
        load.start()
    greeted = 2 + len(x_peers) + len(y_peers) + len(z_peers)

    def second_round():
        for r in y_peers:
            pl.semaphore_signal(round_y, inc=1, device_id=partner(g_flips, r), device_id_type=MESH)
        for dz in (2, zc - 2):
            pl.semaphore_signal(round_z, inc=1, device_id=along_z(dz, 0), device_id_type=MESH)

    lane = lax.broadcasted_iota(I32, (32, 128), 1)
    m, x = lane % 8, lax.broadcasted_iota(I32, (32, 128), 0) % 8
    m1, x1 = m[:8], x[:8]
    lane1, row1 = lane[:8], x[:8]
    is_m = {i: m == i for i in (0, 3, 4, 7)}
    is_x = {i: x == i for i in (3, 4)}

    hx[...] = jnp.zeros_like(hx)
    tc[TXB] = jnp.zeros((128, 128), F32)

    loads[0].wait()

    def faces(g):
        rows, below = group(g), one_plane((4 * g + 15) % 16)
        k = va[0, rows, :]
        tym = jnp.where(lane == 0, 0.0, harmonic(k, roll_y(k, 1)))
        typ = roll_y(tym, 127)
        tc[TYM, rows, :] = tym
        tc[TYP, rows, :] = typ
        tc[TYM1, rows, :] = jnp.where(is_m[4], 0.0, tym)
        tc[TYP1, rows, :] = jnp.where(is_m[3], 0.0, typ)
        txm = jnp.where(x == 0, 0.0, harmonic(k, roll_x(k, 1)))
        tc[TXM, rows, :] = txm
        tc[TXP, rows, :] = roll_x(txm, 7)
        tz = harmonic(k, jnp.concatenate([va[0, below, :], k[0:24]], axis=0))
        tc[TZM, rows, :] = tz
        tc[TZP, below, :] = tz[0:8]
        tc[TZP, slice(g * 32, g * 32 + 24), :] = tz[8:32]
        tc[TZM1, rows, :] = tz
        tc[TZP1, below, :] = tz[0:8]
        tc[TZP1, slice(g * 32, g * 32 + 24), :] = tz[8:32]

    loop(4, faces)
    nil = jnp.zeros((8, 128), F32)
    tc[TZM, 0:8, :] = nil
    tc[TZP, 120:128, :] = nil
    tc[TZM1, 0:8, :] = nil
    tc[TZP1, 120:128, :] = nil
    tc[TZM1, 64:72, :] = nil
    tc[TZP1, 56:64, :] = nil
    for i, (t, z) in enumerate(((TZP, 3), (TZM, 4), (TZP, 11), (TZM, 12))):
        sw[i] = tc[t, 8 * z:8 * z + 8, :]

    loads[1].wait()
    loads[2].wait()

    def first(g):
        rows = group(g)
        vals = []
        for s in range(8):
            on = sup[s, rows, :].astype(F32)
            sf[s, rows, :] = on
            vals.append(bi[s, rows, :] * on)
        inv = 1.0 / sum(vals[1:], vals[0])
        for s in range(8):
            va[1 + s, rows, :] = vals[s] * inv

    loop(2, first)
    loads[3].wait()
    loads[4].wait()
    loop(4, first, 2)

    def exchange(v, off, xs_buf, xr_buf, zr_buf, base):
        for i, s in enumerate(B0):
            xs_buf[0, off + i] = v[off + s, pl.ds(0, 16, stride=8), :]
            xs_buf[1, off + i] = v[off + s, pl.ds(7, 16, stride=8), :]
        if off:
            xs_buf[0, 0] = v[0, pl.ds(0, 16, stride=8), :]
            xs_buf[1, 0] = v[0, pl.ds(7, 16, stride=8), :]
            pl.semaphore_wait(barrier, greeted)
        last, lead = v.at[pl.ds(0, off + 4), pl.ds(120, 8)], v.at[pl.ds(0, off + 4), pl.ds(0, 8)]
        copies = []
        for j, (src, dst, who) in enumerate((
            (xs_buf.at[1], xr_buf.at[0], up_x), (xs_buf.at[0], xr_buf.at[1], down_x),
            (last, zr_buf.at[0], up_z), (lead, zr_buf.at[1], down_z),
        )):
            copies.append(pltpu.make_async_remote_copy(
                src_ref=src, dst_ref=dst, send_sem=halo_s.at[base + j // 2], recv_sem=halo_r.at[base + j // 2],
                device_id=who, device_id_type=MESH))
        for copy in copies:
            copy.start()
        if off:
            second_round()
        return [pltpu.make_async_remote_copy(
            src_ref=buf, dst_ref=buf, send_sem=halo_s.at[base + j], recv_sem=halo_r.at[base + j],
            device_id=up_x, device_id_type=MESH) for j, buf in enumerate((xr_buf, zr_buf))]

    def inner(v, off):
        def part(g):
            rows = group(g)
            odd = g % 2
            below, above = one_plane((4 * g + 15) % 16), one_plane((4 * g + 4) % 16)
            for s in range(8):
                if s % 4 == 0:
                    vals = [v[off + s + i, rows, :] for i in range(4)]
                    txm, txp = tc[TXM, rows, :], tc[TXP, rows, :]
                    tym, typ = [tc[i, rows, :] for i in (TYM, TYM1)], [tc[i, rows, :] for i in (TYP, TYP1)]
                    zm, zp = tc[TZM1 if s else TZM, rows, :], tc[TZP1 if s else TZP, rows, :]
                here, by_y, by_x, turn = vals[s % 4], vals[s % 4 ^ 1], vals[s % 4 ^ 2], 4 - (s & 4) * 2
                near = tym[s & 1] * roll_y(jnp.where(is_m[7], by_y, here), 1)
                near += typ[s & 1] * roll_y(jnp.where(is_m[0], by_y, here), 127)
                near += txm * roll_x(jnp.where(is_x[3], by_x, here), 1)
                near += txp * roll_x(jnp.where(is_x[4], by_x, here), 7)
                lo, hi = v[off + s + turn * odd, below, :], v[off + s + turn * (1 - odd), above, :]
                near += zm * jnp.concatenate([lo, here[0:24]], axis=0)
                near += zp * jnp.concatenate([here[8:32], hi], axis=0)
                nn[s, rows, :] = near

        loop(4, part)

    def outer(v, off, new, off2, xr_buf, zr_buf, extra):
        for i in range(4):
            hx[i, pl.ds(0, 16, stride=8), :] = xr_buf[0, extra + i]
            hx[i, pl.ds(7, 16, stride=8), :] = xr_buf[1, extra + i]
            nn[i, 0:8, :] += tzb[0] * zr_buf[0, extra + i]
            nn[i, 120:128, :] += tzb[1] * zr_buf[1, extra + i]

        def part(g):
            rows = group(g)
            rd, txb = tc[RD, rows, :], tc[TXB, rows, :]
            vals = []
            for s in range(8):
                near = nn[s, rows, :]
                if s in B0:
                    near += txb * hx[B0.index(s), rows, :]
                vals.append((v[off + s, rows, :] * THIRD + rd * near) * sf[s, rows, :])
            inv = 1.0 / sum(vals[1:], vals[0])
            for s in range(8):
                new[off2 + s, rows, :] = vals[s] * inv

        loop(4, part)

    sent = exchange(va, 1, hxs, hxr, hzr, 0)
    inner(va, 1)

    for load in loads[5:]:
        load.wait()
    label = blk[0, 0:1, :]
    for u, (j, r) in enumerate(((0, 0), (0, 4), (1, 0), (1, 4), (2, 0), (2, 4), (1, 0), (1, 4))):
        label = jnp.where(m1[0:1] == u, blk[j, r:r + 1, :], label)
    t_rows, labels = tab.shape[0], cr1.shape[0]
    tab[labels // 128:, :] = jnp.zeros((t_rows - labels // 128, 128), I32)

    def table(t):
        tab[t:t + 1, :] = cr1[pl.ds(t * 128, 128)].reshape(1, 128)

    loop(labels // 128, table)
    if labels % 128:
        t = labels // 128
        tab[t:t + 1, 0:labels % 128] = cr1[pl.ds(t * 128, labels % 128)].reshape(1, labels % 128)
    l_hi, l_lo = label >> 7, label & 127
    w_iota = lax.broadcasted_iota(I32, (128, 128), 0)
    pick = jnp.where(w_iota == l_lo, 1.0, 0.0).astype(BF16)
    ranks = tab[...]
    parts = jnp.concatenate([(ranks >> 7).astype(F32), (ranks & 127).astype(F32)], axis=0).astype(BF16)
    looked = jnp.dot(parts, pick, preferred_element_type=F32)
    t_iota = lax.broadcasted_iota(I32, (t_rows, 128), 0)
    looked = looked[:t_rows] * 128.0 + looked[t_rows:]
    rank = jnp.sum(jnp.where(t_iota == l_hi, looked, 0.0), axis=0, keepdims=True)
    rank = rank.astype(I32)
    rks[...] = rank
    rkr[0] = rank

    def diagonal(g):
        rows = group(g)
        diag = aa[rows, :]
        for t in (TYM, TYP, TXM, TXP, TZM, TZP):
            diag += tc[t, rows, :]
        tc[RD, rows, :] = diag

    loop(4, diagonal)

    def every(buf, sems):
        return pltpu.make_async_remote_copy(
            src_ref=buf.at[pl.ds(1, buf.shape[0] - 1)], dst_ref=buf.at[pl.ds(1, buf.shape[0] - 1)],
            send_sem=sems[0], recv_sem=sems[1], device_id=partner(g_flips, 1), device_id_type=MESH)

    def rank_copy(r):
        return pltpu.make_async_remote_copy(
            src_ref=rks, dst_ref=rkr.at[r], send_sem=rk_s, recv_sem=rk_r,
            device_id=partner(g_flips, r), device_id_type=MESH)

    for copy in sent:
        copy.wait_recv()

    tc[TXB, pl.ds(0, 16, stride=8), :] = jnp.where(mp > 0, harmonic(hxs[0, 0], hxr[0, 0]), 0.0)
    tc[TXB, pl.ds(7, 16, stride=8), :] = jnp.where(mp < plane - 1, harmonic(hxs[1, 0], hxr[1, 0]), 0.0)
    tzb[0] = jnp.where(ml > 0, harmonic(va[0, 0:8, :], hzr[0, 0]), 0.0)
    tzb[1] = jnp.where(ml < lx - 1, harmonic(va[0, 120:128, :], hzr[1, 0]), 0.0)

    tc[RD, 0:8, :] += tzb[0]
    tc[RD, 120:128, :] += tzb[1]
    tc[RD] = TWO_THIRDS / (tc[RD] + tc[TXB])

    outer(va, 1, vb, 0, hxr, hzr, 1)
    sent2 = exchange(vb, 0, hxs2, hxr2, hzr2, 2)

    es[...] = jnp.zeros_like(es)

    inner(vb, 0)
    pl.semaphore_wait(round_y, len(y_peers))
    loop(gn, lambda r: rank_copy(r).start(), 1)

    def weigh(g):
        rows = group(g)
        tym, typ, txm, txp = (tc[i, rows, :] for i in (TYM, TYP, TXM, TXP))
        sx0 = jnp.where(is_x[3], txp, 0.0) + jnp.where(is_x[4], txm, 0.0)
        sx1 = sx0 + tc[TXB, rows, :]
        sy0 = jnp.where(is_m[7], typ, 0.0) + jnp.where(is_m[0], tym, 0.0)
        sy1 = sy0 + jnp.where(is_m[3], typ, 0.0) + jnp.where(is_m[4], tym, 0.0)
        for s in range(4):
            d = aa[rows, :] + (sx1 if s & 2 else sx0) + (sy1 if s & 1 else sy0)
            ec[s, rows, :] = d
            ec[4 + s, rows, :] = d
        ec[8, rows, :] = sx0
        ec[9, rows, :] = sy0

    loop(4, weigh)
    for i, z in enumerate((3, 4, 11, 12)):
        for s in range(8):
            ec[s, 8 * z:8 * z + 8, :] += sw[i]
    for t, z in ((tzb[0], 0), (tc[TZP, 56:64, :], 7), (tc[TZM, 64:72, :], 8), (tzb[1], 15)):
        for s in range(4, 8):
            ec[s, 8 * z:8 * z + 8, :] += t

    def x_swap(q):
        return roll_x(q, 4)

    def y_swap(q):
        return jnp.where(m1 == 7, roll_y(q, 127), jnp.where(m1 == 0, roll_y(q, 1), 0.0))

    def far(g):
        return one_plane(4 * g + 4 - 5 * (g % 2))

    def rest(g):
        rows = group(g)
        here = pp[rows, :]
        full = plane_sum(ec[0, rows, :] * here - ss[rows, :]) - sw[g] * pp[far(g), :]
        fl[8, one_plane(g), :] = (
            full - x_swap(plane_sum(ec[8, rows, :] * here)) - y_swap(plane_sum(ec[9, rows, :] * here)))

    loop(4, rest)

    for copy in sent2:
        copy.wait_recv()
    for copy in sent:
        copy.wait_send()
    outer(vb, 0, va, 1, hxr2, hzr2, 0)
    store = pltpu.make_async_copy(va.at[pl.ds(1, 8)], v_out, out_sem.at[0])

    def gather(g):
        rows = group(g)
        sx0, sy0 = ec[8, rows, :], ec[9, rows, :]
        vals = [va[1 + s, rows, :] for s in range(8)]
        qx = [x_swap(plane_sum(sx0 * v)) for v in vals]
        qy = [y_swap(plane_sum(sy0 * v)) for v in vals]
        for s in range(8):
            full = plane_sum(ec[s, rows, :] * vals[s]) - sw[g] * va[1 + (s ^ 4), far(g), :]
            fl[s, one_plane(g), :] = full - qx[s ^ 2] - qy[s ^ 1]

    loop(4, gather)

    def z_part(j, pz, s):
        groups = ((0,), (1, 2), (3,))[j] if pz == 1 else {(1, 0): (1,), (2, 0): (3,), (0, 2): (0,), (1, 2): (2,)}[j, pz]
        term = fl[s, one_plane(groups[0]), :]
        for g in groups[1:]:
            term += fl[s, one_plane(g), :]
        return term

    for k, (j, halves) in enumerate(((0, (1, 2)), (1, (1, 2)), (2, (1, 0)), (1, (0,)))):
        for half, pz in enumerate(halves):
            for b in range(2):
                at, s = 64 * half + 24 * b, (0 if pz == 1 else 4) + 2 * b
                side = z_part(j, pz, s + 1)
                es[k, at:at + 8, :] = jnp.where(m1 < 4, side, 0.0)
                es[k, at + 8:at + 16, :] = z_part(j, pz, s)
                es[k, at + 16:at + 24, :] = jnp.where(m1 < 4, 0.0, side)
        if k < 3:
            es[k, 48:56, :] = -z_part(j, 1, 8)

    m16 = m[:16]
    sums = []
    for k in range(4):
        for xi in range(2):
            t = es[k, pl.ds(4 * xi, 16, stride=8), :]
            for i in range(1, 4):
                t += es[k, pl.ds(4 * xi + i, 16, stride=8), :]
            sums.append(t)
    for bit in (4, 2, 1):
        high = (m16 & bit) != 0
        merged = []
        for u in range(bit):
            one, two = sums[u], sums[u + bit]
            move = jnp.where(high, one, two)
            merged.append(jnp.where(high, two, one) + jnp.where(high, roll_y(move, bit), roll_y(move, 128 - bit)))
        sums = merged
    rows_out = sums[0]
    second = pltpu.roll(rows_out[8:16], 7, 0)
    for buf in (cs, crv.at[0]):
        buf[0:8, :] = jnp.where(x1 == 7, second, rows_out[0:8])
        buf[8:13, :] = second[0:5]

    def g_copy(r):
        return pltpu.make_async_remote_copy(
            src_ref=cs, dst_ref=crv.at[r], send_sem=g_s, recv_sem=g_r,
            device_id=partner(g_flips, r), device_id_type=MESH)

    for r in far_first(G_BITS):
        g_copy(r).start()
    store.start()

    def wanted(t):
        q, idx = (t, lane1) if t < 4 else (lane1 >> 5, 128 + (lane1 & 31))
        peer = jnp.zeros_like(idx)
        for p in range(1, hn):
            peer += jnp.where(idx >= p * width, 1, 0)
        col = idx - peer * width + q * width
        dev = jnp.zeros_like(idx) + (ml * plane + mp)
        for b, (on_layer, step) in enumerate(h_flips):
            dev += ((peer >> b) & 1) * (step * plane if on_layer else step)
        return jnp.where((col < own) & (idx < n_idx), dev * own + col, -7)

    wants = [wanted(t) for t in range(5)]
    every(rkr, (rk_s, rk_r)).wait_recv()
    turned = jnp.concatenate([rkr[r] for r in range(gn)] + [jnp.zeros((128 - gn, 128), I32)], axis=0).astype(F32).T
    rkt[...] = turned.astype(I32)
    for r in range(gn):
        have = jnp.broadcast_to(rkt[:, r:r + 1], (128, 128))
        for t in range(5):
            want = jnp.concatenate([wants[t]] * 16, axis=0)
            oh[128 * r:128 * r + 128, 128 * t:128 * t + 128] = jnp.where(have == want, 1.0, 0.0).astype(BF16)

    odd = m1 % 2 == 1
    b1 = (x1 >= 3) & (x1 < 6)
    b1_odd = b1 & odd

    def spread(r):
        got1, got2 = crv[r, 0:8, :], pltpu.roll(crv[r, 5:13, :], 6, 0)
        pz1 = jnp.where((m1 < 6) & (x1 < 7), got1, 0.0)
        pz2 = jnp.where(m1 < 4, got2, 0.0)
        pz0 = jnp.where(m1 < 4, 0.0, jnp.where(m1 < 6, got2, got1))
        low1, low2, low0 = (jnp.where(b1_odd, v, 0.0) for v in (pz1, pz2, pz0))
        last = pltpu.roll(low1, 5, 0) + low2 + jnp.where(x1 >= 6, pltpu.roll(low0, 3, 0), 0.0)
        vals = jnp.concatenate([
            pz1 - low1 + jnp.where(x1 == 7, pltpu.roll(low0, 2, 0), 0.0), pz2 - low2, pz0 - low0, last], axis=0)
        high = vals.astype(BF16)
        lanes = slice(128 * r, 128 * r + 128)
        xb[0:32, lanes] = high
        xb[32:64, lanes] = (vals - high.astype(F32)).astype(BF16)

    every(crv, (g_s, g_r)).wait_recv()
    loop(gn, spread)
    routed = jnp.dot(xb[...], oh[...], preferred_element_type=F32)
    both = routed[0:32] + routed[32:64]
    parts = [both[:, 128 * q:128 * q + 128] for q in range(4)]
    over = both[:, 512:640]
    packed = jnp.concatenate([
        jnp.concatenate(parts, axis=0).T,
        jnp.concatenate([roll_y(over, (128 - 32 * q) % 128) if q else over for q in range(4)], axis=0).T], axis=0)

    def h_copy(r):
        return pltpu.make_async_remote_copy(
            src_ref=hs.at[r], dst_ref=hr.at[r], send_sem=h_s, recv_sem=h_r,
            device_id=partner(h_flips, r), device_id_type=MESH)

    pl.semaphore_wait(round_z, 2)
    for r in sorted(far_first(H_BITS), key=lambda r: r < hn // 2):
        hs[r] = packed[r * width:(r + 1) * width]
        h_copy(r).start()
    hs[0] = packed[0:width]
    store.wait()
    for copy in sent2:
        copy.wait_send()
    every(rkr, (rk_s, rk_r)).wait_send()
    every(crv, (g_s, g_r)).wait_send()
    every(hr, (h_s, h_r)).wait_send()
    every(hr, (h_s, h_r)).wait_recv()
    final = hs[0]
    for r in range(1, hn):
        final += hr[r]
    f_out[0:width, :] = final


def finish(own, width, v_in, f_in, v_out, cm_hbm, cr_hbm, ft, cm_out, cr_out, sem):
    stores = [pltpu.make_async_copy(src, dst, sem.at[i]) for i, (src, dst) in enumerate((
        (v_in, v_out), (cm_out, cm_hbm), (cr_out, cr_hbm)))]
    stores[0].start()
    ft[0:16, :] = f_in[...]
    turned = ft[...].T
    lane = lax.broadcasted_iota(I32, (32, 128), 1)
    done = jnp.zeros((32, 128), F32)
    for q in range(4):
        part = turned[32 * q:32 * q + 32]
        here = (lane >= q * width) & (lane < (q + 1) * width)
        done = jnp.where(here, pltpu.roll(part, q * width, 1) if q else part, done)
    for pz, px, base in (
        (1, 1, 0), (1, 2, 3), (2, 1, 8), (2, 2, 11), (0, 1, 16), (0, 2, 19), (1, 0, 24), (2, 0, 27)):
        k = 9 * pz + 3 * px
        cm_out[k:k + 3, :] = done[base:base + 3, 0:own]
    cm_out[0:2, :] = done[30:32, 0:own]
    cm_out[2:3, :] = done[7:8, 0:own]
    cr_out[...] = done[6:7, 0:own]
    stores[1].start()
    stores[2].start()
    for store in stores:
        store.wait()


def per_device(sizes, basis_init, permeability, accumulation, pressure, source, support, block_of, curve_rank):
    lx, plane = sizes
    gn, hn = 2 ** len(G_BITS), 2 ** len(H_BITS)
    devices = lx * plane
    own = (curve_rank.shape[0] + devices - 1) // devices
    width = (own + 3) // 4
    flat = lambda v: v.reshape(v.shape[:-3] + (128, 128))
    t_rows = -(-curve_rank.shape[0] // 2048) * 16
    anywhere = pl.BlockSpec(memory_space=pl.ANY)
    vmem = pl.BlockSpec(memory_space=pltpu.VMEM)
    dma = pltpu.SemaphoreType.DMA
    cells = lambda *lead: pltpu.VMEM(lead + (128, 128), F32)
    basis, rows = pl.pallas_call(
        functools.partial(kernel, (lx, plane, own, width)),
        out_shape=(
            jax.ShapeDtypeStruct((8, 128, 128), F32),
            jax.ShapeDtypeStruct((16, 128), F32),
        ),
        in_specs=[anywhere] * 8,
        out_specs=(anywhere, vmem),
        scratch_shapes=[
            cells(8), pltpu.VMEM((8, 128, 128), I32), cells(), cells(), cells(),
            pltpu.VMEM((3, 8, 128), I32), pltpu.VMEM(curve_rank.shape, I32), pltpu.VMEM((t_rows, 128), I32),
            cells(9), cells(8), cells(8), cells(8), cells(12),
            pltpu.VMEM((2, 8, 128), F32), cells(10), pltpu.VMEM((4, 8, 128), F32),
            pltpu.VMEM((9, 32, 128), F32), cells(4),
            pltpu.VMEM((2, 5, 16, 128), F32), pltpu.VMEM((2, 5, 16, 128), F32), pltpu.VMEM((2, 5, 8, 128), F32),
            pltpu.VMEM((2, 4, 16, 128), F32), pltpu.VMEM((2, 4, 16, 128), F32), pltpu.VMEM((2, 4, 8, 128), F32),
            pltpu.VMEM((1, 128), I32), pltpu.VMEM((gn, 1, 128), I32),
            pltpu.VMEM((128, 128), I32), pltpu.VMEM((gn * 128, 640), BF16),
            pltpu.VMEM((64, gn * 128), BF16), pltpu.VMEM((4, 128, 128), F32),
            pltpu.VMEM((13, 128), F32), pltpu.VMEM((gn, 13, 128), F32),
            pltpu.VMEM((hn, width, 128), F32), pltpu.VMEM((hn, width, 128), F32),
            pltpu.SemaphoreType.REGULAR, pltpu.SemaphoreType.REGULAR, dma((12,)), dma((1,)), dma((4,)), dma((4,)),
            dma, dma, dma, dma, dma, dma,
        ],
        compiler_params=pltpu.CompilerParams(
            collective_id=0, has_side_effects=True, vmem_limit_bytes=VMEM_GRANT),
        cost_estimate=pl.CostEstimate(flops=20_000_000, bytes_accessed=2_000_000, transcendentals=0),
    )(*(pltpu.with_memory_space_constraint(v, pltpu.HBM) for v in (
        flat(basis_init), flat(permeability), flat(accumulation), flat(pressure), flat(source),
        flat(support), flat(block_of), curve_rank,
    )))
    basis, matrix, residual = pl.pallas_call(
        functools.partial(finish, own, width),
        out_shape=(
            jax.ShapeDtypeStruct((8, 128, 128), F32),
            jax.ShapeDtypeStruct((27, own), F32),
            jax.ShapeDtypeStruct((1, own), F32),
        ),
        in_specs=[anywhere, vmem],
        out_specs=(anywhere, anywhere, anywhere),
        scratch_shapes=[cells(), pltpu.VMEM((27, own), F32), pltpu.VMEM((1, own), F32), dma((3,))],
        compiler_params=pltpu.CompilerParams(vmem_limit_bytes=VMEM_GRANT),
    )(basis, rows)
    return basis.reshape(basis_init.shape), matrix, residual.reshape(own)


def solution(mesh):
    return jax.shard_map(
        functools.partial(per_device, (mesh.shape["layer"], mesh.shape["plane"])),
        mesh=mesh,
        in_specs=(
            P(None, "layer", "plane", None),
            P("layer", "plane", None),
            P("layer", "plane", None),
            P("layer", "plane", None),
            P("layer", "plane", None),
            P(None, "layer", "plane", None),
            P("layer", "plane", None),
            P(),
        ),
        out_specs=(
            P(None, "layer", "plane", None),
            P(None, ("layer", "plane")),
            P(("layer", "plane")),
        ),
        check_vma=False,
    )
```

```python
import functools

import jax
import jax.numpy as jnp
from jax import lax
from jax.experimental import pallas as pl
from jax.experimental.pallas import tpu as pltpu
from jax.sharding import PartitionSpec as P

MESH = pl.DeviceIdType.MESH
F32, BF16, I32 = jnp.float32, jnp.bfloat16, jnp.int32

G_BITS = (("layer", 1), ("layer", 2), ("plane", 16), ("plane", 32))
H_BITS = (("plane", 1), ("plane", 2), ("plane", 4), ("plane", 8))
VMEM_GRANT = 32 * 1024 * 1024
THIRD, TWO_THIRDS = 1.0 / 3.0, 2.0 / 3.0
B0 = (0, 1, 4, 5)
A0 = (0, 1, 2, 3)
TYM, TYP, TYM1, TYP1, TXM, TXP, TZM, TZP, TZM1, TZP1, TXB, RD = range(12)


def roll_x(v, shift):
    rows = v.shape[0]
    return pltpu.roll(v.reshape(rows // 8, 8, 128), shift, 1).reshape(rows, 128)


def roll_y(v, shift):
    return pltpu.roll(v, shift, 1)


def harmonic(k, n):
    return 2.0 * k * n / (k + n)


def plane_sum(v):
    return v.reshape(-1, 8, 128).sum(axis=0)


def far_first(bits):
    def hops(r):
        reach = {"layer": 0, "y": 0, "z": 0}
        for i, (axis, bit) in enumerate(bits):
            if (r >> i) & 1:
                kind, step = (axis, bit) if axis == "layer" else ("y", bit // 16) if bit >= 16 else ("z", bit // 2)
                reach[kind] += step
        return sum(min(n, size - n) for n, size in ((reach["layer"], 4), (reach["y"], 4), (reach["z"], 8)))

    return sorted(range(1, 2 ** len(bits)), key=lambda r: -hops(r))


def kernel(
    dims,
    bi_hbm, k_hbm, a_hbm, p_hbm, s_hbm, sup_hbm, blk_hbm, cr_hbm,
    v_out, f_out,
    bi, sup, aa, pp, ss, blk, cr1, tab,
    va, vb, sf, nn, tc, tzb, ec, sw, fl, hx, hxs, hxr, hzr, hxs2, hxr2, hzr2,
    rks, rkr, rkt, oh, xb, es, cs, crv, hs, hr,
    round_y, round_z, in_sem, out_sem, halo_s, halo_r, rk_s, rk_r, g_s, g_r, h_s, h_r,
):
    lx, plane, own, width = dims
    gn, hn = 2 ** len(G_BITS), 2 ** len(H_BITS)
    zc = hn // 2
    n_idx = hn * width
    ml, mp = lax.axis_index("layer"), lax.axis_index("plane")

    def flips(bits):
        steps = []
        for axis, bit in bits:
            at = ml if axis == "layer" else mp
            steps.append((axis == "layer", bit * (1 - 2 * ((at // bit) % 2))))
        return steps

    g_flips, h_flips = flips(G_BITS), flips(H_BITS)

    def partner(steps, r):
        to_l, to_p = ml, mp
        for i, (on_layer, step) in enumerate(steps):
            if (r >> i) & 1:
                to_l, to_p = (to_l + step, to_p) if on_layer else (to_l, to_p + step)
        return (to_l, to_p)

    up_x, down_x = (ml, (mp + 1) % plane), (ml, (mp + plane - 1) % plane)
    up_z, down_z = ((ml + 1) % lx, mp), ((ml + lx - 1) % lx, mp)

    def loop(n, body, start=0):
        for i in range(start, n):
            body(i)

    def group(g):
        return slice(g * 32, g * 32 + 32)

    def one_plane(z):
        return slice(z * 8, z * 8 + 8)

    loads = [
        pltpu.make_async_copy(k_hbm, va.at[0], in_sem.at[0]),
        pltpu.make_async_copy(bi_hbm.at[:, pl.ds(0, 64)], bi.at[:, pl.ds(0, 64)], in_sem.at[1]),
        pltpu.make_async_copy(sup_hbm.at[:, pl.ds(0, 64)], sup.at[:, pl.ds(0, 64)], in_sem.at[2]),
        pltpu.make_async_copy(bi_hbm.at[:, pl.ds(64, 64)], bi.at[:, pl.ds(64, 64)], in_sem.at[10]),
        pltpu.make_async_copy(sup_hbm.at[:, pl.ds(64, 64)], sup.at[:, pl.ds(64, 64)], in_sem.at[11]),
        pltpu.make_async_copy(a_hbm, aa, in_sem.at[3]),
        pltpu.make_async_copy(cr_hbm, cr1, in_sem.at[4]),
        pltpu.make_async_copy(p_hbm, pp, in_sem.at[5]),
        pltpu.make_async_copy(s_hbm, ss, in_sem.at[6]),
    ]
    for j, z in enumerate((0, 4, 12)):
        loads.append(pltpu.make_async_copy(blk_hbm.at[pl.ds(8 * z, 8)], blk.at[j], in_sem.at[7 + j]))
    barrier = pltpu.get_barrier_semaphore()

    def greet(who):
        pl.semaphore_signal(barrier, inc=1, device_id=who, device_id_type=MESH)

    def along_z(dz, dc):
        return (ml, mp + dc * (1 - 2 * (mp % 2)) + 2 * ((mp // 2 + dz) % zc - (mp // 2) % zc))

    x_mask = sum(1 << i for i, (axis, _) in enumerate(G_BITS) if axis == "layer")
    x_peers = [r for r in range(1, gn) if r & x_mask == r]
    y_peers = [r for r in range(1, gn) if r & x_mask == 0]
    z_peers = [(dz, dc) for dz in (1, zc - 1, 2, zc - 2) for dc in (0, 1)] + [(0, 1)]
    greet(up_x)
    greet(down_x)
    for dz, dc in z_peers[4:8]:
        greet(along_z(dz, dc))
    for peers in (x_peers, y_peers):
        for r in peers[1:2]:
            greet(partner(g_flips, r))
    for load in loads[:5]:
        load.start()
    for peers in (x_peers, y_peers):
        for r in peers[:1] + peers[2:]:
            greet(partner(g_flips, r))
    for dz, dc in z_peers[:4] + z_peers[8:]:
        greet(along_z(dz, dc))
    for load in loads[5:]:
        load.start()
    greeted = 2 + len(x_peers) + len(y_peers) + len(z_peers)

    def second_round():
        for r in y_peers:
            pl.semaphore_signal(round_y, inc=1, device_id=partner(g_flips, r), device_id_type=MESH)
        for dz in (2, zc - 2):
            pl.semaphore_signal(round_z, inc=1, device_id=along_z(dz, 0), device_id_type=MESH)

    lane = lax.broadcasted_iota(I32, (32, 128), 1)
    m, x = lane % 8, lax.broadcasted_iota(I32, (32, 128), 0) % 8
    m1, x1 = m[:8], x[:8]
    lane1, row1 = lane[:8], x[:8]
    is_m = {i: m == i for i in (0, 3, 4, 7)}
    is_x = {i: x == i for i in (3, 4)}

    hx[...] = jnp.zeros_like(hx)
    tc[TXB] = jnp.zeros((128, 128), F32)

    loads[0].wait()

    def faces(g):
        rows, below = group(g), one_plane((4 * g + 15) % 16)
        k = va[0, rows, :]
        tym = jnp.where(lane == 0, 0.0, harmonic(k, roll_y(k, 1)))
        typ = roll_y(tym, 127)
        tc[TYM, rows, :] = tym
        tc[TYP, rows, :] = typ
        tc[TYM1, rows, :] = jnp.where(is_m[4], 0.0, tym)
        tc[TYP1, rows, :] = jnp.where(is_m[3], 0.0, typ)
        txm = jnp.where(x == 0, 0.0, harmonic(k, roll_x(k, 1)))
        tc[TXM, rows, :] = txm
        tc[TXP, rows, :] = roll_x(txm, 7)
        tz = harmonic(k, jnp.concatenate([va[0, below, :], k[0:24]], axis=0))
        tc[TZM, rows, :] = tz
        tc[TZP, below, :] = tz[0:8]
        tc[TZP, slice(g * 32, g * 32 + 24), :] = tz[8:32]
        tc[TZM1, rows, :] = tz
        tc[TZP1, below, :] = tz[0:8]
        tc[TZP1, slice(g * 32, g * 32 + 24), :] = tz[8:32]

    loop(4, faces)
    nil = jnp.zeros((8, 128), F32)
    tc[TZM, 0:8, :] = nil
    tc[TZP, 120:128, :] = nil
    tc[TZM1, 0:8, :] = nil
    tc[TZP1, 120:128, :] = nil
    tc[TZM1, 64:72, :] = nil
    tc[TZP1, 56:64, :] = nil
    for i, (t, z) in enumerate(((TZP, 3), (TZM, 4), (TZP, 11), (TZM, 12))):
        sw[i] = tc[t, 8 * z:8 * z + 8, :]

    loads[1].wait()
    loads[2].wait()

    def first(g):
        rows = group(g)
        vals = []
        for s in range(8):
            on = sup[s, rows, :].astype(F32)
            sf[s, rows, :] = on
            vals.append(bi[s, rows, :] * on)
        inv = 1.0 / sum(vals[1:], vals[0])
        for s in range(8):
            va[1 + s, rows, :] = vals[s] * inv

    loop(2, first)
    loads[3].wait()
    loads[4].wait()
    loop(4, first, 2)

    def exchange(v, off, xs_buf, xr_buf, zr_buf, base):
        for i, s in enumerate(B0):
            xs_buf[0, off + i] = v[off + s, pl.ds(0, 16, stride=8), :]
            xs_buf[1, off + i] = v[off + s, pl.ds(7, 16, stride=8), :]
        if off:
            xs_buf[0, 0] = v[0, pl.ds(0, 16, stride=8), :]
            xs_buf[1, 0] = v[0, pl.ds(7, 16, stride=8), :]
            pl.semaphore_wait(barrier, greeted)
        last, lead = v.at[pl.ds(0, off + 4), pl.ds(120, 8)], v.at[pl.ds(0, off + 4), pl.ds(0, 8)]
        copies = []
        for j, (src, dst, who) in enumerate((
            (xs_buf.at[1], xr_buf.at[0], up_x), (xs_buf.at[0], xr_buf.at[1], down_x),
            (last, zr_buf.at[0], up_z), (lead, zr_buf.at[1], down_z),
        )):
            copies.append(pltpu.make_async_remote_copy(
                src_ref=src, dst_ref=dst, send_sem=halo_s.at[base + j // 2], recv_sem=halo_r.at[base + j // 2],
                device_id=who, device_id_type=MESH))
        for copy in copies:
            copy.start()
        if off:
            second_round()
        return [pltpu.make_async_remote_copy(
            src_ref=buf, dst_ref=buf, send_sem=halo_s.at[base + j], recv_sem=halo_r.at[base + j],
            device_id=up_x, device_id_type=MESH) for j, buf in enumerate((xr_buf, zr_buf))]

    def inner(v, off):
        def part(g):
            rows = group(g)
            odd = g % 2
            below, above = one_plane((4 * g + 15) % 16), one_plane((4 * g + 4) % 16)
            for s in range(8):
                if s % 4 == 0:
                    vals = [v[off + s + i, rows, :] for i in range(4)]
                    txm, txp = tc[TXM, rows, :], tc[TXP, rows, :]
                    tym, typ = [tc[i, rows, :] for i in (TYM, TYM1)], [tc[i, rows, :] for i in (TYP, TYP1)]
                    zm, zp = tc[TZM1 if s else TZM, rows, :], tc[TZP1 if s else TZP, rows, :]
                here, by_y, by_x, turn = vals[s % 4], vals[s % 4 ^ 1], vals[s % 4 ^ 2], 4 - (s & 4) * 2
                near = tym[s & 1] * roll_y(jnp.where(is_m[7], by_y, here), 1)
                near += typ[s & 1] * roll_y(jnp.where(is_m[0], by_y, here), 127)
                near += txm * roll_x(jnp.where(is_x[3], by_x, here), 1)
                near += txp * roll_x(jnp.where(is_x[4], by_x, here), 7)
                lo, hi = v[off + s + turn * odd, below, :], v[off + s + turn * (1 - odd), above, :]
                near += zm * jnp.concatenate([lo, here[0:24]], axis=0)
                near += zp * jnp.concatenate([here[8:32], hi], axis=0)
                nn[s, rows, :] = near

        loop(4, part)

    def outer(v, off, new, off2, xr_buf, zr_buf, extra):
        for i in range(4):
            hx[i, pl.ds(0, 16, stride=8), :] = xr_buf[0, extra + i]
            hx[i, pl.ds(7, 16, stride=8), :] = xr_buf[1, extra + i]
            nn[i, 0:8, :] += tzb[0] * zr_buf[0, extra + i]
            nn[i, 120:128, :] += tzb[1] * zr_buf[1, extra + i]

        def part(g):
            rows = group(g)
            rd, txb = tc[RD, rows, :], tc[TXB, rows, :]
            vals = []
            for s in range(8):
                near = nn[s, rows, :]
                if s in B0:
                    near += txb * hx[B0.index(s), rows, :]
                vals.append((v[off + s, rows, :] * THIRD + rd * near) * sf[s, rows, :])
            inv = 1.0 / sum(vals[1:], vals[0])
            for s in range(8):
                new[off2 + s, rows, :] = vals[s] * inv

        loop(4, part)

    sent = exchange(va, 1, hxs, hxr, hzr, 0)
    inner(va, 1)

    for load in loads[5:]:
        load.wait()
    label = blk[0, 0:1, :]
    for u, (j, r) in enumerate(((0, 0), (0, 4), (1, 0), (1, 4), (2, 0), (2, 4), (1, 0), (1, 4))):
        label = jnp.where(m1[0:1] == u, blk[j, r:r + 1, :], label)
    t_rows, labels = tab.shape[0], cr1.shape[0]
    tab[labels // 128:, :] = jnp.zeros((t_rows - labels // 128, 128), I32)

    def table(t):
        tab[t:t + 1, :] = cr1[pl.ds(t * 128, 128)].reshape(1, 128)

    loop(labels // 128, table)
    if labels % 128:
        t = labels // 128
        tab[t:t + 1, 0:labels % 128] = cr1[pl.ds(t * 128, labels % 128)].reshape(1, labels % 128)
    l_hi, l_lo = label >> 7, label & 127
    w_iota = lax.broadcasted_iota(I32, (128, 128), 0)
    pick = jnp.where(w_iota == l_lo, 1.0, 0.0).astype(BF16)
    ranks = tab[...]
    parts = jnp.concatenate([(ranks >> 7).astype(F32), (ranks & 127).astype(F32)], axis=0).astype(BF16)
    looked = jnp.dot(parts, pick, preferred_element_type=F32)
    t_iota = lax.broadcasted_iota(I32, (t_rows, 128), 0)
    looked = looked[:t_rows] * 128.0 + looked[t_rows:]
    rank = jnp.sum(jnp.where(t_iota == l_hi, looked, 0.0), axis=0, keepdims=True)
    rank = rank.astype(I32)
    rks[...] = rank
    rkr[0] = rank

    def diagonal(g):
        rows = group(g)
        diag = aa[rows, :]
        for t in (TYM, TYP, TXM, TXP, TZM, TZP):
            diag += tc[t, rows, :]
        tc[RD, rows, :] = diag

    loop(4, diagonal)

    def every(buf, sems):
        return pltpu.make_async_remote_copy(
            src_ref=buf.at[pl.ds(1, buf.shape[0] - 1)], dst_ref=buf.at[pl.ds(1, buf.shape[0] - 1)],
            send_sem=sems[0], recv_sem=sems[1], device_id=partner(g_flips, 1), device_id_type=MESH)

    def rank_copy(r):
        return pltpu.make_async_remote_copy(
            src_ref=rks, dst_ref=rkr.at[r], send_sem=rk_s, recv_sem=rk_r,
            device_id=partner(g_flips, r), device_id_type=MESH)

    for copy in sent:
        copy.wait_recv()

    tc[TXB, pl.ds(0, 16, stride=8), :] = jnp.where(mp > 0, harmonic(hxs[0, 0], hxr[0, 0]), 0.0)
    tc[TXB, pl.ds(7, 16, stride=8), :] = jnp.where(mp < plane - 1, harmonic(hxs[1, 0], hxr[1, 0]), 0.0)
    tzb[0] = jnp.where(ml > 0, harmonic(va[0, 0:8, :], hzr[0, 0]), 0.0)
    tzb[1] = jnp.where(ml < lx - 1, harmonic(va[0, 120:128, :], hzr[1, 0]), 0.0)

    tc[RD, 0:8, :] += tzb[0]
    tc[RD, 120:128, :] += tzb[1]
    tc[RD] = TWO_THIRDS / (tc[RD] + tc[TXB])

    outer(va, 1, vb, 0, hxr, hzr, 1)
    sent2 = exchange(vb, 0, hxs2, hxr2, hzr2, 2)

    es[...] = jnp.zeros_like(es)

    inner(vb, 0)
    pl.semaphore_wait(round_y, len(y_peers))
    loop(gn, lambda r: rank_copy(r).start(), 1)

    def weigh(g):
        rows = group(g)
        tym, typ, txm, txp = (tc[i, rows, :] for i in (TYM, TYP, TXM, TXP))
        sx0 = jnp.where(is_x[3], txp, 0.0) + jnp.where(is_x[4], txm, 0.0)
        sx1 = sx0 + tc[TXB, rows, :]
        sy0 = jnp.where(is_m[7], typ, 0.0) + jnp.where(is_m[0], tym, 0.0)
        sy1 = sy0 + jnp.where(is_m[3], typ, 0.0) + jnp.where(is_m[4], tym, 0.0)
        for s in range(4):
            d = aa[rows, :] + (sx1 if s & 2 else sx0) + (sy1 if s & 1 else sy0)
            ec[s, rows, :] = d
            ec[4 + s, rows, :] = d
        ec[8, rows, :] = sx0
        ec[9, rows, :] = sy0

    loop(4, weigh)
    for i, z in enumerate((3, 4, 11, 12)):
        for s in range(8):
            ec[s, 8 * z:8 * z + 8, :] += sw[i]
    for t, z in ((tzb[0], 0), (tc[TZP, 56:64, :], 7), (tc[TZM, 64:72, :], 8), (tzb[1], 15)):
        for s in range(4, 8):
            ec[s, 8 * z:8 * z + 8, :] += t

    def x_swap(q):
        return roll_x(q, 4)

    def y_swap(q):
        return jnp.where(m1 == 7, roll_y(q, 127), jnp.where(m1 == 0, roll_y(q, 1), 0.0))

    def far(g):
        return one_plane(4 * g + 4 - 5 * (g % 2))

    def rest(g):
        rows = group(g)
        here = pp[rows, :]
        full = plane_sum(ec[0, rows, :] * here - ss[rows, :]) - sw[g] * pp[far(g), :]
        fl[8, one_plane(g), :] = (
            full - x_swap(plane_sum(ec[8, rows, :] * here)) - y_swap(plane_sum(ec[9, rows, :] * here)))

    loop(4, rest)

    for copy in sent2:
        copy.wait_recv()
    for copy in sent:
        copy.wait_send()
    outer(vb, 0, va, 1, hxr2, hzr2, 0)
    store = pltpu.make_async_copy(va.at[pl.ds(1, 8)], v_out, out_sem.at[0])

    def gather(g):
        rows = group(g)
        sx0, sy0 = ec[8, rows, :], ec[9, rows, :]
        vals = [va[1 + s, rows, :] for s in range(8)]
        qx = [x_swap(plane_sum(sx0 * v)) for v in vals]
        qy = [y_swap(plane_sum(sy0 * v)) for v in vals]
        for s in range(8):
            full = plane_sum(ec[s, rows, :] * vals[s]) - sw[g] * va[1 + (s ^ 4), far(g), :]
            fl[s, one_plane(g), :] = full - qx[s ^ 2] - qy[s ^ 1]

    loop(4, gather)

    def z_part(j, pz, s):
        groups = ((0,), (1, 2), (3,))[j] if pz == 1 else {(1, 0): (1,), (2, 0): (3,), (0, 2): (0,), (1, 2): (2,)}[j, pz]
        term = fl[s, one_plane(groups[0]), :]
        for g in groups[1:]:
            term += fl[s, one_plane(g), :]
        return term

    for k, (j, halves) in enumerate(((0, (1, 2)), (1, (1, 2)), (2, (1, 0)), (1, (0,)))):
        for half, pz in enumerate(halves):
            for b in range(2):
                at, s = 64 * half + 24 * b, (0 if pz == 1 else 4) + 2 * b
                side = z_part(j, pz, s + 1)
                es[k, at:at + 8, :] = jnp.where(m1 < 4, side, 0.0)
                es[k, at + 8:at + 16, :] = z_part(j, pz, s)
                es[k, at + 16:at + 24, :] = jnp.where(m1 < 4, 0.0, side)
        if k < 3:
            es[k, 48:56, :] = -z_part(j, 1, 8)

    m16 = m[:16]
    sums = []
    for k in range(4):
        for xi in range(2):
            t = es[k, pl.ds(4 * xi, 16, stride=8), :]
            for i in range(1, 4):
                t += es[k, pl.ds(4 * xi + i, 16, stride=8), :]
            sums.append(t)
    for bit in (4, 2, 1):
        high = (m16 & bit) != 0
        merged = []
        for u in range(bit):
            one, two = sums[u], sums[u + bit]
            move = jnp.where(high, one, two)
            merged.append(jnp.where(high, two, one) + jnp.where(high, roll_y(move, bit), roll_y(move, 128 - bit)))
        sums = merged
    rows_out = sums[0]
    second = pltpu.roll(rows_out[8:16], 7, 0)
    for buf in (cs, crv.at[0]):
        buf[0:8, :] = jnp.where(x1 == 7, second, rows_out[0:8])
        buf[8:13, :] = second[0:5]

    def g_copy(r):
        return pltpu.make_async_remote_copy(
            src_ref=cs, dst_ref=crv.at[r], send_sem=g_s, recv_sem=g_r,
            device_id=partner(g_flips, r), device_id_type=MESH)

    for r in far_first(G_BITS):
        g_copy(r).start()
    store.start()

    def wanted(t):
        q, idx = (t, lane1) if t < 4 else (lane1 >> 5, 128 + (lane1 & 31))
        peer = jnp.zeros_like(idx)
        for p in range(1, hn):
            peer += jnp.where(idx >= p * width, 1, 0)
        col = idx - peer * width + q * width
        dev = jnp.zeros_like(idx) + (ml * plane + mp)
        for b, (on_layer, step) in enumerate(h_flips):
            dev += ((peer >> b) & 1) * (step * plane if on_layer else step)
        return jnp.where((col < own) & (idx < n_idx), dev * own + col, -7)

    wants = [wanted(t) for t in range(5)]
    every(rkr, (rk_s, rk_r)).wait_recv()
    turned = jnp.concatenate([rkr[r] for r in range(gn)] + [jnp.zeros((128 - gn, 128), I32)], axis=0).astype(F32).T
    rkt[...] = turned.astype(I32)
    for r in range(gn):
        have = jnp.broadcast_to(rkt[:, r:r + 1], (128, 128))
        for t in range(5):
            want = jnp.concatenate([wants[t]] * 16, axis=0)
            oh[128 * r:128 * r + 128, 128 * t:128 * t + 128] = jnp.where(have == want, 1.0, 0.0).astype(BF16)

    odd = m1 % 2 == 1
    b1 = (x1 >= 3) & (x1 < 6)
    b1_odd = b1 & odd

    def spread(r):
        got1, got2 = crv[r, 0:8, :], pltpu.roll(crv[r, 5:13, :], 6, 0)
        pz1 = jnp.where((m1 < 6) & (x1 < 7), got1, 0.0)
        pz2 = jnp.where(m1 < 4, got2, 0.0)
        pz0 = jnp.where(m1 < 4, 0.0, jnp.where(m1 < 6, got2, got1))
        low1, low2, low0 = (jnp.where(b1_odd, v, 0.0) for v in (pz1, pz2, pz0))
        last = pltpu.roll(low1, 5, 0) + low2 + jnp.where(x1 >= 6, pltpu.roll(low0, 3, 0), 0.0)
        vals = jnp.concatenate([
            pz1 - low1 + jnp.where(x1 == 7, pltpu.roll(low0, 2, 0), 0.0), pz2 - low2, pz0 - low0, last], axis=0)
        high = vals.astype(BF16)
        lanes = slice(128 * r, 128 * r + 128)
        xb[0:32, lanes] = high
        xb[32:64, lanes] = (vals - high.astype(F32)).astype(BF16)

    every(crv, (g_s, g_r)).wait_recv()
    loop(gn, spread)
    routed = jnp.dot(xb[...], oh[...], preferred_element_type=F32)
    both = routed[0:32] + routed[32:64]
    parts = [both[:, 128 * q:128 * q + 128] for q in range(4)]
    over = both[:, 512:640]
    packed = jnp.concatenate([
        jnp.concatenate(parts, axis=0).T,
        jnp.concatenate([roll_y(over, (128 - 32 * q) % 128) if q else over for q in range(4)], axis=0).T], axis=0)

    def h_copy(r):
        return pltpu.make_async_remote_copy(
            src_ref=hs.at[r], dst_ref=hr.at[r], send_sem=h_s, recv_sem=h_r,
            device_id=partner(h_flips, r), device_id_type=MESH)

    pl.semaphore_wait(round_z, 2)
    for r in sorted(far_first(H_BITS), key=lambda r: r < hn // 2):
        hs[r] = packed[r * width:(r + 1) * width]
        h_copy(r).start()
    hs[0] = packed[0:width]
    store.wait()
    for copy in sent2:
        copy.wait_send()
    every(rkr, (rk_s, rk_r)).wait_send()
    every(crv, (g_s, g_r)).wait_send()
    every(hr, (h_s, h_r)).wait_send()
    every(hr, (h_s, h_r)).wait_recv()
    final = hs[0]
    for r in range(1, hn):
        final += hr[r]
    f_out[0:width, :] = final


def finish(own, width, v_in, f_in, v_out, cm_hbm, cr_hbm, ft, cm_out, cr_out, sem):
    stores = [pltpu.make_async_copy(src, dst, sem.at[i]) for i, (src, dst) in enumerate((
        (v_in, v_out), (cm_out, cm_hbm), (cr_out, cr_hbm)))]
    stores[0].start()
    ft[0:16, :] = f_in[...]
    turned = ft[...].T
    lane = lax.broadcasted_iota(I32, (32, 128), 1)
    done = jnp.zeros((32, 128), F32)
    for q in range(4):
        part = turned[32 * q:32 * q + 32]
        here = (lane >= q * width) & (lane < (q + 1) * width)
        done = jnp.where(here, pltpu.roll(part, q * width, 1) if q else part, done)
    for pz, px, base in (
        (1, 1, 0), (1, 2, 3), (2, 1, 8), (2, 2, 11), (0, 1, 16), (0, 2, 19), (1, 0, 24), (2, 0, 27)):
        k = 9 * pz + 3 * px
        cm_out[k:k + 3, :] = done[base:base + 3, 0:own]
    cm_out[0:2, :] = done[30:32, 0:own]
    cm_out[2:3, :] = done[7:8, 0:own]
    cr_out[...] = done[6:7, 0:own]
    stores[1].start()
    stores[2].start()
    for store in stores:
        store.wait()


def per_device(sizes, basis_init, permeability, accumulation, pressure, source, support, block_of, curve_rank):
    lx, plane = sizes
    gn, hn = 2 ** len(G_BITS), 2 ** len(H_BITS)
    devices = lx * plane
    own = (curve_rank.shape[0] + devices - 1) // devices
    width = (own + 3) // 4
    flat = lambda v: v.reshape(v.shape[:-3] + (128, 128))
    t_rows = -(-curve_rank.shape[0] // 2048) * 16
    anywhere = pl.BlockSpec(memory_space=pl.ANY)
    vmem = pl.BlockSpec(memory_space=pltpu.VMEM)
    dma = pltpu.SemaphoreType.DMA
    cells = lambda *lead: pltpu.VMEM(lead + (128, 128), F32)
    basis, rows = pl.pallas_call(
        functools.partial(kernel, (lx, plane, own, width)),
        out_shape=(
            jax.ShapeDtypeStruct((8, 128, 128), F32),
            jax.ShapeDtypeStruct((16, 128), F32),
        ),
        in_specs=[anywhere] * 8,
        out_specs=(anywhere, vmem),
        scratch_shapes=[
            cells(8), pltpu.VMEM((8, 128, 128), I32), cells(), cells(), cells(),
            pltpu.VMEM((3, 8, 128), I32), pltpu.VMEM(curve_rank.shape, I32), pltpu.VMEM((t_rows, 128), I32),
            cells(9), cells(8), cells(8), cells(8), cells(12),
            pltpu.VMEM((2, 8, 128), F32), cells(10), pltpu.VMEM((4, 8, 128), F32),
            pltpu.VMEM((9, 32, 128), F32), cells(4),
            pltpu.VMEM((2, 5, 16, 128), F32), pltpu.VMEM((2, 5, 16, 128), F32), pltpu.VMEM((2, 5, 8, 128), F32),
            pltpu.VMEM((2, 4, 16, 128), F32), pltpu.VMEM((2, 4, 16, 128), F32), pltpu.VMEM((2, 4, 8, 128), F32),
            pltpu.VMEM((1, 128), I32), pltpu.VMEM((gn, 1, 128), I32),
            pltpu.VMEM((128, 128), I32), pltpu.VMEM((gn * 128, 640), BF16),
            pltpu.VMEM((64, gn * 128), BF16), pltpu.VMEM((4, 128, 128), F32),
            pltpu.VMEM((13, 128), F32), pltpu.VMEM((gn, 13, 128), F32),
            pltpu.VMEM((hn, width, 128), F32), pltpu.VMEM((hn, width, 128), F32),
            pltpu.SemaphoreType.REGULAR, pltpu.SemaphoreType.REGULAR, dma((12,)), dma((1,)), dma((4,)), dma((4,)),
            dma, dma, dma, dma, dma, dma,
        ],
        compiler_params=pltpu.CompilerParams(
            collective_id=0, has_side_effects=True, vmem_limit_bytes=VMEM_GRANT),
        cost_estimate=pl.CostEstimate(flops=20_000_000, bytes_accessed=2_000_000, transcendentals=0),
    )(*(pltpu.with_memory_space_constraint(v, pltpu.HBM) for v in (
        flat(basis_init), flat(permeability), flat(accumulation), flat(pressure), flat(source),
        flat(support), flat(block_of), curve_rank,
    )))
    basis, matrix, residual = pl.pallas_call(
        functools.partial(finish, own, width),
        out_shape=(
            jax.ShapeDtypeStruct((8, 128, 128), F32),
            jax.ShapeDtypeStruct((27, own), F32),
            jax.ShapeDtypeStruct((1, own), F32),
        ),
        in_specs=[anywhere, vmem],
        out_specs=(anywhere, anywhere, anywhere),
        scratch_shapes=[cells(), pltpu.VMEM((27, own), F32), pltpu.VMEM((1, own), F32), dma((3,))],
        compiler_params=pltpu.CompilerParams(vmem_limit_bytes=VMEM_GRANT),
    )(basis, rows)
    return basis.reshape(basis_init.shape), matrix, residual.reshape(own)


def solution(mesh):
    return jax.shard_map(
        functools.partial(per_device, (mesh.shape["layer"], mesh.shape["plane"])),
        mesh=mesh,
        in_specs=(
            P(None, "layer", "plane", None),
            P("layer", "plane", None),
            P("layer", "plane", None),
            P("layer", "plane", None),
            P("layer", "plane", None),
            P(None, "layer", "plane", None),
            P("layer", "plane", None),
            P(),
        ),
        out_specs=(
            P(None, "layer", "plane", None),
            P(None, ("layer", "plane")),
            P(("layer", "plane")),
        ),
        check_vma=False,
    )
```

```python
import functools

import jax
import jax.numpy as jnp
from jax import lax
from jax.experimental import pallas as pl
from jax.experimental.pallas import tpu as pltpu
from jax.sharding import PartitionSpec as P

MESH = pl.DeviceIdType.MESH
F32, BF16, I32 = jnp.float32, jnp.bfloat16, jnp.int32

G_BITS = (("layer", 1), ("layer", 2), ("plane", 16), ("plane", 32))
H_BITS = (("plane", 1), ("plane", 2), ("plane", 4), ("plane", 8))
VMEM_GRANT = 32 * 1024 * 1024
THIRD, TWO_THIRDS = 1.0 / 3.0, 2.0 / 3.0
B0 = (0, 1, 4, 5)
A0 = (0, 1, 2, 3)
TYM, TYP, TYM1, TYP1, TXM, TXP, TZM, TZP, TZM1, TZP1, TXB, RD = range(12)


def roll_x(v, shift):
    rows = v.shape[0]
    return pltpu.roll(v.reshape(rows // 8, 8, 128), shift, 1).reshape(rows, 128)


def roll_y(v, shift):
    return pltpu.roll(v, shift, 1)


def harmonic(k, n):
    return 2.0 * k * n / (k + n)


def plane_sum(v):
    return v.reshape(-1, 8, 128).sum(axis=0)


def far_first(bits):
    def hops(r):
        reach = {"layer": 0, "y": 0, "z": 0}
        for i, (axis, bit) in enumerate(bits):
            if (r >> i) & 1:
                kind, step = (axis, bit) if axis == "layer" else ("y", bit // 16) if bit >= 16 else ("z", bit // 2)
                reach[kind] += step
        return sum(min(n, size - n) for n, size in ((reach["layer"], 4), (reach["y"], 4), (reach["z"], 8)))

    return sorted(range(1, 2 ** len(bits)), key=lambda r: -hops(r))


def kernel(
    dims,
    bi_hbm, k_hbm, a_hbm, p_hbm, s_hbm, sup_hbm, blk_hbm, cr_hbm,
    v_out, f_out,
    bi, sup, aa, pp, ss, blk, cr1, tab,
    va, vb, sf, nn, tc, tzb, ec, sw, fl, hx, hxs, hxr, hzr, hxs2, hxr2, hzr2,
    rks, rkr, rkt, oh, xb, es, cs, crv, hs, hr,
    round_y, round_z, in_sem, out_sem, halo_s, halo_r, rk_s, rk_r, g_s, g_r, h_s, h_r,
):
    lx, plane, own, width = dims
    gn, hn = 2 ** len(G_BITS), 2 ** len(H_BITS)
    zc = hn // 2
    n_idx = hn * width
    ml, mp = lax.axis_index("layer"), lax.axis_index("plane")

    def flips(bits):
        steps = []
        for axis, bit in bits:
            at = ml if axis == "layer" else mp
            steps.append((axis == "layer", bit * (1 - 2 * ((at // bit) % 2))))
        return steps

    g_flips, h_flips = flips(G_BITS), flips(H_BITS)

    def partner(steps, r):
        to_l, to_p = ml, mp
        for i, (on_layer, step) in enumerate(steps):
            if (r >> i) & 1:
                to_l, to_p = (to_l + step, to_p) if on_layer else (to_l, to_p + step)
        return (to_l, to_p)

    up_x, down_x = (ml, (mp + 1) % plane), (ml, (mp + plane - 1) % plane)
    up_z, down_z = ((ml + 1) % lx, mp), ((ml + lx - 1) % lx, mp)

    def loop(n, body, start=0):
        for i in range(start, n):
            body(i)

    def group(g):
        return slice(g * 32, g * 32 + 32)

    def one_plane(z):
        return slice(z * 8, z * 8 + 8)

    loads = [
        pltpu.make_async_copy(k_hbm, va.at[0], in_sem.at[0]),
        pltpu.make_async_copy(bi_hbm.at[:, pl.ds(0, 64)], bi.at[:, pl.ds(0, 64)], in_sem.at[1]),
        pltpu.make_async_copy(sup_hbm.at[:, pl.ds(0, 64)], sup.at[:, pl.ds(0, 64)], in_sem.at[2]),
        pltpu.make_async_copy(bi_hbm.at[:, pl.ds(64, 64)], bi.at[:, pl.ds(64, 64)], in_sem.at[10]),
        pltpu.make_async_copy(sup_hbm.at[:, pl.ds(64, 64)], sup.at[:, pl.ds(64, 64)], in_sem.at[11]),
        pltpu.make_async_copy(a_hbm, aa, in_sem.at[3]),
        pltpu.make_async_copy(cr_hbm, cr1, in_sem.at[4]),
        pltpu.make_async_copy(p_hbm, pp, in_sem.at[5]),
        pltpu.make_async_copy(s_hbm, ss, in_sem.at[6]),
    ]
    for j, z in enumerate((0, 4, 12)):
        loads.append(pltpu.make_async_copy(blk_hbm.at[pl.ds(8 * z, 8)], blk.at[j], in_sem.at[7 + j]))
    barrier = pltpu.get_barrier_semaphore()

    def greet(who):
        pl.semaphore_signal(barrier, inc=1, device_id=who, device_id_type=MESH)

    def along_z(dz, dc):
        return (ml, mp + dc * (1 - 2 * (mp % 2)) + 2 * ((mp // 2 + dz) % zc - (mp // 2) % zc))

    x_mask = sum(1 << i for i, (axis, _) in enumerate(G_BITS) if axis == "layer")
    x_peers = [r for r in range(1, gn) if r & x_mask == r]
    y_peers = [r for r in range(1, gn) if r & x_mask == 0]
    z_peers = [(dz, dc) for dz in (1, zc - 1, 2, zc - 2) for dc in (0, 1)] + [(0, 1)]
    greet(up_x)
    greet(down_x)
    for r in x_peers:
        greet(partner(g_flips, r))
    for load in loads[:5]:
        load.start()
    for r in y_peers:
        greet(partner(g_flips, r))
    for dz, dc in z_peers:
        greet(along_z(dz, dc))
    for load in loads[5:]:
        load.start()
    greeted = 2 + len(x_peers) + len(y_peers) + len(z_peers)

    def second_round():
        for r in y_peers:
            pl.semaphore_signal(round_y, inc=1, device_id=partner(g_flips, r), device_id_type=MESH)
        for dz in (2, zc - 2):
            pl.semaphore_signal(round_z, inc=1, device_id=along_z(dz, 0), device_id_type=MESH)

    lane = lax.broadcasted_iota(I32, (32, 128), 1)
    m, x = lane % 8, lax.broadcasted_iota(I32, (32, 128), 0) % 8
    m1, x1 = m[:8], x[:8]
    lane1, row1 = lane[:8], x[:8]
    is_m = {i: m == i for i in (0, 3, 4, 7)}
    is_x = {i: x == i for i in (3, 4)}

    hx[...] = jnp.zeros_like(hx)
    tc[TXB] = jnp.zeros((128, 128), F32)

    loads[0].wait()

    def faces(g):
        rows, below = group(g), one_plane((4 * g + 15) % 16)
        k = va[0, rows, :]
        tym = jnp.where(lane == 0, 0.0, harmonic(k, roll_y(k, 1)))
        typ = roll_y(tym, 127)
        tc[TYM, rows, :] = tym
        tc[TYP, rows, :] = typ
        tc[TYM1, rows, :] = jnp.where(is_m[4], 0.0, tym)
        tc[TYP1, rows, :] = jnp.where(is_m[3], 0.0, typ)
        txm = jnp.where(x == 0, 0.0, harmonic(k, roll_x(k, 1)))
        tc[TXM, rows, :] = txm
        tc[TXP, rows, :] = roll_x(txm, 7)
        tz = harmonic(k, jnp.concatenate([va[0, below, :], k[0:24]], axis=0))
        tc[TZM, rows, :] = tz
        tc[TZP, below, :] = tz[0:8]
        tc[TZP, slice(g * 32, g * 32 + 24), :] = tz[8:32]
        tc[TZM1, rows, :] = tz
        tc[TZP1, below, :] = tz[0:8]
        tc[TZP1, slice(g * 32, g * 32 + 24), :] = tz[8:32]

    loop(4, faces)
    nil = jnp.zeros((8, 128), F32)
    tc[TZM, 0:8, :] = nil
    tc[TZP, 120:128, :] = nil
    tc[TZM1, 0:8, :] = nil
    tc[TZP1, 120:128, :] = nil
    tc[TZM1, 64:72, :] = nil
    tc[TZP1, 56:64, :] = nil
    for i, (t, z) in enumerate(((TZP, 3), (TZM, 4), (TZP, 11), (TZM, 12))):
        sw[i] = tc[t, 8 * z:8 * z + 8, :]

    loads[1].wait()
    loads[2].wait()

    def first(g):
        rows = group(g)
        vals = []
        for s in range(8):
            on = sup[s, rows, :].astype(F32)
            sf[s, rows, :] = on
            vals.append(bi[s, rows, :] * on)
        inv = 1.0 / sum(vals[1:], vals[0])
        for s in range(8):
            va[1 + s, rows, :] = vals[s] * inv

    loop(2, first)
    loads[3].wait()
    loads[4].wait()
    loop(4, first, 2)

    def exchange(v, off, xs_buf, xr_buf, zr_buf, base):
        for i, s in enumerate(B0):
            xs_buf[0, off + i] = v[off + s, pl.ds(0, 16, stride=8), :]
            xs_buf[1, off + i] = v[off + s, pl.ds(7, 16, stride=8), :]
        if off:
            xs_buf[0, 0] = v[0, pl.ds(0, 16, stride=8), :]
            xs_buf[1, 0] = v[0, pl.ds(7, 16, stride=8), :]
            pl.semaphore_wait(barrier, greeted)
        last, lead = v.at[pl.ds(0, off + 4), pl.ds(120, 8)], v.at[pl.ds(0, off + 4), pl.ds(0, 8)]
        copies = []
        for j, (src, dst, who) in enumerate((
            (xs_buf.at[1], xr_buf.at[0], up_x), (xs_buf.at[0], xr_buf.at[1], down_x),
            (last, zr_buf.at[0], up_z), (lead, zr_buf.at[1], down_z),
        )):
            copies.append(pltpu.make_async_remote_copy(
                src_ref=src, dst_ref=dst, send_sem=halo_s.at[base + j // 2], recv_sem=halo_r.at[base + j // 2],
                device_id=who, device_id_type=MESH))
        for copy in copies:
            copy.start()
        if off:
            second_round()
        return [pltpu.make_async_remote_copy(
            src_ref=buf, dst_ref=buf, send_sem=halo_s.at[base + j], recv_sem=halo_r.at[base + j],
            device_id=up_x, device_id_type=MESH) for j, buf in enumerate((xr_buf, zr_buf))]

    def inner(v, off):
        def part(g):
            rows = group(g)
            odd = g % 2
            below, above = one_plane((4 * g + 15) % 16), one_plane((4 * g + 4) % 16)
            for s in range(8):
                if s % 4 == 0:
                    vals = [v[off + s + i, rows, :] for i in range(4)]
                    txm, txp = tc[TXM, rows, :], tc[TXP, rows, :]
                    tym, typ = [tc[i, rows, :] for i in (TYM, TYM1)], [tc[i, rows, :] for i in (TYP, TYP1)]
                    zm, zp = tc[TZM1 if s else TZM, rows, :], tc[TZP1 if s else TZP, rows, :]
                here, by_y, by_x, turn = vals[s % 4], vals[s % 4 ^ 1], vals[s % 4 ^ 2], 4 - (s & 4) * 2
                near = tym[s & 1] * roll_y(jnp.where(is_m[7], by_y, here), 1)
                near += typ[s & 1] * roll_y(jnp.where(is_m[0], by_y, here), 127)
                near += txm * roll_x(jnp.where(is_x[3], by_x, here), 1)
                near += txp * roll_x(jnp.where(is_x[4], by_x, here), 7)
                lo, hi = v[off + s + turn * odd, below, :], v[off + s + turn * (1 - odd), above, :]
                near += zm * jnp.concatenate([lo, here[0:24]], axis=0)
                near += zp * jnp.concatenate([here[8:32], hi], axis=0)
                nn[s, rows, :] = near

        loop(4, part)

    def outer(v, off, new, off2, xr_buf, zr_buf, extra):
        for i in range(4):
            hx[i, pl.ds(0, 16, stride=8), :] = xr_buf[0, extra + i]
            hx[i, pl.ds(7, 16, stride=8), :] = xr_buf[1, extra + i]
            nn[i, 0:8, :] += tzb[0] * zr_buf[0, extra + i]
            nn[i, 120:128, :] += tzb[1] * zr_buf[1, extra + i]

        def part(g):
            rows = group(g)
            rd, txb = tc[RD, rows, :], tc[TXB, rows, :]
            vals = []
            for s in range(8):
                near = nn[s, rows, :]
                if s in B0:
                    near += txb * hx[B0.index(s), rows, :]
                vals.append((v[off + s, rows, :] * THIRD + rd * near) * sf[s, rows, :])
            inv = 1.0 / sum(vals[1:], vals[0])
            for s in range(8):
                new[off2 + s, rows, :] = vals[s] * inv

        loop(4, part)

    sent = exchange(va, 1, hxs, hxr, hzr, 0)
    inner(va, 1)

    for load in loads[5:]:
        load.wait()
    label = blk[0, 0:1, :]
    for u, (j, r) in enumerate(((0, 0), (0, 4), (1, 0), (1, 4), (2, 0), (2, 4), (1, 0), (1, 4))):
        label = jnp.where(m1[0:1] == u, blk[j, r:r + 1, :], label)
    t_rows, labels = tab.shape[0], cr1.shape[0]
    tab[labels // 128:, :] = jnp.zeros((t_rows - labels // 128, 128), I32)

    def table(t):
        tab[t:t + 1, :] = cr1[pl.ds(t * 128, 128)].reshape(1, 128)

    loop(labels // 128, table)
    if labels % 128:
        t = labels // 128
        tab[t:t + 1, 0:labels % 128] = cr1[pl.ds(t * 128, labels % 128)].reshape(1, labels % 128)
    l_hi, l_lo = label >> 7, label & 127
    w_iota = lax.broadcasted_iota(I32, (128, 128), 0)
    pick = jnp.where(w_iota == l_lo, 1.0, 0.0).astype(BF16)
    ranks = tab[...]
    parts = jnp.concatenate([(ranks >> 7).astype(F32), (ranks & 127).astype(F32)], axis=0).astype(BF16)
    looked = jnp.dot(parts, pick, preferred_element_type=F32)
    t_iota = lax.broadcasted_iota(I32, (t_rows, 128), 0)
    looked = looked[:t_rows] * 128.0 + looked[t_rows:]
    rank = jnp.sum(jnp.where(t_iota == l_hi, looked, 0.0), axis=0, keepdims=True)
    rank = rank.astype(I32)
    rks[...] = rank
    rkr[0] = rank

    def diagonal(g):
        rows = group(g)
        diag = aa[rows, :]
        for t in (TYM, TYP, TXM, TXP, TZM, TZP):
            diag += tc[t, rows, :]
        tc[RD, rows, :] = diag

    loop(4, diagonal)

    def every(buf, sems):
        return pltpu.make_async_remote_copy(
            src_ref=buf.at[pl.ds(1, buf.shape[0] - 1)], dst_ref=buf.at[pl.ds(1, buf.shape[0] - 1)],
            send_sem=sems[0], recv_sem=sems[1], device_id=partner(g_flips, 1), device_id_type=MESH)

    def rank_copy(r):
        return pltpu.make_async_remote_copy(
            src_ref=rks, dst_ref=rkr.at[r], send_sem=rk_s, recv_sem=rk_r,
            device_id=partner(g_flips, r), device_id_type=MESH)

    for copy in sent:
        copy.wait_recv()

    tc[TXB, pl.ds(0, 16, stride=8), :] = jnp.where(mp > 0, harmonic(hxs[0, 0], hxr[0, 0]), 0.0)
    tc[TXB, pl.ds(7, 16, stride=8), :] = jnp.where(mp < plane - 1, harmonic(hxs[1, 0], hxr[1, 0]), 0.0)
    tzb[0] = jnp.where(ml > 0, harmonic(va[0, 0:8, :], hzr[0, 0]), 0.0)
    tzb[1] = jnp.where(ml < lx - 1, harmonic(va[0, 120:128, :], hzr[1, 0]), 0.0)

    tc[RD, 0:8, :] += tzb[0]
    tc[RD, 120:128, :] += tzb[1]
    tc[RD] = TWO_THIRDS / (tc[RD] + tc[TXB])

    outer(va, 1, vb, 0, hxr, hzr, 1)
    sent2 = exchange(vb, 0, hxs2, hxr2, hzr2, 2)

    es[...] = jnp.zeros_like(es)

    inner(vb, 0)
    pl.semaphore_wait(round_y, len(y_peers))
    loop(gn, lambda r: rank_copy(r).start(), 1)

    def weigh(g):
        rows = group(g)
        tym, typ, txm, txp = (tc[i, rows, :] for i in (TYM, TYP, TXM, TXP))
        sx0 = jnp.where(is_x[3], txp, 0.0) + jnp.where(is_x[4], txm, 0.0)
        sx1 = sx0 + tc[TXB, rows, :]
        sy0 = jnp.where(is_m[7], typ, 0.0) + jnp.where(is_m[0], tym, 0.0)
        sy1 = sy0 + jnp.where(is_m[3], typ, 0.0) + jnp.where(is_m[4], tym, 0.0)
        for s in range(4):
            d = aa[rows, :] + (sx1 if s & 2 else sx0) + (sy1 if s & 1 else sy0)
            ec[s, rows, :] = d
            ec[4 + s, rows, :] = d
        ec[8, rows, :] = sx0
        ec[9, rows, :] = sy0

    loop(4, weigh)
    for i, z in enumerate((3, 4, 11, 12)):
        for s in range(8):
            ec[s, 8 * z:8 * z + 8, :] += sw[i]
    for t, z in ((tzb[0], 0), (tc[TZP, 56:64, :], 7), (tc[TZM, 64:72, :], 8), (tzb[1], 15)):
        for s in range(4, 8):
            ec[s, 8 * z:8 * z + 8, :] += t

    def x_swap(q):
        return roll_x(q, 4)

    def y_swap(q):
        return jnp.where(m1 == 7, roll_y(q, 127), jnp.where(m1 == 0, roll_y(q, 1), 0.0))

    def far(g):
        return one_plane(4 * g + 4 - 5 * (g % 2))

    def rest(g):
        rows = group(g)
        here = pp[rows, :]
        full = plane_sum(ec[0, rows, :] * here - ss[rows, :]) - sw[g] * pp[far(g), :]
        fl[8, one_plane(g), :] = (
            full - x_swap(plane_sum(ec[8, rows, :] * here)) - y_swap(plane_sum(ec[9, rows, :] * here)))

    loop(4, rest)

    for copy in sent2:
        copy.wait_recv()
    for copy in sent:
        copy.wait_send()
    outer(vb, 0, va, 1, hxr2, hzr2, 0)
    store = pltpu.make_async_copy(va.at[pl.ds(1, 8)], v_out, out_sem.at[0])

    def gather(g):
        rows = group(g)
        sx0, sy0 = ec[8, rows, :], ec[9, rows, :]
        vals = [va[1 + s, rows, :] for s in range(8)]
        qx = [x_swap(plane_sum(sx0 * v)) for v in vals]
        qy = [y_swap(plane_sum(sy0 * v)) for v in vals]
        for s in range(8):
            full = plane_sum(ec[s, rows, :] * vals[s]) - sw[g] * va[1 + (s ^ 4), far(g), :]
            fl[s, one_plane(g), :] = full - qx[s ^ 2] - qy[s ^ 1]

    loop(4, gather)

    def z_part(j, pz, s):
        groups = ((0,), (1, 2), (3,))[j] if pz == 1 else {(1, 0): (1,), (2, 0): (3,), (0, 2): (0,), (1, 2): (2,)}[j, pz]
        term = fl[s, one_plane(groups[0]), :]
        for g in groups[1:]:
            term += fl[s, one_plane(g), :]
        return term

    for k, (j, halves) in enumerate(((0, (1, 2)), (1, (1, 2)), (2, (1, 0)), (1, (0,)))):
        for half, pz in enumerate(halves):
            for b in range(2):
                at, s = 64 * half + 24 * b, (0 if pz == 1 else 4) + 2 * b
                side = z_part(j, pz, s + 1)
                es[k, at:at + 8, :] = jnp.where(m1 < 4, side, 0.0)
                es[k, at + 8:at + 16, :] = z_part(j, pz, s)
                es[k, at + 16:at + 24, :] = jnp.where(m1 < 4, 0.0, side)
        if k < 3:
            es[k, 48:56, :] = -z_part(j, 1, 8)

    m16 = m[:16]
    sums = []
    for k in range(4):
        for xi in range(2):
            t = es[k, pl.ds(4 * xi, 16, stride=8), :]
            for i in range(1, 4):
                t += es[k, pl.ds(4 * xi + i, 16, stride=8), :]
            sums.append(t)
    for bit in (4, 2, 1):
        high = (m16 & bit) != 0
        merged = []
        for u in range(bit):
            one, two = sums[u], sums[u + bit]
            move = jnp.where(high, one, two)
            merged.append(jnp.where(high, two, one) + jnp.where(high, roll_y(move, bit), roll_y(move, 128 - bit)))
        sums = merged
    rows_out = sums[0]
    second = pltpu.roll(rows_out[8:16], 7, 0)
    first_rows = jnp.where(x1 == 7, second, rows_out[0:8])
    cs[0:8, :] = first_rows
    cs[8:13, :] = second[0:5]

    def g_copy(r):
        return pltpu.make_async_remote_copy(
            src_ref=cs, dst_ref=crv.at[r], send_sem=g_s, recv_sem=g_r,
            device_id=partner(g_flips, r), device_id_type=MESH)

    for r in far_first(G_BITS):
        g_copy(r).start()
    store.start()
    crv[0, 0:8, :] = first_rows
    crv[0, 8:13, :] = second[0:5]

    def wanted(t):
        q, idx = (t, lane1) if t < 4 else (lane1 >> 5, 128 + (lane1 & 31))
        peer = jnp.zeros_like(idx)
        for p in range(1, hn):
            peer += jnp.where(idx >= p * width, 1, 0)
        col = idx - peer * width + q * width
        dev = jnp.zeros_like(idx) + (ml * plane + mp)
        for b, (on_layer, step) in enumerate(h_flips):
            dev += ((peer >> b) & 1) * (step * plane if on_layer else step)
        return jnp.where((col < own) & (idx < n_idx), dev * own + col, -7)

    wants = [wanted(t) for t in range(5)]
    every(rkr, (rk_s, rk_r)).wait_recv()
    turned = jnp.concatenate([rkr[r] for r in range(gn)] + [jnp.zeros((128 - gn, 128), I32)], axis=0).astype(F32).T
    rkt[...] = turned.astype(I32)
    for r in range(gn):
        have = jnp.broadcast_to(rkt[:, r:r + 1], (128, 128))
        for t in range(5):
            want = jnp.concatenate([wants[t]] * 16, axis=0)
            oh[128 * r:128 * r + 128, 128 * t:128 * t + 128] = jnp.where(have == want, 1.0, 0.0).astype(BF16)

    odd = m1 % 2 == 1
    b1 = (x1 >= 3) & (x1 < 6)
    b1_odd = b1 & odd

    def spread(r):
        got1, got2 = crv[r, 0:8, :], pltpu.roll(crv[r, 5:13, :], 6, 0)
        pz1 = jnp.where((m1 < 6) & (x1 < 7), got1, 0.0)
        pz2 = jnp.where(m1 < 4, got2, 0.0)
        pz0 = jnp.where(m1 < 4, 0.0, jnp.where(m1 < 6, got2, got1))
        low1, low2, low0 = (jnp.where(b1_odd, v, 0.0) for v in (pz1, pz2, pz0))
        last = pltpu.roll(low1, 5, 0) + low2 + jnp.where(x1 >= 6, pltpu.roll(low0, 3, 0), 0.0)
        vals = jnp.concatenate([
            pz1 - low1 + jnp.where(x1 == 7, pltpu.roll(low0, 2, 0), 0.0), pz2 - low2, pz0 - low0, last], axis=0)
        high = vals.astype(BF16)
        lanes = slice(128 * r, 128 * r + 128)
        xb[0:32, lanes] = high
        xb[32:64, lanes] = (vals - high.astype(F32)).astype(BF16)

    spread(0)
    pl.semaphore_wait(round_z, 2)
    every(crv, (g_s, g_r)).wait_recv()
    loop(gn, spread, 1)
    routed = jnp.dot(xb[...], oh[...], preferred_element_type=F32)
    both = routed[0:32] + routed[32:64]
    parts = [both[:, 128 * q:128 * q + 128] for q in range(4)]
    over = both[:, 512:640]
    packed = jnp.concatenate([
        jnp.concatenate(parts, axis=0).T,
        jnp.concatenate([roll_y(over, (128 - 32 * q) % 128) if q else over for q in range(4)], axis=0).T], axis=0)

    def h_copy(r):
        return pltpu.make_async_remote_copy(
            src_ref=hs.at[r], dst_ref=hr.at[r], send_sem=h_s, recv_sem=h_r,
            device_id=partner(h_flips, r), device_id_type=MESH)

    for r in sorted(far_first(H_BITS), key=lambda r: r < hn // 2):
        hs[r] = packed[r * width:(r + 1) * width]
        h_copy(r).start()
    hs[0] = packed[0:width]
    store.wait()
    for copy in sent2:
        copy.wait_send()
    every(rkr, (rk_s, rk_r)).wait_send()
    every(crv, (g_s, g_r)).wait_send()
    every(hr, (h_s, h_r)).wait_send()
    every(hr, (h_s, h_r)).wait_recv()
    final = hs[0]
    for r in range(1, hn):
        final += hr[r]
    f_out[0:width, :] = final


def finish(own, width, v_in, f_in, v_out, cm_hbm, cr_hbm, ft, cm_out, cr_out, sem):
    stores = [pltpu.make_async_copy(src, dst, sem.at[i]) for i, (src, dst) in enumerate((
        (v_in, v_out), (cm_out, cm_hbm), (cr_out, cr_hbm)))]
    stores[0].start()
    ft[0:16, :] = f_in[...]
    turned = ft[...].T
    lane = lax.broadcasted_iota(I32, (32, 128), 1)
    done = jnp.zeros((32, 128), F32)
    for q in range(4):
        part = turned[32 * q:32 * q + 32]
        here = (lane >= q * width) & (lane < (q + 1) * width)
        done = jnp.where(here, pltpu.roll(part, q * width, 1) if q else part, done)
    for pz, px, base in (
        (1, 1, 0), (1, 2, 3), (2, 1, 8), (2, 2, 11), (0, 1, 16), (0, 2, 19), (1, 0, 24), (2, 0, 27)):
        k = 9 * pz + 3 * px
        cm_out[k:k + 3, :] = done[base:base + 3, 0:own]
    cm_out[0:2, :] = done[30:32, 0:own]
    cm_out[2:3, :] = done[7:8, 0:own]
    cr_out[...] = done[6:7, 0:own]
    stores[1].start()
    stores[2].start()
    for store in stores:
        store.wait()


def per_device(sizes, basis_init, permeability, accumulation, pressure, source, support, block_of, curve_rank):
    lx, plane = sizes
    gn, hn = 2 ** len(G_BITS), 2 ** len(H_BITS)
    devices = lx * plane
    own = (curve_rank.shape[0] + devices - 1) // devices
    width = (own + 3) // 4
    flat = lambda v: v.reshape(v.shape[:-3] + (128, 128))
    t_rows = -(-curve_rank.shape[0] // 2048) * 16
    anywhere = pl.BlockSpec(memory_space=pl.ANY)
    vmem = pl.BlockSpec(memory_space=pltpu.VMEM)
    dma = pltpu.SemaphoreType.DMA
    cells = lambda *lead: pltpu.VMEM(lead + (128, 128), F32)
    basis, rows = pl.pallas_call(
        functools.partial(kernel, (lx, plane, own, width)),
        out_shape=(
            jax.ShapeDtypeStruct((8, 128, 128), F32),
            jax.ShapeDtypeStruct((16, 128), F32),
        ),
        in_specs=[anywhere] * 8,
        out_specs=(anywhere, vmem),
        scratch_shapes=[
            cells(8), pltpu.VMEM((8, 128, 128), I32), cells(), cells(), cells(),
            pltpu.VMEM((3, 8, 128), I32), pltpu.VMEM(curve_rank.shape, I32), pltpu.VMEM((t_rows, 128), I32),
            cells(9), cells(8), cells(8), cells(8), cells(12),
            pltpu.VMEM((2, 8, 128), F32), cells(10), pltpu.VMEM((4, 8, 128), F32),
            pltpu.VMEM((9, 32, 128), F32), cells(4),
            pltpu.VMEM((2, 5, 16, 128), F32), pltpu.VMEM((2, 5, 16, 128), F32), pltpu.VMEM((2, 5, 8, 128), F32),
            pltpu.VMEM((2, 4, 16, 128), F32), pltpu.VMEM((2, 4, 16, 128), F32), pltpu.VMEM((2, 4, 8, 128), F32),
            pltpu.VMEM((1, 128), I32), pltpu.VMEM((gn, 1, 128), I32),
            pltpu.VMEM((128, 128), I32), pltpu.VMEM((gn * 128, 640), BF16),
            pltpu.VMEM((64, gn * 128), BF16), pltpu.VMEM((4, 128, 128), F32),
            pltpu.VMEM((13, 128), F32), pltpu.VMEM((gn, 13, 128), F32),
            pltpu.VMEM((hn, width, 128), F32), pltpu.VMEM((hn, width, 128), F32),
            pltpu.SemaphoreType.REGULAR, pltpu.SemaphoreType.REGULAR, dma((12,)), dma((1,)), dma((4,)), dma((4,)),
            dma, dma, dma, dma, dma, dma,
        ],
        compiler_params=pltpu.CompilerParams(
            collective_id=0, has_side_effects=True, vmem_limit_bytes=VMEM_GRANT),
        cost_estimate=pl.CostEstimate(flops=20_000_000, bytes_accessed=2_000_000, transcendentals=0),
    )(*(pltpu.with_memory_space_constraint(v, pltpu.HBM) for v in (
        flat(basis_init), flat(permeability), flat(accumulation), flat(pressure), flat(source),
        flat(support), flat(block_of), curve_rank,
    )))
    basis, matrix, residual = pl.pallas_call(
        functools.partial(finish, own, width),
        out_shape=(
            jax.ShapeDtypeStruct((8, 128, 128), F32),
            jax.ShapeDtypeStruct((27, own), F32),
            jax.ShapeDtypeStruct((1, own), F32),
        ),
        in_specs=[anywhere, vmem],
        out_specs=(anywhere, anywhere, anywhere),
        scratch_shapes=[cells(), pltpu.VMEM((27, own), F32), pltpu.VMEM((1, own), F32), dma((3,))],
        compiler_params=pltpu.CompilerParams(vmem_limit_bytes=VMEM_GRANT),
    )(basis, rows)
    return basis.reshape(basis_init.shape), matrix, residual.reshape(own)


def solution(mesh):
    return jax.shard_map(
        functools.partial(per_device, (mesh.shape["layer"], mesh.shape["plane"])),
        mesh=mesh,
        in_specs=(
            P(None, "layer", "plane", None),
            P("layer", "plane", None),
            P("layer", "plane", None),
            P("layer", "plane", None),
            P("layer", "plane", None),
            P(None, "layer", "plane", None),
            P("layer", "plane", None),
            P(),
        ),
        out_specs=(
            P(None, "layer", "plane", None),
            P(None, ("layer", "plane")),
            P(("layer", "plane")),
        ),
        check_vma=False,
    )
```
